32 devices in a mesh: dp: 4 (over y, x), expert: 8 (over z, core).
Axes of the slice: x: 2, y: 2, z: 4, core: 2. Of those that a mesh axis runs over, the one named last changes fastest.
Arguments:
- tokens: bfloat16 [4096, 1024], P(('dp', 'expert')), may hold values from -6 to 6
- cotangent: bfloat16 [4096, 1024], P(('dp', 'expert')), may hold values from -6 to 6
- gain_attention: float32 [1024], replicated, may hold values from 0.5 to 1.5
- gain_feedforward: float32 [1024], replicated, may hold values from 0.5 to 1.5
- query_weight: bfloat16 [1024, 512], replicated, may hold values from -0.1875 to 0.1875
- key_weight: bfloat16 [1024, 512], replicated, may hold values from -0.1875 to 0.1875
- value_weight: bfloat16 [1024, 2560], replicated, may hold values from -0.1875 to 0.1875
- output_weight: bfloat16 [2560, 1024], replicated, may hold values from -2 to 2
- value_router: bfloat16 [1024, 20], replicated, may hold values from -0.125 to 0.125
- output_router: bfloat16 [1024, 20], replicated, may hold values from -0.125 to 0.125
- expert_router: bfloat16 [1024, 96], replicated, may hold values from -0.09375 to 0.09375
- expert_first: bfloat16 [96, 1024, 128], P(('dp', 'expert')), may hold values from -0.1875 to 0.1875
- expert_second: bfloat16 [96, 128, 1024], P(('dp', 'expert')), may hold values from -0.5 to 0.5
- segments: int32 [32, 128], P(('dp', 'expert')), may hold values from 0 to 3, never falling along the last dimension, each value on 1 to 64 neighbouring positions
- value_ids: int32 [1, 4096, 4, 2], P(None, ('dp', 'expert')), may hold values from 0 to 4, all different within a row
- output_ids: int32 [1, 4096, 4, 2], P(None, ('dp', 'expert')), may hold values from 0 to 4, all different within a row
- ffn_ids: int32 [1, 4096, 16], P(None, ('dp', 'expert')), may hold values from 0 to 95, all different within a row; in each aligned block of 128 rows (0 to 127, 128 to 255, ..., all dimensions but the last counted through in order) at most 32 rows name the same one
Outputs:
- block_output: bfloat16 [4096, 1024], P(('dp', 'expert'))
- input_gradient: float32 [4096, 1024], P(('dp', 'expert'))
- gain_attention_gradient: float32 [1024], replicated
- gain_feedforward_gradient: float32 [1024], replicated
- query_gradient: float32 [1024, 512], replicated
- key_gradient: float32 [1024, 512], replicated
- value_gradient: float32 [1024, 2560], replicated
- output_gradient: float32 [2560, 1024], replicated
- value_router_gradient: float32 [1024, 20], replicated
- output_router_gradient: float32 [1024, 20], replicated
- expert_router_gradient: float32 [1024, 96], replicated
- first_gradient: float32 [96, 1024, 128], P(('dp', 'expert'))
- second_gradient: float32 [96, 128, 1024], P(('dp', 'expert'))
The draws below stay inside these ranges and needn't reach their ends.
Inputs may be any that keep to these rules, and one draw needn't show every extreme that they name: `ffn_ids`: in each repeat, among the 128 rows of one device no expert is named by more than 32 rows, a bound that some block reaches; the 16 experts of a row differ. `value_ids`: the 2 experts of one token and head differ. `output_ids`: the 2 experts of one token and head differ. `segments`: along a sequence the numbers never fall; every document has 1 to 64 tokens, one exactly that many.
All inputs are finite; a program needn't handle non-finite values.
Results may differ from the reference program's by a relative error of at most 0.015.
The reference program's roundings to bfloat16 on the way count: a program that leaves them out, or rounds other values in their place, can miss the bound.
Values may be sent and summed in bfloat16 or wider, within the bound.
A program may use at most 192 MiB of HBM per device.

```python
import math
from functools import partial
import jax
import jax.numpy as jnp
import numpy as np
from jax import lax

D = 1024
HEADS = 4
HEAD = 128
ATT_EXP = 5
ATT_TOP = 2
EXPERT_W = 128
TOPK = 16
REPEATS = 1
DOCS = 4
TOK_DEV = 128
NSEQ = 32
TOKENS = 4096
EXPERTS = 96
CAP = 32


def block_levels(key, shape, shards, least, top_value):
    loudness, own = 1.0, jax.random.fold_in(key, 6)
    for dim, blocks in shards:
        steps = jnp.exp(jax.random.uniform(jax.random.fold_in(own, dim), (blocks,), jnp.float32, least / len(shards), top_value / len(shards)))
        loudness = loudness * jnp.repeat(steps, shape[dim] // blocks).reshape([-1 if axis == dim else 1 for axis in range(len(shape))])
    return loudness


def choose_distinct(stream_key, rows, amount, top, lift):
    ranking = jax.random.permutation(jax.random.fold_in(stream_key, 1), amount)
    pull = ranking
    for power in range(3):
        pull = pull * pull // amount
    pull = pull * lift // amount
    tickets = jax.random.randint(jax.random.fold_in(stream_key, 2), (rows, amount), 0, 4096) + pull
    sure = jax.random.permutation(jax.random.fold_in(stream_key, 3), rows)[jnp.arange(amount) % rows]
    tickets = jnp.where(jnp.arange(rows)[:, None] == sure[None, :], 1 << 14, tickets)
    priority = tickets * amount + jnp.arange(amount)
    return lax.top_k(priority.astype(jnp.int32), top)[1].astype(jnp.int32)


def profile(amount, total, most, skew):
    loads = [(1 << 20) // math.isqrt(standing ** skew) + 1 for standing in range(2, amount + 1)]
    surplus, given = total - most - (amount - 1), [1] * (amount - 1)
    while surplus > 0:
        free = [i for i in range(amount - 1) if given[i] < most]
        pool, budget = sum([loads[i] for i in free]), surplus
        for i in free:
            more = min(most - given[i], max(1, budget * loads[i] // pool), surplus)
            given[i] = given[i] + more
            surplus = surplus - more
    return np.array([most] + given)


def ragged(stream_key, count, total, reach, slope):
    if count == 2:
        one = jax.random.randint(stream_key, (), max(1, total - reach), min(reach, total - 1) + 1)
        return jnp.stack([one, total - one])
    tallies = jnp.asarray(profile(count, total, reach, slope), jnp.int32)
    pairs = (count - 1) // 2
    giver, taker = tallies[1:1 + 2 * pairs:2], tallies[2:2 + 2 * pairs:2]
    room = jnp.minimum(giver - 1, reach - taker)
    passed = jax.random.randint(jax.random.fold_in(stream_key, 1), (pairs,), 0, 1 << 20) % (room + 1)
    tallies = tallies.at[1:1 + 2 * pairs:2].set(giver - passed).at[2:2 + 2 * pairs:2].set(taker + passed)
    return tallies[jax.random.permutation(jax.random.fold_in(stream_key, 2), count)]


def deal_out(stream_key, own, number, rows, number_of, top, bound, skew):
    order = jax.random.permutation(stream_key, number_of)
    heavy_load, common = shares(number_of, rows * top, bound, skew, True), shares(number_of, rows * top, bound, skew, False)
    places = jnp.arange(number_of)

    def named(lengths, rotation):
        used = int((lengths > 0).sum())
        fixed = max(1, used // 4)
        moved = fixed + (places - fixed + rotation * (used - fixed)) % max(1, number_of - fixed)
        return jnp.zeros((number_of,), jnp.int32).at[order[jnp.where(places < fixed, places, moved)]].set(jnp.asarray(lengths, jnp.int32))

    lengths = jnp.where(number % 4 == 0, named(heavy_load, number // 4), named(common, number - number // 4 - 1))
    mixed = jax.random.permutation(jax.random.fold_in(own, 3), number_of)
    source_of, receiver = mixed[0:number_of // 2 * 2:2], mixed[1:number_of // 2 * 2:2]
    slack = jnp.minimum(lengths[source_of] - 1, bound - lengths[receiver]) // 2
    slack = jnp.where((source_of == order[0]) | (receiver == order[0]) | (lengths[receiver] == 0), 0, jnp.maximum(slack, 0))
    moved = jax.random.randint(jax.random.fold_in(own, 4), (number_of // 2,), 0, 1 << 20) % (slack + 1)
    lengths = lengths.at[source_of].add(-moved).at[receiver].add(moved)
    members = jnp.searchsorted(jnp.cumsum(lengths), jnp.arange(rows * top), side="right").astype(jnp.int32)
    table = members.reshape(top, rows).T
    table = table[jax.random.permutation(jax.random.fold_in(own, 1), rows)]
    rotation = jax.random.randint(jax.random.fold_in(own, 2), (rows, 1), 0, top)
    return jnp.take_along_axis(table, (jnp.arange(top)[None, :] + rotation) % top, axis=1)


def shares(count, total, limit, slope, full):
    loads = [(1 << 20) // math.isqrt(rank ** slope) + 1 for rank in range(1, count + 1)]
    largest = limit if full else min(limit, max(-(-total // count), total * loads[0] // sum(loads)))
    least = 1 if total - largest >= count - 1 else 0
    given, surplus = [largest] + [least] * (count - 1), total - largest - least * (count - 1)
    while surplus > 0:
        candidates = [i for i in range(1, count) if given[i] < largest] or [i for i in range(1, count) if given[i] < limit]
        pool, left = sum([loads[i] for i in candidates]), surplus
        for i in candidates:
            extra = min(limit - given[i], max(1, left * loads[i] // pool), surplus)
            given[i] = given[i] + extra
            surplus = surplus - extra
    return np.array(given)


def gaussian(key, dims, deviation, reach, shards=(), kind=jnp.bfloat16):
    factor_of = block_levels(key, dims, shards, -0.22, 0.18) if shards else 1.0
    entries = jax.random.normal(key, dims, jnp.float32) * deviation * factor_of
    return jnp.minimum(jnp.maximum(entries, -reach), reach).astype(kind)


def setup_inputs(seed: int = 0) -> dict:
    key_of = jax.random.split(jax.random.key(seed), 18)
    tokens = gaussian(key_of[0], (TOKENS, D), 1.0, 6.0, ((0, 32),))
    cotangent = gaussian(key_of[1], (TOKENS, D), 1.0, 6.0, ((0, 32),))
    gain_attention = jnp.clip(1.0 + 0.1 * jax.random.normal(key_of[2], (D,), jnp.float32), 0.5, 1.5)
    gain_feedforward = jnp.clip(1.0 + 0.1 * jax.random.normal(key_of[3], (D,), jnp.float32), 0.5, 1.5)
    query_weight = gaussian(key_of[4], (D, HEADS * HEAD), D ** -0.5, 0.1875)
    key_weight = gaussian(key_of[5], (D, HEADS * HEAD), D ** -0.5, 0.1875)
    value_weight = gaussian(key_of[6], (D, HEADS * ATT_EXP * HEAD), D ** -0.5, 0.1875)
    output_weight = gaussian(key_of[7], (HEADS * ATT_EXP * HEAD, D), (max(HEAD // 16, 1)) ** -0.5, 2.0)
    value_router = gaussian(key_of[8], (D, HEADS * ATT_EXP), (2 * D) ** -0.5, 0.125)
    output_router = gaussian(key_of[9], (D, HEADS * ATT_EXP), (2 * D) ** -0.5, 0.125)
    expert_router = gaussian(key_of[10], (D, EXPERTS), (4 * D) ** -0.5, 0.09375)
    expert_first = gaussian(key_of[11], (EXPERTS, D, EXPERT_W), D ** -0.5, 0.1875, ((0, 32),))
    expert_second = gaussian(key_of[12], (EXPERTS, EXPERT_W, D), EXPERT_W ** -0.5, 0.5, ((0, 32),))
    segments = jax.vmap(lambda own: jnp.searchsorted(jnp.cumsum(ragged(own, DOCS, TOK_DEV, TOK_DEV // 2, 1)), jnp.arange(TOK_DEV), side="right"))(jax.random.split(key_of[13], NSEQ)).reshape((NSEQ, TOK_DEV)).astype(jnp.int32)
    value_ids = choose_distinct(key_of[14], REPEATS * TOKENS * HEADS, ATT_EXP, ATT_TOP, 0).reshape((REPEATS, TOKENS, HEADS, ATT_TOP))
    output_ids = choose_distinct(key_of[15], REPEATS * TOKENS * HEADS, ATT_EXP, ATT_TOP, 0).reshape((REPEATS, TOKENS, HEADS, ATT_TOP))
    ffn_ids_keys = jax.random.split(jax.random.fold_in(key_of[16], 1), REPEATS * TOKENS // TOK_DEV)
    ffn_ids_turns = jax.random.permutation(jax.random.fold_in(key_of[16], 3), REPEATS * TOKENS // TOK_DEV)
    ffn_ids = jax.vmap(lambda own, number: deal_out(jax.random.fold_in(key_of[16], 2), own, number, TOK_DEV, EXPERTS, TOPK, CAP, 1))(ffn_ids_keys, ffn_ids_turns).reshape((REPEATS, TOKENS, TOPK))
    return dict(tokens=tokens, cotangent=cotangent, gain_attention=gain_attention, gain_feedforward=gain_feedforward, query_weight=query_weight, key_weight=key_weight, value_weight=value_weight, output_weight=output_weight, value_router=value_router, output_router=output_router, expert_router=expert_router, expert_first=expert_first, expert_second=expert_second, segments=segments, value_ids=value_ids, output_ids=output_ids, ffn_ids=ffn_ids)


@jax.custom_vjp
def low(v):
    return lax.optimization_barrier(v.astype(jnp.bfloat16)).astype(jnp.float32)

@jax.custom_vjp
def low_back(v):
    return v

def low_keep(v):
    return (low(v), None)

def low_pass(kept, grad):
    return (grad,)

def back_keep(v):
    return (v, None)

def back_low(kept, grad):
    return (low(grad),)
low.defvjp(low_keep, low_pass)
low_back.defvjp(back_keep, back_low)
HIGHEST_PRECISION = lax.Precision.HIGHEST
NEG_FILL = -1000000000.0

def matmul(left, right):
    return jnp.dot(left, right, precision=HIGHEST_PRECISION)

def contract(formula, left, right):
    return jnp.einsum(formula, left, right, precision=HIGHEST_PRECISION)

def layer_norm(stream, norm_gain):
    average = lax.optimization_barrier(jnp.mean(stream, axis=-1, keepdims=True))
    centred = stream - average
    variance = lax.optimization_barrier(jnp.mean(centred * centred, axis=-1, keepdims=True))
    return centred * lax.rsqrt(variance + 1e-05) * norm_gain

def expert_mask(picked_ids, expert_count):
    matches = picked_ids[..., None] == jnp.arange(expert_count, dtype=jnp.int32)
    return lax.optimization_barrier(jnp.sum(matches.astype(jnp.float32), axis=-2))

def slot_tables(picked_ids, expert_count, capacity):
    flat_ids = picked_ids.reshape(-1).astype(jnp.int32)
    onehot = (flat_ids[:, None] == jnp.arange(expert_count, dtype=jnp.int32)[None, :]).astype(jnp.int32)
    before = (jnp.cumsum(onehot, axis=0) - onehot).astype(jnp.int32)
    within = lax.optimization_barrier(jnp.sum(before * onehot, axis=1)).astype(jnp.int32)
    target = (flat_ids * capacity + within).astype(jnp.int32)
    owners = jnp.full((expert_count * capacity,), -1, jnp.int32).at[target].set(jnp.arange(flat_ids.shape[0], dtype=jnp.int32))
    return (target, owners)

def pick_rows(table, index):
    return table[index]

def one_repeat(stream, document_ids, value_picks, output_picks, expert_picks, params):
    gain_attention, gain_feedforward, query_weight, key_weight, value_weight, output_weight, value_router, output_router, expert_router, expert_first, expert_second = params
    groups, length, model_width = stream.shape
    normed = low(layer_norm(stream, gain_attention))
    queries = low(low_back(matmul(normed, query_weight))).reshape(groups, length, HEADS, HEAD)
    key_rows = low(low_back(matmul(normed, key_weight))).reshape(groups, length, HEADS, HEAD)
    value_sig = jax.nn.sigmoid(low_back(matmul(normed, value_router))).reshape(groups, length, HEADS, ATT_EXP)
    output_sig = jax.nn.sigmoid(low_back(matmul(normed, output_router))).reshape(groups, length, HEADS, ATT_EXP)
    value_gates = expert_mask(value_picks, ATT_EXP) * value_sig
    output_gates = expert_mask(output_picks, ATT_EXP) * output_sig
    projected = low_back(matmul(low(stream), value_weight)).reshape(groups, length, HEADS, ATT_EXP, HEAD)
    values = low(low_back(lax.optimization_barrier(jnp.sum(value_gates[..., None] * projected, axis=3))))
    scores = low_back(contract('gqhd,gkhd->ghqk', queries, key_rows) * (1.0 / math.sqrt(HEAD)))
    positions = jnp.arange(length, dtype=jnp.int32)
    causal = positions[:, None] >= positions[None, :]
    allowed = (document_ids[:, :, None] == document_ids[:, None, :]) & causal[None]
    scores = jnp.where(allowed[:, None], scores, NEG_FILL)
    probability = low(jax.nn.softmax(scores, axis=-1))
    mixed = low_back(contract('ghqk,gkhd->gqhd', probability, values))
    gated_rows = low(low_back(output_gates[..., None] * mixed[:, :, :, None, :]))
    gated_rows = gated_rows.reshape(groups, length, HEADS * ATT_EXP * HEAD)
    after_attention = stream + low_back(matmul(gated_rows, output_weight))
    normed_ffn = low(layer_norm(after_attention, gain_feedforward))
    logits = low_back(matmul(normed_ffn, expert_router))
    chosen = jnp.take_along_axis(logits, expert_picks, axis=2)
    gate_values = low(low_back(jax.nn.sigmoid(chosen)))
    target, owners = jax.vmap(partial(slot_tables, expert_count=EXPERTS, capacity=CAP))(expert_picks)
    present = owners >= 0
    source = jnp.where(present, owners, 0) // TOPK
    packet = jax.vmap(pick_rows)(low(after_attention), source)
    packet = low_back(jnp.where(present[..., None], packet, 0.0)).reshape(groups, EXPERTS, CAP, model_width)
    hidden_pre = low_back(contract('gecd,edf->gecf', packet, expert_first))
    hidden = low(jax.nn.gelu(hidden_pre))
    result = low(low_back(contract('gecf,efd->gecd', hidden, expert_second)))
    result = result.reshape(groups, EXPERTS * CAP, model_width)
    returned = jax.vmap(pick_rows)(result, target).reshape(groups, length, TOPK, model_width)
    feedforward = low_back(contract('gsk,gskd->gsd', gate_values, returned))
    return after_attention + feedforward

def forward(tokens, gain_attention, gain_feedforward, query_weight, key_weight, value_weight, output_weight, value_router, output_router, expert_router, expert_first, expert_second, segments, value_ids, output_ids, ffn_ids):
    params = (gain_attention, gain_feedforward, query_weight, key_weight, value_weight, output_weight, value_router, output_router, expert_router, expert_first, expert_second)
    group_size = math.gcd(NSEQ, max(1, 1024 // TOK_DEV))
    blocks = NSEQ // group_size
    stream = tokens.reshape(blocks, group_size, TOK_DEV, D)
    document_ids = segments.reshape(blocks, group_size, TOK_DEV)

    def block_step(packed):
        return one_repeat(packed[0], packed[1], packed[2], packed[3], packed[4], params)
    checked = jax.checkpoint(block_step)
    for repeat_index in range(REPEATS):
        value_picks = value_ids[repeat_index].reshape(blocks, group_size, TOK_DEV, HEADS, ATT_TOP)
        output_picks = output_ids[repeat_index].reshape(blocks, group_size, TOK_DEV, HEADS, ATT_TOP)
        expert_picks = ffn_ids[repeat_index].reshape(blocks, group_size, TOK_DEV, TOPK)
        stream = lax.map(checked, (stream, document_ids, value_picks, output_picks, expert_picks))
    return stream.reshape(TOKENS, D)

def reference(tokens, cotangent, gain_attention, gain_feedforward, query_weight, key_weight, value_weight, output_weight, value_router, output_router, expert_router, expert_first, expert_second, segments, value_ids, output_ids, ffn_ids):
    floats = (tokens.astype(jnp.float32), gain_attention.astype(jnp.float32), gain_feedforward.astype(jnp.float32), query_weight.astype(jnp.float32), key_weight.astype(jnp.float32), value_weight.astype(jnp.float32), output_weight.astype(jnp.float32), value_router.astype(jnp.float32), output_router.astype(jnp.float32), expert_router.astype(jnp.float32), expert_first.astype(jnp.float32), expert_second.astype(jnp.float32))

    def run(*inputs_float):
        return forward(*inputs_float, segments, value_ids, output_ids, ffn_ids)
    final, pullback = jax.vjp(run, *floats)
    gradients = pullback(cotangent.astype(jnp.float32))
    return (final.astype(jnp.bfloat16), gradients[0], gradients[1], gradients[2], gradients[3], gradients[4], gradients[5], gradients[6], gradients[7], gradients[8], gradients[9], gradients[10], gradients[11])
```

```python
import math

import jax
import jax.numpy as jnp
from jax import lax
from jax.sharding import PartitionSpec as P

HEADS = 4
HEAD = 128
ATT_EXP = 5


NEG_FILL = -1000000000.0


def layer_norm(stream, norm_gain):
    average = jnp.mean(stream, axis=-1, keepdims=True)
    centred = stream - average
    variance = jnp.mean(centred * centred, axis=-1, keepdims=True)
    return centred * lax.rsqrt(variance + 1e-05) * norm_gain


def expert_mask(picked_ids, expert_count):
    matches = picked_ids[..., None] == jnp.arange(expert_count, dtype=jnp.int32)
    return jnp.sum(matches.astype(jnp.float32), axis=-2)


def attention_forward(stream, document_ids, value_picks, output_picks, shared):
    (
        gain_attention,
        query_weight,
        key_weight,
        value_weight,
        output_weight,
        value_router,
        output_router,
    ) = shared
    length = stream.shape[0]
    normed_low = layer_norm(stream, gain_attention).astype(jnp.bfloat16)
    queries = (
        jnp.dot(normed_low, query_weight, preferred_element_type=jnp.float32)
        .astype(jnp.bfloat16)
        .reshape(length, HEADS, HEAD)
    )
    key_rows = (
        jnp.dot(normed_low, key_weight, preferred_element_type=jnp.float32)
        .astype(jnp.bfloat16)
        .reshape(length, HEADS, HEAD)
    )
    value_sig = jax.nn.sigmoid(
        jnp.dot(normed_low, value_router, preferred_element_type=jnp.float32)
    ).reshape(length, HEADS, ATT_EXP)
    output_sig = jax.nn.sigmoid(
        jnp.dot(normed_low, output_router, preferred_element_type=jnp.float32)
    ).reshape(length, HEADS, ATT_EXP)
    value_mask = expert_mask(value_picks, ATT_EXP)
    output_mask = expert_mask(output_picks, ATT_EXP)
    value_gates = value_mask * value_sig
    output_gates = output_mask * output_sig
    stream_low = stream.astype(jnp.bfloat16)
    projected = jnp.dot(stream_low, value_weight, preferred_element_type=jnp.float32).reshape(
        length, HEADS, ATT_EXP, HEAD
    )
    values = jnp.sum(value_gates[..., None] * projected, axis=2).astype(jnp.bfloat16)
    scores = jnp.einsum("qhd,khd->hqk", queries, key_rows, preferred_element_type=jnp.float32) * (
        1.0 / math.sqrt(HEAD)
    )
    positions = jnp.arange(length, dtype=jnp.int32)
    allowed = (document_ids[:, None] == document_ids[None, :]) & (
        positions[:, None] >= positions[None, :]
    )
    scores = jnp.where(allowed[None], scores, NEG_FILL)
    row_max = jnp.max(scores, axis=-1, keepdims=True)
    exponent = jnp.exp(scores - row_max)
    row_total = jnp.sum(exponent, axis=-1, keepdims=True)
    probability = exponent / row_total
    weights_low = probability.astype(jnp.bfloat16)
    mixed = jnp.einsum("hqk,khd->qhd", weights_low, values, preferred_element_type=jnp.float32)
    gated_rows = (
        (output_gates[..., None] * mixed[:, :, None, :])
        .reshape(length, HEADS * ATT_EXP * HEAD)
        .astype(jnp.bfloat16)
    )
    after_attention = stream + jnp.dot(
        gated_rows, output_weight, preferred_element_type=jnp.float32
    )
    saved_parts = (
        normed_low,
        queries,
        key_rows,
        value_sig,
        output_sig,
        value_mask,
        output_mask,
        value_gates,
        output_gates,
        stream_low,
        projected,
        values,
        probability,
        weights_low,
        mixed,
        gated_rows,
    )
    return (after_attention, saved_parts)


def attention_backward(after_grad, saved_parts, stream, shared):
    (
        gain_attention,
        query_weight,
        key_weight,
        value_weight,
        output_weight,
        value_router,
        output_router,
    ) = shared
    (
        normed_low,
        queries,
        key_rows,
        value_sig,
        output_sig,
        value_mask,
        output_mask,
        value_gates,
        output_gates,
        stream_low,
        projected,
        values,
        probability,
        weights_low,
        mixed,
        gated_rows,
    ) = saved_parts
    length = after_grad.shape[0]
    scale = 1.0 / math.sqrt(HEAD)
    after_low = after_grad.astype(jnp.bfloat16)
    output_part = jnp.einsum("sa,sb->ab", gated_rows, after_low, preferred_element_type=jnp.float32)
    gated_grad = jnp.einsum(
        "sb,ab->sa", after_low, output_weight, preferred_element_type=jnp.float32
    ).astype(jnp.bfloat16)
    gated_grad = gated_grad.reshape(length, HEADS, ATT_EXP, HEAD).astype(jnp.float32)
    mixed_grad = jnp.sum(output_gates[..., None] * gated_grad, axis=2).astype(jnp.bfloat16)
    output_gate_grad = jnp.sum(gated_grad * mixed[:, :, None, :], axis=3)
    prob_grad = jnp.einsum("qhd,khd->hqk", mixed_grad, values, preferred_element_type=jnp.float32)
    values_grad = jnp.einsum(
        "hqk,qhd->khd", weights_low, mixed_grad, preferred_element_type=jnp.float32
    ).astype(jnp.bfloat16)
    values_grad = values_grad.astype(jnp.float32)
    score_grad = (
        probability * (prob_grad - jnp.sum(probability * prob_grad, axis=-1, keepdims=True))
    ).astype(jnp.bfloat16)
    query_grad = (
        (
            jnp.einsum("hqk,khd->qhd", score_grad, key_rows, preferred_element_type=jnp.float32)
            * scale
        )
        .astype(jnp.bfloat16)
        .reshape(length, HEADS * HEAD)
    )
    key_grad = (
        (
            jnp.einsum("hqk,qhd->khd", score_grad, queries, preferred_element_type=jnp.float32)
            * scale
        )
        .astype(jnp.bfloat16)
        .reshape(length, HEADS * HEAD)
    )
    projected_grad = (
        (value_gates[..., None] * values_grad[:, :, None, :])
        .astype(jnp.bfloat16)
        .reshape(length, HEADS * ATT_EXP * HEAD)
    )
    value_gate_grad = jnp.sum(values_grad[:, :, None, :] * projected, axis=3)
    value_logit_grad = (
        (value_gate_grad * value_mask * value_sig * (1.0 - value_sig))
        .astype(jnp.bfloat16)
        .reshape(length, HEADS * ATT_EXP)
    )
    output_logit_grad = (
        (output_gate_grad * output_mask * output_sig * (1.0 - output_sig))
        .astype(jnp.bfloat16)
        .reshape(length, HEADS * ATT_EXP)
    )
    value_part = jnp.einsum(
        "sa,sb->ab", stream_low, projected_grad, preferred_element_type=jnp.float32
    )
    query_part = jnp.einsum("sa,sb->ab", normed_low, query_grad, preferred_element_type=jnp.float32)
    key_part = jnp.einsum("sa,sb->ab", normed_low, key_grad, preferred_element_type=jnp.float32)
    value_router_part = jnp.einsum(
        "sa,sb->ab", normed_low, value_logit_grad, preferred_element_type=jnp.float32
    )
    output_router_part = jnp.einsum(
        "sa,sb->ab", normed_low, output_logit_grad, preferred_element_type=jnp.float32
    )
    normed_grad = jnp.einsum(
        "sb,ab->sa", query_grad, query_weight, preferred_element_type=jnp.float32
    )
    normed_grad = normed_grad + jnp.einsum(
        "sb,ab->sa", key_grad, key_weight, preferred_element_type=jnp.float32
    )
    normed_grad = normed_grad + jnp.einsum(
        "sb,ab->sa", value_logit_grad, value_router, preferred_element_type=jnp.float32
    )
    normed_grad = normed_grad + jnp.einsum(
        "sb,ab->sa", output_logit_grad, output_router, preferred_element_type=jnp.float32
    )
    norm_value, norm_pull = jax.vjp(layer_norm, stream, gain_attention)
    stream_extra, gain_part = norm_pull(normed_grad)
    value_input = jnp.einsum(
        "sb,ab->sa", projected_grad, value_weight, preferred_element_type=jnp.float32
    )
    stream_grad = after_grad + stream_extra + value_input
    return (
        stream_grad,
        (
            gain_part,
            query_part,
            key_part,
            value_part,
            output_part,
            value_router_part,
            output_router_part,
        ),
    )


def expert_pass(rows, upstream_rows, gates, expert_first, expert_second):
    local_count, model_width, hidden_width = expert_first.shape
    wide = local_count * hidden_width
    first = expert_first.transpose(1, 0, 2).reshape(model_width, wide)
    second = expert_second.reshape(wide, model_width)
    gates_wide = jnp.repeat(gates.astype(jnp.float32), hidden_width, axis=1)
    hidden_pre = jnp.dot(rows, first, preferred_element_type=jnp.float32)
    hidden, gelu_pull = jax.vjp(jax.nn.gelu, hidden_pre)
    hidden = hidden.astype(jnp.bfloat16).astype(jnp.float32)
    gated_hidden = (gates_wide * hidden).astype(jnp.bfloat16)
    back = jnp.einsum("sd,fd->sf", upstream_rows, second, preferred_element_type=jnp.float32)
    gate_grad = jnp.sum((back * hidden).reshape(-1, local_count, hidden_width), axis=2)
    pre_grad = gelu_pull(gates_wide * back)[0].astype(jnp.bfloat16)
    result = jnp.dot(gated_hidden, second, preferred_element_type=jnp.float32)
    row_grad = jnp.einsum("sf,df->sd", pre_grad, first, preferred_element_type=jnp.float32)
    second_sum = jnp.einsum(
        "sf,sd->fd", gated_hidden, upstream_rows, preferred_element_type=jnp.float32
    )
    first_sum = jnp.einsum("sd,sf->df", rows, pre_grad, preferred_element_type=jnp.float32)
    first_sum = first_sum.reshape(model_width, local_count, hidden_width).transpose(1, 0, 2)
    return (
        result.astype(jnp.bfloat16),
        row_grad.astype(jnp.bfloat16),
        gate_grad.astype(jnp.bfloat16),
        first_sum,
        second_sum.reshape(expert_second.shape),
    )


BOTH = ("dp", "expert")


def expert_piece(after_low, upstream_low, dense_gates, expert_first, expert_second):
    local_count = expert_first.shape[0]
    me = lax.axis_index("dp") * lax.axis_size("expert") + lax.axis_index("expert")
    upstream_rows = lax.all_gather(upstream_low, BOTH, axis=0, tiled=True)
    rows = lax.all_gather(after_low, BOTH, axis=0, tiled=True)
    gates = lax.all_gather(dense_gates, BOTH, axis=0, tiled=True)
    gates = lax.dynamic_slice_in_dim(gates, me * local_count, local_count, axis=1)
    result, row_grad, gate_grad, first_sum, second_sum = expert_pass(
        rows, upstream_rows, gates, expert_first, expert_second
    )
    gate_back = lax.all_to_all(gate_grad, BOTH, split_axis=0, concat_axis=1, tiled=True)
    token_grad = lax.psum_scatter(row_grad, BOTH, scatter_dimension=0, tiled=True)
    result = lax.psum_scatter(result, BOTH, scatter_dimension=0, tiled=True)
    return (result, token_grad, gate_back), (first_sum, second_sum)


def expert_exchange(after_low, upstream_low, dense_gates, expert_first, expert_second, pieces):
    if pieces == 1:
        back, sums = expert_piece(
            after_low, upstream_low, dense_gates, expert_first, expert_second
        )
        return (*back, *sums)

    def step(totals, piece):
        back, sums = expert_piece(*piece, expert_first, expert_second)
        return (totals[0] + sums[0], totals[1] + sums[1]), back

    cut = lambda array: array.reshape(pieces, -1, array.shape[1])
    start = (
        jnp.zeros(expert_first.shape, jnp.float32),
        jnp.zeros(expert_second.shape, jnp.float32),
    )
    sums, back = lax.scan(step, start, (cut(after_low), cut(upstream_low), cut(dense_gates)))
    return (*(part.reshape(-1, part.shape[2]) for part in back), *sums)


def body(
    tokens,
    cotangent,
    gain_attention,
    gain_feedforward,
    query_weight,
    key_weight,
    value_weight,
    output_weight,
    value_router,
    output_router,
    expert_router,
    expert_first,
    expert_second,
    segments,
    value_ids,
    output_ids,
    ffn_ids,
):
    owner_total = lax.axis_size("dp") * lax.axis_size("expert")
    local_count = expert_first.shape[0]
    expert_count = local_count * owner_total
    shared = (
        gain_attention,
        query_weight,
        key_weight,
        value_weight,
        output_weight,
        value_router,
        output_router,
    )
    stream = tokens.astype(jnp.float32)
    upstream = cotangent.astype(jnp.float32)
    after_attention, saved_parts = attention_forward(
        stream, segments[0], value_ids[0], output_ids[0], shared
    )
    normed_low = layer_norm(after_attention, gain_feedforward).astype(jnp.bfloat16)
    logits = jnp.dot(normed_low, expert_router, preferred_element_type=jnp.float32)
    sigmoid_out = jax.nn.sigmoid(logits)
    mask = expert_mask(ffn_ids[0], expert_count)
    dense_gates = (sigmoid_out * mask).astype(jnp.bfloat16)
    result, token_grad, gate_back, first_sum, second_sum = expert_exchange(
        after_attention.astype(jnp.bfloat16),
        cotangent,
        dense_gates,
        expert_first,
        expert_second,
        max(1, owner_total // 32),
    )
    block_output = (after_attention + result.astype(jnp.float32)).astype(jnp.bfloat16)
    logit_grad = (
        gate_back.astype(jnp.float32) * mask * sigmoid_out * (1.0 - sigmoid_out)
    ).astype(jnp.bfloat16)
    router_sum = jnp.einsum("sa,sb->ab", normed_low, logit_grad, preferred_element_type=jnp.float32)
    normed_grad = jnp.einsum(
        "sb,ab->sa", logit_grad, expert_router, preferred_element_type=jnp.float32
    )
    norm_value, norm_pull = jax.vjp(layer_norm, after_attention, gain_feedforward)
    after_extra, feed_gain_part = norm_pull(normed_grad)
    after_grad = upstream + token_grad.astype(jnp.float32) + after_extra
    stream_grad, attention_parts = attention_backward(after_grad, saved_parts, stream, shared)
    gain_part, query_part, key_part, value_part, output_part, value_router_part, output_router_part = attention_parts
    low = lambda part: part.astype(jnp.bfloat16)
    summed = lax.psum(
        (
            gain_part,
            feed_gain_part,
            low(query_part),
            low(key_part),
            low(value_part),
            low(output_part),
            value_router_part,
            output_router_part,
            router_sum,
        ),
        BOTH,
    )
    return (
        block_output,
        stream_grad,
        *(part.astype(jnp.float32) for part in summed),
        first_sum,
        second_sum,
    )


def solution(mesh):
    placed = (
        P(("dp", "expert"), None),
        P(("dp", "expert"), None),
        P(),
        P(),
        P(),
        P(),
        P(),
        P(),
        P(),
        P(),
        P(),
        P(("dp", "expert"), None, None),
        P(("dp", "expert"), None, None),
        P(("dp", "expert"), None),
        P(None, ("dp", "expert"), None, None),
        P(None, ("dp", "expert"), None, None),
        P(None, ("dp", "expert"), None),
    )
    return jax.shard_map(
        body,
        mesh=mesh,
        in_specs=placed,
        out_specs=(
            P(("dp", "expert"), None),
            P(("dp", "expert"), None),
            P(),
            P(),
            P(),
            P(),
            P(),
            P(),
            P(),
            P(),
            P(),
            P(("dp", "expert"), None, None),
            P(("dp", "expert"), None, None),
        ),
        check_vma=False,
    )
```

```python
import functools
import math

import jax
import jax.numpy as jnp
from jax import lax
from jax.experimental import pallas as pl
from jax.experimental.pallas import tpu as pltpu
from jax.sharding import PartitionSpec as P

HEADS = 4
HEAD = 128
ATT_EXP = 5


NEG_FILL = -1000000000.0


def layer_norm(stream, norm_gain):
    average = jnp.mean(stream, axis=-1, keepdims=True)
    centred = stream - average
    variance = jnp.mean(centred * centred, axis=-1, keepdims=True)
    return centred * lax.rsqrt(variance + 1e-05) * norm_gain


def expert_mask(picked_ids, expert_count):
    matches = picked_ids[..., None] == jnp.arange(expert_count, dtype=jnp.int32)
    return jnp.sum(matches.astype(jnp.float32), axis=-2)


def attention_forward(stream, document_ids, value_picks, output_picks, shared):
    (
        gain_attention,
        query_weight,
        key_weight,
        value_weight,
        output_weight,
        value_router,
        output_router,
    ) = shared
    length = stream.shape[0]
    normed_low = layer_norm(stream, gain_attention).astype(jnp.bfloat16)
    queries = (
        jnp.dot(normed_low, query_weight, preferred_element_type=jnp.float32)
        .astype(jnp.bfloat16)
        .reshape(length, HEADS, HEAD)
    )
    key_rows = (
        jnp.dot(normed_low, key_weight, preferred_element_type=jnp.float32)
        .astype(jnp.bfloat16)
        .reshape(length, HEADS, HEAD)
    )
    value_sig = jax.nn.sigmoid(
        jnp.dot(normed_low, value_router, preferred_element_type=jnp.float32)
    ).reshape(length, HEADS, ATT_EXP)
    output_sig = jax.nn.sigmoid(
        jnp.dot(normed_low, output_router, preferred_element_type=jnp.float32)
    ).reshape(length, HEADS, ATT_EXP)
    value_mask = expert_mask(value_picks, ATT_EXP)
    output_mask = expert_mask(output_picks, ATT_EXP)
    value_gates = value_mask * value_sig
    output_gates = output_mask * output_sig
    stream_low = stream.astype(jnp.bfloat16)
    projected = jnp.dot(stream_low, value_weight, preferred_element_type=jnp.float32).reshape(
        length, HEADS, ATT_EXP, HEAD
    )
    values = jnp.sum(value_gates[..., None] * projected, axis=2).astype(jnp.bfloat16)
    scores = jnp.einsum("qhd,khd->hqk", queries, key_rows, preferred_element_type=jnp.float32) * (
        1.0 / math.sqrt(HEAD)
    )
    positions = jnp.arange(length, dtype=jnp.int32)
    allowed = (document_ids[:, None] == document_ids[None, :]) & (
        positions[:, None] >= positions[None, :]
    )
    scores = jnp.where(allowed[None], scores, NEG_FILL)
    row_max = jnp.max(scores, axis=-1, keepdims=True)
    exponent = jnp.exp(scores - row_max)
    row_total = jnp.sum(exponent, axis=-1, keepdims=True)
    probability = exponent / row_total
    weights_low = probability.astype(jnp.bfloat16)
    mixed = jnp.einsum("hqk,khd->qhd", weights_low, values, preferred_element_type=jnp.float32)
    gated_rows = (
        (output_gates[..., None] * mixed[:, :, None, :])
        .reshape(length, HEADS * ATT_EXP * HEAD)
        .astype(jnp.bfloat16)
    )
    after_attention = stream + jnp.dot(
        gated_rows, output_weight, preferred_element_type=jnp.float32
    )
    saved_parts = (
        normed_low,
        queries,
        key_rows,
        value_sig,
        output_sig,
        value_mask,
        output_mask,
        value_gates,
        output_gates,
        stream_low,
        projected,
        values,
        probability,
        weights_low,
        mixed,
        gated_rows,
    )
    return (after_attention, saved_parts)


def attention_backward(after_grad, saved_parts, stream, shared):
    (
        gain_attention,
        query_weight,
        key_weight,
        value_weight,
        output_weight,
        value_router,
        output_router,
    ) = shared
    (
        normed_low,
        queries,
        key_rows,
        value_sig,
        output_sig,
        value_mask,
        output_mask,
        value_gates,
        output_gates,
        stream_low,
        projected,
        values,
        probability,
        weights_low,
        mixed,
        gated_rows,
    ) = saved_parts
    length = after_grad.shape[0]
    scale = 1.0 / math.sqrt(HEAD)
    after_low = after_grad.astype(jnp.bfloat16)
    output_part = jnp.einsum("sa,sb->ab", gated_rows, after_low, preferred_element_type=jnp.float32)
    gated_grad = jnp.einsum(
        "sb,ab->sa", after_low, output_weight, preferred_element_type=jnp.float32
    ).astype(jnp.bfloat16)
    gated_grad = gated_grad.reshape(length, HEADS, ATT_EXP, HEAD).astype(jnp.float32)
    mixed_grad = jnp.sum(output_gates[..., None] * gated_grad, axis=2).astype(jnp.bfloat16)
    output_gate_grad = jnp.sum(gated_grad * mixed[:, :, None, :], axis=3)
    prob_grad = jnp.einsum("qhd,khd->hqk", mixed_grad, values, preferred_element_type=jnp.float32)
    values_grad = jnp.einsum(
        "hqk,qhd->khd", weights_low, mixed_grad, preferred_element_type=jnp.float32
    ).astype(jnp.bfloat16)
    values_grad = values_grad.astype(jnp.float32)
    score_grad = (
        probability * (prob_grad - jnp.sum(probability * prob_grad, axis=-1, keepdims=True))
    ).astype(jnp.bfloat16)
    query_grad = (
        (
            jnp.einsum("hqk,khd->qhd", score_grad, key_rows, preferred_element_type=jnp.float32)
            * scale
        )
        .astype(jnp.bfloat16)
        .reshape(length, HEADS * HEAD)
    )
    key_grad = (
        (
            jnp.einsum("hqk,qhd->khd", score_grad, queries, preferred_element_type=jnp.float32)
            * scale
        )
        .astype(jnp.bfloat16)
        .reshape(length, HEADS * HEAD)
    )
    projected_grad = (
        (value_gates[..., None] * values_grad[:, :, None, :])
        .astype(jnp.bfloat16)
        .reshape(length, HEADS * ATT_EXP * HEAD)
    )
    value_gate_grad = jnp.sum(values_grad[:, :, None, :] * projected, axis=3)
    value_logit_grad = (
        (value_gate_grad * value_mask * value_sig * (1.0 - value_sig))
        .astype(jnp.bfloat16)
        .reshape(length, HEADS * ATT_EXP)
    )
    output_logit_grad = (
        (output_gate_grad * output_mask * output_sig * (1.0 - output_sig))
        .astype(jnp.bfloat16)
        .reshape(length, HEADS * ATT_EXP)
    )
    value_part = jnp.einsum(
        "sa,sb->ab", stream_low, projected_grad, preferred_element_type=jnp.float32
    )
    query_part = jnp.einsum("sa,sb->ab", normed_low, query_grad, preferred_element_type=jnp.float32)
    key_part = jnp.einsum("sa,sb->ab", normed_low, key_grad, preferred_element_type=jnp.float32)
    value_router_part = jnp.einsum(
        "sa,sb->ab", normed_low, value_logit_grad, preferred_element_type=jnp.float32
    )
    output_router_part = jnp.einsum(
        "sa,sb->ab", normed_low, output_logit_grad, preferred_element_type=jnp.float32
    )
    normed_grad = jnp.einsum(
        "sb,ab->sa", query_grad, query_weight, preferred_element_type=jnp.float32
    )
    normed_grad = normed_grad + jnp.einsum(
        "sb,ab->sa", key_grad, key_weight, preferred_element_type=jnp.float32
    )
    normed_grad = normed_grad + jnp.einsum(
        "sb,ab->sa", value_logit_grad, value_router, preferred_element_type=jnp.float32
    )
    normed_grad = normed_grad + jnp.einsum(
        "sb,ab->sa", output_logit_grad, output_router, preferred_element_type=jnp.float32
    )
    norm_value, norm_pull = jax.vjp(layer_norm, stream, gain_attention)
    stream_extra, gain_part = norm_pull(normed_grad)
    value_input = jnp.einsum(
        "sb,ab->sa", projected_grad, value_weight, preferred_element_type=jnp.float32
    )
    stream_grad = after_grad + stream_extra + value_input
    return (
        stream_grad,
        (
            gain_part,
            query_part,
            key_part,
            value_part,
            output_part,
            value_router_part,
            output_router_part,
        ),
    )


def expert_pass(rows, upstream_rows, gates, expert_first, expert_second):
    local_count, model_width, hidden_width = expert_first.shape
    wide = local_count * hidden_width
    first = expert_first.transpose(1, 0, 2).reshape(model_width, wide)
    second = expert_second.reshape(wide, model_width)
    gates_wide = jnp.repeat(gates.astype(jnp.float32), hidden_width, axis=1)
    hidden_pre = jnp.dot(rows, first, preferred_element_type=jnp.float32)
    hidden, gelu_pull = jax.vjp(jax.nn.gelu, hidden_pre)
    hidden = hidden.astype(jnp.bfloat16).astype(jnp.float32)
    gated_hidden = (gates_wide * hidden).astype(jnp.bfloat16)
    back = jnp.einsum("sd,fd->sf", upstream_rows, second, preferred_element_type=jnp.float32)
    gate_grad = jnp.sum((back * hidden).reshape(-1, local_count, hidden_width), axis=2)
    pre_grad = gelu_pull(gates_wide * back)[0].astype(jnp.bfloat16)
    result = jnp.dot(gated_hidden, second, preferred_element_type=jnp.float32)
    row_grad = jnp.einsum("sf,df->sd", pre_grad, first, preferred_element_type=jnp.float32)
    second_sum = jnp.einsum(
        "sf,sd->fd", gated_hidden, upstream_rows, preferred_element_type=jnp.float32
    )
    first_sum = jnp.einsum("sd,sf->df", rows, pre_grad, preferred_element_type=jnp.float32)
    first_sum = first_sum.reshape(model_width, local_count, hidden_width).transpose(1, 0, 2)
    return (
        result.astype(jnp.bfloat16),
        row_grad.astype(jnp.bfloat16),
        gate_grad.astype(jnp.bfloat16),
        first_sum,
        second_sum.reshape(expert_second.shape),
    )


BOTH = ("dp", "expert")


def expert_piece(after_low, upstream_low, dense_gates, expert_first, expert_second):
    local_count = expert_first.shape[0]
    me = lax.axis_index("dp") * lax.axis_size("expert") + lax.axis_index("expert")
    upstream_rows = lax.all_gather(upstream_low, BOTH, axis=0, tiled=True)
    rows = lax.all_gather(after_low, BOTH, axis=0, tiled=True)
    gates = lax.all_gather(dense_gates, BOTH, axis=0, tiled=True)
    gates = lax.dynamic_slice_in_dim(gates, me * local_count, local_count, axis=1)
    result, row_grad, gate_grad, first_sum, second_sum = expert_pass(
        rows, upstream_rows, gates, expert_first, expert_second
    )
    gate_back = lax.all_to_all(gate_grad, BOTH, split_axis=0, concat_axis=1, tiled=True)
    token_grad = lax.psum_scatter(row_grad, BOTH, scatter_dimension=0, tiled=True)
    result = lax.psum_scatter(result, BOTH, scatter_dimension=0, tiled=True)
    return (result, token_grad, gate_back), (first_sum, second_sum)


def expert_exchange(after_low, upstream_low, dense_gates, expert_first, expert_second, pieces):
    if pieces == 1:
        back, sums = expert_piece(
            after_low, upstream_low, dense_gates, expert_first, expert_second
        )
        return (*back, *sums)

    def step(totals, piece):
        back, sums = expert_piece(*piece, expert_first, expert_second)
        return (totals[0] + sums[0], totals[1] + sums[1]), back

    cut = lambda array: array.reshape(pieces, -1, array.shape[1])
    start = (
        jnp.zeros(expert_first.shape, jnp.float32),
        jnp.zeros(expert_second.shape, jnp.float32),
    )
    sums, back = lax.scan(step, start, (cut(after_low), cut(upstream_low), cut(dense_gates)))
    return (*(part.reshape(-1, part.shape[2]) for part in back), *sums)


MESH = pl.DeviceIdType.MESH
GRID = (4, 8)


class Place:
    def __init__(self):
        dp, expert = lax.axis_index("dp"), lax.axis_index("expert")
        self.y, self.x = dp // 2, dp % 2
        self.z, self.core = expert // 2, expert % 2
        self.dp, self.expert = dp, expert
        self.me = dp * GRID[1] + expert
        self.x_peer = (2 * self.y + 1 - self.x, expert)
        self.y_peer = (2 * (1 - self.y) + self.x, expert)
        self.core_peer = (dp, 2 * self.z + 1 - self.core)

    def z_at(self, j):
        return 2 * ((self.z // 2 + j // 2) % 2) + (self.z % 2 + j % 2) % 2

    def z_peer(self, j):
        return (self.dp, 2 * self.z_at(j) + self.core)

    def peers(self):
        return [self.x_peer, self.y_peer, self.core_peer] + [self.z_peer(j) for j in (1, 2, 3)]

    def chip(self, q, j):
        return ((self.y + q // 2) % 2 * 2 + (self.x + q % 2) % 2) * 4 + self.z_at(j)


def enter(place):
    barrier = pltpu.get_barrier_semaphore()
    peers = place.peers()
    for peer in peers:
        pl.semaphore_signal(barrier, inc=1, device_id=peer, device_id_type=MESH)
    pl.semaphore_wait(barrier, len(peers))


def remote(src, dst, send, recv, peer):
    return pltpu.make_async_remote_copy(
        src_ref=src,
        dst_ref=dst,
        send_sem=send,
        recv_sem=recv,
        device_id=peer,
        device_id_type=MESH,
    )


N_SEM = 35


class Gather:
    def __init__(self, place, buf, rows, split, sems):
        self.place, self.buf, self.rows, self.split = place, buf, rows, split
        self.send, self.recv = sems.at[0], sems.at[1]

    def block(self, q, j, part=None):
        start = (2 * self.place.chip(q, j) + self.place.core) * self.rows
        rows = pl.ds(pl.multiple_of(start, self.rows), self.rows)
        if part == "b":
            return self.buf.at[rows, : self.split]
        if part == "a":
            return self.buf.at[rows, self.split :]
        return self.buf.at[rows]

    def copy(self, kind, j, q=0):
        place = self.place
        if kind == "z":
            ref, number, peer = self.block(0, 0), j - 1, place.z_peer(j)
        elif kind == "x":
            ref, number, peer = self.block(0, j), 3 + j, place.x_peer
        elif kind == "y":
            ref, number, peer = self.block(0, j), 7 + j, place.y_peer
        elif kind == "a":
            ref, number, peer = self.block(1, j, "a"), 11 + j, place.y_peer
        elif kind == "b":
            ref, number, peer = self.block(2, j, "b"), 15 + j, place.x_peer
        else:
            ref, number, peer = self.block(q, j), 19 + 4 * q + j, place.core_peer
        return remote(ref, ref, self.send.at[number], self.recv.at[number], peer)

    def line(self, j, first):
        if not first:
            self.copy("z", j).wait_recv()
        self.copy("x", j).start()
        self.copy("y", j).start()
        self.copy("core", j, 0).start()

    def side_x(self, j):
        self.copy("x", j).wait_recv()
        self.copy("a", j).start()
        self.copy("core", j, 1).start()

    def side_y(self, j):
        self.copy("y", j).wait_recv()
        self.copy("b", j).start()
        self.copy("core", j, 2).start()

    def corner(self, j):
        self.copy("a", j).wait_recv()
        self.copy("b", j).wait_recv()
        self.copy("core", j, 3).start()

    def whole(self, q, j):
        self.copy("core", j, q).wait_recv()

    def finish(self):
        for j in (1, 2, 3):
            self.copy("z", j).wait_send()

        def step(j, carry):
            for kind in ("x", "y", "a", "b"):
                self.copy(kind, j).wait_send()
            for q in range(4):
                self.copy("core", j, q).wait_send()
            return carry

        lax.fori_loop(0, 4, step, 0)


class Reduce:
    def __init__(self, place, own, other, other_in, a_in, b_in, x_in, y_in, z_in, split, sems):
        self.place, self.own, self.other, self.other_in = place, own, other, other_in
        self.a_in, self.b_in, self.x_in, self.y_in, self.z_in = a_in, b_in, x_in, y_in, z_in
        self.split = split
        self.send, self.recv = sems.at[0], sems.at[1]

    def copy(self, kind, k):
        place, split = self.place, self.split
        j = k % 4
        if kind == "core":
            src, dst, number, peer = self.other(k), self.other_in.at[k], k, place.core_peer
        elif kind == "a":
            src, dst, number, peer = self.own(k).at[:, split:], self.a_in.at[j], 16 + j, place.y_peer
        elif kind == "b":
            src, dst, number, peer = self.own(k).at[:, :split], self.b_in.at[j], 20 + j, place.x_peer
        elif kind == "x":
            src, dst, number, peer = self.own(k), self.x_in.at[j], 24 + j, place.x_peer
        elif kind == "y":
            src, dst, number, peer = self.own(k), self.y_in.at[j], 28 + j, place.y_peer
        else:
            src, dst, number, peer = self.own(k), self.z_in.at[j - 1], 31 + j, place.z_peer(j)
        return remote(src, dst, self.send.at[number], self.recv.at[number], peer)

    def add(self, k, columns, terms):
        own = self.own(k)
        rows = own.shape[0]

        def step(number, carry):
            at = pl.ds(pl.multiple_of(number * 16, 16), 16)
            total = own[at, columns].astype(jnp.float32)
            for term in terms:
                total = total + term(at).astype(jnp.float32)
            own[at, columns] = total.astype(own.dtype)
            return carry

        lax.fori_loop(0, rows // 16, step, 0)

    def corner(self, j):
        k = 12 + j
        self.copy("core", k).wait_recv()
        self.add(k, slice(None), [lambda at: self.other_in[k, at, :]])
        self.copy("a", k).start()
        self.copy("b", k).start()

    def side_x(self, j):
        k, split = 4 + j, self.split
        self.copy("core", k).wait_recv()
        self.add(k, slice(0, split), [lambda at: self.other_in[k, at, :split]])
        self.copy("a", k).wait_recv()
        self.add(
            k,
            slice(split, None),
            [lambda at: self.other_in[k, at, split:], lambda at: self.a_in[j, at, :]],
        )
        self.copy("x", k).start()

    def side_y(self, j):
        k, split = 8 + j, self.split
        self.copy("core", k).wait_recv()
        self.add(k, slice(split, None), [lambda at: self.other_in[k, at, split:]])
        self.copy("b", k).wait_recv()
        self.add(
            k,
            slice(0, split),
            [lambda at: self.other_in[k, at, :split], lambda at: self.b_in[j, at, :]],
        )
        self.copy("y", k).start()

    def line(self, j):
        self.copy("core", j).wait_recv()
        self.copy("x", j).wait_recv()
        self.copy("y", j).wait_recv()
        boxes = (self.other_in, self.x_in, self.y_in)
        self.add(j, slice(None), [lambda at, box=box: box[j, at, :] for box in boxes])
        self.copy("z", j).start()

    def last(self, put):
        self.copy("core", 0).wait_recv()
        self.copy("x", 0).wait_recv()
        self.copy("y", 0).wait_recv()
        for j in (1, 2, 3):
            self.copy("z", j).wait_recv()
        own = self.own(0)

        def step(number, carry):
            at = pl.ds(pl.multiple_of(number * 16, 16), 16)
            total = own[at, :].astype(jnp.float32)
            for box in (self.other_in, self.x_in, self.y_in):
                total = total + box[0, at, :].astype(jnp.float32)
            for j in range(3):
                total = total + self.z_in[j, at, :].astype(jnp.float32)
            put(at, total)
            return carry

        lax.fori_loop(0, own.shape[0] // 16, step, 0)

    def finish(self):
        def step(j, carry):
            for kind, q in (("a", 3), ("b", 3), ("x", 1), ("y", 2)):
                self.copy(kind, 4 * q + j).wait_send()
            for q in range(4):
                self.copy("core", 4 * q + j).wait_send()
            return carry

        lax.fori_loop(0, 4, step, 0)
        for j in (1, 2, 3):
            self.copy("z", j).wait_send()


def reduce_scratch(rows, width, split):
    low = jnp.bfloat16
    return [
        pltpu.VMEM((16, rows, width), low),
        pltpu.VMEM((4, rows, width - split), low),
        pltpu.VMEM((4, rows, split), low),
        pltpu.VMEM((4, rows, width), low),
        pltpu.VMEM((4, rows, width), low),
        pltpu.VMEM((3, rows, width), low),
    ]


GELU_C = math.sqrt(2.0 / math.pi)
GELU_K = 0.044715


def mm(left, right):
    return jnp.dot(left, right, preferred_element_type=jnp.float32)


def mm_tn(left, right):
    return lax.dot_general(left, right, (((0,), (0,)), ((), ())), preferred_element_type=jnp.float32)


def expert_kernel(
    model_width,
    local_count,
    packed_ref,
    first_ref,
    first_t_ref,
    second_ref,
    second_t_ref,
    pick_ref,
    rows_out,
    result_out,
    first_out,
    second_out,
    gathered,
    gated_hidden,
    pre_grads,
    partial,
    other_in,
    a_in,
    b_in,
    x_in,
    y_in,
    z_in,
    result_stage,
    gather_sems,
    reduce_sems,
    result_sems,
):
    place = Place()
    length = packed_ref.shape[0]
    pair = 2 * length
    half = model_width // 2
    gate_width = pick_ref.shape[0]
    hidden_width = first_ref.shape[1] // local_count
    split = model_width
    enter(place)
    gather = Gather(place, gathered, length, split, gather_sems)
    gathered[pl.ds(pl.multiple_of(place.me * length, length), length), :] = packed_ref[...]

    def own(k):
        return partial.at[k, pl.ds(pl.multiple_of(place.core * length, length), length)]

    def other(k):
        return partial.at[k, pl.ds(pl.multiple_of((1 - place.core) * length, length), length)]

    reduce = Reduce(
        place,
        own,
        other,
        other_in,
        a_in,
        b_in,
        x_in,
        y_in,
        z_in,
        model_width // 2,
        reduce_sems,
    )

    def result_copy(slot, chip):
        return pltpu.make_async_copy(
            result_stage.at[slot],
            result_out.at[pl.ds(pl.multiple_of(chip * pair, pair), pair)],
            result_sems.at[slot],
        )

    def compute(step, q, j):
        chip = place.chip(q, j)
        rows = pl.ds(pl.multiple_of(chip * pair, pair), pair)
        hidden_pre = mm(gathered[rows, half : half + model_width], first_ref[...])
        back = mm(gathered[rows, :half], second_t_ref[:half])
        back = back + mm(gathered[rows, 3 * half + gate_width :], second_t_ref[half:])
        gates = mm(gathered[rows, 3 * half : 3 * half + gate_width], pick_ref[...])
        square = hidden_pre * hidden_pre
        bent = jnp.tanh(GELU_C * hidden_pre * (1.0 + GELU_K * square))
        grow = 0.5 * (1.0 + bent)
        slope = grow + 0.5 * hidden_pre * (1.0 - bent * bent) * (
            GELU_C * (1.0 + 3.0 * GELU_K * square)
        )
        hidden = (hidden_pre * grow).astype(jnp.bfloat16).astype(jnp.float32)
        gated = (gates * hidden).astype(jnp.bfloat16)
        pre_grad = (gates * back * slope).astype(jnp.bfloat16)
        gated_hidden[rows, :] = gated
        pre_grads[rows, :] = pre_grad
        k = 4 * q + j
        partial[k, :, :model_width] = mm(pre_grad, first_t_ref[...]).astype(jnp.bfloat16)
        product = hidden * back
        column = lax.broadcasted_iota(jnp.int32, (pair, gate_width), 1) - place.me * local_count
        gate_grad = jnp.zeros((pair, gate_width), jnp.float32)
        for e in range(local_count):
            own_sum = jnp.sum(
                product[:, e * hidden_width : (e + 1) * hidden_width], axis=1, keepdims=True
            )
            gate_grad = jnp.where(column == e, own_sum, gate_grad)
        partial[k, :, model_width:] = gate_grad.astype(jnp.bfloat16)
        reduce.copy("core", k).start()
        slot = step % 2

        @pl.when(step >= 2)
        def _():
            result_copy(slot, chip).wait()

        result_stage[slot] = mm(gated, second_ref[...]).astype(jnp.bfloat16)
        result_copy(slot, chip).start()

    gather.copy("z", 1).start()
    gather.line(0, True)
    gather.copy("z", 2).start()
    gather.copy("z", 3).start()

    def arrive(actions):
        for kind, j in actions:
            if kind == "line":
                gather.line(j, False)
            else:
                getattr(gather, kind)(j)

    before = {
        1: [("side_x", 0), ("side_y", 0), ("line", 1)],
        4: [("corner", 0), ("side_x", 1), ("side_y", 1), ("line", 2)],
        8: [("corner", 1), ("side_x", 2), ("side_y", 2), ("line", 3)],
        12: [("corner", 2), ("side_x", 3), ("side_y", 3)],
        15: [("corner", 3)],
    }
    order = [(0, 0), (1, 0), (2, 0), (0, 1), (3, 0), (1, 1), (2, 1), (0, 2)]
    order += [(3, 1), (1, 2), (2, 2), (0, 3), (3, 2), (1, 3), (2, 3), (3, 3)]

    def pick(step, values):
        total = 0
        for number, value in enumerate(values):
            total = total + value * jnp.where(step == number, 1, 0)
        return total

    def walk(step, carry):
        for number, actions in before.items():
            pl.when(step == number)(functools.partial(arrive, actions))
        q = pick(step, [pair_[0] for pair_ in order])
        j = pick(step, [pair_[1] for pair_ in order])
        gather.whole(q, j)
        compute(step, q, j)
        return carry

    lax.fori_loop(0, 16, walk, 0)
    piece = 512
    pieces = gathered.shape[0] // piece

    def weight_piece(number):
        rows = pl.ds(pl.multiple_of(number * piece, piece), piece)
        left = mm_tn(gated_hidden[rows, :], gathered[rows, :half])
        right = mm_tn(gated_hidden[rows, :], gathered[rows, 3 * half + gate_width :])
        first = mm_tn(pre_grads[rows, :], gathered[rows, half : half + model_width])

        @pl.when(number == 0)
        def _():
            second_out[:, :half] = left
            second_out[:, half:] = right
            first_out[...] = first

        @pl.when(number > 0)
        def _():
            second_out[:, :half] += left
            second_out[:, half:] += right
            first_out[...] += first

    def give(step, carry):
        j = 3 - step % 4

        @pl.when(step < 4)
        def _():
            reduce.corner(j)

        @pl.when(step >= 4)
        def _():
            reduce.side_x(j)
            reduce.side_y(j)

        weight_piece(step)
        return carry

    lax.fori_loop(0, pieces, give, 0)
    lax.fori_loop(0, 3, lambda step, carry: (reduce.line(3 - step), carry)[1], 0)

    def put(at, total):
        rows_out[at, :] = total

    reduce.last(put)
    for slot in range(2):
        result_copy(slot, 0).wait()
    gather.finish()
    reduce.finish()


def call_experts(packed, expert_first, expert_second, pick):
    local_count, model_width, hidden_width = expert_first.shape
    wide = local_count * hidden_width
    length, width = packed.shape
    total = GRID[0] * GRID[1] * length
    gate_width = pick.shape[0]
    first = expert_first.transpose(1, 0, 2).reshape(model_width, wide)
    first_t = expert_first.transpose(0, 2, 1).reshape(wide, model_width)
    second = expert_second.reshape(wide, model_width)
    second_t = expert_second.transpose(2, 0, 1).reshape(model_width, wide)
    out_width = model_width + gate_width
    split = model_width // 2
    vmem = pl.BlockSpec(memory_space=pltpu.VMEM)
    flops = 12 * total * model_width * wide
    rows_sum, result, first_sum, second_sum = pl.pallas_call(
        functools.partial(expert_kernel, model_width, local_count),
        out_shape=(
            jax.ShapeDtypeStruct((length, out_width), jnp.float32),
            jax.ShapeDtypeStruct((total, model_width), jnp.bfloat16),
            jax.ShapeDtypeStruct((wide, model_width), jnp.float32),
            jax.ShapeDtypeStruct((wide, model_width), jnp.float32),
        ),
        in_specs=[vmem] * 6,
        out_specs=(vmem, pl.BlockSpec(memory_space=pl.ANY), vmem, vmem),
        scratch_shapes=[
            pltpu.VMEM((total, width), jnp.bfloat16),
            pltpu.VMEM((total, wide), jnp.bfloat16),
            pltpu.VMEM((total, wide), jnp.bfloat16),
            pltpu.VMEM((16, 2 * length, out_width), jnp.bfloat16),
            *reduce_scratch(length, out_width, split),
            pltpu.VMEM((2, 2 * length, model_width), jnp.bfloat16),
            pltpu.SemaphoreType.DMA((2, N_SEM)),
            pltpu.SemaphoreType.DMA((2, N_SEM)),
            pltpu.SemaphoreType.DMA((2,)),
        ],
        compiler_params=pltpu.CompilerParams(
            collective_id=0, has_side_effects=True, vmem_limit_bytes=62 * 2**20
        ),
        cost_estimate=pl.CostEstimate(
            flops=flops, bytes_accessed=4 * total * model_width, transcendentals=total * wide
        ),
        name="experts",
    )(packed, first, first_t, second, second_t, pick)
    first_sum = first_sum.reshape(local_count, hidden_width, model_width).transpose(0, 2, 1)
    return rows_sum, result, first_sum, second_sum.reshape(expert_second.shape)


def sums_kernel(shapes, *refs):
    count = len(shapes)
    ins, refs = refs[:count], refs[count:]
    first_out, outs, refs = refs[0], refs[1:count], refs[count:]
    place = Place()
    enter(place)
    reduces, gathers, loads = [], [], []
    for number, (rows, width, split) in enumerate(shapes):
        held, refs = refs[0], refs[1:]
        boxes, refs = refs[:6], refs[6:]
        sems, load_sem, refs = refs[0], refs[1], refs[2:]

        def source(k, core, rows=rows, ref=ins[number]):
            start = (2 * place.chip(k // 4, k % 4) + core) * rows
            return ref.at[pl.ds(pl.multiple_of(start, rows), rows)]

        reduces.append(
            Reduce(
                place,
                lambda k, held=held: held.at[k],
                lambda k, source=source: source(k, 1 - place.core),
                *boxes,
                split,
                sems,
            )
        )
        loads.append(
            lambda k, source=source, held=held, sem=load_sem: pltpu.make_async_copy(
                source(k, place.core), held.at[k], sem.at[k]
            )
        )
        if number:
            buf, gather_sems, out_sem, refs = refs[0], refs[1], refs[2], refs[3:]
            gathers.append((Gather(place, buf, rows, split, gather_sems), outs[number - 1], out_sem))

    def begin(step, carry):
        k = 15 - step
        for reduce, load in zip(reduces, loads):
            load(k).start()
            reduce.copy("core", k).start()
        return carry

    lax.fori_loop(0, 16, begin, 0)

    def corner(step, carry):
        for reduce, load in zip(reduces, loads):
            load(15 - step).wait()
            reduce.corner(3 - step)
        return carry

    def side(step, carry):
        for reduce, load in zip(reduces, loads):
            load(7 - step).wait()
            load(11 - step).wait()
            reduce.side_x(3 - step)
            reduce.side_y(3 - step)
        return carry

    def line(step, carry):
        for reduce, load in zip(reduces, loads):
            load(3 - step).wait()
            reduce.line(3 - step)
        return carry

    lax.fori_loop(0, 4, corner, 0)
    lax.fori_loop(0, 4, side, 0)
    lax.fori_loop(0, 3, line, 0)
    for number in reversed(range(count)):
        reduce, load = reduces[number], loads[number]
        load(0).wait()
        mine = first_out if number == 0 else gathers[number - 1][0].block(0, 0)

        def put(at, total, mine=mine):
            mine[at, :] = total.astype(mine.dtype)

        reduce.last(put)
        if number == 0:
            continue
        gather = gathers[number - 1][0]
        gather.copy("z", 1).start()
        gather.line(0, True)
        gather.copy("z", 2).start()
        gather.copy("z", 3).start()

    def pair_copy(number, q, j):
        gather, out, sem = gathers[number]
        rows = 2 * gather.rows
        at = pl.ds(pl.multiple_of(place.chip(q, j) * rows, rows), rows)
        return pltpu.make_async_copy(gather.buf.at[at], out.at[at], sem.at[4 * q + j])

    def store(q, j):
        for number in range(count - 1):
            gathers[number][0].whole(q, j)
            pair_copy(number, q, j).start()

    def spread(j, carry):
        for gather, _, _ in gathers:
            gather.side_x(j)
            gather.side_y(j)

        @pl.when(j < 3)
        def _():
            for gather, _, _ in gathers:
                gather.line(j + 1, False)

        store(0, j)
        store(1, j)
        store(2, j)
        for gather, _, _ in gathers:
            gather.corner(j)
        store(3, j)
        return carry

    lax.fori_loop(0, 4, spread, 0)

    def drain(k, carry):
        for number in range(count - 1):
            pair_copy(number, k // 4, k % 4).wait()
        return carry

    lax.fori_loop(0, 16, drain, 0)
    for reduce in reduces:
        reduce.finish()
    for gather, _, _ in gathers:
        gather.finish()


def call_sums(parts):
    total = GRID[0] * GRID[1]
    shapes = []
    for part in parts:
        width = part.shape[1]
        shapes.append((part.shape[0] // total, width, width // 256 * 128))
    scratch = []
    for number, (rows, width, split) in enumerate(shapes):
        scratch += [
            pltpu.VMEM((16, rows, width), jnp.bfloat16),
            *reduce_scratch(rows, width, split),
            pltpu.SemaphoreType.DMA((2, N_SEM)),
            pltpu.SemaphoreType.DMA((16,)),
        ]
        if number:
            scratch += [
                pltpu.VMEM((total * rows, width), jnp.bfloat16),
                pltpu.SemaphoreType.DMA((2, N_SEM)),
                pltpu.SemaphoreType.DMA((16,)),
            ]
    hbm = pl.BlockSpec(memory_space=pl.ANY)
    rows, width, _ = shapes[0]
    return pl.pallas_call(
        functools.partial(sums_kernel, shapes),
        out_shape=(
            jax.ShapeDtypeStruct((rows, width), jnp.float32),
            *(jax.ShapeDtypeStruct(part.shape, jnp.bfloat16) for part in parts[1:]),
        ),
        in_specs=[hbm] * len(parts),
        out_specs=(pl.BlockSpec(memory_space=pltpu.VMEM), *([hbm] * (len(parts) - 1))),
        scratch_shapes=scratch,
        compiler_params=pltpu.CompilerParams(
            collective_id=1, has_side_effects=True, vmem_limit_bytes=62 * 2**20
        ),
        name="sums",
    )(*parts)


def body(
    tokens,
    cotangent,
    gain_attention,
    gain_feedforward,
    query_weight,
    key_weight,
    value_weight,
    output_weight,
    value_router,
    output_router,
    expert_router,
    expert_first,
    expert_second,
    segments,
    value_ids,
    output_ids,
    ffn_ids,
):
    owner_total = lax.axis_size("dp") * lax.axis_size("expert")
    local_count = expert_first.shape[0]
    expert_count = local_count * owner_total
    shared = (
        gain_attention,
        query_weight,
        key_weight,
        value_weight,
        output_weight,
        value_router,
        output_router,
    )
    stream = tokens.astype(jnp.float32)
    upstream = cotangent.astype(jnp.float32)
    after_attention, saved_parts = attention_forward(
        stream, segments[0], value_ids[0], output_ids[0], shared
    )
    normed_low = layer_norm(after_attention, gain_feedforward).astype(jnp.bfloat16)
    logits = jnp.dot(normed_low, expert_router, preferred_element_type=jnp.float32)
    sigmoid_out = jax.nn.sigmoid(logits)
    mask = expert_mask(ffn_ids[0], expert_count)
    dense_gates = (sigmoid_out * mask).astype(jnp.bfloat16)
    after_low = after_attention.astype(jnp.bfloat16)
    own_kernels = (lax.axis_size("dp"), lax.axis_size("expert")) == GRID
    if own_kernels:
        model_width = tokens.shape[1]
        gate_width = -(-expert_count // 128) * 128
        me = lax.axis_index("dp") * lax.axis_size("expert") + lax.axis_index("expert")
        owner = me * local_count + jnp.arange(local_count * expert_first.shape[2]) // expert_first.shape[2]
        pick = (jnp.arange(gate_width)[:, None] == owner[None, :]).astype(jnp.bfloat16)
        padded = jnp.pad(dense_gates, ((0, 0), (0, gate_width - expert_count)))
        half = model_width // 2
        packed = jnp.concatenate(
            [cotangent[:, :half], after_low, padded, cotangent[:, half:]], axis=1
        )
        rows_sum, result, first_sum, second_sum = call_experts(
            packed, expert_first, expert_second, pick
        )
        token_grad = rows_sum[:, :model_width]
        gate_back = rows_sum[:, model_width : model_width + expert_count]
    else:
        result, token_grad, gate_back, first_sum, second_sum = expert_exchange(
            after_low,
            cotangent,
            dense_gates,
            expert_first,
            expert_second,
            max(1, owner_total // 32),
        )
    logit_grad = (
        gate_back.astype(jnp.float32) * mask * sigmoid_out * (1.0 - sigmoid_out)
    ).astype(jnp.bfloat16)
    router_sum = jnp.einsum("sa,sb->ab", normed_low, logit_grad, preferred_element_type=jnp.float32)
    normed_grad = jnp.einsum(
        "sb,ab->sa", logit_grad, expert_router, preferred_element_type=jnp.float32
    )
    norm_value, norm_pull = jax.vjp(layer_norm, after_attention, gain_feedforward)
    after_extra, feed_gain_part = norm_pull(normed_grad)
    after_grad = upstream + token_grad.astype(jnp.float32) + after_extra
    stream_grad, attention_parts = attention_backward(after_grad, saved_parts, stream, shared)
    gain_part, query_part, key_part, value_part, output_part, value_router_part, output_router_part = attention_parts
    parts = (
        query_part,
        key_part,
        value_part,
        value_router_part,
        output_router_part,
        router_sum,
        gain_part[:, None],
        feed_gain_part[:, None],
    )
    low = jnp.concatenate([part.astype(jnp.bfloat16) for part in parts], axis=1)
    low = jnp.pad(low, ((0, 0), (0, -low.shape[1] % 256)))
    output_low = output_part.astype(jnp.bfloat16)
    if own_kernels:
        result, low, output_low = call_sums([result, low, output_low])
    else:
        low, output_low = lax.psum((low, output_low), BOTH)
    block_output = (after_attention + result.astype(jnp.float32)).astype(jnp.bfloat16)
    summed, start = [], 0
    for part in parts:
        summed.append(low[:, start : start + part.shape[1]].astype(jnp.float32))
        start += part.shape[1]
    query_sum, key_sum, value_sum, value_router_sum, output_router_sum, router_sum, *gains = summed
    summed = (
        gains[0][:, 0],
        gains[1][:, 0],
        query_sum,
        key_sum,
        value_sum,
        output_low.astype(jnp.float32),
        value_router_sum,
        output_router_sum,
        router_sum,
    )
    return (
        block_output,
        stream_grad,
        *summed,
        first_sum,
        second_sum,
    )


def solution(mesh):
    placed = (
        P(("dp", "expert"), None),
        P(("dp", "expert"), None),
        P(),
        P(),
        P(),
        P(),
        P(),
        P(),
        P(),
        P(),
        P(),
        P(("dp", "expert"), None, None),
        P(("dp", "expert"), None, None),
        P(("dp", "expert"), None),
        P(None, ("dp", "expert"), None, None),
        P(None, ("dp", "expert"), None, None),
        P(None, ("dp", "expert"), None),
    )
    return jax.shard_map(
        body,
        mesh=mesh,
        in_specs=placed,
        out_specs=(
            P(("dp", "expert"), None),
            P(("dp", "expert"), None),
            P(),
            P(),
            P(),
            P(),
            P(),
            P(),
            P(),
            P(),
            P(),
            P(("dp", "expert"), None, None),
            P(("dp", "expert"), None, None),
        ),
        check_vma=False,
    )
```

```python
import functools
import math

import jax
import jax.numpy as jnp
from jax import lax
from jax.experimental import pallas as pl
from jax.experimental.pallas import tpu as pltpu
from jax.sharding import PartitionSpec as P

HEADS = 4
HEAD = 128
ATT_EXP = 5


NEG_FILL = -1000000000.0


def layer_norm(stream, norm_gain):
    average = jnp.mean(stream, axis=-1, keepdims=True)
    centred = stream - average
    variance = jnp.mean(centred * centred, axis=-1, keepdims=True)
    return centred * lax.rsqrt(variance + 1e-05) * norm_gain


def expert_mask(picked_ids, expert_count):
    matches = picked_ids[..., None] == jnp.arange(expert_count, dtype=jnp.int32)
    return jnp.sum(matches.astype(jnp.float32), axis=-2)


def attention_forward(stream, document_ids, value_picks, output_picks, shared):
    (
        gain_attention,
        query_weight,
        key_weight,
        value_weight,
        output_weight,
        value_router,
        output_router,
    ) = shared
    length = stream.shape[0]
    normed_low = layer_norm(stream, gain_attention).astype(jnp.bfloat16)
    queries = (
        jnp.dot(normed_low, query_weight, preferred_element_type=jnp.float32)
        .astype(jnp.bfloat16)
        .reshape(length, HEADS, HEAD)
    )
    key_rows = (
        jnp.dot(normed_low, key_weight, preferred_element_type=jnp.float32)
        .astype(jnp.bfloat16)
        .reshape(length, HEADS, HEAD)
    )
    value_sig = jax.nn.sigmoid(
        jnp.dot(normed_low, value_router, preferred_element_type=jnp.float32)
    ).reshape(length, HEADS, ATT_EXP)
    output_sig = jax.nn.sigmoid(
        jnp.dot(normed_low, output_router, preferred_element_type=jnp.float32)
    ).reshape(length, HEADS, ATT_EXP)
    value_mask = expert_mask(value_picks, ATT_EXP)
    output_mask = expert_mask(output_picks, ATT_EXP)
    value_gates = value_mask * value_sig
    output_gates = output_mask * output_sig
    stream_low = stream.astype(jnp.bfloat16)
    projected = jnp.dot(stream_low, value_weight, preferred_element_type=jnp.float32).reshape(
        length, HEADS, ATT_EXP, HEAD
    )
    values = jnp.sum(value_gates[..., None] * projected, axis=2).astype(jnp.bfloat16)
    scores = jnp.einsum("qhd,khd->hqk", queries, key_rows, preferred_element_type=jnp.float32) * (
        1.0 / math.sqrt(HEAD)
    )
    positions = jnp.arange(length, dtype=jnp.int32)
    allowed = (document_ids[:, None] == document_ids[None, :]) & (
        positions[:, None] >= positions[None, :]
    )
    scores = jnp.where(allowed[None], scores, NEG_FILL)
    row_max = jnp.max(scores, axis=-1, keepdims=True)
    exponent = jnp.exp(scores - row_max)
    row_total = jnp.sum(exponent, axis=-1, keepdims=True)
    probability = exponent / row_total
    weights_low = probability.astype(jnp.bfloat16)
    mixed = jnp.einsum("hqk,khd->qhd", weights_low, values, preferred_element_type=jnp.float32)
    gated_rows = (
        (output_gates[..., None] * mixed[:, :, None, :])
        .reshape(length, HEADS * ATT_EXP * HEAD)
        .astype(jnp.bfloat16)
    )
    after_attention = stream + jnp.dot(
        gated_rows, output_weight, preferred_element_type=jnp.float32
    )
    saved_parts = (
        normed_low,
        queries,
        key_rows,
        value_gates * (1.0 - value_sig),
        output_gates * (1.0 - output_sig),
        value_gates,
        output_gates,
        stream_low,
        projected,
        values,
        probability,
        weights_low,
        mixed,
        gated_rows,
    )
    return (after_attention, saved_parts)


def attention_backward(after_grad, saved_parts, stream, shared):
    (
        gain_attention,
        query_weight,
        key_weight,
        value_weight,
        output_weight,
        value_router,
        output_router,
    ) = shared
    (
        normed_low,
        queries,
        key_rows,
        value_slope,
        output_slope,
        value_gates,
        output_gates,
        stream_low,
        projected,
        values,
        probability,
        weights_low,
        mixed,
        gated_rows,
    ) = saved_parts
    length = after_grad.shape[0]
    scale = 1.0 / math.sqrt(HEAD)
    after_low = after_grad.astype(jnp.bfloat16)
    output_part = jnp.einsum("sa,sb->ab", gated_rows, after_low, preferred_element_type=jnp.float32)
    gated_grad = jnp.einsum(
        "sb,ab->sa", after_low, output_weight, preferred_element_type=jnp.float32
    ).astype(jnp.bfloat16)
    gated_grad = gated_grad.reshape(length, HEADS, ATT_EXP, HEAD).astype(jnp.float32)
    mixed_grad = jnp.sum(output_gates[..., None] * gated_grad, axis=2).astype(jnp.bfloat16)
    output_gate_grad = jnp.sum(gated_grad * mixed[:, :, None, :], axis=3)
    prob_grad = jnp.einsum("qhd,khd->hqk", mixed_grad, values, preferred_element_type=jnp.float32)
    values_grad = jnp.einsum(
        "hqk,qhd->khd", weights_low, mixed_grad, preferred_element_type=jnp.float32
    ).astype(jnp.bfloat16)
    values_grad = values_grad.astype(jnp.float32)
    score_grad = (
        probability * (prob_grad - jnp.sum(probability * prob_grad, axis=-1, keepdims=True))
    ).astype(jnp.bfloat16)
    query_grad = (
        (
            jnp.einsum("hqk,khd->qhd", score_grad, key_rows, preferred_element_type=jnp.float32)
            * scale
        )
        .astype(jnp.bfloat16)
        .reshape(length, HEADS * HEAD)
    )
    key_grad = (
        (
            jnp.einsum("hqk,qhd->khd", score_grad, queries, preferred_element_type=jnp.float32)
            * scale
        )
        .astype(jnp.bfloat16)
        .reshape(length, HEADS * HEAD)
    )
    projected_grad = (
        (value_gates[..., None] * values_grad[:, :, None, :])
        .astype(jnp.bfloat16)
        .reshape(length, HEADS * ATT_EXP * HEAD)
    )
    value_gate_grad = jnp.sum(values_grad[:, :, None, :] * projected, axis=3)
    value_logit_grad = (
        (value_gate_grad * value_slope)
        .astype(jnp.bfloat16)
        .reshape(length, HEADS * ATT_EXP)
    )
    output_logit_grad = (
        (output_gate_grad * output_slope)
        .astype(jnp.bfloat16)
        .reshape(length, HEADS * ATT_EXP)
    )
    value_part = jnp.einsum(
        "sa,sb->ab", stream_low, projected_grad, preferred_element_type=jnp.float32
    )
    query_part = jnp.einsum("sa,sb->ab", normed_low, query_grad, preferred_element_type=jnp.float32)
    key_part = jnp.einsum("sa,sb->ab", normed_low, key_grad, preferred_element_type=jnp.float32)
    value_router_part = jnp.einsum(
        "sa,sb->ab", normed_low, value_logit_grad, preferred_element_type=jnp.float32
    )
    output_router_part = jnp.einsum(
        "sa,sb->ab", normed_low, output_logit_grad, preferred_element_type=jnp.float32
    )
    normed_grad = jnp.einsum(
        "sb,ab->sa", query_grad, query_weight, preferred_element_type=jnp.float32
    )
    normed_grad = normed_grad + jnp.einsum(
        "sb,ab->sa", key_grad, key_weight, preferred_element_type=jnp.float32
    )
    normed_grad = normed_grad + jnp.einsum(
        "sb,ab->sa", value_logit_grad, value_router, preferred_element_type=jnp.float32
    )
    normed_grad = normed_grad + jnp.einsum(
        "sb,ab->sa", output_logit_grad, output_router, preferred_element_type=jnp.float32
    )
    norm_value, norm_pull = jax.vjp(layer_norm, stream, gain_attention)
    stream_extra, gain_part = norm_pull(normed_grad)
    value_input = jnp.einsum(
        "sb,ab->sa", projected_grad, value_weight, preferred_element_type=jnp.float32
    )
    stream_grad = after_grad + stream_extra + value_input
    return (
        stream_grad,
        (
            gain_part,
            query_part,
            key_part,
            value_part,
            output_part,
            value_router_part,
            output_router_part,
        ),
    )


def expert_pass(rows, upstream_rows, gates, expert_first, expert_second):
    local_count, model_width, hidden_width = expert_first.shape
    wide = local_count * hidden_width
    first = expert_first.transpose(1, 0, 2).reshape(model_width, wide)
    second = expert_second.reshape(wide, model_width)
    gates_wide = jnp.repeat(gates.astype(jnp.float32), hidden_width, axis=1)
    hidden_pre = jnp.dot(rows, first, preferred_element_type=jnp.float32)
    hidden, gelu_pull = jax.vjp(jax.nn.gelu, hidden_pre)
    hidden = hidden.astype(jnp.bfloat16).astype(jnp.float32)
    gated_hidden = (gates_wide * hidden).astype(jnp.bfloat16)
    back = jnp.einsum("sd,fd->sf", upstream_rows, second, preferred_element_type=jnp.float32)
    gate_grad = jnp.sum((back * hidden).reshape(-1, local_count, hidden_width), axis=2)
    pre_grad = gelu_pull(gates_wide * back)[0].astype(jnp.bfloat16)
    result = jnp.dot(gated_hidden, second, preferred_element_type=jnp.float32)
    row_grad = jnp.einsum("sf,df->sd", pre_grad, first, preferred_element_type=jnp.float32)
    second_sum = jnp.einsum(
        "sf,sd->fd", gated_hidden, upstream_rows, preferred_element_type=jnp.float32
    )
    first_sum = jnp.einsum("sd,sf->df", rows, pre_grad, preferred_element_type=jnp.float32)
    first_sum = first_sum.reshape(model_width, local_count, hidden_width).transpose(1, 0, 2)
    return (
        result.astype(jnp.bfloat16),
        row_grad.astype(jnp.bfloat16),
        gate_grad.astype(jnp.bfloat16),
        first_sum,
        second_sum.reshape(expert_second.shape),
    )


BOTH = ("dp", "expert")


def expert_piece(after_low, upstream_low, dense_gates, expert_first, expert_second):
    local_count = expert_first.shape[0]
    me = lax.axis_index("dp") * lax.axis_size("expert") + lax.axis_index("expert")
    upstream_rows = lax.all_gather(upstream_low, BOTH, axis=0, tiled=True)
    rows = lax.all_gather(after_low, BOTH, axis=0, tiled=True)
    gates = lax.all_gather(dense_gates, BOTH, axis=0, tiled=True)
    gates = lax.dynamic_slice_in_dim(gates, me * local_count, local_count, axis=1)
    result, row_grad, gate_grad, first_sum, second_sum = expert_pass(
        rows, upstream_rows, gates, expert_first, expert_second
    )
    gate_back = lax.all_to_all(gate_grad, BOTH, split_axis=0, concat_axis=1, tiled=True)
    token_grad = lax.psum_scatter(row_grad, BOTH, scatter_dimension=0, tiled=True)
    result = lax.psum_scatter(result, BOTH, scatter_dimension=0, tiled=True)
    return (result, token_grad, gate_back), (first_sum, second_sum)


def expert_exchange(after_low, upstream_low, dense_gates, expert_first, expert_second, pieces):
    if pieces == 1:
        back, sums = expert_piece(
            after_low, upstream_low, dense_gates, expert_first, expert_second
        )
        return (*back, *sums)

    def step(totals, piece):
        back, sums = expert_piece(*piece, expert_first, expert_second)
        return (totals[0] + sums[0], totals[1] + sums[1]), back

    cut = lambda array: array.reshape(pieces, -1, array.shape[1])
    start = (
        jnp.zeros(expert_first.shape, jnp.float32),
        jnp.zeros(expert_second.shape, jnp.float32),
    )
    sums, back = lax.scan(step, start, (cut(after_low), cut(upstream_low), cut(dense_gates)))
    return (*(part.reshape(-1, part.shape[2]) for part in back), *sums)


MESH = pl.DeviceIdType.MESH
GRID = (4, 8)
N_SEM = 47


class Place:
    def __init__(self):
        dp, expert = lax.axis_index("dp"), lax.axis_index("expert")
        self.y, self.x = dp // 2, dp % 2
        self.z, self.core = expert // 2, expert % 2
        self.dp = dp
        self.me = dp * GRID[1] + expert
        self.x_peer = (2 * self.y + 1 - self.x, expert)
        self.y_peer = (2 * (1 - self.y) + self.x, expert)
        self.core_peer = (dp, 2 * self.z + 1 - self.core)
        self.middle = (self.z + self.z // 2) % 2
        self.main = 1 + self.z % 2
        self.minor = 3 * (self.z // 2)

    def along_z(self, z):
        return (self.dp, 2 * z + self.core)

    def z_at(self, j):
        near = j + self.middle * (1 - 2 * j) * (1 - j // 2)
        return near + self.z // 2 * (3 - 2 * near)

    def chip(self, q, j):
        return ((self.y + q // 2) % 2 * 2 + (self.x + q % 2) % 2) * 4 + self.z_at(j)

    def if_middle(self, action):
        pl.when(self.middle == 1)(action)


def enter(place):
    barrier = pltpu.get_barrier_semaphore()

    def signal(peer):
        pl.semaphore_signal(barrier, inc=1, device_id=peer, device_id_type=MESH)

    for peer in (place.x_peer, place.y_peer, place.core_peer, place.along_z(place.main)):
        signal(peer)
    place.if_middle(lambda: signal(place.along_z(place.minor)))
    pl.when(place.middle == 0)(lambda: pl.semaphore_wait(barrier, 4))
    place.if_middle(lambda: pl.semaphore_wait(barrier, 5))


def remote(src, dst, send, recv, peer):
    return pltpu.make_async_remote_copy(
        src_ref=src,
        dst_ref=dst,
        send_sem=send,
        recv_sem=recv,
        device_id=peer,
        device_id_type=MESH,
    )


def cut_columns(width):
    tiles = width // 128
    split = tiles // 2
    outer = max(1, tiles * 3 // 10)
    return outer * 128, split * 128, (tiles - outer) * 128


class Gather:
    def __init__(self, place, buf, rows, sems):
        self.place, self.buf, self.rows = place, buf, rows
        self.width = buf.shape[1]
        self.d_end, self.split, self.c_start = cut_columns(self.width)
        self.send, self.recv = sems.at[0], sems.at[1]

    def block(self, q, j, columns=slice(None)):
        start = (2 * self.place.chip(q, j) + self.place.core) * self.rows
        return self.buf.at[pl.ds(pl.multiple_of(start, self.rows), self.rows), columns]

    def copy(self, kind, j, q=0):
        place = self.place
        if kind == "x0":
            ref, number, peer = self.block(0, 0), 15, place.x_peer
        elif kind == "y0":
            ref, number, peer = self.block(0, 0), 19, place.y_peer
        elif kind == "x":
            ref, number, peer = self.block(0, j, slice(0, self.c_start)), 15 + j, place.x_peer
        elif kind == "y":
            ref, number, peer = self.block(0, j, slice(self.d_end, None)), 19 + j, place.y_peer
        elif kind == "a":
            ref, number, peer = self.block(1, j, slice(self.split, None)), 23 + j, place.y_peer
        elif kind == "b":
            ref, number, peer = self.block(2, j, slice(0, self.split)), 27 + j, place.x_peer
        else:
            ref, number, peer = self.block(q, j), 31 + 4 * q + j, place.core_peer
        return remote(ref, ref, self.send.at[number], self.recv.at[number], peer)

    def z_copy(self, part, j, number, z, receiver_j):
        columns = (slice(None), slice(self.c_start, None), slice(0, self.d_end))[part]
        ref = self.block(part, j, columns)
        return remote(
            ref,
            ref,
            self.send.at[5 * part + number],
            self.recv.at[3 * part + receiver_j - 1],
            self.place.along_z(z),
        )

    def z_own(self, part):
        place = self.place
        self.z_copy(part, 0, 0, place.main, 1 + place.middle).start()
        place.if_middle(lambda: self.z_copy(part, 0, 1, place.minor, 1).start())

    def outer_own(self, middle):
        @pl.when(self.place.middle == middle)
        def _():
            self.z_own(1)
            self.z_own(2)

    def z_pass(self, part, j):
        place = self.place
        first = 1 - (j + 2) // 4
        z = place.minor + first * (place.main - place.minor)
        return self.z_copy(part, j, 1 + j, z, j + 2 * first)

    def z_arrive(self, part, j):
        self.z_copy(part, j, 0, self.place.main, j).wait_recv()
        self.place.if_middle(lambda: self.z_pass(part, j).start())

    def begin(self):
        self.z_own(0)
        self.copy("x0", 0).start()
        self.copy("y0", 0).start()
        self.copy("core", 0, 0).start()

    def line(self, j):
        self.z_arrive(0, j)
        self.copy("x", j).start()
        self.copy("y", j).start()
        self.copy("core", j, 0).start()
        if j == 3:
            self.outer_own(1)

    def sides_first(self):
        self.copy("x0", 0).wait_recv()
        self.copy("a", 0).start()
        self.copy("core", 0, 1).start()
        self.copy("y0", 0).wait_recv()
        self.copy("b", 0).start()
        self.copy("core", 0, 2).start()
        self.outer_own(0)

    def sides(self, j):
        self.z_arrive(1, j)
        self.z_arrive(2, j)
        self.copy("x", j).wait_recv()
        self.copy("a", j).start()
        self.copy("core", j, 1).start()
        self.copy("y", j).wait_recv()
        self.copy("b", j).start()
        self.copy("core", j, 2).start()

    def corner(self, j):
        self.copy("a", j).wait_recv()
        self.copy("b", j).wait_recv()
        self.copy("core", j, 3).start()

    def whole(self, q, j):
        self.copy("core", j, q).wait_recv()

    def finish(self):
        place = self.place
        for part in range(3):
            self.z_copy(part, 0, 0, place.main, 1).wait_send()

        def middle():
            for part in range(3):
                self.z_copy(part, 0, 1, place.minor, 1).wait_send()

                def passed(j, carry):
                    self.z_pass(part, j).wait_send()
                    return carry

                lax.fori_loop(1, 4, passed, 0)

        place.if_middle(middle)
        self.copy("x0", 0).wait_send()
        self.copy("y0", 0).wait_send()

        def line(j, carry):
            self.copy("x", j).wait_send()
            self.copy("y", j).wait_send()
            return carry

        lax.fori_loop(1, 4, line, 0)

        def step(j, carry):
            self.copy("a", j).wait_send()
            self.copy("b", j).wait_send()
            for q in range(4):
                self.copy("core", j, q).wait_send()
            return carry

        lax.fori_loop(0, 4, step, 0)


class Reduce:
    def __init__(self, place, own, other, boxes, sems):
        self.place, self.own, self.other = place, own, other
        self.other_in, self.a_in, self.b_in, self.x_in, self.y_in = boxes[:5]
        self.z_in = boxes[5:]
        self.rows, self.width = self.other_in.shape[1:]
        self.d_end, self.split, self.c_start = cut_columns(self.width)
        self.send, self.recv = sems.at[0], sems.at[1]

    def copy(self, kind, k):
        place = self.place
        j = k % 4
        if kind == "core":
            src, dst, number, peer = self.other(k), self.other_in.at[k], k, place.core_peer
        elif kind == "a":
            src = self.own(k).at[:, self.split :]
            dst, number, peer = self.a_in.at[j], 16 + j, place.y_peer
        elif kind == "b":
            src = self.own(k).at[:, : self.split]
            dst, number, peer = self.b_in.at[j], 20 + j, place.x_peer
        elif kind == "x0":
            src, dst, number, peer = self.own(k), self.x_in.at[0], 24, place.x_peer
        elif kind == "y0":
            src, dst, number, peer = self.own(k), self.y_in.at[0], 28, place.y_peer
        elif kind == "x":
            src = self.own(k).at[:, : self.c_start]
            dst, number, peer = self.x_in.at[j, :, : self.c_start], 24 + j, place.x_peer
        else:
            src = self.own(k).at[:, self.d_end :]
            dst, number, peer = self.y_in.at[j, :, self.d_end :], 28 + j, place.y_peer
        return remote(src, dst, self.send.at[number], self.recv.at[number], peer)

    def z_columns(self, part):
        return (slice(None), slice(self.c_start, None), slice(0, self.d_end))[part]

    def z_copy(self, part, j):
        place = self.place
        first = 1 - (j + 2) // 4
        box = place.middle * (j // 3) + (1 - place.middle) * (j + 1)
        z = place.main + place.middle * first * (place.minor - place.main)
        return remote(
            self.own(4 * part + j).at[:, self.z_columns(part)],
            self.z_in[part].at[box],
            self.send.at[32 + 5 * part + j],
            self.recv.at[32 + 5 * part + box],
            place.along_z(z),
        )

    def z_wait(self, part, box):
        self.copy_box(part, box).wait_recv()

    def copy_box(self, part, box):
        ref = self.z_in[part].at[box]
        return remote(
            ref,
            ref,
            self.send.at[32 + 5 * part],
            self.recv.at[32 + 5 * part + box],
            self.place.along_z(self.place.main),
        )

    def z_give(self, part, j):
        def middle():
            box = j + (j + 2) // 4
            self.z_wait(part, box)
            self.add(4 * part + j, self.z_columns(part), [lambda at: self.z_in[part][box, at, :]])

        self.place.if_middle(middle)
        self.z_copy(part, j).start()

    def z_last(self, part):
        columns = self.z_columns(part)
        self.z_wait(part, 0)
        self.add(4 * part, columns, [lambda at: self.z_in[part][0, at, :]])

        def middle():
            self.z_wait(part, 2)
            self.add(4 * part, columns, [lambda at: self.z_in[part][2, at, :]])

        self.place.if_middle(middle)

    def add(self, k, columns, terms):
        own = self.own(k)

        def step(number, carry):
            at = pl.ds(pl.multiple_of(number * 16, 16), 16)
            total = own[at, columns].astype(jnp.float32)
            for term in terms:
                total = total + term(at).astype(jnp.float32)
            own[at, columns] = total.astype(own.dtype)
            return carry

        lax.fori_loop(0, self.rows // 16, step, 0)

    def corner(self, j):
        k = 12 + j
        self.copy("core", k).wait_recv()
        self.add(k, slice(None), [lambda at: self.other_in[k, at, :]])
        self.copy("a", k).start()
        self.copy("b", k).start()

    def side_x(self, j):
        k, split = 4 + j, self.split
        self.copy("core", k).wait_recv()
        self.add(k, slice(0, split), [lambda at: self.other_in[k, at, :split]])
        self.copy("a", k).wait_recv()
        self.add(
            k,
            slice(split, None),
            [lambda at: self.other_in[k, at, split:], lambda at: self.a_in[j, at, :]],
        )

    def side_y(self, j):
        k, split = 8 + j, self.split
        self.copy("core", k).wait_recv()
        self.add(k, slice(split, None), [lambda at: self.other_in[k, at, split:]])
        self.copy("b", k).wait_recv()
        self.add(
            k,
            slice(0, split),
            [lambda at: self.other_in[k, at, :split], lambda at: self.b_in[j, at, :]],
        )

    def sides(self, j):
        self.side_x(j)
        self.copy("x", 4 + j).start()
        self.z_give(1, j)
        self.side_y(j)
        self.copy("y", 8 + j).start()
        self.z_give(2, j)

    def sides_last(self):
        self.side_x(0)
        self.side_y(0)
        self.z_last(1)
        self.copy("x0", 4).start()
        self.z_last(2)
        self.copy("y0", 8).start()

    def line(self, j):
        self.copy("core", j).wait_recv()
        self.copy("x", j).wait_recv()
        self.copy("y", j).wait_recv()
        d_end, c_start = self.d_end, self.c_start
        boxes = (self.other_in, self.x_in, self.y_in)
        for columns, used in (
            (slice(0, d_end), boxes[:2]),
            (slice(d_end, c_start), boxes),
            (slice(c_start, None), (boxes[0], boxes[2])),
        ):
            self.add(j, columns, [lambda at, box=box: box[j, at, columns] for box in used])
        self.z_give(0, j)

    def last(self, put):
        self.copy("core", 0).wait_recv()
        self.copy("x0", 0).wait_recv()
        self.copy("y0", 0).wait_recv()
        self.z_wait(0, 0)
        own = self.own(0)

        def sum_up(middle):
            def step(number, carry):
                at = pl.ds(pl.multiple_of(number * 16, 16), 16)
                total = own[at, :].astype(jnp.float32)
                for box in (self.other_in, self.x_in, self.y_in, self.z_in[0]):
                    total = total + box[0, at, :].astype(jnp.float32)
                if middle:
                    total = total + self.z_in[0][2, at, :].astype(jnp.float32)
                put(at, total)
                return carry

            lax.fori_loop(0, own.shape[0] // 16, step, 0)

        @pl.when(self.place.middle == 1)
        def _():
            self.z_wait(0, 2)
            sum_up(True)

        pl.when(self.place.middle == 0)(lambda: sum_up(False))

    def finish(self):
        def step(j, carry):
            self.copy("a", 12 + j).wait_send()
            self.copy("b", 12 + j).wait_send()
            for q in range(4):
                self.copy("core", 4 * q + j).wait_send()
            return carry

        lax.fori_loop(0, 4, step, 0)

        def outer(j, carry):
            self.copy("x", 4 + j).wait_send()
            self.copy("y", 8 + j).wait_send()
            for part in range(3):
                self.z_copy(part, j).wait_send()
            return carry

        lax.fori_loop(1, 4, outer, 0)
        self.copy("x0", 4).wait_send()
        self.copy("y0", 8).wait_send()


RETURN_ORDER = (
    ("corner", (3,)),
    ("corner", (2,)),
    ("corner", (1,)),
    ("sides", (3,)),
    ("corner", (0,)),
    ("sides", (2,)),
    ("sides", (1,)),
    ("line", (3,)),
    ("sides_last", ()),
    ("line", (2,)),
    ("line", (1,)),
)
SPREAD_ORDER = (
    ("line", (1,), [(0, 0)]),
    ("sides_first", (), [(0, 1)]),
    ("line", (2,), [(1, 0), (2, 0)]),
    ("line", (3,), [(0, 2)]),
    ("corner", (0,), [(0, 3)]),
    ("sides", (1,), [(3, 0)]),
    ("sides", (2,), [(1, 1), (2, 1)]),
    ("sides", (3,), [(1, 2), (2, 2)]),
    ("corner", (1,), [(1, 3), (2, 3)]),
    ("corner", (2,), [(3, 1)]),
    ("corner", (3,), [(3, 2), (3, 3)]),
)


def reduce_scratch(rows, width):
    low = jnp.bfloat16
    d_end, split, c_start = cut_columns(width)
    return [
        pltpu.VMEM((16, rows, width), low),
        pltpu.VMEM((4, rows, width - split), low),
        pltpu.VMEM((4, rows, split), low),
        pltpu.VMEM((4, rows, width), low),
        pltpu.VMEM((4, rows, width), low),
        pltpu.VMEM((5, rows, width), low),
        pltpu.VMEM((5, rows, width - c_start), low),
        pltpu.VMEM((5, rows, d_end), low),
    ]


GELU_C = math.sqrt(2.0 / math.pi)
GELU_K = 0.044715


def mm(left, right):
    return jnp.dot(left, right, preferred_element_type=jnp.float32)


def mm_tn(left, right):
    return lax.dot_general(left, right, (((0,), (0,)), ((), ())), preferred_element_type=jnp.float32)


def norm_parts(stream):
    average = jnp.mean(stream, axis=-1, keepdims=True)
    centred = stream - average
    variance = jnp.mean(centred * centred, axis=-1, keepdims=True)
    return centred, lax.rsqrt(variance + 1e-05)


def mm_nt(left, right):
    return lax.dot_general(left, right, (((1,), (1,)), ((), ())), preferred_element_type=jnp.float32)


def picked_mask(ids, groups, per_group, group_size, width):
    column = lax.broadcasted_iota(jnp.int32, (ids.shape[0], width), 1)
    mask = jnp.zeros((ids.shape[0], width), jnp.float32)
    for group in range(groups):
        for number in range(per_group):
            at = group * per_group + number
            mask = jnp.where(column == ids[:, at : at + 1] + group * group_size, 1.0, mask)
    return mask


def attention_kernel(
    tokens_ref,
    cotangent_ref,
    gain_attention_ref,
    gain_feedforward_ref,
    query_ref,
    key_ref,
    value_ref,
    output_ref,
    value_router_ref,
    output_router_ref,
    expert_router_ref,
    segments_ref,
    value_ids_ref,
    output_ids_ref,
    ffn_ids_ref,
    upstream_out,
    packed_out,
    after_out,
    normed_out,
    normed_ffn_out,
    queries_out,
    keys_out,
    projected_out,
    values_out,
    probability_out,
    mixed_out,
    gated_out,
    value_gates_out,
    value_slope_out,
    output_gates_out,
    output_slope_out,
    expert_slope_out,
    own_sem,
    gather_sems,
):
    place = Place()
    length, model_width = tokens_ref.shape
    expert_count = expert_router_ref.shape[1]
    router_width = value_router_ref.shape[1]
    enter(place)
    gather = Gather(place, upstream_out, length, gather_sems)
    own_copy = pltpu.make_async_copy(cotangent_ref, gather.block(0, 0), own_sem)
    own_copy.start()
    own_copy.wait()
    gather.begin()

    stream_low = tokens_ref[...]
    stream = stream_low.astype(jnp.float32)
    centred, scale = norm_parts(stream)
    normed = (centred * scale * gain_attention_ref[...]).astype(jnp.bfloat16)
    normed_out[...] = normed
    queries_out[...] = mm(normed, query_ref[...]).astype(jnp.bfloat16)
    keys_out[...] = mm(normed, key_ref[...]).astype(jnp.bfloat16)
    value_sig = jax.nn.sigmoid(mm(normed, value_router_ref[...]))
    output_sig = jax.nn.sigmoid(mm(normed, output_router_ref[...]))
    picks = value_ids_ref.shape[1] // HEADS
    value_mask = picked_mask(value_ids_ref[...], HEADS, picks, ATT_EXP, router_width)
    output_mask = picked_mask(output_ids_ref[...], HEADS, picks, ATT_EXP, router_width)
    value_gates = value_mask * value_sig
    output_gates = output_mask * output_sig
    value_gates_out[...] = value_gates
    output_gates_out[...] = output_gates
    value_slope_out[...] = value_gates * (1.0 - value_sig)
    output_slope_out[...] = output_gates * (1.0 - output_sig)
    gather.line(1)
    gather.sides_first()
    gather.line(2)
    head_width = ATT_EXP * HEAD
    for head in range(HEADS):
        columns = slice(head * head_width, (head + 1) * head_width)
        projected_out[:, columns] = mm(stream_low, value_ref[:, columns])
        total = jnp.zeros((length, HEAD), jnp.float32)
        for e in range(ATT_EXP):
            at = head * ATT_EXP + e
            total = total + value_gates[:, at : at + 1] * projected_out[:, at * HEAD : (at + 1) * HEAD]
        values_out[:, head * HEAD : (head + 1) * HEAD] = total.astype(jnp.bfloat16)
    gather.line(3)
    documents = jnp.broadcast_to(segments_ref[...].astype(jnp.float32), (length, length))
    row = lax.broadcasted_iota(jnp.int32, (length, length), 0)
    column = lax.broadcasted_iota(jnp.int32, (length, length), 1)
    allowed = (documents == documents.T) & (row >= column)
    for head in range(HEADS):
        columns = slice(head * HEAD, (head + 1) * HEAD)
        scores = mm_nt(queries_out[:, columns], keys_out[:, columns]) * (1.0 / math.sqrt(HEAD))
        scores = jnp.where(allowed, scores, NEG_FILL)
        exponent = jnp.exp(scores - jnp.max(scores, axis=-1, keepdims=True))
        probability = exponent / jnp.sum(exponent, axis=-1, keepdims=True)
        probability_out[head] = probability
        mixed = mm(probability.astype(jnp.bfloat16), values_out[:, columns])
        mixed_out[:, columns] = mixed
        for e in range(ATT_EXP):
            at = head * ATT_EXP + e
            gated_out[:, at * HEAD : (at + 1) * HEAD] = (
                output_gates[:, at : at + 1] * mixed
            ).astype(jnp.bfloat16)
    after = stream + mm(gated_out[...], output_ref[...])
    after_out[...] = after
    packed_out[:, :model_width] = after.astype(jnp.bfloat16)
    centred, scale = norm_parts(after)
    normed_ffn = (centred * scale * gain_feedforward_ref[...]).astype(jnp.bfloat16)
    normed_ffn_out[...] = normed_ffn
    expert_sig = jax.nn.sigmoid(mm(normed_ffn, expert_router_ref[...]))
    expert_mask_ = picked_mask(ffn_ids_ref[...], 1, ffn_ids_ref.shape[1], 0, expert_count)
    expert_gates = expert_mask_ * expert_sig
    gate_width = packed_out.shape[1] - model_width
    packed_out[:, model_width:] = jnp.zeros((length, gate_width), jnp.bfloat16)
    packed_out[:, model_width : model_width + expert_count] = expert_gates.astype(jnp.bfloat16)
    expert_slope_out[...] = expert_gates * (1.0 - expert_sig)
    gather.corner(0)
    for j in (1, 2, 3):
        gather.sides(j)
    for j in (1, 2, 3):
        gather.corner(j)

    def arrived(k, carry):
        gather.whole(k // 4, k % 4)
        return carry

    lax.fori_loop(0, 16, arrived, 0)
    gather.finish()


def call_attention(
    tokens,
    cotangent,
    gain_attention,
    gain_feedforward,
    shared_weights,
    expert_router,
    segments,
    value_ids,
    output_ids,
    ffn_ids,
    gate_width,
):
    length, model_width = tokens.shape
    total = GRID[0] * GRID[1] * length
    expert_count = expert_router.shape[1]
    wide = shared_weights[3].shape[0]
    narrow = HEADS * HEAD
    router_width = HEADS * ATT_EXP
    low, full = jnp.bfloat16, jnp.float32
    shapes = (
        ((total, model_width), low),
        ((length, model_width + gate_width), low),
        ((length, model_width), full),
        ((length, model_width), low),
        ((length, model_width), low),
        ((length, narrow), low),
        ((length, narrow), low),
        ((length, wide), full),
        ((length, narrow), low),
        ((HEADS, length, length), full),
        ((length, narrow), full),
        ((length, wide), low),
        ((length, router_width), full),
        ((length, router_width), full),
        ((length, router_width), full),
        ((length, router_width), full),
        ((length, expert_count), full),
    )
    vmem = pl.BlockSpec(memory_space=pltpu.VMEM)
    hbm = pl.BlockSpec(memory_space=pl.ANY)
    return pl.pallas_call(
        attention_kernel,
        out_shape=tuple(jax.ShapeDtypeStruct(*shape) for shape in shapes),
        in_specs=[vmem] * 15,
        out_specs=(hbm, *([vmem] * (len(shapes) - 1))),
        scratch_shapes=[pltpu.SemaphoreType.DMA, pltpu.SemaphoreType.DMA((2, N_SEM))],
        compiler_params=pltpu.CompilerParams(
            collective_id=2, has_side_effects=True, vmem_limit_bytes=62 * 2**20
        ),
        name="attention",
    )(
        tokens,
        cotangent,
        gain_attention[None],
        gain_feedforward[None],
        *shared_weights,
        expert_router,
        segments,
        value_ids.reshape(length, -1),
        output_ids.reshape(length, -1),
        ffn_ids,
    )


def expert_kernel(
    model_width,
    local_count,
    packed_ref,
    upstream_ref,
    first_in,
    second_in,
    rows_out,
    result_out,
    first_out,
    second_out,
    gathered,
    upstream,
    first_ref,
    first_t_ref,
    second_t_ref,
    gated_hidden,
    pre_grads,
    partial,
    *refs,
):
    place = Place()
    length = packed_ref.shape[0]
    pair = 2 * length
    gate_width = packed_ref.shape[1] - model_width
    hidden_width = first_ref.shape[1] // local_count
    boxes, (result_stage, gather_sems, reduce_sems, result_sems, upstream_sem) = refs[:8], refs[8:]
    upstream_copy = pltpu.make_async_copy(upstream_ref, upstream, upstream_sem)
    upstream_copy.start()
    enter(place)
    gather = Gather(place, gathered, length, gather_sems)
    gathered[pl.ds(pl.multiple_of(place.me * length, length), length), :] = packed_ref[...]
    gather.begin()
    second_ref = second_in
    for e in range(local_count):
        columns = slice(e * hidden_width, (e + 1) * hidden_width)
        first_ref[:, columns] = first_in[e]
        first_t_ref[columns, :] = first_in[e].astype(jnp.float32).T.astype(jnp.bfloat16)
        second_t_ref[:, columns] = second_in[columns, :].astype(jnp.float32).T.astype(jnp.bfloat16)
    pick_row = lax.broadcasted_iota(jnp.int32, (gate_width, first_ref.shape[1]), 0)
    pick_column = lax.broadcasted_iota(jnp.int32, (gate_width, first_ref.shape[1]), 1)
    pick_gates = jnp.where(
        pick_row == place.me * local_count + pick_column // hidden_width, 1.0, 0.0
    ).astype(jnp.bfloat16)

    def own(k):
        return partial.at[k, pl.ds(pl.multiple_of(place.core * length, length), length)]

    def other(k):
        return partial.at[k, pl.ds(pl.multiple_of((1 - place.core) * length, length), length)]

    reduce = Reduce(place, own, other, boxes, reduce_sems)

    def result_copy(slot, chip):
        return pltpu.make_async_copy(
            result_stage.at[slot],
            result_out.at[pl.ds(pl.multiple_of(chip * pair, pair), pair)],
            result_sems.at[slot],
        )

    def compute(step, q, j):
        chip = place.chip(q, j)
        rows = pl.ds(pl.multiple_of(chip * pair, pair), pair)
        hidden_pre = mm(gathered[rows, :model_width], first_ref[...])
        back = mm(upstream[rows, :], second_t_ref[...])
        gates = mm(gathered[rows, model_width:], pick_gates)
        square = hidden_pre * hidden_pre
        bent = jnp.tanh(GELU_C * hidden_pre * (1.0 + GELU_K * square))
        grow = 0.5 * (1.0 + bent)
        slope = grow + 0.5 * hidden_pre * (1.0 - bent * bent) * (
            GELU_C * (1.0 + 3.0 * GELU_K * square)
        )
        hidden = (hidden_pre * grow).astype(jnp.bfloat16).astype(jnp.float32)
        gated = (gates * hidden).astype(jnp.bfloat16)
        pre_grad = (gates * back * slope).astype(jnp.bfloat16)
        gated_hidden[rows, :] = gated
        pre_grads[rows, :] = pre_grad
        k = 4 * q + j
        partial[k, :, :model_width] = mm(pre_grad, first_t_ref[...]).astype(jnp.bfloat16)
        product = hidden * back
        column = lax.broadcasted_iota(jnp.int32, (pair, gate_width), 1) - place.me * local_count
        gate_grad = jnp.zeros((pair, gate_width), jnp.float32)
        for e in range(local_count):
            own_sum = jnp.sum(
                product[:, e * hidden_width : (e + 1) * hidden_width], axis=1, keepdims=True
            )
            gate_grad = jnp.where(column == e, own_sum, gate_grad)
        partial[k, :, model_width:] = gate_grad.astype(jnp.bfloat16)
        reduce.copy("core", k).start()
        slot = step % 2

        @pl.when(step >= 2)
        def _():
            result_copy(slot, chip).wait()

        result_stage[slot] = mm(gated, second_ref[...]).astype(jnp.bfloat16)
        result_copy(slot, chip).start()

    upstream_copy.wait()

    def arrive(actions):
        for kind, j in actions:
            if kind == "sides_first":
                gather.sides_first()
            elif kind == "line_middle":
                place.if_middle(lambda: gather.line(j))
            elif kind == "line_end":
                pl.when(place.middle == 0)(lambda: gather.line(j))
            else:
                getattr(gather, kind)(j)

    before = {
        1: [("line", 1), ("sides_first", 0), ("line_middle", 2)],
        4: [("corner", 0), ("line_end", 2), ("line_middle", 3)],
        6: [("line_end", 3), ("sides", 1)],
        9: [("corner", 1), ("sides", 2)],
        12: [("corner", 2), ("sides", 3)],
        15: [("corner", 3)],
    }
    order = [(0, 0), (0, 1), (1, 0), (2, 0), (3, 0), (0, 2), (0, 3), (1, 1)]
    order += [(2, 1), (3, 1), (1, 2), (2, 2), (3, 2), (1, 3), (2, 3), (3, 3)]

    def pick(step, values):
        total = 0
        for number, value in enumerate(values):
            total = total + value * jnp.where(step == number, 1, 0)
        return total

    def walk(step, carry):
        for number, actions in before.items():
            pl.when(step == number)(functools.partial(arrive, actions))
        q = pick(step, [pair_[0] for pair_ in order])
        j = pick(step, [pair_[1] for pair_ in order])
        gather.whole(q, j)
        compute(step, q, j)
        return carry

    lax.fori_loop(0, 16, walk, 0)
    piece = gathered.shape[0] // 8

    def weight_piece(number):
        rows = pl.ds(pl.multiple_of(number * piece, piece), piece)
        second = mm_tn(gated_hidden[rows, :], upstream[rows, :])
        first = mm_tn(pre_grads[rows, :], gathered[rows, :model_width])

        @pl.when(number == 0)
        def _():
            second_out[...] = second
            first_out[...] = first

        @pl.when(number > 0)
        def _():
            second_out[...] += second
            first_out[...] += first

    give_back = [
        [("corner", 3), ("corner", 2)],
        [("corner", 1), ("sides", 3)],
        [("corner", 0)],
        [("sides", 2)],
        [("sides", 1)],
        [("line", 3)],
        [("sides_last", 0)],
        [("line", 2)],
    ]

    def give(step, carry):
        for number, actions in enumerate(give_back):

            @pl.when(step == number)
            def _(actions=actions):
                for kind, j in actions:
                    if kind == "sides_last":
                        reduce.sides_last()
                    else:
                        getattr(reduce, kind)(j)

        weight_piece(step)
        return carry

    lax.fori_loop(0, len(give_back), give, 0)
    reduce.line(1)

    def put(at, total):
        rows_out[at, :] = total

    reduce.last(put)
    for slot in range(2):
        result_copy(slot, 0).wait()
    gather.finish()
    reduce.finish()


def call_experts(packed, upstream, expert_first, expert_second):
    local_count, model_width, hidden_width = expert_first.shape
    wide = local_count * hidden_width
    length, width = packed.shape
    total = upstream.shape[0]
    vmem = pl.BlockSpec(memory_space=pltpu.VMEM)
    hbm = pl.BlockSpec(memory_space=pl.ANY)
    low = jnp.bfloat16
    rows_sum, result, first_sum, second_sum = pl.pallas_call(
        functools.partial(expert_kernel, model_width, local_count),
        out_shape=(
            jax.ShapeDtypeStruct((length, width), jnp.float32),
            jax.ShapeDtypeStruct((total, model_width), low),
            jax.ShapeDtypeStruct((wide, model_width), jnp.float32),
            jax.ShapeDtypeStruct((wide, model_width), jnp.float32),
        ),
        in_specs=[vmem, hbm, vmem, vmem],
        out_specs=(vmem, hbm, vmem, vmem),
        scratch_shapes=[
            pltpu.VMEM((total, width), low),
            pltpu.VMEM((total, model_width), low),
            pltpu.VMEM((model_width, wide), low),
            pltpu.VMEM((wide, model_width), low),
            pltpu.VMEM((model_width, wide), low),
            pltpu.VMEM((total, wide), low),
            pltpu.VMEM((total, wide), low),
            pltpu.VMEM((16, 2 * length, width), low),
            *reduce_scratch(length, width),
            pltpu.VMEM((2, 2 * length, model_width), low),
            pltpu.SemaphoreType.DMA((2, N_SEM)),
            pltpu.SemaphoreType.DMA((2, N_SEM)),
            pltpu.SemaphoreType.DMA((2,)),
            pltpu.SemaphoreType.DMA,
        ],
        compiler_params=pltpu.CompilerParams(
            collective_id=0, has_side_effects=True, vmem_limit_bytes=62 * 2**20
        ),
        name="experts",
    )(packed, upstream, expert_first, expert_second.reshape(wide, model_width))
    first_sum = first_sum.reshape(local_count, hidden_width, model_width).transpose(0, 2, 1)
    return rows_sum, result, first_sum, second_sum.reshape(expert_second.shape)


def sums_kernel(shapes, *refs):
    count = len(shapes)
    ins, refs = refs[:count], refs[count:]
    first_out, outs, refs = refs[0], refs[1:count], refs[count:]
    place = Place()
    enter(place)
    reduces, gathers, loads = [], [], []
    for number, (rows, width) in enumerate(shapes):
        held, refs = refs[0], refs[1:]
        boxes, refs = refs[:8], refs[8:]
        sems, load_sem, refs = refs[0], refs[1], refs[2:]

        def source(k, core, rows=rows, ref=ins[number]):
            start = (2 * place.chip(k // 4, k % 4) + core) * rows
            return ref.at[pl.ds(pl.multiple_of(start, rows), rows)]

        reduces.append(
            Reduce(
                place,
                lambda k, held=held: held.at[k],
                lambda k, source=source: source(k, 1 - place.core),
                boxes,
                sems,
            )
        )
        loads.append(
            lambda k, source=source, held=held, sem=load_sem: pltpu.make_async_copy(
                source(k, place.core), held.at[k], sem.at[k]
            )
        )
        if number:
            buf, gather_sems, out_sem, refs = refs[0], refs[1], refs[2], refs[3:]
            gathers.append((Gather(place, buf, rows, gather_sems), outs[number - 1], out_sem))

    def begin(step, carry):
        k = 15 - step
        for reduce, load in zip(reduces, loads):
            load(k).start()
            reduce.copy("core", k).start()
        return carry

    lax.fori_loop(0, 16, begin, 0)

    def arrive(k, carry):
        for load in loads:
            load(k).wait()
        return carry

    lax.fori_loop(0, 16, arrive, 0)
    for kind, j in RETURN_ORDER:
        for reduce in reduces:
            getattr(reduce, kind)(*j)
    for number in reversed(range(count)):
        reduce = reduces[number]
        mine = first_out if number == 0 else gathers[number - 1][0].block(0, 0)

        def put(at, total, mine=mine):
            mine[at, :] = total.astype(mine.dtype)

        reduce.last(put)
        if number == 0:
            continue
        gathers[number - 1][0].begin()

    def pair_copy(number, q, j):
        gather, out, sem = gathers[number]
        rows = 2 * gather.rows
        at = pl.ds(pl.multiple_of(place.chip(q, j) * rows, rows), rows)
        return pltpu.make_async_copy(gather.buf.at[at], out.at[at], sem.at[4 * q + j])

    def store(q, j):
        for number in range(count - 1):
            gathers[number][0].whole(q, j)
            pair_copy(number, q, j).start()

    for kind, j, blocks in SPREAD_ORDER:
        for gather, _, _ in gathers:
            getattr(gather, kind)(*j)
        for block in blocks:
            store(*block)

    def drain(k, carry):
        for number in range(count - 1):
            pair_copy(number, k // 4, k % 4).wait()
        return carry

    lax.fori_loop(0, 16, drain, 0)
    for reduce in reduces:
        reduce.finish()
    for gather, _, _ in gathers:
        gather.finish()


def call_sums(parts):
    total = GRID[0] * GRID[1]
    shapes = []
    for part in parts:
        shapes.append((part.shape[0] // total, part.shape[1]))
    scratch = []
    for number, (rows, width) in enumerate(shapes):
        scratch += [
            pltpu.VMEM((16, rows, width), jnp.bfloat16),
            *reduce_scratch(rows, width),
            pltpu.SemaphoreType.DMA((2, N_SEM)),
            pltpu.SemaphoreType.DMA((16,)),
        ]
        if number:
            scratch += [
                pltpu.VMEM((total * rows, width), jnp.bfloat16),
                pltpu.SemaphoreType.DMA((2, N_SEM)),
                pltpu.SemaphoreType.DMA((16,)),
            ]
    hbm = pl.BlockSpec(memory_space=pl.ANY)
    rows, width = shapes[0]
    return pl.pallas_call(
        functools.partial(sums_kernel, shapes),
        out_shape=(
            jax.ShapeDtypeStruct((rows, width), jnp.float32),
            *(jax.ShapeDtypeStruct(part.shape, jnp.bfloat16) for part in parts[1:]),
        ),
        in_specs=[hbm] * len(parts),
        out_specs=(pl.BlockSpec(memory_space=pltpu.VMEM), *([hbm] * (len(parts) - 1))),
        scratch_shapes=scratch,
        compiler_params=pltpu.CompilerParams(
            collective_id=1, has_side_effects=True, vmem_limit_bytes=62 * 2**20
        ),
        name="sums",
    )(*parts)


def body(
    tokens,
    cotangent,
    gain_attention,
    gain_feedforward,
    query_weight,
    key_weight,
    value_weight,
    output_weight,
    value_router,
    output_router,
    expert_router,
    expert_first,
    expert_second,
    segments,
    value_ids,
    output_ids,
    ffn_ids,
):
    owner_total = lax.axis_size("dp") * lax.axis_size("expert")
    local_count = expert_first.shape[0]
    expert_count = local_count * owner_total
    shared = (
        gain_attention,
        query_weight,
        key_weight,
        value_weight,
        output_weight,
        value_router,
        output_router,
    )
    stream = tokens.astype(jnp.float32)
    upstream = cotangent.astype(jnp.float32)
    own_kernels = (lax.axis_size("dp"), lax.axis_size("expert")) == GRID
    if own_kernels:
        length, model_width = tokens.shape
        gate_width = -(-expert_count // 128) * 128
        (
            upstream_rows,
            packed,
            after_attention,
            normed_attention,
            normed_low,
            queries,
            key_rows,
            projected,
            values,
            probability,
            mixed,
            gated_rows,
            value_gates,
            value_slope,
            output_gates,
            output_slope,
            expert_slope,
        ) = call_attention(
            tokens,
            cotangent,
            gain_attention,
            gain_feedforward,
            shared[1:],
            expert_router,
            segments,
            value_ids[0],
            output_ids[0],
            ffn_ids[0],
            gate_width,
        )
        by_head = (length, HEADS, HEAD)
        by_expert = (length, HEADS, ATT_EXP)
        saved_parts = (
            normed_attention,
            queries.reshape(by_head),
            key_rows.reshape(by_head),
            value_slope.reshape(by_expert),
            output_slope.reshape(by_expert),
            value_gates.reshape(by_expert),
            output_gates.reshape(by_expert),
            tokens,
            projected.reshape(length, HEADS, ATT_EXP, HEAD),
            values.reshape(by_head),
            probability,
            probability.astype(jnp.bfloat16),
            mixed.reshape(by_head),
            gated_rows,
        )
        rows_sum, result, first_sum, second_sum = call_experts(
            packed, upstream_rows, expert_first, expert_second
        )
        token_grad = rows_sum[:, :model_width]
        gate_back = rows_sum[:, model_width : model_width + expert_count]
    else:
        after_attention, saved_parts = attention_forward(
            stream, segments[0], value_ids[0], output_ids[0], shared
        )
        normed_low = layer_norm(after_attention, gain_feedforward).astype(jnp.bfloat16)
        logits = jnp.dot(normed_low, expert_router, preferred_element_type=jnp.float32)
        sigmoid_out = jax.nn.sigmoid(logits)
        dense_gates = sigmoid_out * expert_mask(ffn_ids[0], expert_count)
        expert_slope = dense_gates * (1.0 - sigmoid_out)
        result, token_grad, gate_back, first_sum, second_sum = expert_exchange(
            after_attention.astype(jnp.bfloat16),
            cotangent,
            dense_gates.astype(jnp.bfloat16),
            expert_first,
            expert_second,
            max(1, owner_total // 32),
        )
    logit_grad = (gate_back.astype(jnp.float32) * expert_slope).astype(jnp.bfloat16)
    router_sum = jnp.einsum("sa,sb->ab", normed_low, logit_grad, preferred_element_type=jnp.float32)
    normed_grad = jnp.einsum(
        "sb,ab->sa", logit_grad, expert_router, preferred_element_type=jnp.float32
    )
    norm_value, norm_pull = jax.vjp(layer_norm, after_attention, gain_feedforward)
    after_extra, feed_gain_part = norm_pull(normed_grad)
    after_grad = upstream + token_grad.astype(jnp.float32) + after_extra
    stream_grad, attention_parts = attention_backward(after_grad, saved_parts, stream, shared)
    gain_part, query_part, key_part, value_part, output_part, value_router_part, output_router_part = attention_parts
    parts = (
        query_part,
        key_part,
        value_part,
        value_router_part,
        output_router_part,
        router_sum,
        gain_part[:, None],
        feed_gain_part[:, None],
    )
    low = jnp.concatenate([part.astype(jnp.bfloat16) for part in parts], axis=1)
    low = jnp.pad(low, ((0, 0), (0, -low.shape[1] % 256)))
    output_low = output_part.astype(jnp.bfloat16)
    if own_kernels:
        result, low, output_low = call_sums([result, low, output_low])
    else:
        low, output_low = lax.psum((low, output_low), BOTH)
    block_output = (after_attention + result.astype(jnp.float32)).astype(jnp.bfloat16)
    summed, start = [], 0
    for part in parts:
        summed.append(low[:, start : start + part.shape[1]].astype(jnp.float32))
        start += part.shape[1]
    query_sum, key_sum, value_sum, value_router_sum, output_router_sum, router_sum, *gains = summed
    summed = (
        gains[0][:, 0],
        gains[1][:, 0],
        query_sum,
        key_sum,
        value_sum,
        output_low.astype(jnp.float32),
        value_router_sum,
        output_router_sum,
        router_sum,
    )
    return (
        block_output,
        stream_grad,
        *summed,
        first_sum,
        second_sum,
    )


def solution(mesh):
    placed = (
        P(("dp", "expert"), None),
        P(("dp", "expert"), None),
        P(),
        P(),
        P(),
        P(),
        P(),
        P(),
        P(),
        P(),
        P(),
        P(("dp", "expert"), None, None),
        P(("dp", "expert"), None, None),
        P(("dp", "expert"), None),
        P(None, ("dp", "expert"), None, None),
        P(None, ("dp", "expert"), None, None),
        P(None, ("dp", "expert"), None),
    )
    return jax.shard_map(
        body,
        mesh=mesh,
        in_specs=placed,
        out_specs=(
            P(("dp", "expert"), None),
            P(("dp", "expert"), None),
            P(),
            P(),
            P(),
            P(),
            P(),
            P(),
            P(),
            P(),
            P(),
            P(("dp", "expert"), None, None),
            P(("dp", "expert"), None, None),
        ),
        check_vma=False,
    )
```

```python
import functools
import math

import jax
import jax.numpy as jnp
from jax import lax
from jax.experimental import pallas as pl
from jax.experimental.pallas import tpu as pltpu
from jax.sharding import PartitionSpec as P

HEADS = 4
HEAD = 128
ATT_EXP = 5


NEG_FILL = -1000000000.0


def layer_norm(stream, norm_gain):
    average = jnp.mean(stream, axis=-1, keepdims=True)
    centred = stream - average
    variance = jnp.mean(centred * centred, axis=-1, keepdims=True)
    return centred * lax.rsqrt(variance + 1e-05) * norm_gain


def expert_mask(picked_ids, expert_count):
    matches = picked_ids[..., None] == jnp.arange(expert_count, dtype=jnp.int32)
    return jnp.sum(matches.astype(jnp.float32), axis=-2)


def attention_forward(stream, document_ids, value_picks, output_picks, shared):
    (
        gain_attention,
        query_weight,
        key_weight,
        value_weight,
        output_weight,
        value_router,
        output_router,
    ) = shared
    length = stream.shape[0]
    normed_low = layer_norm(stream, gain_attention).astype(jnp.bfloat16)
    queries = (
        jnp.dot(normed_low, query_weight, preferred_element_type=jnp.float32)
        .astype(jnp.bfloat16)
        .reshape(length, HEADS, HEAD)
    )
    key_rows = (
        jnp.dot(normed_low, key_weight, preferred_element_type=jnp.float32)
        .astype(jnp.bfloat16)
        .reshape(length, HEADS, HEAD)
    )
    value_sig = jax.nn.sigmoid(
        jnp.dot(normed_low, value_router, preferred_element_type=jnp.float32)
    ).reshape(length, HEADS, ATT_EXP)
    output_sig = jax.nn.sigmoid(
        jnp.dot(normed_low, output_router, preferred_element_type=jnp.float32)
    ).reshape(length, HEADS, ATT_EXP)
    value_mask = expert_mask(value_picks, ATT_EXP)
    output_mask = expert_mask(output_picks, ATT_EXP)
    value_gates = value_mask * value_sig
    output_gates = output_mask * output_sig
    stream_low = stream.astype(jnp.bfloat16)
    projected = jnp.dot(stream_low, value_weight, preferred_element_type=jnp.float32).reshape(
        length, HEADS, ATT_EXP, HEAD
    )
    values = jnp.sum(value_gates[..., None] * projected, axis=2).astype(jnp.bfloat16)
    scores = jnp.einsum("qhd,khd->hqk", queries, key_rows, preferred_element_type=jnp.float32) * (
        1.0 / math.sqrt(HEAD)
    )
    positions = jnp.arange(length, dtype=jnp.int32)
    allowed = (document_ids[:, None] == document_ids[None, :]) & (
        positions[:, None] >= positions[None, :]
    )
    scores = jnp.where(allowed[None], scores, NEG_FILL)
    row_max = jnp.max(scores, axis=-1, keepdims=True)
    exponent = jnp.exp(scores - row_max)
    row_total = jnp.sum(exponent, axis=-1, keepdims=True)
    probability = exponent / row_total
    weights_low = probability.astype(jnp.bfloat16)
    mixed = jnp.einsum("hqk,khd->qhd", weights_low, values, preferred_element_type=jnp.float32)
    gated_rows = (
        (output_gates[..., None] * mixed[:, :, None, :])
        .reshape(length, HEADS * ATT_EXP * HEAD)
        .astype(jnp.bfloat16)
    )
    after_attention = stream + jnp.dot(
        gated_rows, output_weight, preferred_element_type=jnp.float32
    )
    saved_parts = (
        normed_low,
        queries,
        key_rows,
        value_gates * (1.0 - value_sig),
        output_gates * (1.0 - output_sig),
        value_gates,
        output_gates,
        stream_low,
        projected,
        values,
        probability,
        weights_low,
        mixed,
        gated_rows,
    )
    return (after_attention, saved_parts)


def attention_backward(after_grad, saved_parts, stream, shared):
    (
        gain_attention,
        query_weight,
        key_weight,
        value_weight,
        output_weight,
        value_router,
        output_router,
    ) = shared
    (
        normed_low,
        queries,
        key_rows,
        value_slope,
        output_slope,
        value_gates,
        output_gates,
        stream_low,
        projected,
        values,
        probability,
        weights_low,
        mixed,
        gated_rows,
    ) = saved_parts
    length = after_grad.shape[0]
    scale = 1.0 / math.sqrt(HEAD)
    after_low = after_grad.astype(jnp.bfloat16)
    output_part = jnp.einsum("sa,sb->ab", gated_rows, after_low, preferred_element_type=jnp.float32)
    gated_grad = jnp.einsum(
        "sb,ab->sa", after_low, output_weight, preferred_element_type=jnp.float32
    ).astype(jnp.bfloat16)
    gated_grad = gated_grad.reshape(length, HEADS, ATT_EXP, HEAD).astype(jnp.float32)
    mixed_grad = jnp.sum(output_gates[..., None] * gated_grad, axis=2).astype(jnp.bfloat16)
    output_gate_grad = jnp.sum(gated_grad * mixed[:, :, None, :], axis=3)
    prob_grad = jnp.einsum("qhd,khd->hqk", mixed_grad, values, preferred_element_type=jnp.float32)
    values_grad = jnp.einsum(
        "hqk,qhd->khd", weights_low, mixed_grad, preferred_element_type=jnp.float32
    ).astype(jnp.bfloat16)
    values_grad = values_grad.astype(jnp.float32)
    score_grad = (
        probability * (prob_grad - jnp.sum(probability * prob_grad, axis=-1, keepdims=True))
    ).astype(jnp.bfloat16)
    query_grad = (
        (
            jnp.einsum("hqk,khd->qhd", score_grad, key_rows, preferred_element_type=jnp.float32)
            * scale
        )
        .astype(jnp.bfloat16)
        .reshape(length, HEADS * HEAD)
    )
    key_grad = (
        (
            jnp.einsum("hqk,qhd->khd", score_grad, queries, preferred_element_type=jnp.float32)
            * scale
        )
        .astype(jnp.bfloat16)
        .reshape(length, HEADS * HEAD)
    )
    projected_grad = (
        (value_gates[..., None] * values_grad[:, :, None, :])
        .astype(jnp.bfloat16)
        .reshape(length, HEADS * ATT_EXP * HEAD)
    )
    value_gate_grad = jnp.sum(values_grad[:, :, None, :] * projected, axis=3)
    value_logit_grad = (
        (value_gate_grad * value_slope)
        .astype(jnp.bfloat16)
        .reshape(length, HEADS * ATT_EXP)
    )
    output_logit_grad = (
        (output_gate_grad * output_slope)
        .astype(jnp.bfloat16)
        .reshape(length, HEADS * ATT_EXP)
    )
    value_part = jnp.einsum(
        "sa,sb->ab", stream_low, projected_grad, preferred_element_type=jnp.float32
    )
    query_part = jnp.einsum("sa,sb->ab", normed_low, query_grad, preferred_element_type=jnp.float32)
    key_part = jnp.einsum("sa,sb->ab", normed_low, key_grad, preferred_element_type=jnp.float32)
    value_router_part = jnp.einsum(
        "sa,sb->ab", normed_low, value_logit_grad, preferred_element_type=jnp.float32
    )
    output_router_part = jnp.einsum(
        "sa,sb->ab", normed_low, output_logit_grad, preferred_element_type=jnp.float32
    )
    normed_grad = jnp.einsum(
        "sb,ab->sa", query_grad, query_weight, preferred_element_type=jnp.float32
    )
    normed_grad = normed_grad + jnp.einsum(
        "sb,ab->sa", key_grad, key_weight, preferred_element_type=jnp.float32
    )
    normed_grad = normed_grad + jnp.einsum(
        "sb,ab->sa", value_logit_grad, value_router, preferred_element_type=jnp.float32
    )
    normed_grad = normed_grad + jnp.einsum(
        "sb,ab->sa", output_logit_grad, output_router, preferred_element_type=jnp.float32
    )
    norm_value, norm_pull = jax.vjp(layer_norm, stream, gain_attention)
    stream_extra, gain_part = norm_pull(normed_grad)
    value_input = jnp.einsum(
        "sb,ab->sa", projected_grad, value_weight, preferred_element_type=jnp.float32
    )
    stream_grad = after_grad + stream_extra + value_input
    return (
        stream_grad,
        (
            gain_part,
            query_part,
            key_part,
            value_part,
            output_part,
            value_router_part,
            output_router_part,
        ),
    )


def expert_pass(rows, upstream_rows, gates, expert_first, expert_second):
    local_count, model_width, hidden_width = expert_first.shape
    wide = local_count * hidden_width
    first = expert_first.transpose(1, 0, 2).reshape(model_width, wide)
    second = expert_second.reshape(wide, model_width)
    gates_wide = jnp.repeat(gates.astype(jnp.float32), hidden_width, axis=1)
    hidden_pre = jnp.dot(rows, first, preferred_element_type=jnp.float32)
    hidden, gelu_pull = jax.vjp(jax.nn.gelu, hidden_pre)
    hidden = hidden.astype(jnp.bfloat16).astype(jnp.float32)
    gated_hidden = (gates_wide * hidden).astype(jnp.bfloat16)
    back = jnp.einsum("sd,fd->sf", upstream_rows, second, preferred_element_type=jnp.float32)
    gate_grad = jnp.sum((back * hidden).reshape(-1, local_count, hidden_width), axis=2)
    pre_grad = gelu_pull(gates_wide * back)[0].astype(jnp.bfloat16)
    result = jnp.dot(gated_hidden, second, preferred_element_type=jnp.float32)
    row_grad = jnp.einsum("sf,df->sd", pre_grad, first, preferred_element_type=jnp.float32)
    second_sum = jnp.einsum(
        "sf,sd->fd", gated_hidden, upstream_rows, preferred_element_type=jnp.float32
    )
    first_sum = jnp.einsum("sd,sf->df", rows, pre_grad, preferred_element_type=jnp.float32)
    first_sum = first_sum.reshape(model_width, local_count, hidden_width).transpose(1, 0, 2)
    return (
        result.astype(jnp.bfloat16),
        row_grad.astype(jnp.bfloat16),
        gate_grad.astype(jnp.bfloat16),
        first_sum,
        second_sum.reshape(expert_second.shape),
    )


BOTH = ("dp", "expert")


def expert_piece(after_low, upstream_low, dense_gates, expert_first, expert_second):
    local_count = expert_first.shape[0]
    me = lax.axis_index("dp") * lax.axis_size("expert") + lax.axis_index("expert")
    upstream_rows = lax.all_gather(upstream_low, BOTH, axis=0, tiled=True)
    rows = lax.all_gather(after_low, BOTH, axis=0, tiled=True)
    gates = lax.all_gather(dense_gates, BOTH, axis=0, tiled=True)
    gates = lax.dynamic_slice_in_dim(gates, me * local_count, local_count, axis=1)
    result, row_grad, gate_grad, first_sum, second_sum = expert_pass(
        rows, upstream_rows, gates, expert_first, expert_second
    )
    gate_back = lax.all_to_all(gate_grad, BOTH, split_axis=0, concat_axis=1, tiled=True)
    token_grad = lax.psum_scatter(row_grad, BOTH, scatter_dimension=0, tiled=True)
    result = lax.psum_scatter(result, BOTH, scatter_dimension=0, tiled=True)
    return (result, token_grad, gate_back), (first_sum, second_sum)


def expert_exchange(after_low, upstream_low, dense_gates, expert_first, expert_second, pieces):
    if pieces == 1:
        back, sums = expert_piece(
            after_low, upstream_low, dense_gates, expert_first, expert_second
        )
        return (*back, *sums)

    def step(totals, piece):
        back, sums = expert_piece(*piece, expert_first, expert_second)
        return (totals[0] + sums[0], totals[1] + sums[1]), back

    cut = lambda array: array.reshape(pieces, -1, array.shape[1])
    start = (
        jnp.zeros(expert_first.shape, jnp.float32),
        jnp.zeros(expert_second.shape, jnp.float32),
    )
    sums, back = lax.scan(step, start, (cut(after_low), cut(upstream_low), cut(dense_gates)))
    return (*(part.reshape(-1, part.shape[2]) for part in back), *sums)


MESH = pl.DeviceIdType.MESH
GRID = (4, 8)
N_SEM = 47


class Place:
    def __init__(self):
        dp, expert = lax.axis_index("dp"), lax.axis_index("expert")
        self.y, self.x = dp // 2, dp % 2
        self.z, self.core = expert // 2, expert % 2
        self.dp = dp
        self.me = dp * GRID[1] + expert
        self.x_peer = (2 * self.y + 1 - self.x, expert)
        self.y_peer = (2 * (1 - self.y) + self.x, expert)
        self.core_peer = (dp, 2 * self.z + 1 - self.core)
        self.middle = (self.z + self.z // 2) % 2
        self.main = 1 + self.z % 2
        self.minor = 3 * (self.z // 2)

    def along_z(self, z):
        return (self.dp, 2 * z + self.core)

    def z_at(self, j):
        near = j + self.middle * (1 - 2 * j) * (1 - j // 2)
        return near + self.z // 2 * (3 - 2 * near)

    def chip(self, q, j):
        return ((self.y + q // 2) % 2 * 2 + (self.x + q % 2) % 2) * 4 + self.z_at(j)

    def if_middle(self, action):
        pl.when(self.middle == 1)(action)


def enter(place):
    barrier = pltpu.get_barrier_semaphore()

    def signal(peer):
        pl.semaphore_signal(barrier, inc=1, device_id=peer, device_id_type=MESH)

    for peer in (place.x_peer, place.y_peer, place.core_peer, place.along_z(place.main)):
        signal(peer)
    place.if_middle(lambda: signal(place.along_z(place.minor)))
    pl.when(place.middle == 0)(lambda: pl.semaphore_wait(barrier, 4))
    place.if_middle(lambda: pl.semaphore_wait(barrier, 5))


def remote(src, dst, send, recv, peer):
    return pltpu.make_async_remote_copy(
        src_ref=src,
        dst_ref=dst,
        send_sem=send,
        recv_sem=recv,
        device_id=peer,
        device_id_type=MESH,
    )


def cut_columns(width):
    tiles = width // 128
    split = tiles // 2
    outer = max(1, tiles * 3 // 10)
    return outer * 128, split * 128, (tiles - outer) * 128


class Gather:
    def __init__(self, place, buf, rows, sems):
        self.place, self.buf, self.rows = place, buf, rows
        self.width = buf.shape[1]
        self.d_end, self.split, self.c_start = cut_columns(self.width)
        self.send, self.recv = sems.at[0], sems.at[1]

    def block(self, q, j, columns=slice(None)):
        start = (2 * self.place.chip(q, j) + self.place.core) * self.rows
        return self.buf.at[pl.ds(pl.multiple_of(start, self.rows), self.rows), columns]

    def copy(self, kind, j, q=0):
        place = self.place
        if kind == "x0":
            ref, number, peer = self.block(0, 0), 15, place.x_peer
        elif kind == "y0":
            ref, number, peer = self.block(0, 0), 19, place.y_peer
        elif kind == "x":
            ref, number, peer = self.block(0, j, slice(0, self.c_start)), 15 + j, place.x_peer
        elif kind == "y":
            ref, number, peer = self.block(0, j, slice(self.d_end, None)), 19 + j, place.y_peer
        elif kind == "a":
            ref, number, peer = self.block(1, j, slice(self.split, None)), 23 + j, place.y_peer
        elif kind == "b":
            ref, number, peer = self.block(2, j, slice(0, self.split)), 27 + j, place.x_peer
        else:
            ref, number, peer = self.block(q, j), 31 + 4 * q + j, place.core_peer
        return remote(ref, ref, self.send.at[number], self.recv.at[number], peer)

    def z_copy(self, part, j, number, z, receiver_j):
        columns = (slice(None), slice(self.c_start, None), slice(0, self.d_end))[part]
        ref = self.block(part, j, columns)
        return remote(
            ref,
            ref,
            self.send.at[5 * part + number],
            self.recv.at[3 * part + receiver_j - 1],
            self.place.along_z(z),
        )

    def z_own(self, part):
        place = self.place
        self.z_copy(part, 0, 0, place.main, 1 + place.middle).start()
        place.if_middle(lambda: self.z_copy(part, 0, 1, place.minor, 1).start())

    def outer_own(self, middle):
        @pl.when(self.place.middle == middle)
        def _():
            self.z_own(1)
            self.z_own(2)

    def z_pass(self, part, j):
        place = self.place
        first = 1 - (j + 2) // 4
        z = place.minor + first * (place.main - place.minor)
        return self.z_copy(part, j, 1 + j, z, j + 2 * first)

    def z_arrive(self, part, j):
        self.z_copy(part, j, 0, self.place.main, j).wait_recv()
        self.place.if_middle(lambda: self.z_pass(part, j).start())

    def begin(self):
        self.z_own(0)
        self.copy("x0", 0).start()
        self.copy("y0", 0).start()
        self.copy("core", 0, 0).start()

    def line(self, j):
        self.z_arrive(0, j)
        self.copy("x", j).start()
        self.copy("y", j).start()
        self.copy("core", j, 0).start()
        if j == 3:
            self.outer_own(1)

    def sides_first(self):
        self.copy("x0", 0).wait_recv()
        self.copy("a", 0).start()
        self.copy("core", 0, 1).start()
        self.copy("y0", 0).wait_recv()
        self.copy("b", 0).start()
        self.copy("core", 0, 2).start()
        self.outer_own(0)

    def sides(self, j):
        self.z_arrive(1, j)
        self.z_arrive(2, j)
        self.copy("x", j).wait_recv()
        self.copy("a", j).start()
        self.copy("core", j, 1).start()
        self.copy("y", j).wait_recv()
        self.copy("b", j).start()
        self.copy("core", j, 2).start()

    def corner(self, j):
        self.copy("a", j).wait_recv()
        self.copy("b", j).wait_recv()
        self.copy("core", j, 3).start()

    def whole(self, q, j):
        self.copy("core", j, q).wait_recv()

    def finish(self):
        place = self.place
        for part in range(3):
            self.z_copy(part, 0, 0, place.main, 1).wait_send()

        def middle():
            for part in range(3):
                self.z_copy(part, 0, 1, place.minor, 1).wait_send()

                def passed(j, carry):
                    self.z_pass(part, j).wait_send()
                    return carry

                lax.fori_loop(1, 4, passed, 0)

        place.if_middle(middle)
        self.copy("x0", 0).wait_send()
        self.copy("y0", 0).wait_send()

        def line(j, carry):
            self.copy("x", j).wait_send()
            self.copy("y", j).wait_send()
            return carry

        lax.fori_loop(1, 4, line, 0)

        def step(j, carry):
            self.copy("a", j).wait_send()
            self.copy("b", j).wait_send()
            for q in range(4):
                self.copy("core", j, q).wait_send()
            return carry

        lax.fori_loop(0, 4, step, 0)


class Reduce:
    def __init__(self, place, own, other, boxes, sems, held=None):
        self.place, self.other = place, other
        self.other_in, self.a_in, self.b_in, self.x_in, self.y_in = boxes[:5]
        self.own = own or (lambda k: self.other_in.at[k])
        self.extra = held or (lambda k: self.other_in.at[k])
        self.z_in = boxes[5:]
        self.rows, self.width = self.other_in.shape[1:]
        self.d_end, self.split, self.c_start = cut_columns(self.width)
        self.send, self.recv = sems.at[0], sems.at[1]

    def copy(self, kind, k):
        place = self.place
        j = k % 4
        if kind == "core":
            src, dst, number, peer = self.other(k), self.other_in.at[k], k, place.core_peer
        elif kind == "a":
            src = self.own(k).at[:, self.split :]
            dst, number, peer = self.a_in.at[j], 16 + j, place.y_peer
        elif kind == "b":
            src = self.own(k).at[:, : self.split]
            dst, number, peer = self.b_in.at[j], 20 + j, place.x_peer
        elif kind == "x0":
            src, dst, number, peer = self.own(k), self.x_in.at[0], 24, place.x_peer
        elif kind == "y0":
            src, dst, number, peer = self.own(k), self.y_in.at[0], 28, place.y_peer
        elif kind == "x":
            src = self.own(k).at[:, : self.c_start]
            dst, number, peer = self.x_in.at[j, :, : self.c_start], 24 + j, place.x_peer
        else:
            src = self.own(k).at[:, self.d_end :]
            dst, number, peer = self.y_in.at[j, :, self.d_end :], 28 + j, place.y_peer
        return remote(src, dst, self.send.at[number], self.recv.at[number], peer)

    def z_columns(self, part):
        return (slice(None), slice(self.c_start, None), slice(0, self.d_end))[part]

    def z_copy(self, part, j):
        place = self.place
        first = 1 - (j + 2) // 4
        box = place.middle * (j // 3) + (1 - place.middle) * (j + 1)
        z = place.main + place.middle * first * (place.minor - place.main)
        return remote(
            self.own(4 * part + j).at[:, self.z_columns(part)],
            self.z_in[part].at[box],
            self.send.at[32 + 5 * part + j],
            self.recv.at[32 + 5 * part + box],
            place.along_z(z),
        )

    def z_wait(self, part, box):
        self.copy_box(part, box).wait_recv()

    def copy_box(self, part, box):
        ref = self.z_in[part].at[box]
        return remote(
            ref,
            ref,
            self.send.at[32 + 5 * part],
            self.recv.at[32 + 5 * part + box],
            self.place.along_z(self.place.main),
        )

    def z_give(self, part, j):
        def middle():
            box = j + (j + 2) // 4
            self.z_wait(part, box)
            self.add(4 * part + j, self.z_columns(part), [lambda at: self.z_in[part][box, at, :]])

        self.place.if_middle(middle)
        self.z_copy(part, j).start()

    def z_last(self, part):
        columns = self.z_columns(part)
        self.z_wait(part, 0)
        self.add(4 * part, columns, [lambda at: self.z_in[part][0, at, :]])

        def middle():
            self.z_wait(part, 2)
            self.add(4 * part, columns, [lambda at: self.z_in[part][2, at, :]])

        self.place.if_middle(middle)

    def add(self, k, columns, terms):
        own = self.own(k)

        def step(number, carry):
            at = pl.ds(pl.multiple_of(number * 16, 16), 16)
            total = own[at, columns].astype(jnp.float32)
            for term in terms:
                total = total + term(at).astype(jnp.float32)
            own[at, columns] = total.astype(own.dtype)
            return carry

        lax.fori_loop(0, self.rows // 16, step, 0)

    def corner(self, j):
        k = 12 + j
        self.copy("core", k).wait_recv()
        self.add(k, slice(None), [lambda at: self.extra(k)[at, :]])
        self.copy("a", k).start()
        self.copy("b", k).start()

    def side_x(self, j):
        k, split = 4 + j, self.split
        self.copy("core", k).wait_recv()
        self.add(k, slice(0, split), [lambda at: self.extra(k)[at, :split]])
        self.copy("a", k).wait_recv()
        self.add(
            k,
            slice(split, None),
            [lambda at: self.extra(k)[at, split:], lambda at: self.a_in[j, at, :]],
        )

    def side_y(self, j):
        k, split = 8 + j, self.split
        self.copy("core", k).wait_recv()
        self.add(k, slice(split, None), [lambda at: self.extra(k)[at, split:]])
        self.copy("b", k).wait_recv()
        self.add(
            k,
            slice(0, split),
            [lambda at: self.extra(k)[at, :split], lambda at: self.b_in[j, at, :]],
        )

    def sides(self, j):
        self.side_x(j)
        self.copy("x", 4 + j).start()
        self.z_give(1, j)
        self.side_y(j)
        self.copy("y", 8 + j).start()
        self.z_give(2, j)

    def sides_last(self):
        self.side_x(0)
        self.side_y(0)
        self.z_last(1)
        self.copy("x0", 4).start()
        self.z_last(2)
        self.copy("y0", 8).start()

    def line(self, j):
        self.copy("core", j).wait_recv()
        self.copy("x", j).wait_recv()
        self.copy("y", j).wait_recv()
        d_end, c_start = self.d_end, self.c_start
        boxes = (self.extra(j), self.x_in.at[j], self.y_in.at[j])
        for columns, used in (
            (slice(0, d_end), boxes[:2]),
            (slice(d_end, c_start), boxes),
            (slice(c_start, None), (boxes[0], boxes[2])),
        ):
            self.add(j, columns, [lambda at, box=box: box[at, columns] for box in used])
        self.z_give(0, j)

    def last(self, put):
        self.copy("core", 0).wait_recv()
        self.copy("x0", 0).wait_recv()
        self.copy("y0", 0).wait_recv()
        self.z_wait(0, 0)
        own = self.own(0)

        def sum_up(middle):
            def step(number, carry):
                at = pl.ds(pl.multiple_of(number * 16, 16), 16)
                total = own[at, :].astype(jnp.float32)
                for box in (self.extra(0), self.x_in.at[0], self.y_in.at[0], self.z_in[0].at[0]):
                    total = total + box[at, :].astype(jnp.float32)
                if middle:
                    total = total + self.z_in[0][2, at, :].astype(jnp.float32)
                put(at, total)
                return carry

            lax.fori_loop(0, own.shape[0] // 16, step, 0)

        @pl.when(self.place.middle == 1)
        def _():
            self.z_wait(0, 2)
            sum_up(True)

        pl.when(self.place.middle == 0)(lambda: sum_up(False))

    def finish(self):
        def step(j, carry):
            self.copy("a", 12 + j).wait_send()
            self.copy("b", 12 + j).wait_send()
            for q in range(4):
                self.copy("core", 4 * q + j).wait_send()
            return carry

        lax.fori_loop(0, 4, step, 0)

        def outer(j, carry):
            self.copy("x", 4 + j).wait_send()
            self.copy("y", 8 + j).wait_send()
            for part in range(3):
                self.z_copy(part, j).wait_send()
            return carry

        lax.fori_loop(1, 4, outer, 0)
        self.copy("x0", 4).wait_send()
        self.copy("y0", 8).wait_send()


def reduce_scratch(rows, width):
    low = jnp.bfloat16
    d_end, split, c_start = cut_columns(width)
    return [
        pltpu.VMEM((16, rows, width), low),
        pltpu.VMEM((4, rows, width - split), low),
        pltpu.VMEM((4, rows, split), low),
        pltpu.VMEM((4, rows, width), low),
        pltpu.VMEM((4, rows, width), low),
        pltpu.VMEM((5, rows, width), low),
        pltpu.VMEM((5, rows, width - c_start), low),
        pltpu.VMEM((5, rows, d_end), low),
    ]


GELU_C = math.sqrt(2.0 / math.pi)
GELU_K = 0.044715


def mm(left, right):
    return jnp.dot(left, right, preferred_element_type=jnp.float32)


def mm_tn(left, right):
    return lax.dot_general(left, right, (((0,), (0,)), ((), ())), preferred_element_type=jnp.float32)


def norm_parts(stream):
    average = jnp.mean(stream, axis=-1, keepdims=True)
    centred = stream - average
    variance = jnp.mean(centred * centred, axis=-1, keepdims=True)
    scale = lax.rsqrt(variance + 1e-05)
    return centred * scale, scale


def norm_pull(normed_grad, unit, scale, gain):
    inner = normed_grad * gain
    mean = jnp.mean(inner, axis=-1, keepdims=True)
    along = jnp.mean(inner * unit, axis=-1, keepdims=True)
    gain_grad = jnp.sum(normed_grad * unit, axis=0, keepdims=True)
    return scale * (inner - mean - unit * along), gain_grad


def mm_nt(left, right):
    return lax.dot_general(left, right, (((1,), (1,)), ((), ())), preferred_element_type=jnp.float32)


OUTPUT_LANE = 32


def join_routers(joined, value_router_ref, output_router_ref):
    count = value_router_ref.shape[0]
    joined[...] = jnp.zeros_like(joined)
    joined[:count, :] = value_router_ref[...]
    joined[OUTPUT_LANE : OUTPUT_LANE + count, :] = output_router_ref[...]


def attention_kernel(
    tokens_ref,
    cotangent_ref,
    gain_attention_ref,
    gain_feedforward_ref,
    query_in,
    key_in,
    value_in,
    output_in,
    value_router_ref,
    output_router_ref,
    expert_router_ref,
    segments_ref,
    value_ids_ref,
    output_ids_ref,
    ffn_ids_ref,
    upstream_out,
    packed_out,
    after_out,
    normed_out,
    normed_ffn_out,
    queries_out,
    keys_out,
    projected_out,
    values_out,
    probability_out,
    mixed_out,
    gated_out,
    gates_out,
    slopes_out,
    expert_slope_out,
    query_ref,
    key_ref,
    value_ref,
    output_ref,
    routers,
    all_ids,
    own_sem,
    weight_sems,
    gather_sems,
):
    place = Place()
    length, model_width = tokens_ref.shape
    expert_count = expert_router_ref.shape[0]
    loads = [
        pltpu.make_async_copy(src, dst, weight_sems.at[number])
        for number, (src, dst) in enumerate(
            (
                (query_in, query_ref),
                (key_in, key_ref),
                (value_in, value_ref),
                (output_in, output_ref),
            )
        )
    ]
    gather = Gather(place, upstream_out, length, gather_sems)
    own_copy = pltpu.make_async_copy(cotangent_ref, gather.block(0, 0), own_sem)
    own_copy.start()
    for load in loads:
        load.start()
    enter(place)
    own_copy.wait()
    gather.begin()

    join_routers(routers, value_router_ref, output_router_ref)
    top = value_ids_ref.shape[1]
    all_ids[...] = jnp.zeros_like(all_ids)
    for head in range(HEADS):
        at = head * top
        all_ids[at : at + top, :] = value_ids_ref[head].astype(jnp.float32) + float(head * ATT_EXP)
        all_ids[16 + at : 16 + at + top, :] = output_ids_ref[head].astype(jnp.float32) + float(
            OUTPUT_LANE + head * ATT_EXP
        )
    ffn_top = ffn_ids_ref.shape[0]
    all_ids[32 : 32 + ffn_top, :] = ffn_ids_ref[...].astype(jnp.float32)
    ids = all_ids[...].T
    lane = lax.broadcasted_iota(jnp.int32, (length, gates_out.shape[1]), 1).astype(jnp.float32)

    def named(columns):
        mask = jnp.zeros(lane.shape, jnp.float32)
        for at in columns:
            mask = jnp.where(lane == ids[:, at : at + 1], 1.0, mask)
        return mask

    stream_low = tokens_ref[...]
    stream = stream_low.astype(jnp.float32)
    unit, _ = norm_parts(stream)
    normed = (unit * gain_attention_ref[...]).astype(jnp.bfloat16)
    normed_out[...] = normed
    sig = jax.nn.sigmoid(mm_nt(normed, routers[...]))
    gates = named([*range(HEADS * top), *range(16, 16 + HEADS * top)]) * sig
    gates_out[...] = gates
    slopes_out[...] = gates * (1.0 - sig)
    loads[0].wait()
    queries_out[...] = mm(normed, query_ref[...]).astype(jnp.bfloat16)
    loads[1].wait()
    keys_out[...] = mm(normed, key_ref[...]).astype(jnp.bfloat16)
    gather.line(1)
    gather.sides_first()
    gather.line(2)
    loads[2].wait()
    head_width = ATT_EXP * HEAD
    for head in range(HEADS):
        columns = slice(head * head_width, (head + 1) * head_width)
        projected_out[:, columns] = mm(stream_low, value_ref[:, columns])
        total = jnp.zeros((length, HEAD), jnp.float32)
        for e in range(ATT_EXP):
            at = head * ATT_EXP + e
            total = total + gates[:, at : at + 1] * projected_out[:, at * HEAD : (at + 1) * HEAD]
        values_out[:, head * HEAD : (head + 1) * HEAD] = total.astype(jnp.bfloat16)
    gather.line(3)
    documents = jnp.broadcast_to(segments_ref[...].astype(jnp.float32), (length, length))
    row = lax.broadcasted_iota(jnp.int32, (length, length), 0)
    column = lax.broadcasted_iota(jnp.int32, (length, length), 1)
    allowed = (documents == documents.T) & (row >= column)
    for head in range(HEADS):
        columns = slice(head * HEAD, (head + 1) * HEAD)
        scores = mm_nt(queries_out[:, columns], keys_out[:, columns]) * (1.0 / math.sqrt(HEAD))
        scores = jnp.where(allowed, scores, NEG_FILL)
        exponent = jnp.exp(scores - jnp.max(scores, axis=-1, keepdims=True))
        probability = exponent / jnp.sum(exponent, axis=-1, keepdims=True)
        probability_out[head] = probability
        mixed = mm(probability.astype(jnp.bfloat16), values_out[:, columns])
        mixed_out[:, columns] = mixed
        for e in range(ATT_EXP):
            at = head * ATT_EXP + e
            gate = gates[:, OUTPUT_LANE + at : OUTPUT_LANE + at + 1]
            gated_out[:, at * HEAD : (at + 1) * HEAD] = (gate * mixed).astype(jnp.bfloat16)
    gather.corner(0)
    loads[3].wait()
    after = stream + mm(gated_out[...], output_ref[...])
    after_out[...] = after
    packed_out[:, :model_width] = after.astype(jnp.bfloat16)
    unit, _ = norm_parts(after)
    normed_ffn = (unit * gain_feedforward_ref[...]).astype(jnp.bfloat16)
    normed_ffn_out[...] = normed_ffn
    expert_sig = jax.nn.sigmoid(mm_nt(normed_ffn, expert_router_ref[...]))
    expert_gates = named(range(32, 32 + ffn_top))[:, :expert_count] * expert_sig
    gate_width = packed_out.shape[1] - model_width
    packed_out[:, model_width:] = jnp.zeros((length, gate_width), jnp.bfloat16)
    packed_out[:, model_width : model_width + expert_count] = expert_gates.astype(jnp.bfloat16)
    expert_slope_out[...] = jnp.zeros((length, gate_width), jnp.float32)
    expert_slope_out[:, :expert_count] = expert_gates * (1.0 - expert_sig)
    for j in (1, 2, 3):
        gather.sides(j)
    for j in (1, 2, 3):
        gather.corner(j)

    def arrived(k, carry):
        gather.whole(k // 4, k % 4)
        return carry

    lax.fori_loop(0, 16, arrived, 0)
    gather.finish()


def call_attention(
    tokens,
    cotangent,
    gains,
    weights,
    routers,
    segments,
    value_ids,
    output_ids,
    ffn_ids,
    gate_width,
):
    length, model_width = tokens.shape
    total = GRID[0] * GRID[1] * length
    wide = weights[3].shape[0]
    narrow = HEADS * HEAD
    low, full = jnp.bfloat16, jnp.float32
    shapes = (
        ((total, model_width), low),
        ((length, model_width + gate_width), low),
        ((length, model_width), full),
        ((length, model_width), low),
        ((length, model_width), low),
        ((length, narrow), low),
        ((length, narrow), low),
        ((length, wide), full),
        ((length, narrow), low),
        ((HEADS, length, length), full),
        ((length, narrow), full),
        ((length, wide), low),
        ((length, 128), full),
        ((length, 128), full),
        ((length, gate_width), full),
    )
    vmem = pl.BlockSpec(memory_space=pltpu.VMEM)
    hbm = pl.BlockSpec(memory_space=pl.ANY)
    return pl.pallas_call(
        attention_kernel,
        out_shape=tuple(jax.ShapeDtypeStruct(*shape) for shape in shapes),
        in_specs=[vmem] * 4 + [hbm] * 4 + [vmem] * 7,
        out_specs=(hbm, *([vmem] * (len(shapes) - 1))),
        scratch_shapes=[
            *(pltpu.VMEM(weight.shape, low) for weight in weights),
            pltpu.VMEM((128, model_width), low),
            pltpu.VMEM((128, length), full),
            pltpu.SemaphoreType.DMA,
            pltpu.SemaphoreType.DMA((4,)),
            pltpu.SemaphoreType.DMA((2, N_SEM)),
        ],
        compiler_params=pltpu.CompilerParams(
            collective_id=2, has_side_effects=True, vmem_limit_bytes=62 * 2**20
        ),
        name="attention",
    )(
        tokens,
        cotangent,
        *gains,
        *weights,
        *routers,
        segments,
        value_ids.transpose(1, 2, 0),
        output_ids.transpose(1, 2, 0),
        ffn_ids.T,
    )


HELD = 6
HELD_ORDER = (15, 14, 13, 7, 11, 12, 6, 10, 5, 9, 3, 4, 8, 2, 1, 0)
GAIN_LANE = 64


def backward_kernel(
    rows_ref,
    tokens_ref,
    cotangent_ref,
    gain_attention_ref,
    gain_feedforward_ref,
    value_router_ref,
    output_router_ref,
    expert_router_ref,
    after_ref,
    normed_ref,
    normed_ffn_ref,
    queries_ref,
    keys_ref,
    projected_ref,
    values_ref,
    probability_ref,
    mixed_ref,
    gated_ref,
    gates_ref,
    slopes_ref,
    expert_slope_ref,
    query_in,
    key_in,
    value_in,
    output_in,
    result_in,
    block_out,
    stream_out,
    low_out,
    output_low_out,
    query_ref,
    key_ref,
    value_ref,
    output_ref,
    routers,
    expert_router,
    after_grad,
    after_low,
    gated_grad,
    projected_grad,
    both_grad,
    held,
    low_part,
    output_part,
    low_own,
    output_own,
    weight_sems,
    held_sems,
    own_sems,
    *refs,
):
    place = Place()
    length, model_width = tokens_ref.shape
    wide = value_ref.shape[1]
    narrow = query_ref.shape[1]
    expert_count = expert_router_ref.shape[0]
    low_rows, output_rows = low_own.shape[0], output_own.shape[0]
    low_type = jnp.bfloat16

    def held_copy(number):
        k = HELD_ORDER[number]
        start = (2 * place.chip(k // 4, k % 4) + place.core) * length
        return pltpu.make_async_copy(
            result_in.at[pl.ds(pl.multiple_of(start, length), length)],
            held.at[number % HELD],
            held_sems.at[number % HELD],
        )

    def other_rows(ref, rows):
        def get(k):
            start = (2 * place.chip(k // 4, k % 4) + 1 - place.core) * rows
            return ref.at[pl.ds(pl.multiple_of(start, rows), rows)]

        return get

    def own_rows(ref, rows):
        def get(k):
            start = (2 * place.chip(k // 4, k % 4) + place.core) * rows
            return ref.at[pl.ds(pl.multiple_of(start, rows), rows)]

        return get

    slots = {k: number % HELD for number, k in enumerate(HELD_ORDER)}
    results = Reduce(
        place,
        None,
        other_rows(result_in, length),
        refs[0:8],
        refs[8],
        lambda k: held.at[slots[k]],
    )
    outputs = Reduce(
        place,
        own_rows(output_part, output_rows),
        other_rows(output_part, output_rows),
        refs[9:17],
        refs[17],
    )
    lows = Reduce(
        place,
        own_rows(low_part, low_rows),
        other_rows(low_part, low_rows),
        refs[18:26],
        refs[26],
    )
    spread_outputs = Gather(place, output_low_out, output_rows, refs[27])
    spread_lows = Gather(place, low_out, low_rows, refs[28])
    weights = ((output_in, output_ref), (query_in, query_ref), (key_in, key_ref), (value_in, value_ref))
    loads = [
        pltpu.make_async_copy(src, dst, weight_sems.at[number])
        for number, (src, dst) in enumerate(weights)
    ]

    def hand_over(reduce):
        def step(number, carry):
            reduce.copy("core", 15 - number).start()
            return carry

        lax.fori_loop(0, 16, step, 0)

    fetched = [0]

    def result_event(kind, *j):
        used = {"corner": 1, "sides": 2, "line": 1, "sides_last": 2, "last": 1}[kind]
        start = fetched[0]
        for number in range(start, start + used):
            held_copy(number).wait()
        if kind == "last":

            def put(at, total):
                block_out[at, :] = (after_ref[at, :] + total).astype(low_type)

            results.last(put)
        else:
            getattr(results, kind)(*j)
        for number in range(start + HELD, start + HELD + used):
            if number < len(HELD_ORDER):
                held_copy(number).start()
        fetched[0] = start + used

    def send_around(reduce, gather, own, own_sem):
        def put(at, total):
            own[at, :] = total.astype(low_type)

        reduce.last(put)
        copy = pltpu.make_async_copy(own, gather.block(0, 0), own_sem)
        copy.start()
        copy.wait()
        gather.begin()

    for number in range(HELD):
        held_copy(number).start()
    for load in loads:
        load.start()
    enter(place)
    hand_over(results)
    result_event("corner", 3)
    result_event("corner", 2)
    result_event("corner", 1)

    join_routers(routers, value_router_ref, output_router_ref)
    expert_router[...] = jnp.zeros_like(expert_router)
    expert_router[:expert_count, :] = expert_router_ref[...]
    logit_grad = (rows_ref[:, model_width:] * expert_slope_ref[...]).astype(low_type)
    unit, scale = norm_parts(after_ref[...])
    through, gain_feedforward_grad = norm_pull(
        mm(logit_grad, expert_router[...]), unit, scale, gain_feedforward_ref[...]
    )
    after_grad[...] = cotangent_ref[...].astype(jnp.float32) + rows_ref[:, :model_width] + through
    after_low[...] = after_grad[...].astype(low_type)
    expert_column = wide + 2 * narrow + 128
    low_part[:, expert_column:] = mm_tn(normed_ffn_ref[...], logit_grad).astype(low_type)
    tile = 256

    def output_tile(number, carry):
        at = pl.ds(pl.multiple_of(number * tile, tile), tile)
        output_part[at, :] = mm_tn(gated_ref[:, at], after_low[...]).astype(low_type)
        return carry

    lax.fori_loop(0, wide // tile, output_tile, 0)
    hand_over(outputs)
    result_event("sides", 3)
    result_event("corner", 0)
    loads[0].wait()

    def gated_tile(number, carry):
        at = pl.ds(pl.multiple_of(number * tile, tile), tile)
        gated_grad[:, at] = mm_nt(after_low[...], output_ref[at, :]).astype(low_type)
        return carry

    lax.fori_loop(0, wide // tile, gated_tile, 0)
    outputs.corner(3)
    result_event("sides", 2)
    outputs.corner(2)
    outputs.corner(1)

    lane = lax.broadcasted_iota(jnp.int32, (length, 128), 1)
    gate_grads = jnp.zeros((length, 128), jnp.float32)
    inverse = 1.0 / math.sqrt(HEAD)
    for head in range(HEADS):
        columns = slice(head * HEAD, (head + 1) * HEAD)
        mixed = mixed_ref[:, columns]
        mixed_grad = jnp.zeros((length, HEAD), jnp.float32)
        for e in range(ATT_EXP):
            at = head * ATT_EXP + e
            part = gated_grad[:, at * HEAD : (at + 1) * HEAD].astype(jnp.float32)
            lane_at = OUTPUT_LANE + at
            mixed_grad = mixed_grad + gates_ref[:, lane_at : lane_at + 1] * part
            gate_grads = jnp.where(
                lane == lane_at, jnp.sum(part * mixed, axis=1, keepdims=True), gate_grads
            )
        mixed_grad = mixed_grad.astype(low_type)
        probability = probability_ref[head]
        prob_grad = mm_nt(mixed_grad, values_ref[:, columns])
        inner = jnp.sum(probability * prob_grad, axis=-1, keepdims=True)
        score_grad = (probability * (prob_grad - inner)).astype(low_type)
        both_grad[:, columns] = (mm(score_grad, keys_ref[:, columns]) * inverse).astype(low_type)
        both_grad[:, narrow + head * HEAD : narrow + (head + 1) * HEAD] = (
            mm_tn(score_grad, queries_ref[:, columns]) * inverse
        ).astype(low_type)
        values_grad = mm_tn(probability.astype(low_type), mixed_grad)
        values_grad = values_grad.astype(low_type).astype(jnp.float32)
        for e in range(ATT_EXP):
            at = head * ATT_EXP + e
            wide_at = slice(at * HEAD, (at + 1) * HEAD)
            projected_grad[:, wide_at] = (gates_ref[:, at : at + 1] * values_grad).astype(low_type)
            gate_grad = jnp.sum(values_grad * projected_ref[:, wide_at], axis=1, keepdims=True)
            gate_grads = jnp.where(lane == at, gate_grad, gate_grads)
    router_grad = (gate_grads * slopes_ref[...]).astype(low_type)
    result_event("sides", 1)
    outputs.sides(3)
    result_event("line", 3)
    outputs.corner(0)

    def value_tile(number, carry):
        at = pl.ds(pl.multiple_of(number * tile, tile), tile)
        to = pl.ds(pl.multiple_of(2 * narrow + number * tile, tile), tile)
        low_part[:, to] = mm_tn(tokens_ref[...], projected_grad[:, at]).astype(low_type)
        return carry

    def both_tile(number, carry):
        at = pl.ds(pl.multiple_of(number * tile, tile), tile)
        low_part[:, at] = mm_tn(normed_ref[...], both_grad[:, at]).astype(low_type)
        return carry

    lax.fori_loop(0, wide // tile, value_tile, 0)
    lax.fori_loop(0, 2 * narrow // tile, both_tile, 0)
    loads[1].wait()
    loads[2].wait()
    normed_grad = mm_nt(both_grad[:, :narrow], query_ref[...])
    normed_grad = normed_grad + mm_nt(both_grad[:, narrow:], key_ref[...])
    normed_grad = normed_grad + mm(router_grad, routers[...])
    unit, scale = norm_parts(tokens_ref[...].astype(jnp.float32))
    through, gain_attention_grad = norm_pull(normed_grad, unit, scale, gain_attention_ref[...])
    stream_out[...] = after_grad[...] + through
    gain_columns = [
        jnp.broadcast_to(grad, (128, model_width)).T
        for grad in (gain_attention_grad, gain_feedforward_grad)
    ]
    small = mm_tn(normed_ref[...], router_grad)
    small_lane = lax.broadcasted_iota(jnp.int32, (model_width, 128), 1)
    small = jnp.where(small_lane == GAIN_LANE, gain_columns[0], small)
    small = jnp.where(small_lane == GAIN_LANE + 1, gain_columns[1], small)
    small_column = wide + 2 * narrow
    low_part[:, small_column:expert_column] = small.astype(low_type)
    hand_over(lows)
    result_event("sides_last")
    outputs.sides(2)
    result_event("line", 2)
    outputs.sides(1)
    result_event("line", 1)
    lows.corner(3)
    outputs.line(3)
    lows.corner(2)
    result_event("last")
    lows.corner(1)
    outputs.sides_last()
    lows.sides(3)
    outputs.line(2)
    lows.corner(0)
    outputs.line(1)
    lows.sides(2)
    send_around(outputs, spread_outputs, output_own, own_sems.at[0])
    loads[3].wait()
    stream_out[...] += mm_nt(projected_grad[...], value_ref[...])
    lows.sides(1)
    spread_outputs.line(1)
    lows.line(3)
    spread_outputs.sides_first()
    lows.sides_last()
    spread_outputs.line(2)
    lows.line(2)
    spread_outputs.line(3)
    lows.line(1)
    spread_outputs.corner(0)
    send_around(lows, spread_lows, low_own, own_sems.at[1])
    for j in (1, 2, 3):
        spread_outputs.sides(j)
    spread_lows.line(1)
    spread_lows.sides_first()
    spread_lows.line(2)
    for j in (1, 2, 3):
        spread_outputs.corner(j)
    spread_lows.line(3)
    spread_lows.corner(0)
    for j in (1, 2, 3):
        spread_lows.sides(j)
    for j in (1, 2, 3):
        spread_lows.corner(j)

    def arrived(k, carry):
        spread_outputs.whole(k // 4, k % 4)
        spread_lows.whole(k // 4, k % 4)
        return carry

    lax.fori_loop(0, 16, arrived, 0)
    for reduce in (results, outputs, lows):
        reduce.finish()
    spread_outputs.finish()
    spread_lows.finish()


def call_backward(rows, tokens, cotangent, gains, routers, saved, weights, result):
    length, model_width = tokens.shape
    total = GRID[0] * GRID[1]
    wide, narrow = weights[2].shape[1], weights[0].shape[1]
    low_width = wide + 2 * narrow + 256
    low_rows, output_rows = model_width // total, wide // total
    low, full = jnp.bfloat16, jnp.float32
    vmem = pl.BlockSpec(memory_space=pltpu.VMEM)
    hbm = pl.BlockSpec(memory_space=pl.ANY)
    sems = pltpu.SemaphoreType.DMA((2, N_SEM))
    return pl.pallas_call(
        backward_kernel,
        out_shape=(
            jax.ShapeDtypeStruct((length, model_width), low),
            jax.ShapeDtypeStruct((length, model_width), full),
            jax.ShapeDtypeStruct((model_width, low_width), low),
            jax.ShapeDtypeStruct((wide, model_width), low),
        ),
        in_specs=[vmem] * 21 + [hbm] * 5,
        out_specs=(vmem, vmem, hbm, hbm),
        scratch_shapes=[
            *(pltpu.VMEM(weight.shape, low) for weight in weights),
            pltpu.VMEM((128, model_width), low),
            pltpu.VMEM((128, model_width), low),
            pltpu.VMEM((length, model_width), full),
            pltpu.VMEM((length, model_width), low),
            pltpu.VMEM((length, wide), low),
            pltpu.VMEM((length, wide), low),
            pltpu.VMEM((length, 2 * narrow), low),
            pltpu.VMEM((HELD, length, model_width), low),
            pltpu.VMEM((model_width, low_width), low),
            pltpu.VMEM((wide, model_width), low),
            pltpu.VMEM((low_rows, low_width), low),
            pltpu.VMEM((output_rows, model_width), low),
            pltpu.SemaphoreType.DMA((4,)),
            pltpu.SemaphoreType.DMA((HELD,)),
            pltpu.SemaphoreType.DMA((2,)),
            *reduce_scratch(length, model_width),
            sems,
            *reduce_scratch(output_rows, model_width),
            sems,
            *reduce_scratch(low_rows, low_width),
            sems,
            sems,
            sems,
        ],
        compiler_params=pltpu.CompilerParams(
            collective_id=1, has_side_effects=True, vmem_limit_bytes=63 * 2**20
        ),
        name="backward",
    )(rows, tokens, cotangent, *gains, *routers, *saved, *weights, result)


def widen_kernel(low_ref, output_low_ref, query, key, value, output, small, expert):
    full = jnp.float32
    narrow, wide = query.shape[1], value.shape[1]
    query[...] = low_ref[:, :narrow].astype(full)
    key[...] = low_ref[:, narrow : 2 * narrow].astype(full)
    value[...] = low_ref[:, 2 * narrow : 2 * narrow + wide].astype(full)
    output[...] = output_low_ref[...].astype(full)
    start = 2 * narrow + wide
    small[...] = low_ref[:, start : start + 128].astype(full).T
    expert[...] = low_ref[:, start + 128 :].astype(full).T


def call_widen(low, output_low, narrow):
    model_width, low_width = low.shape
    wide = output_low.shape[0]
    steps = model_width // 128
    full = jnp.float32
    rows = lambda height, width: pl.BlockSpec((height, width), lambda i: (i, 0))
    columns = pl.BlockSpec((128, 128), lambda i: (0, i))
    return pl.pallas_call(
        widen_kernel,
        grid=(steps,),
        out_shape=(
            jax.ShapeDtypeStruct((model_width, narrow), full),
            jax.ShapeDtypeStruct((model_width, narrow), full),
            jax.ShapeDtypeStruct((model_width, wide), full),
            jax.ShapeDtypeStruct((wide, model_width), full),
            jax.ShapeDtypeStruct((128, model_width), full),
            jax.ShapeDtypeStruct((128, model_width), full),
        ),
        in_specs=[rows(128, low_width), rows(wide // steps, model_width)],
        out_specs=(
            rows(128, narrow),
            rows(128, narrow),
            rows(128, wide),
            rows(wide // steps, model_width),
            columns,
            columns,
        ),
        compiler_params=pltpu.CompilerParams(vmem_limit_bytes=40 * 2**20),
        name="widen",
    )(low, output_low)


def expert_kernel(
    model_width,
    local_count,
    packed_ref,
    upstream_ref,
    first_in,
    second_in,
    rows_out,
    result_out,
    first_out,
    second_out,
    gathered,
    upstream,
    first_ref,
    first_t_ref,
    second_t_ref,
    gated_hidden,
    pre_grads,
    partial,
    *refs,
):
    place = Place()
    length = packed_ref.shape[0]
    pair = 2 * length
    gate_width = packed_ref.shape[1] - model_width
    hidden_width = first_ref.shape[1] // local_count
    boxes, (result_stage, gather_sems, reduce_sems, result_sems, upstream_sem) = refs[:8], refs[8:]
    upstream_copy = pltpu.make_async_copy(upstream_ref, upstream, upstream_sem)
    upstream_copy.start()
    enter(place)
    gather = Gather(place, gathered, length, gather_sems)
    gathered[pl.ds(pl.multiple_of(place.me * length, length), length), :] = packed_ref[...]
    gather.begin()
    second_ref = second_in
    for e in range(local_count):
        columns = slice(e * hidden_width, (e + 1) * hidden_width)
        first_ref[:, columns] = first_in[e]
        first_t_ref[columns, :] = first_in[e].astype(jnp.float32).T.astype(jnp.bfloat16)
        second_t_ref[:, columns] = second_in[columns, :].astype(jnp.float32).T.astype(jnp.bfloat16)
    pick_row = lax.broadcasted_iota(jnp.int32, (gate_width, first_ref.shape[1]), 0)
    pick_column = lax.broadcasted_iota(jnp.int32, (gate_width, first_ref.shape[1]), 1)
    pick_gates = jnp.where(
        pick_row == place.me * local_count + pick_column // hidden_width, 1.0, 0.0
    ).astype(jnp.bfloat16)

    def own(k):
        return partial.at[k, pl.ds(pl.multiple_of(place.core * length, length), length)]

    def other(k):
        return partial.at[k, pl.ds(pl.multiple_of((1 - place.core) * length, length), length)]

    reduce = Reduce(place, own, other, boxes, reduce_sems)

    def result_copy(slot, chip):
        return pltpu.make_async_copy(
            result_stage.at[slot],
            result_out.at[pl.ds(pl.multiple_of(chip * pair, pair), pair)],
            result_sems.at[slot],
        )

    def compute(step, q, j):
        chip = place.chip(q, j)
        rows = pl.ds(pl.multiple_of(chip * pair, pair), pair)
        hidden_pre = mm(gathered[rows, :model_width], first_ref[...])
        back = mm(upstream[rows, :], second_t_ref[...])
        gates = mm(gathered[rows, model_width:], pick_gates)
        square = hidden_pre * hidden_pre
        bent = jnp.tanh(GELU_C * hidden_pre * (1.0 + GELU_K * square))
        grow = 0.5 * (1.0 + bent)
        slope = grow + 0.5 * hidden_pre * (1.0 - bent * bent) * (
            GELU_C * (1.0 + 3.0 * GELU_K * square)
        )
        hidden = (hidden_pre * grow).astype(jnp.bfloat16).astype(jnp.float32)
        gated = (gates * hidden).astype(jnp.bfloat16)
        pre_grad = (gates * back * slope).astype(jnp.bfloat16)
        gated_hidden[rows, :] = gated
        pre_grads[rows, :] = pre_grad
        k = 4 * q + j
        partial[k, :, :model_width] = mm(pre_grad, first_t_ref[...]).astype(jnp.bfloat16)
        product = hidden * back
        column = lax.broadcasted_iota(jnp.int32, (pair, gate_width), 1) - place.me * local_count
        gate_grad = jnp.zeros((pair, gate_width), jnp.float32)
        for e in range(local_count):
            own_sum = jnp.sum(
                product[:, e * hidden_width : (e + 1) * hidden_width], axis=1, keepdims=True
            )
            gate_grad = jnp.where(column == e, own_sum, gate_grad)
        partial[k, :, model_width:] = gate_grad.astype(jnp.bfloat16)
        reduce.copy("core", k).start()
        slot = step % 2

        @pl.when(step >= 2)
        def _():
            result_copy(slot, chip).wait()

        result_stage[slot] = mm(gated, second_ref[...]).astype(jnp.bfloat16)
        result_copy(slot, chip).start()

    upstream_copy.wait()

    def arrive(actions):
        for kind, j in actions:
            if kind == "sides_first":
                gather.sides_first()
            elif kind == "line_middle":
                place.if_middle(lambda: gather.line(j))
            elif kind == "line_end":
                pl.when(place.middle == 0)(lambda: gather.line(j))
            else:
                getattr(gather, kind)(j)

    before = {
        1: [("line", 1), ("sides_first", 0), ("line_middle", 2)],
        4: [("corner", 0), ("line_end", 2), ("line_middle", 3)],
        6: [("line_end", 3), ("sides", 1)],
        9: [("corner", 1), ("sides", 2)],
        12: [("corner", 2), ("sides", 3)],
        15: [("corner", 3)],
    }
    order = [(0, 0), (0, 1), (1, 0), (2, 0), (3, 0), (0, 2), (0, 3), (1, 1)]
    order += [(2, 1), (3, 1), (1, 2), (2, 2), (3, 2), (1, 3), (2, 3), (3, 3)]

    def pick(step, values):
        total = 0
        for number, value in enumerate(values):
            total = total + value * jnp.where(step == number, 1, 0)
        return total

    def walk(step, carry):
        for number, actions in before.items():
            pl.when(step == number)(functools.partial(arrive, actions))
        q = pick(step, [pair_[0] for pair_ in order])
        j = pick(step, [pair_[1] for pair_ in order])
        gather.whole(q, j)
        compute(step, q, j)
        return carry

    lax.fori_loop(0, 16, walk, 0)
    piece = gathered.shape[0] // 8

    def weight_piece(number):
        rows = pl.ds(pl.multiple_of(number * piece, piece), piece)
        second = mm_tn(gated_hidden[rows, :], upstream[rows, :])
        first = mm_tn(pre_grads[rows, :], gathered[rows, :model_width])

        @pl.when(number == 0)
        def _():
            second_out[...] = second
            first_out[...] = first

        @pl.when(number > 0)
        def _():
            second_out[...] += second
            first_out[...] += first

    give_back = [
        [("corner", 3), ("corner", 2)],
        [("corner", 1), ("sides", 3)],
        [("corner", 0)],
        [("sides", 2)],
        [("sides", 1)],
        [("line", 3)],
        [("sides_last", 0)],
        [("line", 2)],
    ]

    def give(step, carry):
        for number, actions in enumerate(give_back):

            @pl.when(step == number)
            def _(actions=actions):
                for kind, j in actions:
                    if kind == "sides_last":
                        reduce.sides_last()
                    else:
                        getattr(reduce, kind)(j)

        weight_piece(step)
        return carry

    lax.fori_loop(0, len(give_back), give, 0)
    reduce.line(1)

    def put(at, total):
        rows_out[at, :] = total

    reduce.last(put)
    for slot in range(2):
        result_copy(slot, 0).wait()
    gather.finish()
    reduce.finish()


def call_experts(packed, upstream, expert_first, expert_second):
    local_count, model_width, hidden_width = expert_first.shape
    wide = local_count * hidden_width
    length, width = packed.shape
    total = upstream.shape[0]
    vmem = pl.BlockSpec(memory_space=pltpu.VMEM)
    hbm = pl.BlockSpec(memory_space=pl.ANY)
    low = jnp.bfloat16
    rows_sum, result, first_sum, second_sum = pl.pallas_call(
        functools.partial(expert_kernel, model_width, local_count),
        out_shape=(
            jax.ShapeDtypeStruct((length, width), jnp.float32),
            jax.ShapeDtypeStruct((total, model_width), low),
            jax.ShapeDtypeStruct((wide, model_width), jnp.float32),
            jax.ShapeDtypeStruct((wide, model_width), jnp.float32),
        ),
        in_specs=[vmem, hbm, vmem, vmem],
        out_specs=(vmem, hbm, vmem, vmem),
        scratch_shapes=[
            pltpu.VMEM((total, width), low),
            pltpu.VMEM((total, model_width), low),
            pltpu.VMEM((model_width, wide), low),
            pltpu.VMEM((wide, model_width), low),
            pltpu.VMEM((model_width, wide), low),
            pltpu.VMEM((total, wide), low),
            pltpu.VMEM((total, wide), low),
            pltpu.VMEM((16, 2 * length, width), low),
            *reduce_scratch(length, width),
            pltpu.VMEM((2, 2 * length, model_width), low),
            pltpu.SemaphoreType.DMA((2, N_SEM)),
            pltpu.SemaphoreType.DMA((2, N_SEM)),
            pltpu.SemaphoreType.DMA((2,)),
            pltpu.SemaphoreType.DMA,
        ],
        compiler_params=pltpu.CompilerParams(
            collective_id=0, has_side_effects=True, vmem_limit_bytes=62 * 2**20
        ),
        name="experts",
    )(packed, upstream, expert_first, expert_second.reshape(wide, model_width))
    first_sum = first_sum.reshape(local_count, hidden_width, model_width).transpose(0, 2, 1)
    return rows_sum, result, first_sum, second_sum.reshape(expert_second.shape)


def general_body(
    tokens,
    cotangent,
    gain_attention,
    gain_feedforward,
    query_weight,
    key_weight,
    value_weight,
    output_weight,
    value_router,
    output_router,
    expert_router,
    expert_first,
    expert_second,
    segments,
    value_ids,
    output_ids,
    ffn_ids,
):
    owner_total = lax.axis_size("dp") * lax.axis_size("expert")
    local_count = expert_first.shape[0]
    expert_count = local_count * owner_total
    shared = (
        gain_attention,
        query_weight,
        key_weight,
        value_weight,
        output_weight,
        value_router,
        output_router,
    )
    stream = tokens.astype(jnp.float32)
    upstream = cotangent.astype(jnp.float32)
    after_attention, saved_parts = attention_forward(
        stream, segments[0], value_ids[0], output_ids[0], shared
    )
    normed_low = layer_norm(after_attention, gain_feedforward).astype(jnp.bfloat16)
    logits = jnp.dot(normed_low, expert_router, preferred_element_type=jnp.float32)
    sigmoid_out = jax.nn.sigmoid(logits)
    dense_gates = sigmoid_out * expert_mask(ffn_ids[0], expert_count)
    expert_slope = dense_gates * (1.0 - sigmoid_out)
    result, token_grad, gate_back, first_sum, second_sum = expert_exchange(
        after_attention.astype(jnp.bfloat16),
        cotangent,
        dense_gates.astype(jnp.bfloat16),
        expert_first,
        expert_second,
        max(1, owner_total // 32),
    )
    logit_grad = (gate_back.astype(jnp.float32) * expert_slope).astype(jnp.bfloat16)
    router_sum = jnp.einsum("sa,sb->ab", normed_low, logit_grad, preferred_element_type=jnp.float32)
    normed_grad = jnp.einsum(
        "sb,ab->sa", logit_grad, expert_router, preferred_element_type=jnp.float32
    )
    norm_value, norm_pull = jax.vjp(layer_norm, after_attention, gain_feedforward)
    after_extra, feed_gain_part = norm_pull(normed_grad)
    after_grad = upstream + token_grad.astype(jnp.float32) + after_extra
    stream_grad, attention_parts = attention_backward(after_grad, saved_parts, stream, shared)
    gain_part, query_part, key_part, value_part, output_part, value_router_part, output_router_part = attention_parts
    parts = (
        query_part,
        key_part,
        value_part,
        value_router_part,
        output_router_part,
        router_sum,
        gain_part[:, None],
        feed_gain_part[:, None],
    )
    low = jnp.concatenate([part.astype(jnp.bfloat16) for part in parts], axis=1)
    low = jnp.pad(low, ((0, 0), (0, -low.shape[1] % 256)))
    output_low = output_part.astype(jnp.bfloat16)
    low, output_low = lax.psum((low, output_low), BOTH)
    block_output = (after_attention + result.astype(jnp.float32)).astype(jnp.bfloat16)
    summed, start = [], 0
    for part in parts:
        summed.append(low[:, start : start + part.shape[1]].astype(jnp.float32))
        start += part.shape[1]
    query_sum, key_sum, value_sum, value_router_sum, output_router_sum, router_sum, *gains = summed
    summed = (
        gains[0][:, 0],
        gains[1][:, 0],
        query_sum,
        key_sum,
        value_sum,
        output_low.astype(jnp.float32),
        value_router_sum,
        output_router_sum,
        router_sum,
    )
    return (
        block_output,
        stream_grad,
        *summed,
        first_sum,
        second_sum,
    )


def kernel_body(
    tokens,
    cotangent,
    gain_attention,
    gain_feedforward,
    query_weight,
    key_weight,
    value_weight,
    output_weight,
    value_router,
    output_router,
    expert_router,
    expert_first,
    expert_second,
    segments,
    value_ids,
    output_ids,
    ffn_ids,
):
    expert_count = expert_router.shape[1]
    gate_width = -(-expert_count // 128) * 128
    gains = (gain_attention[None], gain_feedforward[None])
    weights = (query_weight, key_weight, value_weight, output_weight)
    routers = (value_router.T, output_router.T, expert_router.T)
    upstream_rows, packed, *saved = call_attention(
        tokens,
        cotangent,
        gains,
        weights,
        routers,
        segments,
        value_ids[0],
        output_ids[0],
        ffn_ids[0],
        gate_width,
    )
    rows_sum, result, first_sum, second_sum = call_experts(
        packed, upstream_rows, expert_first, expert_second
    )
    block_output, stream_grad, low, output_low = call_backward(
        rows_sum, tokens, cotangent, gains, routers, saved, weights, result
    )
    query_sum, key_sum, value_sum, output_sum, small, expert_small = call_widen(
        low, output_low, query_weight.shape[1]
    )
    router_width = value_router.shape[1]
    return (
        block_output,
        stream_grad,
        small[GAIN_LANE],
        small[GAIN_LANE + 1],
        query_sum,
        key_sum,
        value_sum,
        output_sum,
        small[:router_width].T,
        small[OUTPUT_LANE : OUTPUT_LANE + router_width].T,
        expert_small[:expert_count].T,
        first_sum,
        second_sum,
    )


def body(*args):
    if (lax.axis_size("dp"), lax.axis_size("expert")) == GRID:
        return kernel_body(*args)
    return general_body(*args)


def solution(mesh):
    placed = (
        P(("dp", "expert"), None),
        P(("dp", "expert"), None),
        P(),
        P(),
        P(),
        P(),
        P(),
        P(),
        P(),
        P(),
        P(),
        P(("dp", "expert"), None, None),
        P(("dp", "expert"), None, None),
        P(("dp", "expert"), None),
        P(None, ("dp", "expert"), None, None),
        P(None, ("dp", "expert"), None, None),
        P(None, ("dp", "expert"), None),
    )
    return jax.shard_map(
        body,
        mesh=mesh,
        in_specs=placed,
        out_specs=(
            P(("dp", "expert"), None),
            P(("dp", "expert"), None),
            P(),
            P(),
            P(),
            P(),
            P(),
            P(),
            P(),
            P(),
            P(),
            P(("dp", "expert"), None, None),
            P(("dp", "expert"), None, None),
        ),
        check_vma=False,
    )
```

```python
import functools
import math

import jax
import jax.numpy as jnp
from jax import lax
from jax.experimental import pallas as pl
from jax.experimental.pallas import tpu as pltpu
from jax.sharding import PartitionSpec as P

HEADS = 4
HEAD = 128
ATT_EXP = 5


NEG_FILL = -1000000000.0


def layer_norm(stream, norm_gain):
    average = jnp.mean(stream, axis=-1, keepdims=True)
    centred = stream - average
    variance = jnp.mean(centred * centred, axis=-1, keepdims=True)
    return centred * lax.rsqrt(variance + 1e-05) * norm_gain


def expert_mask(picked_ids, expert_count):
    matches = picked_ids[..., None] == jnp.arange(expert_count, dtype=jnp.int32)
    return jnp.sum(matches.astype(jnp.float32), axis=-2)


def attention_forward(stream, document_ids, value_picks, output_picks, shared):
    (
        gain_attention,
        query_weight,
        key_weight,
        value_weight,
        output_weight,
        value_router,
        output_router,
    ) = shared
    length = stream.shape[0]
    normed_low = layer_norm(stream, gain_attention).astype(jnp.bfloat16)
    queries = (
        jnp.dot(normed_low, query_weight, preferred_element_type=jnp.float32)
        .astype(jnp.bfloat16)
        .reshape(length, HEADS, HEAD)
    )
    key_rows = (
        jnp.dot(normed_low, key_weight, preferred_element_type=jnp.float32)
        .astype(jnp.bfloat16)
        .reshape(length, HEADS, HEAD)
    )
    value_sig = jax.nn.sigmoid(
        jnp.dot(normed_low, value_router, preferred_element_type=jnp.float32)
    ).reshape(length, HEADS, ATT_EXP)
    output_sig = jax.nn.sigmoid(
        jnp.dot(normed_low, output_router, preferred_element_type=jnp.float32)
    ).reshape(length, HEADS, ATT_EXP)
    value_mask = expert_mask(value_picks, ATT_EXP)
    output_mask = expert_mask(output_picks, ATT_EXP)
    value_gates = value_mask * value_sig
    output_gates = output_mask * output_sig
    stream_low = stream.astype(jnp.bfloat16)
    projected = jnp.dot(stream_low, value_weight, preferred_element_type=jnp.float32).reshape(
        length, HEADS, ATT_EXP, HEAD
    )
    values = jnp.sum(value_gates[..., None] * projected, axis=2).astype(jnp.bfloat16)
    scores = jnp.einsum("qhd,khd->hqk", queries, key_rows, preferred_element_type=jnp.float32) * (
        1.0 / math.sqrt(HEAD)
    )
    positions = jnp.arange(length, dtype=jnp.int32)
    allowed = (document_ids[:, None] == document_ids[None, :]) & (
        positions[:, None] >= positions[None, :]
    )
    scores = jnp.where(allowed[None], scores, NEG_FILL)
    row_max = jnp.max(scores, axis=-1, keepdims=True)
    exponent = jnp.exp(scores - row_max)
    row_total = jnp.sum(exponent, axis=-1, keepdims=True)
    probability = exponent / row_total
    weights_low = probability.astype(jnp.bfloat16)
    mixed = jnp.einsum("hqk,khd->qhd", weights_low, values, preferred_element_type=jnp.float32)
    gated_rows = (
        (output_gates[..., None] * mixed[:, :, None, :])
        .reshape(length, HEADS * ATT_EXP * HEAD)
        .astype(jnp.bfloat16)
    )
    after_attention = stream + jnp.dot(
        gated_rows, output_weight, preferred_element_type=jnp.float32
    )
    saved_parts = (
        normed_low,
        queries,
        key_rows,
        value_gates * (1.0 - value_sig),
        output_gates * (1.0 - output_sig),
        value_gates,
        output_gates,
        stream_low,
        projected,
        values,
        probability,
        weights_low,
        mixed,
        gated_rows,
    )
    return (after_attention, saved_parts)


def attention_backward(after_grad, saved_parts, stream, shared):
    (
        gain_attention,
        query_weight,
        key_weight,
        value_weight,
        output_weight,
        value_router,
        output_router,
    ) = shared
    (
        normed_low,
        queries,
        key_rows,
        value_slope,
        output_slope,
        value_gates,
        output_gates,
        stream_low,
        projected,
        values,
        probability,
        weights_low,
        mixed,
        gated_rows,
    ) = saved_parts
    length = after_grad.shape[0]
    scale = 1.0 / math.sqrt(HEAD)
    after_low = after_grad.astype(jnp.bfloat16)
    output_part = jnp.einsum("sa,sb->ab", gated_rows, after_low, preferred_element_type=jnp.float32)
    gated_grad = jnp.einsum(
        "sb,ab->sa", after_low, output_weight, preferred_element_type=jnp.float32
    ).astype(jnp.bfloat16)
    gated_grad = gated_grad.reshape(length, HEADS, ATT_EXP, HEAD).astype(jnp.float32)
    mixed_grad = jnp.sum(output_gates[..., None] * gated_grad, axis=2).astype(jnp.bfloat16)
    output_gate_grad = jnp.sum(gated_grad * mixed[:, :, None, :], axis=3)
    prob_grad = jnp.einsum("qhd,khd->hqk", mixed_grad, values, preferred_element_type=jnp.float32)
    values_grad = jnp.einsum(
        "hqk,qhd->khd", weights_low, mixed_grad, preferred_element_type=jnp.float32
    ).astype(jnp.bfloat16)
    values_grad = values_grad.astype(jnp.float32)
    score_grad = (
        probability * (prob_grad - jnp.sum(probability * prob_grad, axis=-1, keepdims=True))
    ).astype(jnp.bfloat16)
    query_grad = (
        (
            jnp.einsum("hqk,khd->qhd", score_grad, key_rows, preferred_element_type=jnp.float32)
            * scale
        )
        .astype(jnp.bfloat16)
        .reshape(length, HEADS * HEAD)
    )
    key_grad = (
        (
            jnp.einsum("hqk,qhd->khd", score_grad, queries, preferred_element_type=jnp.float32)
            * scale
        )
        .astype(jnp.bfloat16)
        .reshape(length, HEADS * HEAD)
    )
    projected_grad = (
        (value_gates[..., None] * values_grad[:, :, None, :])
        .astype(jnp.bfloat16)
        .reshape(length, HEADS * ATT_EXP * HEAD)
    )
    value_gate_grad = jnp.sum(values_grad[:, :, None, :] * projected, axis=3)
    value_logit_grad = (
        (value_gate_grad * value_slope)
        .astype(jnp.bfloat16)
        .reshape(length, HEADS * ATT_EXP)
    )
    output_logit_grad = (
        (output_gate_grad * output_slope)
        .astype(jnp.bfloat16)
        .reshape(length, HEADS * ATT_EXP)
    )
    value_part = jnp.einsum(
        "sa,sb->ab", stream_low, projected_grad, preferred_element_type=jnp.float32
    )
    query_part = jnp.einsum("sa,sb->ab", normed_low, query_grad, preferred_element_type=jnp.float32)
    key_part = jnp.einsum("sa,sb->ab", normed_low, key_grad, preferred_element_type=jnp.float32)
    value_router_part = jnp.einsum(
        "sa,sb->ab", normed_low, value_logit_grad, preferred_element_type=jnp.float32
    )
    output_router_part = jnp.einsum(
        "sa,sb->ab", normed_low, output_logit_grad, preferred_element_type=jnp.float32
    )
    normed_grad = jnp.einsum(
        "sb,ab->sa", query_grad, query_weight, preferred_element_type=jnp.float32
    )
    normed_grad = normed_grad + jnp.einsum(
        "sb,ab->sa", key_grad, key_weight, preferred_element_type=jnp.float32
    )
    normed_grad = normed_grad + jnp.einsum(
        "sb,ab->sa", value_logit_grad, value_router, preferred_element_type=jnp.float32
    )
    normed_grad = normed_grad + jnp.einsum(
        "sb,ab->sa", output_logit_grad, output_router, preferred_element_type=jnp.float32
    )
    norm_value, norm_pull = jax.vjp(layer_norm, stream, gain_attention)
    stream_extra, gain_part = norm_pull(normed_grad)
    value_input = jnp.einsum(
        "sb,ab->sa", projected_grad, value_weight, preferred_element_type=jnp.float32
    )
    stream_grad = after_grad + stream_extra + value_input
    return (
        stream_grad,
        (
            gain_part,
            query_part,
            key_part,
            value_part,
            output_part,
            value_router_part,
            output_router_part,
        ),
    )


def expert_pass(rows, upstream_rows, gates, expert_first, expert_second):
    local_count, model_width, hidden_width = expert_first.shape
    wide = local_count * hidden_width
    first = expert_first.transpose(1, 0, 2).reshape(model_width, wide)
    second = expert_second.reshape(wide, model_width)
    gates_wide = jnp.repeat(gates.astype(jnp.float32), hidden_width, axis=1)
    hidden_pre = jnp.dot(rows, first, preferred_element_type=jnp.float32)
    hidden, gelu_pull = jax.vjp(jax.nn.gelu, hidden_pre)
    hidden = hidden.astype(jnp.bfloat16).astype(jnp.float32)
    gated_hidden = (gates_wide * hidden).astype(jnp.bfloat16)
    back = jnp.einsum("sd,fd->sf", upstream_rows, second, preferred_element_type=jnp.float32)
    gate_grad = jnp.sum((back * hidden).reshape(-1, local_count, hidden_width), axis=2)
    pre_grad = gelu_pull(gates_wide * back)[0].astype(jnp.bfloat16)
    result = jnp.dot(gated_hidden, second, preferred_element_type=jnp.float32)
    row_grad = jnp.einsum("sf,df->sd", pre_grad, first, preferred_element_type=jnp.float32)
    second_sum = jnp.einsum(
        "sf,sd->fd", gated_hidden, upstream_rows, preferred_element_type=jnp.float32
    )
    first_sum = jnp.einsum("sd,sf->df", rows, pre_grad, preferred_element_type=jnp.float32)
    first_sum = first_sum.reshape(model_width, local_count, hidden_width).transpose(1, 0, 2)
    return (
        result.astype(jnp.bfloat16),
        row_grad.astype(jnp.bfloat16),
        gate_grad.astype(jnp.bfloat16),
        first_sum,
        second_sum.reshape(expert_second.shape),
    )


BOTH = ("dp", "expert")


def expert_piece(after_low, upstream_low, dense_gates, expert_first, expert_second):
    local_count = expert_first.shape[0]
    me = lax.axis_index("dp") * lax.axis_size("expert") + lax.axis_index("expert")
    upstream_rows = lax.all_gather(upstream_low, BOTH, axis=0, tiled=True)
    rows = lax.all_gather(after_low, BOTH, axis=0, tiled=True)
    gates = lax.all_gather(dense_gates, BOTH, axis=0, tiled=True)
    gates = lax.dynamic_slice_in_dim(gates, me * local_count, local_count, axis=1)
    result, row_grad, gate_grad, first_sum, second_sum = expert_pass(
        rows, upstream_rows, gates, expert_first, expert_second
    )
    gate_back = lax.all_to_all(gate_grad, BOTH, split_axis=0, concat_axis=1, tiled=True)
    token_grad = lax.psum_scatter(row_grad, BOTH, scatter_dimension=0, tiled=True)
    result = lax.psum_scatter(result, BOTH, scatter_dimension=0, tiled=True)
    return (result, token_grad, gate_back), (first_sum, second_sum)


def expert_exchange(after_low, upstream_low, dense_gates, expert_first, expert_second, pieces):
    if pieces == 1:
        back, sums = expert_piece(
            after_low, upstream_low, dense_gates, expert_first, expert_second
        )
        return (*back, *sums)

    def step(totals, piece):
        back, sums = expert_piece(*piece, expert_first, expert_second)
        return (totals[0] + sums[0], totals[1] + sums[1]), back

    cut = lambda array: array.reshape(pieces, -1, array.shape[1])
    start = (
        jnp.zeros(expert_first.shape, jnp.float32),
        jnp.zeros(expert_second.shape, jnp.float32),
    )
    sums, back = lax.scan(step, start, (cut(after_low), cut(upstream_low), cut(dense_gates)))
    return (*(part.reshape(-1, part.shape[2]) for part in back), *sums)


MESH = pl.DeviceIdType.MESH
GRID = (4, 8)
N_SEM = 47
VMEM_LIMIT = 63 * 2**20


class Place:
    def __init__(self):
        dp, expert = lax.axis_index("dp"), lax.axis_index("expert")
        self.y, self.x = dp // 2, dp % 2
        self.z, self.core = expert // 2, expert % 2
        self.dp = dp
        self.me = dp * GRID[1] + expert
        self.x_peer = (2 * self.y + 1 - self.x, expert)
        self.y_peer = (2 * (1 - self.y) + self.x, expert)
        self.core_peer = (dp, 2 * self.z + 1 - self.core)
        self.middle = (self.z + self.z // 2) % 2
        self.main = 1 + self.z % 2
        self.minor = 3 * (self.z // 2)

    def along_z(self, z):
        return (self.dp, 2 * z + self.core)

    def z_at(self, j):
        near = j + self.middle * (1 - 2 * j) * (1 - j // 2)
        return near + self.z // 2 * (3 - 2 * near)

    def chip(self, q, j):
        return ((self.y + q // 2) % 2 * 2 + (self.x + q % 2) % 2) * 4 + self.z_at(j)

    def if_middle(self, action):
        pl.when(self.middle == 1)(action)


def enter(place):
    barrier = pltpu.get_barrier_semaphore()

    def signal(peer):
        pl.semaphore_signal(barrier, inc=1, device_id=peer, device_id_type=MESH)

    for peer in (place.x_peer, place.y_peer, place.core_peer, place.along_z(place.main)):
        signal(peer)
    place.if_middle(lambda: signal(place.along_z(place.minor)))
    pl.when(place.middle == 0)(lambda: pl.semaphore_wait(barrier, 4))
    place.if_middle(lambda: pl.semaphore_wait(barrier, 5))


def remote(src, dst, send, recv, peer):
    return pltpu.make_async_remote_copy(
        src_ref=src,
        dst_ref=dst,
        send_sem=send,
        recv_sem=recv,
        device_id=peer,
        device_id_type=MESH,
    )


def cut_columns(width):
    tiles = width // 128
    split = tiles // 2
    outer = max(1, tiles * 3 // 10)
    return (outer + tiles % 2) * 128, split * 128, (tiles - outer) * 128


class Gather:
    def __init__(self, place, buf, rows, sems):
        self.place, self.buf, self.rows = place, buf, rows
        self.width = buf.shape[1]
        self.d_end, self.split, self.c_start = cut_columns(self.width)
        self.send, self.recv = sems.at[0], sems.at[1]

    def block(self, q, j, columns=slice(None)):
        start = (2 * self.place.chip(q, j) + self.place.core) * self.rows
        return self.buf.at[pl.ds(pl.multiple_of(start, self.rows), self.rows), columns]

    def copy(self, kind, j, q=0):
        place = self.place
        if kind == "x0":
            ref, number, peer = self.block(0, 0), 15, place.x_peer
        elif kind == "y0":
            ref, number, peer = self.block(0, 0), 19, place.y_peer
        elif kind == "x":
            ref, number, peer = self.block(0, j, slice(0, self.c_start)), 15 + j, place.x_peer
        elif kind == "y":
            ref, number, peer = self.block(0, j, slice(self.d_end, None)), 19 + j, place.y_peer
        elif kind == "a":
            ref, number, peer = self.block(1, j, slice(self.split, None)), 23 + j, place.y_peer
        elif kind == "b":
            ref, number, peer = self.block(2, j, slice(0, self.split)), 27 + j, place.x_peer
        else:
            ref, number, peer = self.block(q, j), 31 + 4 * q + j, place.core_peer
        return remote(ref, ref, self.send.at[number], self.recv.at[number], peer)

    def z_copy(self, part, j, number, z, receiver_j):
        columns = (slice(None), slice(self.c_start, None), slice(0, self.d_end))[part]
        ref = self.block(part, j, columns)
        return remote(
            ref,
            ref,
            self.send.at[5 * part + number],
            self.recv.at[3 * part + receiver_j - 1],
            self.place.along_z(z),
        )

    def z_own(self, part):
        place = self.place
        self.z_copy(part, 0, 0, place.main, 1 + place.middle).start()
        place.if_middle(lambda: self.z_copy(part, 0, 1, place.minor, 1).start())

    def outer_own(self, middle):
        @pl.when(self.place.middle == middle)
        def _():
            self.z_own(1)
            self.z_own(2)

    def z_pass(self, part, j):
        place = self.place
        first = 1 - (j + 2) // 4
        z = place.minor + first * (place.main - place.minor)
        return self.z_copy(part, j, 1 + j, z, j + 2 * first)

    def z_arrive(self, part, j):
        self.z_copy(part, j, 0, self.place.main, j).wait_recv()
        self.place.if_middle(lambda: self.z_pass(part, j).start())

    def begin(self):
        self.z_own(0)
        self.copy("x0", 0).start()
        self.copy("y0", 0).start()
        self.copy("core", 0, 0).start()

    def line(self, j):
        self.z_arrive(0, j)
        self.copy("x", j).start()
        self.copy("y", j).start()
        self.copy("core", j, 0).start()
        if j == 3:
            self.outer_own(1)

    def sides_first(self):
        self.copy("x0", 0).wait_recv()
        self.copy("a", 0).start()
        self.copy("core", 0, 1).start()
        self.copy("y0", 0).wait_recv()
        self.copy("b", 0).start()
        self.copy("core", 0, 2).start()
        self.outer_own(0)

    def sides(self, j):
        self.z_arrive(1, j)
        self.z_arrive(2, j)
        self.copy("x", j).wait_recv()
        self.copy("a", j).start()
        self.copy("core", j, 1).start()
        self.copy("y", j).wait_recv()
        self.copy("b", j).start()
        self.copy("core", j, 2).start()

    def corner(self, j):
        self.copy("a", j).wait_recv()
        self.copy("b", j).wait_recv()
        self.copy("core", j, 3).start()

    def whole(self, q, j):
        self.copy("core", j, q).wait_recv()

    def finish(self):
        place = self.place
        for part in range(3):
            self.z_copy(part, 0, 0, place.main, 1).wait_send()

        def middle():
            for part in range(3):
                self.z_copy(part, 0, 1, place.minor, 1).wait_send()

                def passed(j, carry):
                    self.z_pass(part, j).wait_send()
                    return carry

                lax.fori_loop(1, 4, passed, 0)

        place.if_middle(middle)
        self.copy("x0", 0).wait_send()
        self.copy("y0", 0).wait_send()

        def line(j, carry):
            self.copy("x", j).wait_send()
            self.copy("y", j).wait_send()
            return carry

        lax.fori_loop(1, 4, line, 0)

        def step(j, carry):
            self.copy("a", j).wait_send()
            self.copy("b", j).wait_send()
            for q in range(4):
                self.copy("core", j, q).wait_send()
            return carry

        lax.fori_loop(0, 4, step, 0)


class Reduce:
    def __init__(self, place, own, other, boxes, sems, held=None):
        self.place, self.other = place, other
        self.other_in, self.a_in, self.b_in, self.x_in, self.y_in = boxes[:5]
        self.own = own or (lambda k: self.other_in.at[k])
        self.extra = held or (lambda k: self.other_in.at[k])
        self.z_in = boxes[5:]
        self.rows, self.width = self.other_in.shape[1:]
        self.d_end, self.split, self.c_start = cut_columns(self.width)
        self.send, self.recv = sems.at[0], sems.at[1]

    def copy(self, kind, k):
        place = self.place
        j = k % 4
        if kind == "core":
            src, dst, number, peer = self.other(k), self.other_in.at[k], k, place.core_peer
        elif kind == "a":
            src = self.own(k).at[:, self.split :]
            dst, number, peer = self.a_in.at[j], 16 + j, place.y_peer
        elif kind == "b":
            src = self.own(k).at[:, : self.split]
            dst, number, peer = self.b_in.at[j], 20 + j, place.x_peer
        elif kind == "x0":
            src, dst, number, peer = self.own(k), self.x_in.at[0], 24, place.x_peer
        elif kind == "y0":
            src, dst, number, peer = self.own(k), self.y_in.at[0], 28, place.y_peer
        elif kind == "x":
            src = self.own(k).at[:, : self.c_start]
            dst, number, peer = self.x_in.at[j, :, : self.c_start], 24 + j, place.x_peer
        else:
            src = self.own(k).at[:, self.d_end :]
            dst, number, peer = self.y_in.at[j, :, self.d_end :], 28 + j, place.y_peer
        return remote(src, dst, self.send.at[number], self.recv.at[number], peer)

    def z_columns(self, part):
        return (slice(None), slice(self.c_start, None), slice(0, self.d_end))[part]

    def z_copy(self, part, j):
        place = self.place
        first = 1 - (j + 2) // 4
        box = place.middle * (j // 3) + (1 - place.middle) * (j + 1)
        z = place.main + place.middle * first * (place.minor - place.main)
        return remote(
            self.own(4 * part + j).at[:, self.z_columns(part)],
            self.z_in[part].at[box],
            self.send.at[32 + 5 * part + j],
            self.recv.at[32 + 5 * part + box],
            place.along_z(z),
        )

    def z_wait(self, part, box):
        self.copy_box(part, box).wait_recv()

    def copy_box(self, part, box):
        ref = self.z_in[part].at[box]
        return remote(
            ref,
            ref,
            self.send.at[32 + 5 * part],
            self.recv.at[32 + 5 * part + box],
            self.place.along_z(self.place.main),
        )

    def z_give(self, part, j):
        def middle():
            box = j + (j + 2) // 4
            self.z_wait(part, box)
            self.add(4 * part + j, self.z_columns(part), [lambda at: self.z_in[part][box, at, :]])

        self.place.if_middle(middle)
        self.z_copy(part, j).start()

    def z_last(self, part):
        columns = self.z_columns(part)
        self.z_wait(part, 0)
        self.add(4 * part, columns, [lambda at: self.z_in[part][0, at, :]])

        def middle():
            self.z_wait(part, 2)
            self.add(4 * part, columns, [lambda at: self.z_in[part][2, at, :]])

        self.place.if_middle(middle)

    def add(self, k, columns, terms):
        own = self.own(k)

        def step(number, carry):
            at = pl.ds(pl.multiple_of(number * 16, 16), 16)
            total = own[at, columns].astype(jnp.float32)
            for term in terms:
                total = total + term(at).astype(jnp.float32)
            own[at, columns] = total.astype(own.dtype)
            return carry

        lax.fori_loop(0, self.rows // 16, step, 0)

    def corner(self, j):
        k = 12 + j
        self.copy("core", k).wait_recv()
        self.add(k, slice(None), [lambda at: self.extra(k)[at, :]])
        self.copy("a", k).start()
        self.copy("b", k).start()

    def side_x(self, j):
        k, split = 4 + j, self.split
        self.copy("core", k).wait_recv()
        self.add(k, slice(0, split), [lambda at: self.extra(k)[at, :split]])
        self.copy("a", k).wait_recv()
        self.add(
            k,
            slice(split, None),
            [lambda at: self.extra(k)[at, split:], lambda at: self.a_in[j, at, :]],
        )

    def side_y(self, j):
        k, split = 8 + j, self.split
        self.copy("core", k).wait_recv()
        self.add(k, slice(split, None), [lambda at: self.extra(k)[at, split:]])
        self.copy("b", k).wait_recv()
        self.add(
            k,
            slice(0, split),
            [lambda at: self.extra(k)[at, :split], lambda at: self.b_in[j, at, :]],
        )

    def sides(self, j):
        self.side_x(j)
        self.copy("x", 4 + j).start()
        self.z_give(1, j)
        self.side_y(j)
        self.copy("y", 8 + j).start()
        self.z_give(2, j)

    def sides_last(self):
        self.side_x(0)
        self.side_y(0)
        self.z_last(1)
        self.copy("x0", 4).start()
        self.z_last(2)
        self.copy("y0", 8).start()

    def line(self, j):
        self.copy("core", j).wait_recv()
        self.copy("x", j).wait_recv()
        self.copy("y", j).wait_recv()
        d_end, c_start = self.d_end, self.c_start
        boxes = (self.extra(j), self.x_in.at[j], self.y_in.at[j])
        for columns, used in (
            (slice(0, d_end), boxes[:2]),
            (slice(d_end, c_start), boxes),
            (slice(c_start, None), (boxes[0], boxes[2])),
        ):
            self.add(j, columns, [lambda at, box=box: box[at, columns] for box in used])
        self.z_give(0, j)

    def last(self, put):
        self.copy("core", 0).wait_recv()
        self.copy("x0", 0).wait_recv()
        self.copy("y0", 0).wait_recv()
        self.z_wait(0, 0)
        own = self.own(0)

        def sum_up(middle):
            def step(number, carry):
                at = pl.ds(pl.multiple_of(number * 16, 16), 16)
                total = own[at, :].astype(jnp.float32)
                for box in (self.extra(0), self.x_in.at[0], self.y_in.at[0], self.z_in[0].at[0]):
                    total = total + box[at, :].astype(jnp.float32)
                if middle:
                    total = total + self.z_in[0][2, at, :].astype(jnp.float32)
                put(at, total)
                return carry

            lax.fori_loop(0, own.shape[0] // 16, step, 0)

        @pl.when(self.place.middle == 1)
        def _():
            self.z_wait(0, 2)
            sum_up(True)

        pl.when(self.place.middle == 0)(lambda: sum_up(False))

    def finish(self):
        def step(j, carry):
            self.copy("a", 12 + j).wait_send()
            self.copy("b", 12 + j).wait_send()
            for q in range(4):
                self.copy("core", 4 * q + j).wait_send()
            return carry

        lax.fori_loop(0, 4, step, 0)

        def outer(j, carry):
            self.copy("x", 4 + j).wait_send()
            self.copy("y", 8 + j).wait_send()
            for part in range(3):
                self.z_copy(part, j).wait_send()
            return carry

        lax.fori_loop(1, 4, outer, 0)
        self.copy("x0", 4).wait_send()
        self.copy("y0", 8).wait_send()


def reduce_scratch(rows, width):
    low = jnp.bfloat16
    d_end, split, c_start = cut_columns(width)
    return [
        pltpu.VMEM((16, rows, width), low),
        pltpu.VMEM((4, rows, width - split), low),
        pltpu.VMEM((4, rows, split), low),
        pltpu.VMEM((4, rows, width), low),
        pltpu.VMEM((4, rows, width), low),
        pltpu.VMEM((5, rows, width), low),
        pltpu.VMEM((5, rows, width - c_start), low),
        pltpu.VMEM((5, rows, d_end), low),
    ]


GELU_C = math.sqrt(2.0 / math.pi)
GELU_K = 0.044715


def mm(left, right):
    return jnp.dot(left, right, preferred_element_type=jnp.float32)


def mm_tn(left, right):
    return lax.dot_general(left, right, (((0,), (0,)), ((), ())), preferred_element_type=jnp.float32)


def norm_parts(stream):
    average = jnp.mean(stream, axis=-1, keepdims=True)
    centred = stream - average
    variance = jnp.mean(centred * centred, axis=-1, keepdims=True)
    scale = lax.rsqrt(variance + 1e-05)
    return centred * scale, scale


def norm_pull(normed_grad, unit, scale, gain):
    inner = normed_grad * gain
    mean = jnp.mean(inner, axis=-1, keepdims=True)
    along = jnp.mean(inner * unit, axis=-1, keepdims=True)
    gain_grad = jnp.sum(normed_grad * unit, axis=0, keepdims=True)
    return scale * (inner - mean - unit * along), gain_grad


def mm_nt(left, right):
    return lax.dot_general(left, right, (((1,), (1,)), ((), ())), preferred_element_type=jnp.float32)


OUTPUT_LANE = 32


def join_routers(joined, value_router_ref, output_router_ref):
    count = value_router_ref.shape[0]
    joined[...] = jnp.zeros_like(joined)
    joined[:count, :] = value_router_ref[...]
    joined[OUTPUT_LANE : OUTPUT_LANE + count, :] = output_router_ref[...]


HELD = 6
HELD_ORDER = (15, 14, 13, 7, 11, 12, 6, 10, 5, 9, 3, 4, 8, 2, 1, 0)
GAIN_LANE = 64


def backward_kernel(
    rows_ref,
    tokens_ref,
    cotangent_ref,
    gain_attention_ref,
    gain_feedforward_ref,
    value_router_ref,
    output_router_ref,
    expert_router_ref,
    after_ref,
    normed_ref,
    normed_ffn_ref,
    queries_ref,
    keys_ref,
    projected_ref,
    values_ref,
    probability_ref,
    mixed_ref,
    gated_ref,
    gates_ref,
    slopes_ref,
    expert_slope_ref,
    query_in,
    key_in,
    value_in,
    output_in,
    result_in,
    block_out,
    stream_out,
    low_out,
    output_low_out,
    query_ref,
    key_ref,
    value_ref,
    output_ref,
    routers,
    expert_router,
    after_grad,
    after_low,
    gated_grad,
    projected_grad,
    both_grad,
    held,
    low_part,
    output_part,
    low_own,
    output_own,
    weight_sems,
    held_sems,
    own_sems,
    *refs,
):
    place = Place()
    length, model_width = tokens_ref.shape
    wide = value_ref.shape[1]
    narrow = query_ref.shape[1]
    expert_count = expert_router_ref.shape[0]
    low_rows, output_rows = low_own.shape[0], output_own.shape[0]
    low_type = jnp.bfloat16

    def held_copy(number):
        k = HELD_ORDER[number]
        start = (2 * place.chip(k // 4, k % 4) + place.core) * length
        return pltpu.make_async_copy(
            result_in.at[pl.ds(pl.multiple_of(start, length), length)],
            held.at[number % HELD],
            held_sems.at[number % HELD],
        )

    def other_rows(ref, rows):
        def get(k):
            start = (2 * place.chip(k // 4, k % 4) + 1 - place.core) * rows
            return ref.at[pl.ds(pl.multiple_of(start, rows), rows)]

        return get

    def own_rows(ref, rows):
        def get(k):
            start = (2 * place.chip(k // 4, k % 4) + place.core) * rows
            return ref.at[pl.ds(pl.multiple_of(start, rows), rows)]

        return get

    slots = {k: number % HELD for number, k in enumerate(HELD_ORDER)}
    results = Reduce(
        place,
        None,
        other_rows(result_in, length),
        refs[0:8],
        refs[8],
        lambda k: held.at[slots[k]],
    )
    outputs = Reduce(
        place,
        own_rows(output_part, output_rows),
        other_rows(output_part, output_rows),
        refs[9:17],
        refs[17],
    )
    lows = Reduce(
        place,
        own_rows(low_part, low_rows),
        other_rows(low_part, low_rows),
        refs[18:26],
        refs[26],
    )
    spread_outputs = Gather(place, output_low_out, output_rows, refs[27])
    spread_lows = Gather(place, low_out, low_rows, refs[28])
    weights = ((output_in, output_ref), (query_in, query_ref), (key_in, key_ref), (value_in, value_ref))
    loads = [
        pltpu.make_async_copy(src, dst, weight_sems.at[number])
        for number, (src, dst) in enumerate(weights)
    ]

    def hand_over(reduce):
        def step(number, carry):
            reduce.copy("core", 15 - number).start()
            return carry

        lax.fori_loop(0, 16, step, 0)

    fetched = [0]

    def result_event(kind, *j):
        used = {"corner": 1, "sides": 2, "line": 1, "sides_last": 2, "last": 1}[kind]
        start = fetched[0]
        for number in range(start, start + used):
            held_copy(number).wait()
        if kind == "last":

            def put(at, total):
                block_out[at, :] = (after_ref[at, :] + total).astype(low_type)

            results.last(put)
        else:
            getattr(results, kind)(*j)
        for number in range(start + HELD, start + HELD + used):
            if number < len(HELD_ORDER):
                held_copy(number).start()
        fetched[0] = start + used

    def send_around(reduce, gather, own, own_sem):
        def put(at, total):
            own[at, :] = total.astype(low_type)

        reduce.last(put)
        copy = pltpu.make_async_copy(own, gather.block(0, 0), own_sem)
        copy.start()
        copy.wait()
        gather.begin()

    for number in range(HELD):
        held_copy(number).start()
    for load in loads:
        load.start()
    enter(place)
    hand_over(results)
    result_event("corner", 3)
    result_event("corner", 2)
    result_event("corner", 1)

    join_routers(routers, value_router_ref, output_router_ref)
    expert_router[...] = jnp.zeros_like(expert_router)
    expert_router[:expert_count, :] = expert_router_ref[...]
    logit_grad = (rows_ref[:, model_width:] * expert_slope_ref[...]).astype(low_type)
    unit, scale = norm_parts(after_ref[...])
    through, gain_feedforward_grad = norm_pull(
        mm(logit_grad, expert_router[...]), unit, scale, gain_feedforward_ref[...]
    )
    after_grad[...] = cotangent_ref[...].astype(jnp.float32) + rows_ref[:, :model_width] + through
    after_low[...] = after_grad[...].astype(low_type)
    expert_column = wide + 2 * narrow + 128
    low_part[:, expert_column:] = mm_tn(normed_ffn_ref[...], logit_grad).astype(low_type)
    tile = 256

    def output_tile(number, carry):
        at = pl.ds(pl.multiple_of(number * tile, tile), tile)
        output_part[at, :] = mm_tn(gated_ref[:, at], after_low[...]).astype(low_type)
        return carry

    lax.fori_loop(0, wide // tile, output_tile, 0)
    hand_over(outputs)
    result_event("sides", 3)
    result_event("corner", 0)
    loads[0].wait()

    def gated_tile(number, carry):
        at = pl.ds(pl.multiple_of(number * tile, tile), tile)
        gated_grad[:, at] = mm_nt(after_low[...], output_ref[at, :]).astype(low_type)
        return carry

    lax.fori_loop(0, wide // tile, gated_tile, 0)
    outputs.corner(3)
    result_event("sides", 2)
    outputs.corner(2)
    outputs.corner(1)

    lane = lax.broadcasted_iota(jnp.int32, (length, 128), 1)
    gate_grads = jnp.zeros((length, 128), jnp.float32)
    inverse = 1.0 / math.sqrt(HEAD)
    for head in range(HEADS):
        columns = slice(head * HEAD, (head + 1) * HEAD)
        mixed = mixed_ref[:, columns]
        mixed_grad = jnp.zeros((length, HEAD), jnp.float32)
        for e in range(ATT_EXP):
            at = head * ATT_EXP + e
            part = gated_grad[:, at * HEAD : (at + 1) * HEAD].astype(jnp.float32)
            lane_at = OUTPUT_LANE + at
            mixed_grad = mixed_grad + gates_ref[:, lane_at : lane_at + 1] * part
            gate_grads = jnp.where(
                lane == lane_at, jnp.sum(part * mixed, axis=1, keepdims=True), gate_grads
            )
        mixed_grad = mixed_grad.astype(low_type)
        probability = probability_ref[head]
        prob_grad = mm_nt(mixed_grad, values_ref[:, columns])
        inner = jnp.sum(probability * prob_grad, axis=-1, keepdims=True)
        score_grad = (probability * (prob_grad - inner)).astype(low_type)
        both_grad[:, columns] = (mm(score_grad, keys_ref[:, columns]) * inverse).astype(low_type)
        both_grad[:, narrow + head * HEAD : narrow + (head + 1) * HEAD] = (
            mm_tn(score_grad, queries_ref[:, columns]) * inverse
        ).astype(low_type)
        values_grad = mm_tn(probability.astype(low_type), mixed_grad)
        values_grad = values_grad.astype(low_type).astype(jnp.float32)
        for e in range(ATT_EXP):
            at = head * ATT_EXP + e
            wide_at = slice(at * HEAD, (at + 1) * HEAD)
            projected_grad[:, wide_at] = (gates_ref[:, at : at + 1] * values_grad).astype(low_type)
            gate_grad = jnp.sum(values_grad * projected_ref[:, wide_at], axis=1, keepdims=True)
            gate_grads = jnp.where(lane == at, gate_grad, gate_grads)
    router_grad = (gate_grads * slopes_ref[...]).astype(low_type)
    result_event("sides", 1)
    outputs.sides(3)
    result_event("line", 3)
    outputs.corner(0)

    def value_tile(number, carry):
        at = pl.ds(pl.multiple_of(number * tile, tile), tile)
        to = pl.ds(pl.multiple_of(2 * narrow + number * tile, tile), tile)
        low_part[:, to] = mm_tn(tokens_ref[...], projected_grad[:, at]).astype(low_type)
        return carry

    def both_tile(number, carry):
        at = pl.ds(pl.multiple_of(number * tile, tile), tile)
        low_part[:, at] = mm_tn(normed_ref[...], both_grad[:, at]).astype(low_type)
        return carry

    lax.fori_loop(0, wide // tile, value_tile, 0)
    lax.fori_loop(0, 2 * narrow // tile, both_tile, 0)
    loads[1].wait()
    loads[2].wait()
    normed_grad = mm_nt(both_grad[:, :narrow], query_ref[...])
    normed_grad = normed_grad + mm_nt(both_grad[:, narrow:], key_ref[...])
    normed_grad = normed_grad + mm(router_grad, routers[...])
    unit, scale = norm_parts(tokens_ref[...].astype(jnp.float32))
    through, gain_attention_grad = norm_pull(normed_grad, unit, scale, gain_attention_ref[...])
    stream_out[...] = after_grad[...] + through
    gain_columns = [
        jnp.broadcast_to(grad, (128, model_width)).T
        for grad in (gain_attention_grad, gain_feedforward_grad)
    ]
    small = mm_tn(normed_ref[...], router_grad)
    small_lane = lax.broadcasted_iota(jnp.int32, (model_width, 128), 1)
    small = jnp.where(small_lane == GAIN_LANE, gain_columns[0], small)
    small = jnp.where(small_lane == GAIN_LANE + 1, gain_columns[1], small)
    small_column = wide + 2 * narrow
    low_part[:, small_column:expert_column] = small.astype(low_type)
    hand_over(lows)
    result_event("sides_last")
    outputs.sides(2)
    result_event("line", 2)
    outputs.sides(1)
    result_event("line", 1)
    lows.corner(3)
    outputs.line(3)
    lows.corner(2)
    result_event("last")
    lows.corner(1)
    outputs.sides_last()
    lows.sides(3)
    outputs.line(2)
    lows.corner(0)
    outputs.line(1)
    lows.sides(2)
    send_around(outputs, spread_outputs, output_own, own_sems.at[0])
    loads[3].wait()
    stream_out[...] += mm_nt(projected_grad[...], value_ref[...])
    lows.sides(1)
    spread_outputs.line(1)
    lows.line(3)
    spread_outputs.sides_first()
    lows.sides_last()
    spread_outputs.line(2)
    lows.line(2)
    spread_outputs.line(3)
    lows.line(1)
    spread_outputs.corner(0)
    send_around(lows, spread_lows, low_own, own_sems.at[1])
    for j in (1, 2, 3):
        spread_outputs.sides(j)
    spread_lows.line(1)
    spread_lows.sides_first()
    spread_lows.line(2)
    for j in (1, 2, 3):
        spread_outputs.corner(j)
    spread_lows.line(3)
    spread_lows.corner(0)
    for j in (1, 2, 3):
        spread_lows.sides(j)
    for j in (1, 2, 3):
        spread_lows.corner(j)

    def arrived(k, carry):
        spread_outputs.whole(k // 4, k % 4)
        spread_lows.whole(k // 4, k % 4)
        return carry

    lax.fori_loop(0, 16, arrived, 0)
    for reduce in (results, outputs, lows):
        reduce.finish()
    spread_outputs.finish()
    spread_lows.finish()


def call_backward(rows, tokens, cotangent, gains, routers, saved, weights, result):
    length, model_width = tokens.shape
    total = GRID[0] * GRID[1]
    wide, narrow = weights[2].shape[1], weights[0].shape[1]
    low_width = wide + 2 * narrow + 256
    low_rows, output_rows = model_width // total, wide // total
    low, full = jnp.bfloat16, jnp.float32
    vmem = pl.BlockSpec(memory_space=pltpu.VMEM)
    hbm = pl.BlockSpec(memory_space=pl.ANY)
    sems = pltpu.SemaphoreType.DMA((2, N_SEM))
    return pl.pallas_call(
        backward_kernel,
        out_shape=(
            jax.ShapeDtypeStruct((length, model_width), low),
            jax.ShapeDtypeStruct((length, model_width), full),
            jax.ShapeDtypeStruct((model_width, low_width), low),
            jax.ShapeDtypeStruct((wide, model_width), low),
        ),
        in_specs=[vmem] * 21 + [hbm] * 5,
        out_specs=(vmem, vmem, hbm, hbm),
        scratch_shapes=[
            *(pltpu.VMEM(weight.shape, low) for weight in weights),
            pltpu.VMEM((128, model_width), low),
            pltpu.VMEM((128, model_width), low),
            pltpu.VMEM((length, model_width), full),
            pltpu.VMEM((length, model_width), low),
            pltpu.VMEM((length, wide), low),
            pltpu.VMEM((length, wide), low),
            pltpu.VMEM((length, 2 * narrow), low),
            pltpu.VMEM((HELD, length, model_width), low),
            pltpu.VMEM((model_width, low_width), low),
            pltpu.VMEM((wide, model_width), low),
            pltpu.VMEM((low_rows, low_width), low),
            pltpu.VMEM((output_rows, model_width), low),
            pltpu.SemaphoreType.DMA((4,)),
            pltpu.SemaphoreType.DMA((HELD,)),
            pltpu.SemaphoreType.DMA((2,)),
            *reduce_scratch(length, model_width),
            sems,
            *reduce_scratch(output_rows, model_width),
            sems,
            *reduce_scratch(low_rows, low_width),
            sems,
            sems,
            sems,
        ],
        compiler_params=pltpu.CompilerParams(
            collective_id=1, has_side_effects=True, vmem_limit_bytes=VMEM_LIMIT
        ),
        name="backward",
    )(rows, tokens, cotangent, *gains, *routers, *saved, *weights, result)


def widen_kernel(
    low_ref,
    output_low_ref,
    first_ref,
    second_ref,
    block_ref,
    stream_ref,
    query,
    key,
    value,
    output,
    value_router,
    output_router,
    expert_router,
    gain_attention,
    gain_feedforward,
    first,
    second,
    block,
    stream,
):
    full = jnp.float32
    narrow, wide = query.shape[1], value.shape[1]
    query[...] = low_ref[:, :narrow].astype(full)
    key[...] = low_ref[:, narrow : 2 * narrow].astype(full)
    value[...] = low_ref[:, 2 * narrow : 2 * narrow + wide].astype(full)
    output[...] = output_low_ref[...].astype(full)
    start = 2 * narrow + wide
    small = low_ref[:, start : start + 128].astype(full).T
    count = value_router.shape[0]
    value_router[...] = small[:count]
    output_router[...] = small[OUTPUT_LANE : OUTPUT_LANE + count]
    gain_attention[...] = small[GAIN_LANE : GAIN_LANE + 1]
    gain_feedforward[...] = small[GAIN_LANE + 1 : GAIN_LANE + 2]
    expert_router[...] = low_ref[:, start + 128 :].astype(full).T[: expert_router.shape[0]]
    hidden_width = second.shape[1]
    for e in range(first.shape[0]):
        rows = slice(e * hidden_width, (e + 1) * hidden_width)
        first[e] = first_ref[rows, :].T
        second[e] = second_ref[rows, :]
    block[...] = block_ref[...]
    stream[...] = stream_ref[...]


def call_widen(low, output_low, first_sum, second_sum, block_output, stream_grad, narrow, expert_count, local_count):
    model_width, low_width = low.shape
    wide = output_low.shape[0]
    hidden = first_sum.shape[0]
    hidden_width = hidden // local_count
    length = block_output.shape[0]
    steps = model_width // 128
    full = jnp.float32
    router_width = HEADS * ATT_EXP
    rows = lambda height, width: pl.BlockSpec((height, width), lambda i: (i, 0))
    columns = lambda height: pl.BlockSpec((height, 128), lambda i: (0, i))
    first_spec = pl.BlockSpec((local_count, 128, hidden_width), lambda i: (0, i, 0))
    second_spec = pl.BlockSpec((local_count, hidden_width, 128), lambda i: (0, 0, i))
    shape = lambda *dims, kind=full: jax.ShapeDtypeStruct(dims, kind)
    return pl.pallas_call(
        widen_kernel,
        grid=(steps,),
        out_shape=(
            shape(model_width, narrow),
            shape(model_width, narrow),
            shape(model_width, wide),
            shape(wide, model_width),
            shape(router_width, model_width),
            shape(router_width, model_width),
            shape(expert_count, model_width),
            shape(1, model_width),
            shape(1, model_width),
            shape(local_count, model_width, hidden_width),
            shape(local_count, hidden_width, model_width),
            shape(length, model_width, kind=block_output.dtype),
            shape(length, model_width),
        ),
        in_specs=[
            rows(128, low_width),
            rows(wide // steps, model_width),
            columns(hidden),
            columns(hidden),
            rows(length // steps, model_width),
            rows(length // steps, model_width),
        ],
        out_specs=(
            rows(128, narrow),
            rows(128, narrow),
            rows(128, wide),
            rows(wide // steps, model_width),
            columns(router_width),
            columns(router_width),
            columns(expert_count),
            columns(1),
            columns(1),
            first_spec,
            second_spec,
            rows(length // steps, model_width),
            rows(length // steps, model_width),
        ),
        compiler_params=pltpu.CompilerParams(vmem_limit_bytes=VMEM_LIMIT),
        name="widen",
    )(low, output_low, first_sum, second_sum, block_output, stream_grad)


def run_events(events, sources):
    for name, method, arguments, where in events:
        action = functools.partial(getattr(sources[name], method), *arguments)
        if where == "all":
            action()
        else:
            pl.when(sources["place"].middle == (1 if where == "middle" else 0))(action)


def ev(name, method, *arguments, where="all"):
    return (name, method, arguments, where)


AFTER_ATTENTION = (
    ev("u", "line", 2, where="end"),
    ev("u", "line", 3, where="middle"),
    ev("u", "corner", 0),
    ev("u", "sides", 1),
)
WALK = (
    (0, 0, ()),
    (
        0,
        1,
        (
            ev("u", "line", 3, where="end"),
            ev("u", "sides", 2),
            ev("u", "corner", 1),
            ev("x", "line", 1),
            ev("x", "sides_first"),
            ev("x", "line", 2, where="middle"),
        ),
    ),
    (1, 0, ()),
    (2, 0, ()),
    (
        3,
        0,
        (
            ev("x", "corner", 0),
            ev("x", "line", 2, where="end"),
            ev("x", "line", 3, where="middle"),
            ev("u", "sides", 3),
            ev("u", "corner", 2),
        ),
    ),
    (0, 2, (ev("u", "corner", 3),)),
    (0, 3, (ev("x", "line", 3, where="end"), ev("x", "sides", 1))),
    (1, 1, ()),
    (2, 1, (ev("r", "corner", 0),)),
    (3, 1, (ev("x", "corner", 1), ev("x", "sides", 2))),
    (1, 2, ()),
    (2, 2, (ev("r", "corner", 1),)),
    (3, 2, (ev("x", "corner", 2), ev("x", "sides", 3))),
    (1, 3, ()),
    (2, 3, (ev("r", "corner", 2),)),
    (3, 3, (ev("x", "corner", 3),)),
)
GIVE_BACK = (
    (ev("r", "corner", 3),),
    (ev("r", "sides", 3),),
    (ev("r", "sides", 2),),
    (ev("r", "sides", 1),),
    (ev("r", "line", 3),),
    (ev("r", "sides_last"),),
    (ev("r", "line", 2),),
    (ev("r", "line", 1),),
)


def layer_kernel(
    local_count,
    tokens_ref,
    cotangent_ref,
    gain_attention_ref,
    gain_feedforward_ref,
    value_router_ref,
    output_router_ref,
    expert_router_ref,
    segments_ref,
    value_ids_ref,
    output_ids_ref,
    ffn_ids_ref,
    first_in,
    second_ref,
    query_in,
    key_in,
    value_in,
    output_in,
    rows_out,
    first_out,
    second_out,
    after_out,
    normed_out,
    normed_ffn_out,
    queries_out,
    keys_out,
    projected_out,
    values_out,
    probability_out,
    mixed_out,
    gated_out,
    gates_out,
    slopes_out,
    expert_slope_out,
    result_out,
    routers,
    all_ids,
    gathered,
    upstream,
    first_ref,
    first_t_ref,
    second_t_ref,
    hidden_parts,
    partial,
    result_stage,
    weight_sems,
    upstream_sems,
    gather_sems,
    reduce_sems,
    result_sems,
    *boxes,
):
    place = Place()
    length, model_width = tokens_ref.shape
    pair = 2 * length
    expert_count = expert_router_ref.shape[0]
    width = gathered.shape[1]
    gate_width = width - model_width
    hidden_width = first_ref.shape[1] // local_count
    narrow, wide = query_in.shape[1], value_in.shape[1]
    mine = pl.ds(pl.multiple_of(place.me * length, length), length)

    pieces = [
        (start, min(wide, start + width), number)
        for number, start in enumerate(range(0, wide, width), 1)
    ]
    value_refs = [
        partial.at[number * model_width : (number + 1) * model_width, : end - start]
        for start, end, number in pieces
    ]
    query_ref = partial.at[:model_width, :narrow]
    key_ref = partial.at[:model_width, narrow : 2 * narrow]
    hidden = first_ref.shape[1]
    gated_hidden = hidden_parts.at[:, :hidden]
    pre_grads = hidden_parts.at[:, hidden:]
    main_columns, side_columns = 2 * hidden, model_width - 2 * hidden
    last_rows = len(pieces) * model_width
    output_parts = [
        (0, wide, slice(0, main_columns), hidden_parts.at[:wide, :])
    ]
    for number, start in enumerate(range(0, wide, model_width), 1):
        end = min(wide, start + model_width)
        place_at = slice(number * side_columns, (number + 1) * side_columns)
        ref = partial.at[last_rows : last_rows + end - start, place_at]
        output_parts.append((start, end, slice(main_columns, None), ref))
    loads = [
        pltpu.make_async_copy(src, dst, weight_sems.at[number])
        for number, (src, dst) in enumerate(
            [
                (query_in, query_ref),
                (key_in, key_ref),
                *(
                    (value_in.at[:, start:end], ref)
                    for (start, end, _), ref in zip(pieces, value_refs)
                ),
                *(
                    (output_in.at[start:end, columns], ref)
                    for start, end, columns, ref in output_parts
                ),
            ]
        )
    ]
    for load in loads:
        load.start()
    upstream[mine, :] = cotangent_ref[...]
    enter(place)
    gather_upstream = Gather(place, upstream, length, upstream_sems)
    gather_upstream.begin()

    join_routers(routers, value_router_ref, output_router_ref)
    top = value_ids_ref.shape[1]
    all_ids[...] = jnp.zeros_like(all_ids)
    for head in range(HEADS):
        at = head * top
        all_ids[at : at + top, :] = value_ids_ref[head].astype(jnp.float32) + float(head * ATT_EXP)
        all_ids[16 + at : 16 + at + top, :] = output_ids_ref[head].astype(jnp.float32) + float(
            OUTPUT_LANE + head * ATT_EXP
        )
    ffn_top = ffn_ids_ref.shape[0]
    all_ids[32 : 32 + ffn_top, :] = ffn_ids_ref[...].astype(jnp.float32)
    ids = all_ids[...].T
    lane = lax.broadcasted_iota(jnp.int32, (length, gates_out.shape[1]), 1).astype(jnp.float32)

    def named(columns):
        mask = jnp.zeros(lane.shape, jnp.float32)
        for at in columns:
            mask = jnp.where(lane == ids[:, at : at + 1], 1.0, mask)
        return mask

    stream_low = tokens_ref[...]
    stream = stream_low.astype(jnp.float32)
    unit, _ = norm_parts(stream)
    normed = (unit * gain_attention_ref[...]).astype(jnp.bfloat16)
    normed_out[...] = normed
    sig = jax.nn.sigmoid(mm_nt(normed, routers[...]))
    gates = named([*range(HEADS * top), *range(16, 16 + HEADS * top)]) * sig
    gates_out[...] = gates
    slopes_out[...] = gates * (1.0 - sig)
    loads[0].wait()
    queries_out[...] = mm(normed, query_ref[...]).astype(jnp.bfloat16)
    loads[1].wait()
    keys_out[...] = mm(normed, key_ref[...]).astype(jnp.bfloat16)
    for (start, end, _), ref, load in zip(pieces, value_refs, loads[2:]):
        load.wait()
        projected_out[:, start:end] = mm(stream_low, ref[...])
    for head in range(HEADS):
        total = jnp.zeros((length, HEAD), jnp.float32)
        for e in range(ATT_EXP):
            at = head * ATT_EXP + e
            total = total + gates[:, at : at + 1] * projected_out[:, at * HEAD : (at + 1) * HEAD]
        values_out[:, head * HEAD : (head + 1) * HEAD] = total.astype(jnp.bfloat16)
    documents = jnp.broadcast_to(segments_ref[...].astype(jnp.float32), (length, length))
    row = lax.broadcasted_iota(jnp.int32, (length, length), 0)
    column = lax.broadcasted_iota(jnp.int32, (length, length), 1)
    allowed = (documents == documents.T) & (row >= column)
    for head in range(HEADS):
        columns = slice(head * HEAD, (head + 1) * HEAD)
        scores = mm_nt(queries_out[:, columns], keys_out[:, columns]) * (1.0 / math.sqrt(HEAD))
        scores = jnp.where(allowed, scores, NEG_FILL)
        exponent = jnp.exp(scores - jnp.max(scores, axis=-1, keepdims=True))
        probability = exponent / jnp.sum(exponent, axis=-1, keepdims=True)
        probability_out[head] = probability
        mixed = mm(probability.astype(jnp.bfloat16), values_out[:, columns])
        mixed_out[:, columns] = mixed
        for e in range(ATT_EXP):
            at = head * ATT_EXP + e
            gate = gates[:, OUTPUT_LANE + at : OUTPUT_LANE + at + 1]
            gated_out[:, at * HEAD : (at + 1) * HEAD] = (gate * mixed).astype(jnp.bfloat16)
    gather_upstream.line(1)
    gather_upstream.sides_first()
    place.if_middle(lambda: gather_upstream.line(2))
    side = stream[:, main_columns:]
    for (start, end, columns, ref), load in zip(output_parts, loads[2 + len(pieces) :]):
        load.wait()
        if start == 0 and end == wide:
            after_out[:, columns] = stream[:, columns] + mm(gated_out[...], ref[...])
        else:
            side = side + mm(gated_out[:, start:end], ref[...])
    after_out[:, main_columns:] = side
    after = after_out[...]
    gathered[mine, :model_width] = after.astype(jnp.bfloat16)
    unit, _ = norm_parts(after)
    normed_ffn = (unit * gain_feedforward_ref[...]).astype(jnp.bfloat16)
    normed_ffn_out[...] = normed_ffn
    expert_sig = jax.nn.sigmoid(mm_nt(normed_ffn, expert_router_ref[...]))
    expert_gates = named(range(32, 32 + ffn_top))[:, :expert_count] * expert_sig
    gathered[mine, model_width:] = jnp.zeros((length, gate_width), jnp.bfloat16)
    gathered[mine, model_width : model_width + expert_count] = expert_gates.astype(jnp.bfloat16)
    expert_slope_out[...] = jnp.zeros((length, gate_width), jnp.float32)
    expert_slope_out[:, :expert_count] = expert_gates * (1.0 - expert_sig)
    gather = Gather(place, gathered, length, gather_sems)
    gather.begin()

    for e in range(local_count):
        columns = slice(e * hidden_width, (e + 1) * hidden_width)
        first_ref[:, columns] = first_in[e]
        first_t_ref[columns, :] = first_in[e].astype(jnp.float32).T.astype(jnp.bfloat16)
        second_t_ref[:, columns] = second_ref[columns, :].astype(jnp.float32).T.astype(jnp.bfloat16)
    pick_row = lax.broadcasted_iota(jnp.int32, (gate_width, first_ref.shape[1]), 0)
    pick_column = lax.broadcasted_iota(jnp.int32, (gate_width, first_ref.shape[1]), 1)
    pick_gates = jnp.where(
        pick_row == place.me * local_count + pick_column // hidden_width, 1.0, 0.0
    ).astype(jnp.bfloat16)

    def share(k, core):
        return partial.at[pl.ds(pl.multiple_of(k * pair + core * length, length), length)]

    reduce = Reduce(
        place,
        lambda k: share(k, place.core),
        lambda k: share(k, 1 - place.core),
        boxes,
        reduce_sems,
    )
    sources = {"place": place, "u": gather_upstream, "x": gather, "r": reduce}

    def result_copy(slot, chip):
        return pltpu.make_async_copy(
            result_stage.at[slot],
            result_out.at[pl.ds(pl.multiple_of(chip * pair, pair), pair)],
            result_sems.at[slot],
        )

    def compute(step, q, j):
        chip = place.chip(q, j)
        rows = pl.ds(pl.multiple_of(chip * pair, pair), pair)
        hidden_pre = mm(gathered[rows, :model_width], first_ref[...])
        back = mm(upstream[rows, :], second_t_ref[...])
        gates = mm(gathered[rows, model_width:], pick_gates)
        square = hidden_pre * hidden_pre
        bent = jnp.tanh(GELU_C * hidden_pre * (1.0 + GELU_K * square))
        grow = 0.5 * (1.0 + bent)
        slope = grow + 0.5 * hidden_pre * (1.0 - bent * bent) * (
            GELU_C * (1.0 + 3.0 * GELU_K * square)
        )
        hidden = (hidden_pre * grow).astype(jnp.bfloat16).astype(jnp.float32)
        gated = (gates * hidden).astype(jnp.bfloat16)
        pre_grad = (gates * back * slope).astype(jnp.bfloat16)
        gated_hidden[rows, :] = gated
        pre_grads[rows, :] = pre_grad
        k = 4 * q + j
        to = pl.ds(pl.multiple_of(k * pair, pair), pair)
        partial[to, :model_width] = mm(pre_grad, first_t_ref[...]).astype(jnp.bfloat16)
        product = hidden * back
        column = lax.broadcasted_iota(jnp.int32, (pair, gate_width), 1) - place.me * local_count
        gate_grad = jnp.zeros((pair, gate_width), jnp.float32)
        for e in range(local_count):
            own_sum = jnp.sum(
                product[:, e * hidden_width : (e + 1) * hidden_width], axis=1, keepdims=True
            )
            gate_grad = jnp.where(column == e, own_sum, gate_grad)
        partial[to, model_width:] = gate_grad.astype(jnp.bfloat16)
        reduce.copy("core", k).start()
        slot = step % 2

        @pl.when(step >= 2)
        def _():
            result_copy(slot, chip).wait()

        result_stage[slot] = mm(gated, second_ref[...]).astype(jnp.bfloat16)
        result_copy(slot, chip).start()

    run_events(AFTER_ATTENTION, sources)

    def pick(step, values):
        total = 0
        for number, value in enumerate(values):
            total = total + value * jnp.where(step == number, 1, 0)
        return total

    def walk(step, carry):
        for number, (_, _, events) in enumerate(WALK):
            if events:
                pl.when(step == number)(functools.partial(run_events, events, sources))
        q = pick(step, [stop[0] for stop in WALK])
        j = pick(step, [stop[1] for stop in WALK])
        gather.whole(q, j)
        gather_upstream.whole(q, j)
        compute(step, q, j)
        return carry

    lax.fori_loop(0, 16, walk, 0)
    piece = gathered.shape[0] // len(GIVE_BACK)

    def weight_piece(number):
        rows = pl.ds(pl.multiple_of(number * piece, piece), piece)
        second = mm_tn(gated_hidden[rows, :], upstream[rows, :])
        first = mm_tn(pre_grads[rows, :], gathered[rows, :model_width])

        @pl.when(number == 0)
        def _():
            second_out[...] = second
            first_out[...] = first

        @pl.when(number > 0)
        def _():
            second_out[...] += second
            first_out[...] += first

    def give(step, carry):
        for number, events in enumerate(GIVE_BACK):
            pl.when(step == number)(functools.partial(run_events, events, sources))
        weight_piece(step)
        return carry

    lax.fori_loop(0, len(GIVE_BACK), give, 0)

    def put(at, total):
        rows_out[at, :] = total

    reduce.last(put)
    for slot in range(2):
        result_copy(slot, 0).wait()
    gather_upstream.finish()
    gather.finish()
    reduce.finish()


def call_layer(
    tokens,
    cotangent,
    gains,
    weights,
    routers,
    segments,
    value_ids,
    output_ids,
    ffn_ids,
    expert_first,
    expert_second,
):
    length, model_width = tokens.shape
    local_count, _, hidden_width = expert_first.shape
    hidden = local_count * hidden_width
    expert_count = routers[2].shape[0]
    gate_width = -(-expert_count // 128) * 128
    width = model_width + gate_width
    total = GRID[0] * GRID[1] * length
    wide = weights[3].shape[0]
    narrow = HEADS * HEAD
    low, full = jnp.bfloat16, jnp.float32
    shapes = (
        ((length, width), full),
        ((hidden, model_width), full),
        ((hidden, model_width), full),
        ((length, model_width), full),
        ((length, model_width), low),
        ((length, model_width), low),
        ((length, narrow), low),
        ((length, narrow), low),
        ((length, wide), full),
        ((length, narrow), low),
        ((HEADS, length, length), full),
        ((length, narrow), full),
        ((length, wide), low),
        ((length, 128), full),
        ((length, 128), full),
        ((length, gate_width), full),
        ((total, model_width), low),
    )
    vmem = pl.BlockSpec(memory_space=pltpu.VMEM)
    hbm = pl.BlockSpec(memory_space=pl.ANY)
    sems = pltpu.SemaphoreType.DMA((2, N_SEM))
    return pl.pallas_call(
        functools.partial(layer_kernel, local_count),
        out_shape=tuple(jax.ShapeDtypeStruct(*shape) for shape in shapes),
        in_specs=[vmem] * 13 + [hbm] * 4,
        out_specs=(*([vmem] * (len(shapes) - 1)), hbm),
        scratch_shapes=[
            pltpu.VMEM((128, model_width), low),
            pltpu.VMEM((128, length), full),
            pltpu.VMEM((total, width), low),
            pltpu.VMEM((total, model_width), low),
            pltpu.VMEM((model_width, hidden), low),
            pltpu.VMEM((hidden, model_width), low),
            pltpu.VMEM((model_width, hidden), low),
            pltpu.VMEM((total, 2 * hidden), low),
            pltpu.VMEM((total, width), low),
            pltpu.VMEM((2, 2 * length, model_width), low),
            pltpu.SemaphoreType.DMA((3 + -(-wide // width) + -(-wide // model_width),)),
            sems,
            sems,
            sems,
            pltpu.SemaphoreType.DMA((2,)),
            *reduce_scratch(length, width),
        ],
        compiler_params=pltpu.CompilerParams(
            collective_id=0, has_side_effects=True, vmem_limit_bytes=VMEM_LIMIT
        ),
        name="layer",
    )(
        tokens,
        cotangent,
        *gains,
        *routers,
        segments,
        value_ids.transpose(1, 2, 0),
        output_ids.transpose(1, 2, 0),
        ffn_ids.T,
        expert_first,
        expert_second.reshape(hidden, model_width),
        *weights,
    )


def general_body(
    tokens,
    cotangent,
    gain_attention,
    gain_feedforward,
    query_weight,
    key_weight,
    value_weight,
    output_weight,
    value_router,
    output_router,
    expert_router,
    expert_first,
    expert_second,
    segments,
    value_ids,
    output_ids,
    ffn_ids,
):
    owner_total = lax.axis_size("dp") * lax.axis_size("expert")
    local_count = expert_first.shape[0]
    expert_count = local_count * owner_total
    shared = (
        gain_attention,
        query_weight,
        key_weight,
        value_weight,
        output_weight,
        value_router,
        output_router,
    )
    stream = tokens.astype(jnp.float32)
    upstream = cotangent.astype(jnp.float32)
    after_attention, saved_parts = attention_forward(
        stream, segments[0], value_ids[0], output_ids[0], shared
    )
    normed_low = layer_norm(after_attention, gain_feedforward).astype(jnp.bfloat16)
    logits = jnp.dot(normed_low, expert_router, preferred_element_type=jnp.float32)
    sigmoid_out = jax.nn.sigmoid(logits)
    dense_gates = sigmoid_out * expert_mask(ffn_ids[0], expert_count)
    expert_slope = dense_gates * (1.0 - sigmoid_out)
    result, token_grad, gate_back, first_sum, second_sum = expert_exchange(
        after_attention.astype(jnp.bfloat16),
        cotangent,
        dense_gates.astype(jnp.bfloat16),
        expert_first,
        expert_second,
        max(1, owner_total // 32),
    )
    logit_grad = (gate_back.astype(jnp.float32) * expert_slope).astype(jnp.bfloat16)
    router_sum = jnp.einsum("sa,sb->ab", normed_low, logit_grad, preferred_element_type=jnp.float32)
    normed_grad = jnp.einsum(
        "sb,ab->sa", logit_grad, expert_router, preferred_element_type=jnp.float32
    )
    norm_value, norm_pull = jax.vjp(layer_norm, after_attention, gain_feedforward)
    after_extra, feed_gain_part = norm_pull(normed_grad)
    after_grad = upstream + token_grad.astype(jnp.float32) + after_extra
    stream_grad, attention_parts = attention_backward(after_grad, saved_parts, stream, shared)
    gain_part, query_part, key_part, value_part, output_part, value_router_part, output_router_part = attention_parts
    parts = (
        query_part,
        key_part,
        value_part,
        value_router_part,
        output_router_part,
        router_sum,
        gain_part[:, None],
        feed_gain_part[:, None],
    )
    low = jnp.concatenate([part.astype(jnp.bfloat16) for part in parts], axis=1)
    low = jnp.pad(low, ((0, 0), (0, -low.shape[1] % 256)))
    output_low = output_part.astype(jnp.bfloat16)
    low, output_low = lax.psum((low, output_low), BOTH)
    block_output = (after_attention + result.astype(jnp.float32)).astype(jnp.bfloat16)
    summed, start = [], 0
    for part in parts:
        summed.append(low[:, start : start + part.shape[1]].astype(jnp.float32))
        start += part.shape[1]
    query_sum, key_sum, value_sum, value_router_sum, output_router_sum, router_sum, *gains = summed
    summed = (
        gains[0][:, 0],
        gains[1][:, 0],
        query_sum,
        key_sum,
        value_sum,
        output_low.astype(jnp.float32),
        value_router_sum,
        output_router_sum,
        router_sum,
    )
    return (
        block_output,
        stream_grad,
        *summed,
        first_sum,
        second_sum,
    )


def kernel_body(
    tokens,
    cotangent,
    gain_attention,
    gain_feedforward,
    query_weight,
    key_weight,
    value_weight,
    output_weight,
    value_router,
    output_router,
    expert_router,
    expert_first,
    expert_second,
    segments,
    value_ids,
    output_ids,
    ffn_ids,
):
    gains = (gain_attention[None], gain_feedforward[None])
    weights = (query_weight, key_weight, value_weight, output_weight)
    routers = (value_router.T, output_router.T, expert_router.T)
    rows_sum, first_sum, second_sum, *saved, result = call_layer(
        tokens,
        cotangent,
        gains,
        weights,
        routers,
        segments,
        value_ids[0],
        output_ids[0],
        ffn_ids[0],
        expert_first,
        expert_second,
    )
    block_output, stream_grad, low, output_low = call_backward(
        rows_sum, tokens, cotangent, gains, routers, saved, weights, result
    )
    (
        query_sum,
        key_sum,
        value_sum,
        output_sum,
        value_router_sum,
        output_router_sum,
        expert_router_sum,
        gain_attention_sum,
        gain_feedforward_sum,
        first_sum,
        second_sum,
        block_output,
        stream_grad,
    ) = call_widen(
        low,
        output_low,
        first_sum,
        second_sum,
        block_output,
        stream_grad,
        query_weight.shape[1],
        expert_router.shape[1],
        expert_first.shape[0],
    )
    return (
        block_output,
        stream_grad,
        gain_attention_sum[0],
        gain_feedforward_sum[0],
        query_sum,
        key_sum,
        value_sum,
        output_sum,
        value_router_sum.T,
        output_router_sum.T,
        expert_router_sum.T,
        first_sum,
        second_sum,
    )


def body(*args):
    if (lax.axis_size("dp"), lax.axis_size("expert")) == GRID:
        return kernel_body(*args)
    return general_body(*args)


def solution(mesh):
    placed = (
        P(("dp", "expert"), None),
        P(("dp", "expert"), None),
        P(),
        P(),
        P(),
        P(),
        P(),
        P(),
        P(),
        P(),
        P(),
        P(("dp", "expert"), None, None),
        P(("dp", "expert"), None, None),
        P(("dp", "expert"), None),
        P(None, ("dp", "expert"), None, None),
        P(None, ("dp", "expert"), None, None),
        P(None, ("dp", "expert"), None),
    )
    return jax.shard_map(
        body,
        mesh=mesh,
        in_specs=placed,
        out_specs=(
            P(("dp", "expert"), None),
            P(("dp", "expert"), None),
            P(),
            P(),
            P(),
            P(),
            P(),
            P(),
            P(),
            P(),
            P(),
            P(("dp", "expert"), None, None),
            P(("dp", "expert"), None, None),
        ),
        check_vma=False,
    )
```

```python
import functools
import math

import jax
import jax.numpy as jnp
from jax import lax
from jax.experimental import pallas as pl
from jax.experimental.pallas import tpu as pltpu
from jax.sharding import PartitionSpec as P

HEADS = 4
HEAD = 128
ATT_EXP = 5


NEG_FILL = -1000000000.0


def layer_norm(stream, norm_gain):
    average = jnp.mean(stream, axis=-1, keepdims=True)
    centred = stream - average
    variance = jnp.mean(centred * centred, axis=-1, keepdims=True)
    return centred * lax.rsqrt(variance + 1e-05) * norm_gain


def expert_mask(picked_ids, expert_count):
    matches = picked_ids[..., None] == jnp.arange(expert_count, dtype=jnp.int32)
    return jnp.sum(matches.astype(jnp.float32), axis=-2)


def attention_forward(stream, document_ids, value_picks, output_picks, shared):
    (
        gain_attention,
        query_weight,
        key_weight,
        value_weight,
        output_weight,
        value_router,
        output_router,
    ) = shared
    length = stream.shape[0]
    normed_low = layer_norm(stream, gain_attention).astype(jnp.bfloat16)
    queries = (
        jnp.dot(normed_low, query_weight, preferred_element_type=jnp.float32)
        .astype(jnp.bfloat16)
        .reshape(length, HEADS, HEAD)
    )
    key_rows = (
        jnp.dot(normed_low, key_weight, preferred_element_type=jnp.float32)
        .astype(jnp.bfloat16)
        .reshape(length, HEADS, HEAD)
    )
    value_sig = jax.nn.sigmoid(
        jnp.dot(normed_low, value_router, preferred_element_type=jnp.float32)
    ).reshape(length, HEADS, ATT_EXP)
    output_sig = jax.nn.sigmoid(
        jnp.dot(normed_low, output_router, preferred_element_type=jnp.float32)
    ).reshape(length, HEADS, ATT_EXP)
    value_mask = expert_mask(value_picks, ATT_EXP)
    output_mask = expert_mask(output_picks, ATT_EXP)
    value_gates = value_mask * value_sig
    output_gates = output_mask * output_sig
    stream_low = stream.astype(jnp.bfloat16)
    projected = jnp.dot(stream_low, value_weight, preferred_element_type=jnp.float32).reshape(
        length, HEADS, ATT_EXP, HEAD
    )
    values = jnp.sum(value_gates[..., None] * projected, axis=2).astype(jnp.bfloat16)
    scores = jnp.einsum("qhd,khd->hqk", queries, key_rows, preferred_element_type=jnp.float32) * (
        1.0 / math.sqrt(HEAD)
    )
    positions = jnp.arange(length, dtype=jnp.int32)
    allowed = (document_ids[:, None] == document_ids[None, :]) & (
        positions[:, None] >= positions[None, :]
    )
    scores = jnp.where(allowed[None], scores, NEG_FILL)
    row_max = jnp.max(scores, axis=-1, keepdims=True)
    exponent = jnp.exp(scores - row_max)
    row_total = jnp.sum(exponent, axis=-1, keepdims=True)
    probability = exponent / row_total
    weights_low = probability.astype(jnp.bfloat16)
    mixed = jnp.einsum("hqk,khd->qhd", weights_low, values, preferred_element_type=jnp.float32)
    gated_rows = (
        (output_gates[..., None] * mixed[:, :, None, :])
        .reshape(length, HEADS * ATT_EXP * HEAD)
        .astype(jnp.bfloat16)
    )
    after_attention = stream + jnp.dot(
        gated_rows, output_weight, preferred_element_type=jnp.float32
    )
    saved_parts = (
        normed_low,
        queries,
        key_rows,
        value_gates * (1.0 - value_sig),
        output_gates * (1.0 - output_sig),
        value_gates,
        output_gates,
        stream_low,
        projected,
        values,
        probability,
        weights_low,
        mixed,
        gated_rows,
    )
    return (after_attention, saved_parts)


def attention_backward(after_grad, saved_parts, stream, shared):
    (
        gain_attention,
        query_weight,
        key_weight,
        value_weight,
        output_weight,
        value_router,
        output_router,
    ) = shared
    (
        normed_low,
        queries,
        key_rows,
        value_slope,
        output_slope,
        value_gates,
        output_gates,
        stream_low,
        projected,
        values,
        probability,
        weights_low,
        mixed,
        gated_rows,
    ) = saved_parts
    length = after_grad.shape[0]
    scale = 1.0 / math.sqrt(HEAD)
    after_low = after_grad.astype(jnp.bfloat16)
    output_part = jnp.einsum("sa,sb->ab", gated_rows, after_low, preferred_element_type=jnp.float32)
    gated_grad = jnp.einsum(
        "sb,ab->sa", after_low, output_weight, preferred_element_type=jnp.float32
    ).astype(jnp.bfloat16)
    gated_grad = gated_grad.reshape(length, HEADS, ATT_EXP, HEAD).astype(jnp.float32)
    mixed_grad = jnp.sum(output_gates[..., None] * gated_grad, axis=2).astype(jnp.bfloat16)
    output_gate_grad = jnp.sum(gated_grad * mixed[:, :, None, :], axis=3)
    prob_grad = jnp.einsum("qhd,khd->hqk", mixed_grad, values, preferred_element_type=jnp.float32)
    values_grad = jnp.einsum(
        "hqk,qhd->khd", weights_low, mixed_grad, preferred_element_type=jnp.float32
    ).astype(jnp.bfloat16)
    values_grad = values_grad.astype(jnp.float32)
    score_grad = (
        probability * (prob_grad - jnp.sum(probability * prob_grad, axis=-1, keepdims=True))
    ).astype(jnp.bfloat16)
    query_grad = (
        (
            jnp.einsum("hqk,khd->qhd", score_grad, key_rows, preferred_element_type=jnp.float32)
            * scale
        )
        .astype(jnp.bfloat16)
        .reshape(length, HEADS * HEAD)
    )
    key_grad = (
        (
            jnp.einsum("hqk,qhd->khd", score_grad, queries, preferred_element_type=jnp.float32)
            * scale
        )
        .astype(jnp.bfloat16)
        .reshape(length, HEADS * HEAD)
    )
    projected_grad = (
        (value_gates[..., None] * values_grad[:, :, None, :])
        .astype(jnp.bfloat16)
        .reshape(length, HEADS * ATT_EXP * HEAD)
    )
    value_gate_grad = jnp.sum(values_grad[:, :, None, :] * projected, axis=3)
    value_logit_grad = (
        (value_gate_grad * value_slope)
        .astype(jnp.bfloat16)
        .reshape(length, HEADS * ATT_EXP)
    )
    output_logit_grad = (
        (output_gate_grad * output_slope)
        .astype(jnp.bfloat16)
        .reshape(length, HEADS * ATT_EXP)
    )
    value_part = jnp.einsum(
        "sa,sb->ab", stream_low, projected_grad, preferred_element_type=jnp.float32
    )
    query_part = jnp.einsum("sa,sb->ab", normed_low, query_grad, preferred_element_type=jnp.float32)
    key_part = jnp.einsum("sa,sb->ab", normed_low, key_grad, preferred_element_type=jnp.float32)
    value_router_part = jnp.einsum(
        "sa,sb->ab", normed_low, value_logit_grad, preferred_element_type=jnp.float32
    )
    output_router_part = jnp.einsum(
        "sa,sb->ab", normed_low, output_logit_grad, preferred_element_type=jnp.float32
    )
    normed_grad = jnp.einsum(
        "sb,ab->sa", query_grad, query_weight, preferred_element_type=jnp.float32
    )
    normed_grad = normed_grad + jnp.einsum(
        "sb,ab->sa", key_grad, key_weight, preferred_element_type=jnp.float32
    )
    normed_grad = normed_grad + jnp.einsum(
        "sb,ab->sa", value_logit_grad, value_router, preferred_element_type=jnp.float32
    )
    normed_grad = normed_grad + jnp.einsum(
        "sb,ab->sa", output_logit_grad, output_router, preferred_element_type=jnp.float32
    )
    norm_value, norm_pull = jax.vjp(layer_norm, stream, gain_attention)
    stream_extra, gain_part = norm_pull(normed_grad)
    value_input = jnp.einsum(
        "sb,ab->sa", projected_grad, value_weight, preferred_element_type=jnp.float32
    )
    stream_grad = after_grad + stream_extra + value_input
    return (
        stream_grad,
        (
            gain_part,
            query_part,
            key_part,
            value_part,
            output_part,
            value_router_part,
            output_router_part,
        ),
    )


def expert_pass(rows, upstream_rows, gates, expert_first, expert_second):
    local_count, model_width, hidden_width = expert_first.shape
    wide = local_count * hidden_width
    first = expert_first.transpose(1, 0, 2).reshape(model_width, wide)
    second = expert_second.reshape(wide, model_width)
    gates_wide = jnp.repeat(gates.astype(jnp.float32), hidden_width, axis=1)
    hidden_pre = jnp.dot(rows, first, preferred_element_type=jnp.float32)
    hidden, gelu_pull = jax.vjp(jax.nn.gelu, hidden_pre)
    hidden = hidden.astype(jnp.bfloat16).astype(jnp.float32)
    gated_hidden = (gates_wide * hidden).astype(jnp.bfloat16)
    back = jnp.einsum("sd,fd->sf", upstream_rows, second, preferred_element_type=jnp.float32)
    gate_grad = jnp.sum((back * hidden).reshape(-1, local_count, hidden_width), axis=2)
    pre_grad = gelu_pull(gates_wide * back)[0].astype(jnp.bfloat16)
    result = jnp.dot(gated_hidden, second, preferred_element_type=jnp.float32)
    row_grad = jnp.einsum("sf,df->sd", pre_grad, first, preferred_element_type=jnp.float32)
    second_sum = jnp.einsum(
        "sf,sd->fd", gated_hidden, upstream_rows, preferred_element_type=jnp.float32
    )
    first_sum = jnp.einsum("sd,sf->df", rows, pre_grad, preferred_element_type=jnp.float32)
    first_sum = first_sum.reshape(model_width, local_count, hidden_width).transpose(1, 0, 2)
    return (
        result.astype(jnp.bfloat16),
        row_grad.astype(jnp.bfloat16),
        gate_grad.astype(jnp.bfloat16),
        first_sum,
        second_sum.reshape(expert_second.shape),
    )


BOTH = ("dp", "expert")


def expert_piece(after_low, upstream_low, dense_gates, expert_first, expert_second):
    local_count = expert_first.shape[0]
    me = lax.axis_index("dp") * lax.axis_size("expert") + lax.axis_index("expert")
    upstream_rows = lax.all_gather(upstream_low, BOTH, axis=0, tiled=True)
    rows = lax.all_gather(after_low, BOTH, axis=0, tiled=True)
    gates = lax.all_gather(dense_gates, BOTH, axis=0, tiled=True)
    gates = lax.dynamic_slice_in_dim(gates, me * local_count, local_count, axis=1)
    result, row_grad, gate_grad, first_sum, second_sum = expert_pass(
        rows, upstream_rows, gates, expert_first, expert_second
    )
    gate_back = lax.all_to_all(gate_grad, BOTH, split_axis=0, concat_axis=1, tiled=True)
    token_grad = lax.psum_scatter(row_grad, BOTH, scatter_dimension=0, tiled=True)
    result = lax.psum_scatter(result, BOTH, scatter_dimension=0, tiled=True)
    return (result, token_grad, gate_back), (first_sum, second_sum)


def expert_exchange(after_low, upstream_low, dense_gates, expert_first, expert_second, pieces):
    if pieces == 1:
        back, sums = expert_piece(
            after_low, upstream_low, dense_gates, expert_first, expert_second
        )
        return (*back, *sums)

    def step(totals, piece):
        back, sums = expert_piece(*piece, expert_first, expert_second)
        return (totals[0] + sums[0], totals[1] + sums[1]), back

    cut = lambda array: array.reshape(pieces, -1, array.shape[1])
    start = (
        jnp.zeros(expert_first.shape, jnp.float32),
        jnp.zeros(expert_second.shape, jnp.float32),
    )
    sums, back = lax.scan(step, start, (cut(after_low), cut(upstream_low), cut(dense_gates)))
    return (*(part.reshape(-1, part.shape[2]) for part in back), *sums)


MESH = pl.DeviceIdType.MESH
GRID = (4, 8)
N_SEM = 47
VMEM_LIMIT = 63 * 2**20


class Place:
    def __init__(self):
        dp, expert = lax.axis_index("dp"), lax.axis_index("expert")
        self.y, self.x = dp // 2, dp % 2
        self.z, self.core = expert // 2, expert % 2
        self.dp = dp
        self.me = dp * GRID[1] + expert
        self.x_peer = (2 * self.y + 1 - self.x, expert)
        self.y_peer = (2 * (1 - self.y) + self.x, expert)
        self.core_peer = (dp, 2 * self.z + 1 - self.core)
        self.middle = (self.z + self.z // 2) % 2
        self.main = 1 + self.z % 2
        self.minor = 3 * (self.z // 2)

    def along_z(self, z):
        return (self.dp, 2 * z + self.core)

    def z_at(self, j):
        near = j + self.middle * (1 - 2 * j) * (1 - j // 2)
        return near + self.z // 2 * (3 - 2 * near)

    def chip(self, q, j):
        return ((self.y + q // 2) % 2 * 2 + (self.x + q % 2) % 2) * 4 + self.z_at(j)

    def fixed(self, middle):
        known = Place.__new__(Place)
        known.__dict__.update(self.__dict__)
        known.middle = middle
        return known

    def if_middle(self, action):
        if not isinstance(self.middle, int):
            pl.when(self.middle == 1)(action)
        elif self.middle:
            action()


def enter(place):
    barrier = pltpu.get_barrier_semaphore()

    def signal(peer):
        pl.semaphore_signal(barrier, inc=1, device_id=peer, device_id_type=MESH)

    for peer in (place.x_peer, place.y_peer, place.core_peer, place.along_z(place.main)):
        signal(peer)
    place.if_middle(lambda: signal(place.along_z(place.minor)))
    pl.when(place.middle == 0)(lambda: pl.semaphore_wait(barrier, 4))
    place.if_middle(lambda: pl.semaphore_wait(barrier, 5))


def remote(src, dst, send, recv, peer):
    return pltpu.make_async_remote_copy(
        src_ref=src,
        dst_ref=dst,
        send_sem=send,
        recv_sem=recv,
        device_id=peer,
        device_id_type=MESH,
    )


def cut_columns(width):
    tiles = width // 128
    split = tiles // 2
    outer = max(1, tiles * 3 // 10)
    return (outer + tiles % 2) * 128, split * 128, (tiles - outer) * 128


class Gather:
    def __init__(self, place, buf, rows, sems):
        self.place, self.buf, self.rows = place, buf, rows
        self.width = buf.shape[1]
        self.d_end, self.split, self.c_start = cut_columns(self.width)
        self.send, self.recv = sems.at[0], sems.at[1]

    def block(self, q, j, columns=slice(None)):
        start = (2 * self.place.chip(q, j) + self.place.core) * self.rows
        return self.buf.at[pl.ds(pl.multiple_of(start, self.rows), self.rows), columns]

    def copy(self, kind, j, q=0):
        place = self.place
        if kind == "x0":
            ref, number, peer = self.block(0, 0), 15, place.x_peer
        elif kind == "y0":
            ref, number, peer = self.block(0, 0), 19, place.y_peer
        elif kind == "x":
            ref, number, peer = self.block(0, j, slice(0, self.c_start)), 15 + j, place.x_peer
        elif kind == "y":
            ref, number, peer = self.block(0, j, slice(self.d_end, None)), 19 + j, place.y_peer
        elif kind == "a":
            ref, number, peer = self.block(1, j, slice(self.split, None)), 23 + j, place.y_peer
        elif kind == "b":
            ref, number, peer = self.block(2, j, slice(0, self.split)), 27 + j, place.x_peer
        else:
            ref, number, peer = self.block(q, j), 31 + 4 * q + j, place.core_peer
        return remote(ref, ref, self.send.at[number], self.recv.at[number], peer)

    def z_copy(self, part, j, number, z, receiver_j):
        columns = (slice(None), slice(self.c_start, None), slice(0, self.d_end))[part]
        ref = self.block(part, j, columns)
        return remote(
            ref,
            ref,
            self.send.at[5 * part + number],
            self.recv.at[3 * part + receiver_j - 1],
            self.place.along_z(z),
        )

    def z_own(self, part):
        place = self.place
        self.z_copy(part, 0, 0, place.main, 1 + place.middle).start()
        place.if_middle(lambda: self.z_copy(part, 0, 1, place.minor, 1).start())

    def z_pass(self, part, j):
        place = self.place
        first = 1 - (j + 2) // 4
        z = place.minor + first * (place.main - place.minor)
        return self.z_copy(part, j, 1 + j, z, j + 2 * first)

    def z_arrive(self, part, j):
        self.z_copy(part, j, 0, self.place.main, j).wait_recv()
        self.place.if_middle(lambda: self.z_pass(part, j).start())

    def begin(self):
        self.z_own(0)
        self.copy("x0", 0).start()
        self.copy("y0", 0).start()
        self.copy("core", 0, 0).start()

    def line(self, j):
        self.z_arrive(0, j)
        self.copy("x", j).start()
        self.copy("y", j).start()
        self.copy("core", j, 0).start()

    def side_x(self, j):
        self.copy("x" if j else "x0", j).wait_recv()
        self.copy("a", j).start()
        self.copy("core", j, 1).start()

    def side_y(self, j):
        self.copy("y" if j else "y0", j).wait_recv()
        self.copy("b", j).start()
        self.copy("core", j, 2).start()

    def own_c(self):
        self.z_own(1)

    def own_d(self):
        self.z_own(2)

    def pass_c(self, j):
        self.z_arrive(1, j)

    def pass_d(self, j):
        self.z_arrive(2, j)

    def corner(self, j):
        self.copy("a", j).wait_recv()
        self.copy("b", j).wait_recv()
        self.copy("core", j, 3).start()

    def whole(self, q, j):
        self.copy("core", j, q).wait_recv()

    def wait_all(self):
        def step(k, carry):
            self.whole(k // 4, k % 4)
            return carry

        lax.fori_loop(0, 16, step, 0)

    def finish(self):
        place = self.place
        for part in range(3):
            self.z_copy(part, 0, 0, place.main, 1).wait_send()

        def middle():
            for part in range(3):
                self.z_copy(part, 0, 1, place.minor, 1).wait_send()

                def passed(j, carry):
                    self.z_pass(part, j).wait_send()
                    return carry

                lax.fori_loop(1, 4, passed, 0)

        place.if_middle(middle)
        self.copy("x0", 0).wait_send()
        self.copy("y0", 0).wait_send()

        def line(j, carry):
            self.copy("x", j).wait_send()
            self.copy("y", j).wait_send()
            return carry

        lax.fori_loop(1, 4, line, 0)

        def step(j, carry):
            self.copy("a", j).wait_send()
            self.copy("b", j).wait_send()
            for q in range(4):
                self.copy("core", j, q).wait_send()
            return carry

        lax.fori_loop(0, 4, step, 0)


class Reduce:
    def __init__(self, place, own, other, boxes, sems, held=None):
        self.place, self.other = place, other
        self.other_in, self.a_in, self.b_in, self.x_in, self.y_in = boxes[:5]
        self.own = own or (lambda k: self.other_in.at[k])
        self.extra = held or (lambda k: self.other_in.at[k])
        self.z_in = boxes[5:]
        self.rows, self.width = self.other_in.shape[1:]
        self.d_end, self.split, self.c_start = cut_columns(self.width)
        self.send, self.recv = sems.at[0], sems.at[1]

    def copy(self, kind, k):
        place = self.place
        j = k % 4
        if kind == "core":
            src, dst, number, peer = self.other(k), self.other_in.at[k], k, place.core_peer
        elif kind == "a":
            src = self.own(k).at[:, self.split :]
            dst, number, peer = self.a_in.at[j], 16 + j, place.y_peer
        elif kind == "b":
            src = self.own(k).at[:, : self.split]
            dst, number, peer = self.b_in.at[j], 20 + j, place.x_peer
        elif kind == "x0":
            src, dst, number, peer = self.own(k), self.x_in.at[0], 24, place.x_peer
        elif kind == "y0":
            src, dst, number, peer = self.own(k), self.y_in.at[0], 28, place.y_peer
        elif kind == "x":
            src = self.own(k).at[:, : self.c_start]
            dst, number, peer = self.x_in.at[j, :, : self.c_start], 24 + j, place.x_peer
        else:
            src = self.own(k).at[:, self.d_end :]
            dst, number, peer = self.y_in.at[j, :, self.d_end :], 28 + j, place.y_peer
        return remote(src, dst, self.send.at[number], self.recv.at[number], peer)

    def z_columns(self, part):
        return (slice(None), slice(self.c_start, None), slice(0, self.d_end))[part]

    def z_copy(self, part, j):
        place = self.place
        first = 1 - (j + 2) // 4
        box = place.middle * (j // 3) + (1 - place.middle) * (j + 1)
        z = place.main + place.middle * first * (place.minor - place.main)
        return remote(
            self.own(4 * part + j).at[:, self.z_columns(part)],
            self.z_in[part].at[box],
            self.send.at[32 + 5 * part + j],
            self.recv.at[32 + 5 * part + box],
            place.along_z(z),
        )

    def z_wait(self, part, box):
        self.copy_box(part, box).wait_recv()

    def copy_box(self, part, box):
        ref = self.z_in[part].at[box]
        return remote(
            ref,
            ref,
            self.send.at[32 + 5 * part],
            self.recv.at[32 + 5 * part + box],
            self.place.along_z(self.place.main),
        )

    def z_give(self, part, j):
        def middle():
            box = j + (j + 2) // 4
            self.z_wait(part, box)
            self.add(4 * part + j, self.z_columns(part), [lambda at: self.z_in[part][box, at, :]])

        self.place.if_middle(middle)
        self.z_copy(part, j).start()

    def z_last(self, part):
        columns = self.z_columns(part)
        self.z_wait(part, 0)
        self.add(4 * part, columns, [lambda at: self.z_in[part][0, at, :]])

        def middle():
            self.z_wait(part, 2)
            self.add(4 * part, columns, [lambda at: self.z_in[part][2, at, :]])

        self.place.if_middle(middle)

    def add(self, k, columns, terms):
        own = self.own(k)

        def step(number, carry):
            at = pl.ds(pl.multiple_of(number * 16, 16), 16)
            total = own[at, columns].astype(jnp.float32)
            for term in terms:
                total = total + term(at).astype(jnp.float32)
            own[at, columns] = total.astype(own.dtype)
            return carry

        lax.fori_loop(0, self.rows // 16, step, 0)

    def corner(self, j):
        k = 12 + j
        self.copy("core", k).wait_recv()
        self.add(k, slice(None), [lambda at: self.extra(k)[at, :]])
        self.copy("a", k).start()
        self.copy("b", k).start()

    def side_x(self, j):
        k, split = 4 + j, self.split
        self.copy("core", k).wait_recv()
        self.add(k, slice(0, split), [lambda at: self.extra(k)[at, :split]])
        self.copy("a", k).wait_recv()
        self.add(
            k,
            slice(split, None),
            [lambda at: self.extra(k)[at, split:], lambda at: self.a_in[j, at, :]],
        )
        if j:
            self.copy("x", k).start()

    def side_y(self, j):
        k, split = 8 + j, self.split
        self.copy("core", k).wait_recv()
        self.add(k, slice(split, None), [lambda at: self.extra(k)[at, split:]])
        self.copy("b", k).wait_recv()
        self.add(
            k,
            slice(0, split),
            [lambda at: self.extra(k)[at, :split], lambda at: self.b_in[j, at, :]],
        )
        if j:
            self.copy("y", k).start()

    def give_c(self, j):
        if j:
            self.z_give(1, j)
        else:
            self.z_last(1)
            self.copy("x0", 4).start()

    def give_d(self, j):
        if j:
            self.z_give(2, j)
        else:
            self.z_last(2)
            self.copy("y0", 8).start()

    def hand_over(self):
        def step(number, carry):
            self.copy("core", 15 - number).start()
            return carry

        lax.fori_loop(0, 16, step, 0)

    def line(self, j):
        self.copy("core", j).wait_recv()
        self.copy("x", j).wait_recv()
        self.copy("y", j).wait_recv()
        d_end, c_start = self.d_end, self.c_start
        boxes = (self.extra(j), self.x_in.at[j], self.y_in.at[j])
        for columns, used in (
            (slice(0, d_end), boxes[:2]),
            (slice(d_end, c_start), boxes),
            (slice(c_start, None), (boxes[0], boxes[2])),
        ):
            self.add(j, columns, [lambda at, box=box: box[at, columns] for box in used])
        self.z_give(0, j)

    def last(self, put):
        self.copy("core", 0).wait_recv()
        self.copy("x0", 0).wait_recv()
        self.copy("y0", 0).wait_recv()
        self.z_wait(0, 0)
        own = self.own(0)

        def sum_up(middle):
            def step(number, carry):
                at = pl.ds(pl.multiple_of(number * 16, 16), 16)
                total = own[at, :].astype(jnp.float32)
                for box in (self.extra(0), self.x_in.at[0], self.y_in.at[0], self.z_in[0].at[0]):
                    total = total + box[at, :].astype(jnp.float32)
                if middle:
                    total = total + self.z_in[0][2, at, :].astype(jnp.float32)
                put(at, total)
                return carry

            lax.fori_loop(0, own.shape[0] // 16, step, 0)

        if self.place.middle:
            self.z_wait(0, 2)
        sum_up(self.place.middle == 1)

    def finish(self):
        def step(j, carry):
            self.copy("a", 12 + j).wait_send()
            self.copy("b", 12 + j).wait_send()
            for q in range(4):
                self.copy("core", 4 * q + j).wait_send()
            return carry

        lax.fori_loop(0, 4, step, 0)

        def outer(j, carry):
            self.copy("x", 4 + j).wait_send()
            self.copy("y", 8 + j).wait_send()
            for part in range(3):
                self.z_copy(part, j).wait_send()
            return carry

        lax.fori_loop(1, 4, outer, 0)
        self.copy("x0", 4).wait_send()
        self.copy("y0", 8).wait_send()


def reduce_scratch(rows, width):
    low = jnp.bfloat16
    d_end, split, c_start = cut_columns(width)
    return [
        pltpu.VMEM((16, rows, width), low),
        pltpu.VMEM((4, rows, width - split), low),
        pltpu.VMEM((4, rows, split), low),
        pltpu.VMEM((4, rows, width), low),
        pltpu.VMEM((4, rows, width), low),
        pltpu.VMEM((5, rows, width), low),
        pltpu.VMEM((5, rows, width - c_start), low),
        pltpu.VMEM((5, rows, d_end), low),
    ]


GELU_C = math.sqrt(2.0 / math.pi)
GELU_K = 0.044715


def mm(left, right):
    return jnp.dot(left, right, preferred_element_type=jnp.float32)


def mm_tn(left, right):
    return lax.dot_general(left, right, (((0,), (0,)), ((), ())), preferred_element_type=jnp.float32)


def norm_parts(stream):
    average = jnp.mean(stream, axis=-1, keepdims=True)
    centred = stream - average
    variance = jnp.mean(centred * centred, axis=-1, keepdims=True)
    scale = lax.rsqrt(variance + 1e-05)
    return centred * scale, scale


def norm_pull(normed_grad, unit, scale, gain):
    inner = normed_grad * gain
    mean = jnp.mean(inner, axis=-1, keepdims=True)
    along = jnp.mean(inner * unit, axis=-1, keepdims=True)
    gain_grad = jnp.sum(normed_grad * unit, axis=0, keepdims=True)
    return scale * (inner - mean - unit * along), gain_grad


def mm_nt(left, right):
    return lax.dot_general(left, right, (((1,), (1,)), ((), ())), preferred_element_type=jnp.float32)


OUTPUT_LANE = 32


def join_routers(joined, value_router_ref, output_router_ref):
    count = value_router_ref.shape[0]
    joined[...] = jnp.zeros_like(joined)
    joined[:count, :] = value_router_ref[...]
    joined[OUTPUT_LANE : OUTPUT_LANE + count, :] = output_router_ref[...]


HELD = 6
GAIN_LANE = 64


def backward_kernel(
    rows_ref,
    tokens_ref,
    cotangent_ref,
    gain_attention_ref,
    gain_feedforward_ref,
    value_router_ref,
    output_router_ref,
    expert_router_ref,
    after_ref,
    normed_ref,
    normed_ffn_ref,
    queries_ref,
    keys_ref,
    projected_ref,
    values_ref,
    probability_ref,
    mixed_ref,
    gated_ref,
    gates_ref,
    slopes_ref,
    expert_slope_ref,
    query_in,
    key_in,
    value_in,
    output_in,
    result_in,
    block_out,
    stream_out,
    low_out,
    output_low_out,
    query_ref,
    key_ref,
    value_ref,
    output_ref,
    routers,
    expert_router,
    after_grad,
    after_low,
    gated_grad,
    projected_grad,
    both_grad,
    held,
    low_part,
    output_part,
    low_own,
    output_own,
    weight_sems,
    held_sems,
    own_sems,
    *refs,
):
    place = Place()
    length, model_width = tokens_ref.shape
    wide = value_ref.shape[1]
    narrow = query_ref.shape[1]
    expert_count = expert_router_ref.shape[0]
    low_rows, output_rows = low_own.shape[0], output_own.shape[0]
    low_type = jnp.bfloat16

    def other_rows(ref, rows, place):
        def get(k):
            start = (2 * place.chip(k // 4, k % 4) + 1 - place.core) * rows
            return ref.at[pl.ds(pl.multiple_of(start, rows), rows)]

        return get

    def own_rows(ref, rows, place):
        def get(k):
            start = (2 * place.chip(k // 4, k % 4) + place.core) * rows
            return ref.at[pl.ds(pl.multiple_of(start, rows), rows)]

        return get

    weights = ((output_in, output_ref), (query_in, query_ref), (key_in, key_ref), (value_in, value_ref))
    loads = [
        pltpu.make_async_copy(src, dst, weight_sems.at[number])
        for number, (src, dst) in enumerate(weights)
    ]
    tile = 256
    small_column = wide + 2 * narrow
    expert_column = small_column + 128
    first_base = {"corner": 12, "side_x": 4, "side_y": 8, "line": 0, "last": 0}
    values = {}

    def c1():
        join_routers(routers, value_router_ref, output_router_ref)
        expert_router[...] = jnp.zeros_like(expert_router)
        expert_router[:expert_count, :] = expert_router_ref[...]
        logit_grad = (rows_ref[:, model_width:] * expert_slope_ref[...]).astype(low_type)
        unit, scale = norm_parts(after_ref[...])
        through, values["gain_feedforward"] = norm_pull(
            mm(logit_grad, expert_router[...]), unit, scale, gain_feedforward_ref[...]
        )
        after_grad[...] = cotangent_ref[...].astype(jnp.float32) + rows_ref[:, :model_width] + through
        after_low[...] = after_grad[...].astype(low_type)
        low_part[:, expert_column:] = mm_tn(normed_ffn_ref[...], logit_grad).astype(low_type)

    def c2():
        def output_tile(number, carry):
            at = pl.ds(pl.multiple_of(number * tile, tile), tile)
            output_part[at, :] = mm_tn(gated_ref[:, at], after_low[...]).astype(low_type)
            return carry

        lax.fori_loop(0, wide // tile, output_tile, 0)

    def c3():
        loads[0].wait()

        def gated_tile(number, carry):
            at = pl.ds(pl.multiple_of(number * tile, tile), tile)
            gated_grad[:, at] = mm_nt(after_low[...], output_ref[at, :]).astype(low_type)
            return carry

        lax.fori_loop(0, wide // tile, gated_tile, 0)

    def c4():
        lane = lax.broadcasted_iota(jnp.int32, (length, 128), 1)
        gate_grads = jnp.zeros((length, 128), jnp.float32)
        inverse = 1.0 / math.sqrt(HEAD)
        for head in range(HEADS):
            columns = slice(head * HEAD, (head + 1) * HEAD)
            mixed = mixed_ref[:, columns]
            mixed_grad = jnp.zeros((length, HEAD), jnp.float32)
            for e in range(ATT_EXP):
                at = head * ATT_EXP + e
                part = gated_grad[:, at * HEAD : (at + 1) * HEAD].astype(jnp.float32)
                lane_at = OUTPUT_LANE + at
                mixed_grad = mixed_grad + gates_ref[:, lane_at : lane_at + 1] * part
                gate_grads = jnp.where(
                    lane == lane_at, jnp.sum(part * mixed, axis=1, keepdims=True), gate_grads
                )
            mixed_grad = mixed_grad.astype(low_type)
            probability = probability_ref[head]
            prob_grad = mm_nt(mixed_grad, values_ref[:, columns])
            inner = jnp.sum(probability * prob_grad, axis=-1, keepdims=True)
            score_grad = (probability * (prob_grad - inner)).astype(low_type)
            both_grad[:, columns] = (mm(score_grad, keys_ref[:, columns]) * inverse).astype(low_type)
            both_grad[:, narrow + head * HEAD : narrow + (head + 1) * HEAD] = (
                mm_tn(score_grad, queries_ref[:, columns]) * inverse
            ).astype(low_type)
            values_grad = mm_tn(probability.astype(low_type), mixed_grad)
            values_grad = values_grad.astype(low_type).astype(jnp.float32)
            for e in range(ATT_EXP):
                at = head * ATT_EXP + e
                wide_at = slice(at * HEAD, (at + 1) * HEAD)
                projected_grad[:, wide_at] = (gates_ref[:, at : at + 1] * values_grad).astype(low_type)
                gate_grad = jnp.sum(values_grad * projected_ref[:, wide_at], axis=1, keepdims=True)
                gate_grads = jnp.where(lane == at, gate_grad, gate_grads)
        values["router"] = (gate_grads * slopes_ref[...]).astype(low_type)

    def c5a():
        def value_tile(number, carry):
            at = pl.ds(pl.multiple_of(number * tile, tile), tile)
            to = pl.ds(pl.multiple_of(2 * narrow + number * tile, tile), tile)
            low_part[:, to] = mm_tn(tokens_ref[...], projected_grad[:, at]).astype(low_type)
            return carry

        lax.fori_loop(0, wide // tile, value_tile, 0)

    def c5b():
        def both_tile(number, carry):
            at = pl.ds(pl.multiple_of(number * tile, tile), tile)
            low_part[:, at] = mm_tn(normed_ref[...], both_grad[:, at]).astype(low_type)
            return carry

        lax.fori_loop(0, 2 * narrow // tile, both_tile, 0)

    def c6():
        loads[1].wait()
        loads[2].wait()
        normed_grad = mm_nt(both_grad[:, :narrow], query_ref[...])
        normed_grad = normed_grad + mm_nt(both_grad[:, narrow:], key_ref[...])
        normed_grad = normed_grad + mm(values["router"], routers[...])
        unit, scale = norm_parts(tokens_ref[...].astype(jnp.float32))
        through, gain_attention_grad = norm_pull(normed_grad, unit, scale, gain_attention_ref[...])
        after_grad[...] += through
        gain_columns = [
            jnp.broadcast_to(grad, (128, model_width)).T
            for grad in (gain_attention_grad, values["gain_feedforward"])
        ]
        small = mm_tn(normed_ref[...], values["router"])
        small_lane = lax.broadcasted_iota(jnp.int32, (model_width, 128), 1)
        small = jnp.where(small_lane == GAIN_LANE, gain_columns[0], small)
        small = jnp.where(small_lane == GAIN_LANE + 1, gain_columns[1], small)
        low_part[:, small_column:expert_column] = small.astype(low_type)

    def c7():
        loads[3].wait()
        through_values = mm_nt(projected_grad[...], value_ref[...])
        stream_out[...] = through_values

    computes = {"c1": c1, "c2": c2, "c3": c3, "c4": c4, "c5a": c5a, "c5b": c5b, "c6": c6, "c7": c7}

    def run(middle):
        known = place.fixed(middle)
        order = BACKWARD_ORDER[middle]
        held_order = [
            first_base[event[1]] + (event[2] if len(event) > 2 else 0)
            for event in order
            if event[0] == "Y" and event[1] in first_base
        ]
        slots = {k: number % HELD for number, k in enumerate(held_order)}

        def held_copy(number):
            k = held_order[number]
            start = (2 * known.chip(k // 4, k % 4) + known.core) * length
            return pltpu.make_async_copy(
                result_in.at[pl.ds(pl.multiple_of(start, length), length)],
                held.at[number % HELD],
                held_sems.at[number % HELD],
            )

        reduces = {
            "Y": Reduce(
                known,
                None,
                other_rows(result_in, length, known),
                refs[0:8],
                refs[8],
                lambda k: held.at[slots[k]],
            ),
            "O": Reduce(
                known,
                own_rows(output_part, output_rows, known),
                other_rows(output_part, output_rows, known),
                refs[9:17],
                refs[17],
            ),
            "L": Reduce(
                known,
                own_rows(low_part, low_rows, known),
                other_rows(low_part, low_rows, known),
                refs[18:26],
                refs[26],
            ),
        }
        gathers = {
            "GO": Gather(known, output_low_out, output_rows, refs[27]),
            "GL": Gather(known, low_out, low_rows, refs[28]),
        }
        owns = {"O": ("GO", output_own, own_sems.at[0]), "L": ("GL", low_own, own_sems.at[1])}
        own_copies = {
            target: pltpu.make_async_copy(own, gathers[target].block(0, 0), sem)
            for target, own, sem in owns.values()
        }

        def last(name):
            if name == "Y":

                def put(at, total):
                    block_out[at, :] = (after_ref[at, :] + total).astype(low_type)

            else:
                target, own, _ = owns[name]

                def put(at, total):
                    own[at, :] = total.astype(low_type)

            reduces[name].last(put)
            if name != "Y":
                own_copies[target].start()

        for number in range(HELD):
            held_copy(number).start()
        fetched = 0
        for name, method, *arguments in order:
            if name == "C":
                computes[method]()
                continue
            uses_held = name == "Y" and method in first_base
            if uses_held:
                held_copy(fetched).wait()
            if method == "last":
                last(name)
            else:
                if method == "begin":
                    own_copies[name].wait()
                getattr({**reduces, **gathers}[name], method)(*arguments)
            if uses_held:
                if fetched + HELD < len(held_order):
                    held_copy(fetched + HELD).start()
                fetched += 1
        for item in (*reduces.values(), *gathers.values()):
            item.finish()

    for load in loads:
        load.start()
    enter(place)
    pl.when(place.middle == 0)(lambda: run(0))
    pl.when(place.middle == 1)(lambda: run(1))
    stream_out[...] += after_grad[...]


def call_backward(rows, tokens, cotangent, gains, routers, saved, weights, result):
    length, model_width = tokens.shape
    total = GRID[0] * GRID[1]
    wide, narrow = weights[2].shape[1], weights[0].shape[1]
    low_width = wide + 2 * narrow + 256
    low_rows, output_rows = model_width // total, wide // total
    low, full = jnp.bfloat16, jnp.float32
    vmem = pl.BlockSpec(memory_space=pltpu.VMEM)
    hbm = pl.BlockSpec(memory_space=pl.ANY)
    sems = pltpu.SemaphoreType.DMA((2, N_SEM))
    return pl.pallas_call(
        backward_kernel,
        out_shape=(
            jax.ShapeDtypeStruct((length, model_width), low),
            jax.ShapeDtypeStruct((length, model_width), full),
            jax.ShapeDtypeStruct((model_width, low_width), low),
            jax.ShapeDtypeStruct((wide, model_width), low),
        ),
        in_specs=[vmem] * 21 + [hbm] * 5,
        out_specs=(vmem, vmem, hbm, hbm),
        scratch_shapes=[
            *(pltpu.VMEM(weight.shape, low) for weight in weights),
            pltpu.VMEM((128, model_width), low),
            pltpu.VMEM((128, model_width), low),
            pltpu.VMEM((length, model_width), full),
            pltpu.VMEM((length, model_width), low),
            pltpu.VMEM((length, wide), low),
            pltpu.VMEM((length, wide), low),
            pltpu.VMEM((length, 2 * narrow), low),
            pltpu.VMEM((HELD, length, model_width), low),
            pltpu.VMEM((model_width, low_width), low),
            pltpu.VMEM((wide, model_width), low),
            pltpu.VMEM((low_rows, low_width), low),
            pltpu.VMEM((output_rows, model_width), low),
            pltpu.SemaphoreType.DMA((4,)),
            pltpu.SemaphoreType.DMA((HELD,)),
            pltpu.SemaphoreType.DMA((2,)),
            *reduce_scratch(length, model_width),
            sems,
            *reduce_scratch(output_rows, model_width),
            sems,
            *reduce_scratch(low_rows, low_width),
            sems,
            sems,
            sems,
        ],
        compiler_params=pltpu.CompilerParams(
            collective_id=1, has_side_effects=True, vmem_limit_bytes=VMEM_LIMIT
        ),
        name="backward",
    )(rows, tokens, cotangent, *gains, *routers, *saved, *weights, result)


def widen_kernel(
    low_ref,
    output_low_ref,
    first_ref,
    second_ref,
    block_ref,
    stream_ref,
    query,
    key,
    value,
    output,
    value_router,
    output_router,
    expert_router,
    gain_attention,
    gain_feedforward,
    first,
    second,
    block,
    stream,
):
    full = jnp.float32
    narrow, wide = query.shape[1], value.shape[1]
    query[...] = low_ref[:, :narrow].astype(full)
    key[...] = low_ref[:, narrow : 2 * narrow].astype(full)
    value[...] = low_ref[:, 2 * narrow : 2 * narrow + wide].astype(full)
    output[...] = output_low_ref[...].astype(full)
    start = 2 * narrow + wide
    small = low_ref[:, start : start + 128].astype(full).T
    count = value_router.shape[0]
    value_router[...] = small[:count]
    output_router[...] = small[OUTPUT_LANE : OUTPUT_LANE + count]
    gain_attention[...] = small[GAIN_LANE : GAIN_LANE + 1]
    gain_feedforward[...] = small[GAIN_LANE + 1 : GAIN_LANE + 2]
    expert_router[...] = low_ref[:, start + 128 :].astype(full).T[: expert_router.shape[0]]
    hidden_width = second.shape[1]
    for e in range(first.shape[0]):
        rows = slice(e * hidden_width, (e + 1) * hidden_width)
        first[e] = first_ref[rows, :].T
        second[e] = second_ref[rows, :]
    block[...] = block_ref[...]
    stream[...] = stream_ref[...]


def call_widen(low, output_low, first_sum, second_sum, block_output, stream_grad, narrow, expert_count, local_count):
    model_width, low_width = low.shape
    wide = output_low.shape[0]
    hidden = first_sum.shape[0]
    hidden_width = hidden // local_count
    length = block_output.shape[0]
    steps = model_width // 128
    full = jnp.float32
    router_width = HEADS * ATT_EXP
    rows = lambda height, width: pl.BlockSpec((height, width), lambda i: (i, 0))
    columns = lambda height: pl.BlockSpec((height, 128), lambda i: (0, i))
    first_spec = pl.BlockSpec((local_count, 128, hidden_width), lambda i: (0, i, 0))
    second_spec = pl.BlockSpec((local_count, hidden_width, 128), lambda i: (0, 0, i))
    shape = lambda *dims, kind=full: jax.ShapeDtypeStruct(dims, kind)
    return pl.pallas_call(
        widen_kernel,
        grid=(steps,),
        out_shape=(
            shape(model_width, narrow),
            shape(model_width, narrow),
            shape(model_width, wide),
            shape(wide, model_width),
            shape(router_width, model_width),
            shape(router_width, model_width),
            shape(expert_count, model_width),
            shape(1, model_width),
            shape(1, model_width),
            shape(local_count, model_width, hidden_width),
            shape(local_count, hidden_width, model_width),
            shape(length, model_width, kind=block_output.dtype),
            shape(length, model_width),
        ),
        in_specs=[
            rows(128, low_width),
            rows(wide // steps, model_width),
            columns(hidden),
            columns(hidden),
            rows(length // steps, model_width),
            rows(length // steps, model_width),
        ],
        out_specs=(
            rows(128, narrow),
            rows(128, narrow),
            rows(128, wide),
            rows(wide // steps, model_width),
            columns(router_width),
            columns(router_width),
            columns(expert_count),
            columns(1),
            columns(1),
            first_spec,
            second_spec,
            rows(length // steps, model_width),
            rows(length // steps, model_width),
        ),
        compiler_params=pltpu.CompilerParams(vmem_limit_bytes=VMEM_LIMIT),
        name="widen",
    )(low, output_low, first_sum, second_sum, block_output, stream_grad)


BACKWARD_ORDER = (
    (
        ("Y", "hand_over"), ("Y", "corner", 3), ("C", "c1"), ("Y", "corner", 2), ("Y", "side_y",
        3), ("Y", "side_x", 3), ("Y", "give_d", 3), ("C", "c2"), ("O", "hand_over"), ("O",
        "corner", 3), ("Y", "side_x", 2), ("Y", "side_y", 2), ("O", "corner", 2), ("Y",
        "give_c", 3), ("O", "corner", 1), ("C", "c3"), ("Y", "give_c", 2), ("C", "c4"), ("Y",
        "line", 3), ("Y", "line", 2), ("O", "side_x", 3), ("Y", "corner", 0), ("O", "side_y",
        2), ("O", "give_c", 3), ("O", "side_x", 1), ("Y", "give_d", 2), ("C", "c6"), ("O",
        "corner", 0), ("O", "side_x", 2), ("O", "side_y", 3), ("C", "c5a"), ("C", "c5b"), ("L",
        "hand_over"), ("O", "give_c", 2), ("O", "side_y", 1), ("O", "give_d", 1), ("L",
        "corner", 2), ("O", "give_d", 2), ("Y", "corner", 1), ("O", "give_d", 3), ("L",
        "side_y", 2), ("O", "give_c", 1), ("O", "side_x", 0), ("O", "line", 3), ("L", "side_x",
        2), ("C", "c7"), ("O", "line", 2), ("L", "corner", 3), ("O", "side_y", 0), ("L",
        "give_c", 2), ("L", "corner", 0), ("L", "corner", 1), ("L", "side_y", 3), ("L",
        "side_x", 0), ("O", "give_c", 0), ("L", "give_d", 3), ("L", "side_x", 3), ("L",
        "give_d", 2), ("L", "give_c", 3), ("Y", "side_x", 1), ("Y", "side_y", 1), ("L",
        "side_x", 1), ("O", "give_d", 0), ("O", "line", 1), ("Y", "side_y", 0), ("Y", "give_d",
        1), ("Y", "give_c", 1), ("L", "side_y", 1), ("Y", "side_x", 0), ("Y", "give_d", 0),
        ("L", "give_c", 1), ("L", "side_y", 0), ("L", "give_d", 1), ("L", "line", 3), ("L",
        "give_c", 0), ("O", "last"), ("GO", "begin"), ("L", "line", 2), ("L", "give_d", 0),
        ("GO", "line", 1), ("GO", "pass_d", 2), ("GO", "side_x", 0), ("L", "line", 1), ("Y",
        "give_c", 0), ("GO", "pass_d", 1), ("GO", "line", 2), ("L", "last"), ("GO", "side_y",
        0), ("GO", "own_d"), ("GL", "begin"), ("GO", "side_y", 2), ("GO", "line", 3), ("GO",
        "own_c"), ("GL", "side_y", 0), ("GO", "pass_c", 2), ("GO", "pass_c", 1), ("GL",
        "side_x", 0), ("GL", "own_c"), ("GL", "line", 1), ("GO", "side_x", 2), ("GL", "own_d"),
        ("Y", "line", 1), ("Y", "last"), ("GL", "line", 2), ("GO", "corner", 0), ("GO",
        "pass_c", 3), ("GL", "line", 3), ("GL", "pass_d", 3), ("GO", "side_x", 3), ("GO",
        "pass_d", 3), ("GO", "side_y", 3), ("GL", "pass_c", 3), ("GL", "side_x", 3), ("GO",
        "side_y", 1), ("GL", "pass_c", 1), ("GO", "corner", 2), ("GL", "pass_d", 1), ("GL",
        "side_y", 1), ("GL", "pass_c", 2), ("GL", "side_y", 3), ("GL", "side_x", 1), ("GO",
        "corner", 3), ("GL", "pass_d", 2), ("GO", "side_x", 1), ("GL", "side_x", 2), ("GL",
        "side_y", 2), ("GL", "corner", 0), ("GO", "corner", 1), ("GL", "corner", 3), ("GO",
        "wait_all"), ("GL", "corner", 1), ("GL", "corner", 2), ("GL", "wait_all"),
    ),
    (
        ("Y", "hand_over"), ("Y", "corner", 3), ("Y", "corner", 1), ("C", "c1"), ("Y", "corner",
        0), ("C", "c2"), ("O", "hand_over"), ("Y", "corner", 2), ("Y", "side_y", 3), ("Y",
        "side_x", 3), ("O", "corner", 0), ("C", "c3"), ("Y", "side_y", 1), ("O", "corner", 1),
        ("Y", "give_c", 3), ("Y", "side_x", 1), ("C", "c4"), ("Y", "side_y", 2), ("C", "c5b"),
        ("O", "corner", 2), ("O", "corner", 3), ("Y", "side_x", 0), ("O", "side_y", 0), ("C",
        "c5a"), ("Y", "side_x", 2), ("Y", "side_y", 0), ("Y", "line", 3), ("O", "side_y", 1),
        ("O", "side_y", 2), ("O", "side_x", 1), ("O", "side_x", 2), ("C", "c6"), ("O", "side_y",
        3), ("Y", "line", 2), ("O", "side_x", 3), ("O", "give_c", 2), ("O", "give_c", 3), ("O",
        "give_d", 3), ("O", "give_d", 2), ("Y", "give_d", 3), ("L", "hand_over"), ("L",
        "corner", 2), ("Y", "line", 1), ("O", "side_x", 0), ("L", "corner", 0), ("L", "corner",
        1), ("O", "give_c", 1), ("L", "corner", 3), ("O", "give_d", 1), ("O", "give_c", 0),
        ("Y", "give_d", 1), ("O", "line", 2), ("L", "side_x", 1), ("Y", "give_d", 2), ("O",
        "line", 3), ("O", "give_d", 0), ("L", "side_x", 3), ("L", "side_y", 2), ("Y", "give_c",
        2), ("L", "side_y", 0), ("L", "side_y", 3), ("O", "line", 1), ("L", "side_x", 0), ("L",
        "give_c", 3), ("O", "last"), ("GO", "begin"), ("L", "give_c", 1), ("L", "side_y", 1),
        ("L", "give_d", 3), ("L", "give_d", 2), ("L", "side_x", 2), ("GO", "line", 2), ("GO",
        "side_x", 0), ("GO", "side_y", 0), ("GO", "own_d"), ("GO", "own_c"), ("L", "give_d", 1),
        ("Y", "give_c", 1), ("L", "give_d", 0), ("L", "give_c", 2), ("L", "line", 3), ("GO",
        "pass_c", 2), ("GO", "line", 1), ("GO", "pass_d", 2), ("GO", "side_y", 2), ("L", "line",
        1), ("L", "line", 2), ("L", "give_c", 0), ("GO", "line", 3), ("C", "c7"), ("GO",
        "side_x", 2), ("L", "last"), ("GO", "pass_d", 1), ("GL", "begin"), ("GL", "line", 1),
        ("GL", "line", 2), ("GL", "pass_c", 1), ("GO", "pass_c", 1), ("GO", "pass_d", 3), ("GL",
        "side_x", 0), ("GL", "side_x", 1), ("GL", "line", 3), ("GL", "side_y", 0), ("GO",
        "corner", 0), ("GO", "pass_c", 3), ("GO", "side_y", 3), ("GL", "pass_c", 3), ("GL",
        "own_c"), ("GO", "side_y", 1), ("GL", "pass_d", 1), ("GO", "side_x", 1), ("GL",
        "pass_d", 3), ("GO", "side_x", 3), ("GL", "corner", 0), ("GL", "side_y", 1), ("GL",
        "side_x", 3), ("GL", "side_y", 3), ("GL", "pass_c", 2), ("GL", "side_x", 2), ("GL",
        "own_d"), ("GO", "corner", 3), ("Y", "give_d", 0), ("GO", "corner", 1), ("GL", "pass_d",
        2), ("GL", "side_y", 2), ("GO", "corner", 2), ("Y", "give_c", 0), ("GL", "corner", 2),
        ("GL", "corner", 1), ("GL", "corner", 3), ("GO", "wait_all"), ("Y", "last"), ("GL",
        "wait_all"),
    ),
)
LAYER_ORDER = (
    (
        ("U", "begin"), ("C", "a1"), ("U", "side_x", 0), ("U", "line", 1), ("C", "a2"), ("X",
        "begin"), ("C", "prep"), ("U", "line", 2), ("U", "side_y", 0), ("X", "side_x", 0), ("U",
        "own_d"), ("U", "own_c"), ("S", "go", 1, 0), ("X", "line", 1), ("X", "side_y", 0), ("X",
        "own_d"), ("S", "go", 0, 1), ("U", "line", 3), ("X", "own_c"), ("X", "pass_c", 1), ("U",
        "corner", 0), ("X", "line", 2), ("S", "go", 2, 0), ("X", "line", 3), ("X", "corner", 0),
        ("U", "pass_d", 3), ("X", "side_x", 1), ("S", "go", 0, 0), ("U", "pass_c", 3), ("X",
        "pass_d", 1), ("U", "side_x", 3), ("U", "side_y", 3), ("S", "go", 0, 2), ("X", "pass_d",
        3), ("X", "side_y", 3), ("U", "pass_c", 1), ("X", "pass_c", 3), ("X", "side_x", 3),
        ("X", "side_y", 1), ("S", "go", 0, 3), ("S", "go", 2, 3), ("X", "pass_c", 2), ("X",
        "side_x", 2), ("U", "corner", 3), ("U", "side_x", 1), ("X", "corner", 3), ("U",
        "pass_d", 1), ("X", "pass_d", 2), ("X", "side_y", 2), ("U", "side_y", 1), ("S", "go", 3,
        0), ("U", "pass_c", 2), ("U", "pass_d", 2), ("X", "corner", 1), ("U", "side_y", 2),
        ("S", "go", 3, 3), ("U", "side_x", 2), ("S", "go", 1, 1), ("R", "corner", 3), ("R",
        "corner", 0), ("X", "corner", 2), ("U", "corner", 2), ("U", "corner", 1), ("S", "go", 1,
        3), ("S", "go", 3, 1), ("R", "side_x", 3), ("R", "give_c", 3), ("R", "side_y", 3), ("S",
        "go", 3, 2), ("R", "give_d", 3), ("S", "go", 2, 2), ("R", "corner", 2), ("R", "line",
        3), ("S", "go", 1, 2), ("R", "side_x", 0), ("R", "corner", 1), ("R", "side_y", 2), ("R",
        "side_x", 2), ("R", "give_d", 2), ("S", "go", 2, 1), ("R", "give_c", 2), ("R", "side_x",
        1), ("R", "give_c", 1), ("S", "dw", 0), ("R", "side_y", 1), ("S", "dw", 1), ("R",
        "give_d", 1), ("R", "line", 2), ("S", "dw", 2), ("R", "side_y", 0), ("S", "dw", 3),
        ("S", "dw", 4), ("R", "give_d", 0), ("S", "dw", 5), ("S", "dw", 6), ("S", "dw", 7),
        ("R", "give_c", 0), ("R", "line", 1), ("R", "last"),
    ),
    (
        ("U", "begin"), ("C", "a1"), ("U", "line", 2), ("C", "prep"), ("U", "line", 1), ("C",
        "a2"), ("X", "begin"), ("U", "line", 3), ("U", "side_x", 0), ("X", "side_x", 0), ("U",
        "side_y", 0), ("X", "line", 1), ("U", "pass_d", 1), ("X", "side_y", 0), ("X", "line",
        2), ("X", "own_c"), ("X", "line", 3), ("U", "pass_c", 1), ("U", "pass_d", 3), ("X",
        "pass_c", 1), ("U", "side_y", 1), ("S", "go", 0, 3), ("X", "pass_d", 1), ("U", "pass_c",
        3), ("U", "corner", 0), ("S", "go", 0, 2), ("X", "pass_c", 3), ("X", "own_d"), ("S",
        "go", 2, 0), ("U", "own_c"), ("X", "corner", 0), ("U", "side_x", 1), ("X", "pass_d", 3),
        ("U", "own_d"), ("X", "side_x", 1), ("X", "pass_d", 2), ("S", "go", 1, 0), ("X",
        "side_y", 1), ("S", "go", 2, 1), ("X", "side_y", 3), ("U", "side_x", 3), ("U", "side_y",
        3), ("X", "pass_c", 2), ("X", "side_x", 3), ("S", "go", 0, 1), ("S", "go", 3, 0), ("X",
        "side_y", 2), ("U", "corner", 1), ("X", "corner", 1), ("U", "pass_c", 2), ("U",
        "pass_d", 2), ("U", "side_y", 2), ("X", "side_x", 2), ("S", "go", 2, 3), ("S", "go", 3,
        1), ("U", "corner", 3), ("S", "go", 1, 1), ("X", "corner", 3), ("U", "side_x", 2), ("S",
        "go", 3, 3), ("S", "go", 1, 3), ("U", "corner", 2), ("R", "corner", 3), ("S", "go", 1,
        2), ("R", "corner", 1), ("S", "go", 0, 0), ("R", "side_x", 3), ("R", "corner", 0), ("R",
        "side_y", 3), ("R", "give_c", 3), ("X", "corner", 2), ("S", "go", 3, 2), ("S", "go", 2,
        2), ("R", "corner", 2), ("S", "dw", 0), ("R", "side_x", 1), ("R", "give_c", 1), ("R",
        "side_x", 0), ("R", "give_d", 3), ("R", "side_y", 1), ("R", "line", 3), ("S", "dw", 1),
        ("R", "give_d", 1), ("R", "side_x", 2), ("S", "dw", 2), ("S", "dw", 3), ("S", "dw", 4),
        ("R", "side_y", 2), ("R", "give_d", 2), ("R", "give_c", 2), ("S", "dw", 5), ("S", "dw",
        6), ("R", "side_y", 0), ("S", "dw", 7), ("R", "line", 1), ("R", "give_c", 0), ("R",
        "give_d", 0), ("R", "line", 2), ("R", "last"),
    ),
)


def choose(step, values):
    total = 0
    for number, value in enumerate(values):
        total = total + value * jnp.where(step == number, 1, 0)
    return total


def layer_kernel(
    local_count,
    tokens_ref,
    cotangent_ref,
    gain_attention_ref,
    gain_feedforward_ref,
    value_router_ref,
    output_router_ref,
    expert_router_ref,
    segments_ref,
    value_ids_ref,
    output_ids_ref,
    ffn_ids_ref,
    first_in,
    second_ref,
    query_in,
    key_in,
    value_in,
    output_in,
    rows_out,
    first_out,
    second_out,
    after_out,
    normed_out,
    normed_ffn_out,
    queries_out,
    keys_out,
    projected_out,
    values_out,
    probability_out,
    mixed_out,
    gated_out,
    gates_out,
    slopes_out,
    expert_slope_out,
    result_out,
    routers,
    all_ids,
    gathered,
    upstream,
    first_ref,
    first_t_ref,
    second_t_ref,
    hidden_parts,
    partial,
    result_stage,
    weight_sems,
    upstream_sems,
    gather_sems,
    reduce_sems,
    result_sems,
    *boxes,
):
    place = Place()
    length, model_width = tokens_ref.shape
    pair = 2 * length
    expert_count = expert_router_ref.shape[0]
    width = gathered.shape[1]
    gate_width = width - model_width
    hidden_width = first_ref.shape[1] // local_count
    narrow, wide = query_in.shape[1], value_in.shape[1]
    mine = pl.ds(pl.multiple_of(place.me * length, length), length)

    pieces = [
        (start, min(wide, start + width), number)
        for number, start in enumerate(range(0, wide, width), 1)
    ]
    value_refs = [
        partial.at[number * model_width : (number + 1) * model_width, : end - start]
        for start, end, number in pieces
    ]
    query_ref = partial.at[:model_width, :narrow]
    key_ref = partial.at[:model_width, narrow : 2 * narrow]
    hidden = first_ref.shape[1]
    gated_hidden = hidden_parts.at[:, :hidden]
    pre_grads = hidden_parts.at[:, hidden:]
    main_columns, side_columns = 2 * hidden, model_width - 2 * hidden
    last_rows = len(pieces) * model_width
    output_parts = [
        (0, wide, slice(0, main_columns), hidden_parts.at[:wide, :])
    ]
    for number, start in enumerate(range(0, wide, model_width), 1):
        end = min(wide, start + model_width)
        place_at = slice(number * side_columns, (number + 1) * side_columns)
        ref = partial.at[last_rows : last_rows + end - start, place_at]
        output_parts.append((start, end, slice(main_columns, None), ref))
    loads = [
        pltpu.make_async_copy(src, dst, weight_sems.at[number])
        for number, (src, dst) in enumerate(
            [
                (query_in, query_ref),
                (key_in, key_ref),
                *(
                    (value_in.at[:, start:end], ref)
                    for (start, end, _), ref in zip(pieces, value_refs)
                ),
                *(
                    (output_in.at[start:end, columns], ref)
                    for start, end, columns, ref in output_parts
                ),
            ]
        )
    ]
    values = {}
    lane = lax.broadcasted_iota(jnp.int32, (length, gates_out.shape[1]), 1).astype(jnp.float32)

    def named(columns):
        ids = values["ids"]
        mask = jnp.zeros(lane.shape, jnp.float32)
        for at in columns:
            mask = jnp.where(lane == ids[:, at : at + 1], 1.0, mask)
        return mask

    ffn_top = ffn_ids_ref.shape[0]

    def a1():
        join_routers(routers, value_router_ref, output_router_ref)
        top = value_ids_ref.shape[1]
        all_ids[...] = jnp.zeros_like(all_ids)
        for head in range(HEADS):
            at = head * top
            all_ids[at : at + top, :] = value_ids_ref[head].astype(jnp.float32) + float(head * ATT_EXP)
            all_ids[16 + at : 16 + at + top, :] = output_ids_ref[head].astype(jnp.float32) + float(
                OUTPUT_LANE + head * ATT_EXP
            )
        all_ids[32 : 32 + ffn_top, :] = ffn_ids_ref[...].astype(jnp.float32)
        values["ids"] = all_ids[...].T
        stream_low = tokens_ref[...]
        stream = stream_low.astype(jnp.float32)
        unit, _ = norm_parts(stream)
        normed = (unit * gain_attention_ref[...]).astype(jnp.bfloat16)
        normed_out[...] = normed
        sig = jax.nn.sigmoid(mm_nt(normed, routers[...]))
        gates = named([*range(HEADS * top), *range(16, 16 + HEADS * top)]) * sig
        gates_out[...] = gates
        slopes_out[...] = gates * (1.0 - sig)
        loads[0].wait()
        queries_out[...] = mm(normed, query_ref[...]).astype(jnp.bfloat16)
        loads[1].wait()
        keys_out[...] = mm(normed, key_ref[...]).astype(jnp.bfloat16)
        for (start, end, _), ref, load in zip(pieces, value_refs, loads[2:]):
            load.wait()
            projected_out[:, start:end] = mm(stream_low, ref[...])
        for head in range(HEADS):
            total = jnp.zeros((length, HEAD), jnp.float32)
            for e in range(ATT_EXP):
                at = head * ATT_EXP + e
                total = total + gates[:, at : at + 1] * projected_out[:, at * HEAD : (at + 1) * HEAD]
            values_out[:, head * HEAD : (head + 1) * HEAD] = total.astype(jnp.bfloat16)
        documents = jnp.broadcast_to(segments_ref[...].astype(jnp.float32), (length, length))
        row = lax.broadcasted_iota(jnp.int32, (length, length), 0)
        column = lax.broadcasted_iota(jnp.int32, (length, length), 1)
        allowed = (documents == documents.T) & (row >= column)
        for head in range(HEADS):
            columns = slice(head * HEAD, (head + 1) * HEAD)
            scores = mm_nt(queries_out[:, columns], keys_out[:, columns]) * (1.0 / math.sqrt(HEAD))
            scores = jnp.where(allowed, scores, NEG_FILL)
            exponent = jnp.exp(scores - jnp.max(scores, axis=-1, keepdims=True))
            probability = exponent / jnp.sum(exponent, axis=-1, keepdims=True)
            probability_out[head] = probability
            mixed = mm(probability.astype(jnp.bfloat16), values_out[:, columns])
            mixed_out[:, columns] = mixed
            for e in range(ATT_EXP):
                at = head * ATT_EXP + e
                gate = gates[:, OUTPUT_LANE + at : OUTPUT_LANE + at + 1]
                gated_out[:, at * HEAD : (at + 1) * HEAD] = (gate * mixed).astype(jnp.bfloat16)
    def a2():
        stream = tokens_ref[...].astype(jnp.float32)
        side = stream[:, main_columns:]
        for (start, end, columns, ref), load in zip(output_parts, loads[2 + len(pieces) :]):
            load.wait()
            if start == 0 and end == wide:
                after_out[:, columns] = stream[:, columns] + mm(gated_out[...], ref[...])
            else:
                side = side + mm(gated_out[:, start:end], ref[...])
        after_out[:, main_columns:] = side
        after = after_out[...]
        gathered[mine, :model_width] = after.astype(jnp.bfloat16)
        unit, _ = norm_parts(after)
        normed_ffn = (unit * gain_feedforward_ref[...]).astype(jnp.bfloat16)
        normed_ffn_out[...] = normed_ffn
        expert_sig = jax.nn.sigmoid(mm_nt(normed_ffn, expert_router_ref[...]))
        expert_gates = named(range(32, 32 + ffn_top))[:, :expert_count] * expert_sig
        gathered[mine, model_width:] = jnp.zeros((length, gate_width), jnp.bfloat16)
        gathered[mine, model_width : model_width + expert_count] = expert_gates.astype(jnp.bfloat16)
        expert_slope_out[...] = jnp.zeros((length, gate_width), jnp.float32)
        expert_slope_out[:, :expert_count] = expert_gates * (1.0 - expert_sig)
    def prep():
        for e in range(local_count):
            columns = slice(e * hidden_width, (e + 1) * hidden_width)
            first_ref[:, columns] = first_in[e]
            first_t_ref[columns, :] = first_in[e].astype(jnp.float32).T.astype(jnp.bfloat16)
            second_t_ref[:, columns] = second_ref[columns, :].astype(jnp.float32).T.astype(jnp.bfloat16)
    computes = {"a1": a1, "a2": a2, "prep": prep}
    pick_row = lax.broadcasted_iota(jnp.int32, (gate_width, first_ref.shape[1]), 0)
    pick_column = lax.broadcasted_iota(jnp.int32, (gate_width, first_ref.shape[1]), 1)
    pick_gates = jnp.where(
        pick_row == place.me * local_count + pick_column // hidden_width, 1.0, 0.0
    ).astype(jnp.bfloat16)
    def result_copy(slot, chip):
        return pltpu.make_async_copy(
            result_stage.at[slot],
            result_out.at[pl.ds(pl.multiple_of(chip * pair, pair), pair)],
            result_sems.at[slot],
        )

    def compute(step, place, reduce, q, j):
        chip = place.chip(q, j)
        rows = pl.ds(pl.multiple_of(chip * pair, pair), pair)
        hidden_pre = mm(gathered[rows, :model_width], first_ref[...])
        back = mm(upstream[rows, :], second_t_ref[...])
        gates = mm(gathered[rows, model_width:], pick_gates)
        square = hidden_pre * hidden_pre
        bent = jnp.tanh(GELU_C * hidden_pre * (1.0 + GELU_K * square))
        grow = 0.5 * (1.0 + bent)
        slope = grow + 0.5 * hidden_pre * (1.0 - bent * bent) * (
            GELU_C * (1.0 + 3.0 * GELU_K * square)
        )
        hidden = (hidden_pre * grow).astype(jnp.bfloat16).astype(jnp.float32)
        gated = (gates * hidden).astype(jnp.bfloat16)
        pre_grad = (gates * back * slope).astype(jnp.bfloat16)
        gated_hidden[rows, :] = gated
        pre_grads[rows, :] = pre_grad
        k = 4 * q + j
        to = pl.ds(pl.multiple_of(k * pair, pair), pair)
        partial[to, :model_width] = mm(pre_grad, first_t_ref[...]).astype(jnp.bfloat16)
        product = hidden * back
        column = lax.broadcasted_iota(jnp.int32, (pair, gate_width), 1) - place.me * local_count
        gate_grad = jnp.zeros((pair, gate_width), jnp.float32)
        for e in range(local_count):
            own_sum = jnp.sum(
                product[:, e * hidden_width : (e + 1) * hidden_width], axis=1, keepdims=True
            )
            gate_grad = jnp.where(column == e, own_sum, gate_grad)
        partial[to, model_width:] = gate_grad.astype(jnp.bfloat16)
        reduce.copy("core", k).start()
        slot = step % 2

        @pl.when(step >= 2)
        def _():
            result_copy(slot, chip).wait()

        result_stage[slot] = mm(gated, second_ref[...]).astype(jnp.bfloat16)
        result_copy(slot, chip).start()

    piece = gathered.shape[0] // 8

    def weight_piece(number):
        rows = pl.ds(pl.multiple_of(number * piece, piece), piece)
        second = mm_tn(gated_hidden[rows, :], upstream[rows, :])
        first = mm_tn(pre_grads[rows, :], gathered[rows, :model_width])

        @pl.when(number == 0)
        def _():
            second_out[...] = second
            first_out[...] = first

        @pl.when(number > 0)
        def _():
            second_out[...] += second
            first_out[...] += first

    def run(middle):
        known = place.fixed(middle)

        def share(k, core):
            return partial.at[pl.ds(pl.multiple_of(k * pair + core * length, length), length)]

        items = {
            "U": Gather(known, upstream, length, upstream_sems),
            "X": Gather(known, gathered, length, gather_sems),
            "R": Reduce(
                known,
                lambda k: share(k, known.core),
                lambda k: share(k, 1 - known.core),
                boxes,
                reduce_sems,
            ),
        }

        def put(at, total):
            rows_out[at, :] = total

        def act(events):
            for name, method, *arguments in events:
                if name == "C":
                    computes[method]()
                elif method == "last":
                    items[name].last(put)
                else:
                    getattr(items[name], method)(*arguments)

        stops, pieces_at, waiting = [], [], []
        for event in LAYER_ORDER[middle]:
            if event[0] != "S":
                waiting.append(event)
                continue
            (stops if event[1] == "go" else pieces_at).append((event[2:], waiting))
            waiting = []
        act(stops[0][1])

        def walk(step, carry):
            for number, (_, events) in enumerate(stops):
                if number and events:
                    pl.when(step == number)(functools.partial(act, events))
            q = choose(step, [stop[0] for stop, _ in stops])
            j = choose(step, [stop[1] for stop, _ in stops])
            items["X"].whole(q, j)
            items["U"].whole(q, j)
            compute(step, known, items["R"], q, j)
            return carry

        lax.fori_loop(0, len(stops), walk, 0)

        def give(step, carry):
            for number, (_, events) in enumerate(pieces_at):
                if events:
                    pl.when(step == number)(functools.partial(act, events))
            weight_piece(step)
            return carry

        lax.fori_loop(0, len(pieces_at), give, 0)
        act(waiting)
        for item in items.values():
            item.finish()

    for load in loads:
        load.start()
    upstream[mine, :] = cotangent_ref[...]
    enter(place)
    pl.when(place.middle == 0)(lambda: run(0))
    pl.when(place.middle == 1)(lambda: run(1))
    for slot in range(2):
        result_copy(slot, 0).wait()


def call_layer(
    tokens,
    cotangent,
    gains,
    weights,
    routers,
    segments,
    value_ids,
    output_ids,
    ffn_ids,
    expert_first,
    expert_second,
):
    length, model_width = tokens.shape
    local_count, _, hidden_width = expert_first.shape
    hidden = local_count * hidden_width
    expert_count = routers[2].shape[0]
    gate_width = -(-expert_count // 128) * 128
    width = model_width + gate_width
    total = GRID[0] * GRID[1] * length
    wide = weights[3].shape[0]
    narrow = HEADS * HEAD
    low, full = jnp.bfloat16, jnp.float32
    shapes = (
        ((length, width), full),
        ((hidden, model_width), full),
        ((hidden, model_width), full),
        ((length, model_width), full),
        ((length, model_width), low),
        ((length, model_width), low),
        ((length, narrow), low),
        ((length, narrow), low),
        ((length, wide), full),
        ((length, narrow), low),
        ((HEADS, length, length), full),
        ((length, narrow), full),
        ((length, wide), low),
        ((length, 128), full),
        ((length, 128), full),
        ((length, gate_width), full),
        ((total, model_width), low),
    )
    vmem = pl.BlockSpec(memory_space=pltpu.VMEM)
    hbm = pl.BlockSpec(memory_space=pl.ANY)
    sems = pltpu.SemaphoreType.DMA((2, N_SEM))
    return pl.pallas_call(
        functools.partial(layer_kernel, local_count),
        out_shape=tuple(jax.ShapeDtypeStruct(*shape) for shape in shapes),
        in_specs=[vmem] * 13 + [hbm] * 4,
        out_specs=(*([vmem] * (len(shapes) - 1)), hbm),
        scratch_shapes=[
            pltpu.VMEM((128, model_width), low),
            pltpu.VMEM((128, length), full),
            pltpu.VMEM((total, width), low),
            pltpu.VMEM((total, model_width), low),
            pltpu.VMEM((model_width, hidden), low),
            pltpu.VMEM((hidden, model_width), low),
            pltpu.VMEM((model_width, hidden), low),
            pltpu.VMEM((total, 2 * hidden), low),
            pltpu.VMEM((total, width), low),
            pltpu.VMEM((2, 2 * length, model_width), low),
            pltpu.SemaphoreType.DMA((3 + -(-wide // width) + -(-wide // model_width),)),
            sems,
            sems,
            sems,
            pltpu.SemaphoreType.DMA((2,)),
            *reduce_scratch(length, width),
        ],
        compiler_params=pltpu.CompilerParams(
            collective_id=0, has_side_effects=True, vmem_limit_bytes=VMEM_LIMIT
        ),
        name="layer",
    )(
        tokens,
        cotangent,
        *gains,
        *routers,
        segments,
        value_ids.transpose(1, 2, 0),
        output_ids.transpose(1, 2, 0),
        ffn_ids.T,
        expert_first,
        expert_second.reshape(hidden, model_width),
        *weights,
    )


def general_body(
    tokens,
    cotangent,
    gain_attention,
    gain_feedforward,
    query_weight,
    key_weight,
    value_weight,
    output_weight,
    value_router,
    output_router,
    expert_router,
    expert_first,
    expert_second,
    segments,
    value_ids,
    output_ids,
    ffn_ids,
):
    owner_total = lax.axis_size("dp") * lax.axis_size("expert")
    local_count = expert_first.shape[0]
    expert_count = local_count * owner_total
    shared = (
        gain_attention,
        query_weight,
        key_weight,
        value_weight,
        output_weight,
        value_router,
        output_router,
    )
    stream = tokens.astype(jnp.float32)
    upstream = cotangent.astype(jnp.float32)
    after_attention, saved_parts = attention_forward(
        stream, segments[0], value_ids[0], output_ids[0], shared
    )
    normed_low = layer_norm(after_attention, gain_feedforward).astype(jnp.bfloat16)
    logits = jnp.dot(normed_low, expert_router, preferred_element_type=jnp.float32)
    sigmoid_out = jax.nn.sigmoid(logits)
    dense_gates = sigmoid_out * expert_mask(ffn_ids[0], expert_count)
    expert_slope = dense_gates * (1.0 - sigmoid_out)
    result, token_grad, gate_back, first_sum, second_sum = expert_exchange(
        after_attention.astype(jnp.bfloat16),
        cotangent,
        dense_gates.astype(jnp.bfloat16),
        expert_first,
        expert_second,
        max(1, owner_total // 32),
    )
    logit_grad = (gate_back.astype(jnp.float32) * expert_slope).astype(jnp.bfloat16)
    router_sum = jnp.einsum("sa,sb->ab", normed_low, logit_grad, preferred_element_type=jnp.float32)
    normed_grad = jnp.einsum(
        "sb,ab->sa", logit_grad, expert_router, preferred_element_type=jnp.float32
    )
    norm_value, norm_pull = jax.vjp(layer_norm, after_attention, gain_feedforward)
    after_extra, feed_gain_part = norm_pull(normed_grad)
    after_grad = upstream + token_grad.astype(jnp.float32) + after_extra
    stream_grad, attention_parts = attention_backward(after_grad, saved_parts, stream, shared)
    gain_part, query_part, key_part, value_part, output_part, value_router_part, output_router_part = attention_parts
    parts = (
        query_part,
        key_part,
        value_part,
        value_router_part,
        output_router_part,
        router_sum,
        gain_part[:, None],
        feed_gain_part[:, None],
    )
    low = jnp.concatenate([part.astype(jnp.bfloat16) for part in parts], axis=1)
    low = jnp.pad(low, ((0, 0), (0, -low.shape[1] % 256)))
    output_low = output_part.astype(jnp.bfloat16)
    low, output_low = lax.psum((low, output_low), BOTH)
    block_output = (after_attention + result.astype(jnp.float32)).astype(jnp.bfloat16)
    summed, start = [], 0
    for part in parts:
        summed.append(low[:, start : start + part.shape[1]].astype(jnp.float32))
        start += part.shape[1]
    query_sum, key_sum, value_sum, value_router_sum, output_router_sum, router_sum, *gains = summed
    summed = (
        gains[0][:, 0],
        gains[1][:, 0],
        query_sum,
        key_sum,
        value_sum,
        output_low.astype(jnp.float32),
        value_router_sum,
        output_router_sum,
        router_sum,
    )
    return (
        block_output,
        stream_grad,
        *summed,
        first_sum,
        second_sum,
    )


def kernel_body(
    tokens,
    cotangent,
    gain_attention,
    gain_feedforward,
    query_weight,
    key_weight,
    value_weight,
    output_weight,
    value_router,
    output_router,
    expert_router,
    expert_first,
    expert_second,
    segments,
    value_ids,
    output_ids,
    ffn_ids,
):
    gains = (gain_attention[None], gain_feedforward[None])
    weights = (query_weight, key_weight, value_weight, output_weight)
    routers = (value_router.T, output_router.T, expert_router.T)
    rows_sum, first_sum, second_sum, *saved, result = call_layer(
        tokens,
        cotangent,
        gains,
        weights,
        routers,
        segments,
        value_ids[0],
        output_ids[0],
        ffn_ids[0],
        expert_first,
        expert_second,
    )
    block_output, stream_grad, low, output_low = call_backward(
        rows_sum, tokens, cotangent, gains, routers, saved, weights, result
    )
    (
        query_sum,
        key_sum,
        value_sum,
        output_sum,
        value_router_sum,
        output_router_sum,
        expert_router_sum,
        gain_attention_sum,
        gain_feedforward_sum,
        first_sum,
        second_sum,
        block_output,
        stream_grad,
    ) = call_widen(
        low,
        output_low,
        first_sum,
        second_sum,
        block_output,
        stream_grad,
        query_weight.shape[1],
        expert_router.shape[1],
        expert_first.shape[0],
    )
    return (
        block_output,
        stream_grad,
        gain_attention_sum[0],
        gain_feedforward_sum[0],
        query_sum,
        key_sum,
        value_sum,
        output_sum,
        value_router_sum.T,
        output_router_sum.T,
        expert_router_sum.T,
        first_sum,
        second_sum,
    )


def body(*args):
    if (lax.axis_size("dp"), lax.axis_size("expert")) == GRID:
        return kernel_body(*args)
    return general_body(*args)


def solution(mesh):
    placed = (
        P(("dp", "expert"), None),
        P(("dp", "expert"), None),
        P(),
        P(),
        P(),
        P(),
        P(),
        P(),
        P(),
        P(),
        P(),
        P(("dp", "expert"), None, None),
        P(("dp", "expert"), None, None),
        P(("dp", "expert"), None),
        P(None, ("dp", "expert"), None, None),
        P(None, ("dp", "expert"), None, None),
        P(None, ("dp", "expert"), None),
    )
    return jax.shard_map(
        body,
        mesh=mesh,
        in_specs=placed,
        out_specs=(
            P(("dp", "expert"), None),
            P(("dp", "expert"), None),
            P(),
            P(),
            P(),
            P(),
            P(),
            P(),
            P(),
            P(),
            P(),
            P(("dp", "expert"), None, None),
            P(("dp", "expert"), None, None),
        ),
        check_vma=False,
    )
```

```python
import functools
import math

import jax
import jax.numpy as jnp
from jax import lax
from jax.experimental import pallas as pl
from jax.experimental.pallas import tpu as pltpu
from jax.sharding import PartitionSpec as P

HEADS = 4
HEAD = 128
ATT_EXP = 5


NEG_FILL = -1000000000.0


def layer_norm(stream, norm_gain):
    average = jnp.mean(stream, axis=-1, keepdims=True)
    centred = stream - average
    variance = jnp.mean(centred * centred, axis=-1, keepdims=True)
    return centred * lax.rsqrt(variance + 1e-05) * norm_gain


def expert_mask(picked_ids, expert_count):
    matches = picked_ids[..., None] == jnp.arange(expert_count, dtype=jnp.int32)
    return jnp.sum(matches.astype(jnp.float32), axis=-2)


def attention_forward(stream, document_ids, value_picks, output_picks, shared):
    (
        gain_attention,
        query_weight,
        key_weight,
        value_weight,
        output_weight,
        value_router,
        output_router,
    ) = shared
    length = stream.shape[0]
    normed_low = layer_norm(stream, gain_attention).astype(jnp.bfloat16)
    queries = (
        jnp.dot(normed_low, query_weight, preferred_element_type=jnp.float32)
        .astype(jnp.bfloat16)
        .reshape(length, HEADS, HEAD)
    )
    key_rows = (
        jnp.dot(normed_low, key_weight, preferred_element_type=jnp.float32)
        .astype(jnp.bfloat16)
        .reshape(length, HEADS, HEAD)
    )
    value_sig = jax.nn.sigmoid(
        jnp.dot(normed_low, value_router, preferred_element_type=jnp.float32)
    ).reshape(length, HEADS, ATT_EXP)
    output_sig = jax.nn.sigmoid(
        jnp.dot(normed_low, output_router, preferred_element_type=jnp.float32)
    ).reshape(length, HEADS, ATT_EXP)
    value_mask = expert_mask(value_picks, ATT_EXP)
    output_mask = expert_mask(output_picks, ATT_EXP)
    value_gates = value_mask * value_sig
    output_gates = output_mask * output_sig
    stream_low = stream.astype(jnp.bfloat16)
    projected = jnp.dot(stream_low, value_weight, preferred_element_type=jnp.float32).reshape(
        length, HEADS, ATT_EXP, HEAD
    )
    values = jnp.sum(value_gates[..., None] * projected, axis=2).astype(jnp.bfloat16)
    scores = jnp.einsum("qhd,khd->hqk", queries, key_rows, preferred_element_type=jnp.float32) * (
        1.0 / math.sqrt(HEAD)
    )
    positions = jnp.arange(length, dtype=jnp.int32)
    allowed = (document_ids[:, None] == document_ids[None, :]) & (
        positions[:, None] >= positions[None, :]
    )
    scores = jnp.where(allowed[None], scores, NEG_FILL)
    row_max = jnp.max(scores, axis=-1, keepdims=True)
    exponent = jnp.exp(scores - row_max)
    row_total = jnp.sum(exponent, axis=-1, keepdims=True)
    probability = exponent / row_total
    weights_low = probability.astype(jnp.bfloat16)
    mixed = jnp.einsum("hqk,khd->qhd", weights_low, values, preferred_element_type=jnp.float32)
    gated_rows = (
        (output_gates[..., None] * mixed[:, :, None, :])
        .reshape(length, HEADS * ATT_EXP * HEAD)
        .astype(jnp.bfloat16)
    )
    after_attention = stream + jnp.dot(
        gated_rows, output_weight, preferred_element_type=jnp.float32
    )
    saved_parts = (
        normed_low,
        queries,
        key_rows,
        value_gates * (1.0 - value_sig),
        output_gates * (1.0 - output_sig),
        value_gates,
        output_gates,
        stream_low,
        projected,
        values,
        probability,
        weights_low,
        mixed,
        gated_rows,
    )
    return (after_attention, saved_parts)


def attention_backward(after_grad, saved_parts, stream, shared):
    (
        gain_attention,
        query_weight,
        key_weight,
        value_weight,
        output_weight,
        value_router,
        output_router,
    ) = shared
    (
        normed_low,
        queries,
        key_rows,
        value_slope,
        output_slope,
        value_gates,
        output_gates,
        stream_low,
        projected,
        values,
        probability,
        weights_low,
        mixed,
        gated_rows,
    ) = saved_parts
    length = after_grad.shape[0]
    scale = 1.0 / math.sqrt(HEAD)
    after_low = after_grad.astype(jnp.bfloat16)
    output_part = jnp.einsum("sa,sb->ab", gated_rows, after_low, preferred_element_type=jnp.float32)
    gated_grad = jnp.einsum(
        "sb,ab->sa", after_low, output_weight, preferred_element_type=jnp.float32
    ).astype(jnp.bfloat16)
    gated_grad = gated_grad.reshape(length, HEADS, ATT_EXP, HEAD).astype(jnp.float32)
    mixed_grad = jnp.sum(output_gates[..., None] * gated_grad, axis=2).astype(jnp.bfloat16)
    output_gate_grad = jnp.sum(gated_grad * mixed[:, :, None, :], axis=3)
    prob_grad = jnp.einsum("qhd,khd->hqk", mixed_grad, values, preferred_element_type=jnp.float32)
    values_grad = jnp.einsum(
        "hqk,qhd->khd", weights_low, mixed_grad, preferred_element_type=jnp.float32
    ).astype(jnp.bfloat16)
    values_grad = values_grad.astype(jnp.float32)
    score_grad = (
        probability * (prob_grad - jnp.sum(probability * prob_grad, axis=-1, keepdims=True))
    ).astype(jnp.bfloat16)
    query_grad = (
        (
            jnp.einsum("hqk,khd->qhd", score_grad, key_rows, preferred_element_type=jnp.float32)
            * scale
        )
        .astype(jnp.bfloat16)
        .reshape(length, HEADS * HEAD)
    )
    key_grad = (
        (
            jnp.einsum("hqk,qhd->khd", score_grad, queries, preferred_element_type=jnp.float32)
            * scale
        )
        .astype(jnp.bfloat16)
        .reshape(length, HEADS * HEAD)
    )
    projected_grad = (
        (value_gates[..., None] * values_grad[:, :, None, :])
        .astype(jnp.bfloat16)
        .reshape(length, HEADS * ATT_EXP * HEAD)
    )
    value_gate_grad = jnp.sum(values_grad[:, :, None, :] * projected, axis=3)
    value_logit_grad = (
        (value_gate_grad * value_slope)
        .astype(jnp.bfloat16)
        .reshape(length, HEADS * ATT_EXP)
    )
    output_logit_grad = (
        (output_gate_grad * output_slope)
        .astype(jnp.bfloat16)
        .reshape(length, HEADS * ATT_EXP)
    )
    value_part = jnp.einsum(
        "sa,sb->ab", stream_low, projected_grad, preferred_element_type=jnp.float32
    )
    query_part = jnp.einsum("sa,sb->ab", normed_low, query_grad, preferred_element_type=jnp.float32)
    key_part = jnp.einsum("sa,sb->ab", normed_low, key_grad, preferred_element_type=jnp.float32)
    value_router_part = jnp.einsum(
        "sa,sb->ab", normed_low, value_logit_grad, preferred_element_type=jnp.float32
    )
    output_router_part = jnp.einsum(
        "sa,sb->ab", normed_low, output_logit_grad, preferred_element_type=jnp.float32
    )
    normed_grad = jnp.einsum(
        "sb,ab->sa", query_grad, query_weight, preferred_element_type=jnp.float32
    )
    normed_grad = normed_grad + jnp.einsum(
        "sb,ab->sa", key_grad, key_weight, preferred_element_type=jnp.float32
    )
    normed_grad = normed_grad + jnp.einsum(
        "sb,ab->sa", value_logit_grad, value_router, preferred_element_type=jnp.float32
    )
    normed_grad = normed_grad + jnp.einsum(
        "sb,ab->sa", output_logit_grad, output_router, preferred_element_type=jnp.float32
    )
    norm_value, norm_pull = jax.vjp(layer_norm, stream, gain_attention)
    stream_extra, gain_part = norm_pull(normed_grad)
    value_input = jnp.einsum(
        "sb,ab->sa", projected_grad, value_weight, preferred_element_type=jnp.float32
    )
    stream_grad = after_grad + stream_extra + value_input
    return (
        stream_grad,
        (
            gain_part,
            query_part,
            key_part,
            value_part,
            output_part,
            value_router_part,
            output_router_part,
        ),
    )


def expert_pass(rows, upstream_rows, gates, expert_first, expert_second):
    local_count, model_width, hidden_width = expert_first.shape
    wide = local_count * hidden_width
    first = expert_first.transpose(1, 0, 2).reshape(model_width, wide)
    second = expert_second.reshape(wide, model_width)
    gates_wide = jnp.repeat(gates.astype(jnp.float32), hidden_width, axis=1)
    hidden_pre = jnp.dot(rows, first, preferred_element_type=jnp.float32)
    hidden, gelu_pull = jax.vjp(jax.nn.gelu, hidden_pre)
    hidden = hidden.astype(jnp.bfloat16).astype(jnp.float32)
    gated_hidden = (gates_wide * hidden).astype(jnp.bfloat16)
    back = jnp.einsum("sd,fd->sf", upstream_rows, second, preferred_element_type=jnp.float32)
    gate_grad = jnp.sum((back * hidden).reshape(-1, local_count, hidden_width), axis=2)
    pre_grad = gelu_pull(gates_wide * back)[0].astype(jnp.bfloat16)
    result = jnp.dot(gated_hidden, second, preferred_element_type=jnp.float32)
    row_grad = jnp.einsum("sf,df->sd", pre_grad, first, preferred_element_type=jnp.float32)
    second_sum = jnp.einsum(
        "sf,sd->fd", gated_hidden, upstream_rows, preferred_element_type=jnp.float32
    )
    first_sum = jnp.einsum("sd,sf->df", rows, pre_grad, preferred_element_type=jnp.float32)
    first_sum = first_sum.reshape(model_width, local_count, hidden_width).transpose(1, 0, 2)
    return (
        result.astype(jnp.bfloat16),
        row_grad.astype(jnp.bfloat16),
        gate_grad.astype(jnp.bfloat16),
        first_sum,
        second_sum.reshape(expert_second.shape),
    )


BOTH = ("dp", "expert")


def expert_piece(after_low, upstream_low, dense_gates, expert_first, expert_second):
    local_count = expert_first.shape[0]
    me = lax.axis_index("dp") * lax.axis_size("expert") + lax.axis_index("expert")
    upstream_rows = lax.all_gather(upstream_low, BOTH, axis=0, tiled=True)
    rows = lax.all_gather(after_low, BOTH, axis=0, tiled=True)
    gates = lax.all_gather(dense_gates, BOTH, axis=0, tiled=True)
    gates = lax.dynamic_slice_in_dim(gates, me * local_count, local_count, axis=1)
    result, row_grad, gate_grad, first_sum, second_sum = expert_pass(
        rows, upstream_rows, gates, expert_first, expert_second
    )
    gate_back = lax.all_to_all(gate_grad, BOTH, split_axis=0, concat_axis=1, tiled=True)
    token_grad = lax.psum_scatter(row_grad, BOTH, scatter_dimension=0, tiled=True)
    result = lax.psum_scatter(result, BOTH, scatter_dimension=0, tiled=True)
    return (result, token_grad, gate_back), (first_sum, second_sum)


def expert_exchange(after_low, upstream_low, dense_gates, expert_first, expert_second, pieces):
    if pieces == 1:
        back, sums = expert_piece(
            after_low, upstream_low, dense_gates, expert_first, expert_second
        )
        return (*back, *sums)

    def step(totals, piece):
        back, sums = expert_piece(*piece, expert_first, expert_second)
        return (totals[0] + sums[0], totals[1] + sums[1]), back

    cut = lambda array: array.reshape(pieces, -1, array.shape[1])
    start = (
        jnp.zeros(expert_first.shape, jnp.float32),
        jnp.zeros(expert_second.shape, jnp.float32),
    )
    sums, back = lax.scan(step, start, (cut(after_low), cut(upstream_low), cut(dense_gates)))
    return (*(part.reshape(-1, part.shape[2]) for part in back), *sums)


MESH = pl.DeviceIdType.MESH
GRID = (4, 8)
N_SEM = 47
VMEM_LIMIT = 63 * 2**20


class Place:
    def __init__(self):
        dp, expert = lax.axis_index("dp"), lax.axis_index("expert")
        self.y, self.x = dp // 2, dp % 2
        self.z, self.core = expert // 2, expert % 2
        self.dp = dp
        self.me = dp * GRID[1] + expert
        self.x_peer = (2 * self.y + 1 - self.x, expert)
        self.y_peer = (2 * (1 - self.y) + self.x, expert)
        self.core_peer = (dp, 2 * self.z + 1 - self.core)
        self.middle = (self.z + self.z // 2) % 2
        self.main = 1 + self.z % 2
        self.minor = 3 * (self.z // 2)

    def along_z(self, z):
        return (self.dp, 2 * z + self.core)

    def z_at(self, j):
        near = j + self.middle * (1 - 2 * j) * (1 - j // 2)
        return near + self.z // 2 * (3 - 2 * near)

    def chip(self, q, j):
        return ((self.y + q // 2) % 2 * 2 + (self.x + q % 2) % 2) * 4 + self.z_at(j)

    def fixed(self, middle):
        known = Place.__new__(Place)
        known.__dict__.update(self.__dict__)
        known.middle = middle
        return known

    def if_middle(self, action):
        if not isinstance(self.middle, int):
            pl.when(self.middle == 1)(action)
        elif self.middle:
            action()


def enter(place):
    barrier = pltpu.get_barrier_semaphore()

    def signal(peer):
        pl.semaphore_signal(barrier, inc=1, device_id=peer, device_id_type=MESH)

    for peer in (place.x_peer, place.y_peer, place.core_peer, place.along_z(place.main)):
        signal(peer)
    place.if_middle(lambda: signal(place.along_z(place.minor)))
    pl.when(place.middle == 0)(lambda: pl.semaphore_wait(barrier, 4))
    place.if_middle(lambda: pl.semaphore_wait(barrier, 5))


def remote(src, dst, send, recv, peer):
    return pltpu.make_async_remote_copy(
        src_ref=src,
        dst_ref=dst,
        send_sem=send,
        recv_sem=recv,
        device_id=peer,
        device_id_type=MESH,
    )


CUTS = {
    "U": (2, 3),
    "X": (3, 3),
    "R": (3, 3),
    "Y": (2, 3),
    "O": (3, 2),
    "L": (10, 10),
    "GO": (3, 2),
    "GL": (10, 10),
}


def cut_columns(name, width):
    c_tiles, d_tiles = CUTS[name]
    return d_tiles * 128, width // 256 * 128, width - c_tiles * 128


class Gather:
    def __init__(self, name, place, buf, rows, sems, own=None):
        self.place, self.buf, self.rows, self.own = place, buf, rows, own
        self.width = buf.shape[1]
        self.d_end, self.split, self.c_start = cut_columns(name, self.width)
        self.send, self.recv = sems.at[0], sems.at[1]

    def block(self, q, j, columns=slice(None)):
        start = (2 * self.place.chip(q, j) + self.place.core) * self.rows
        return self.buf.at[pl.ds(pl.multiple_of(start, self.rows), self.rows), columns]

    def copy(self, kind, j, q=0):
        place = self.place
        if kind == "x0":
            ref, number, peer = self.block(0, 0), 15, place.x_peer
        elif kind == "y0":
            ref, number, peer = self.block(0, 0), 19, place.y_peer
        elif kind == "x":
            ref, number, peer = self.block(0, j, slice(0, self.c_start)), 15 + j, place.x_peer
        elif kind == "y":
            ref, number, peer = self.block(0, j, slice(self.d_end, None)), 19 + j, place.y_peer
        elif kind == "a":
            ref, number, peer = self.block(1, j, slice(self.split, None)), 23 + j, place.y_peer
        elif kind == "b":
            ref, number, peer = self.block(2, j, slice(0, self.split)), 27 + j, place.x_peer
        else:
            ref, number, peer = self.block(q, j), 31 + 4 * q + j, place.core_peer
        if kind in ("a", "b"):
            return remote(ref, ref, self.send.at[number], self.recv.at[number], peer)
        return remote(self.source(ref, q, j), ref, self.send.at[number], self.recv.at[number], peer)

    def source(self, ref, q, j):
        mine = self.own is not None and isinstance(j, int) and q == 0 and j == 0
        return self.own if mine else ref

    def z_copy(self, part, j, number, z, receiver_j):
        columns = (slice(None), slice(self.c_start, None), slice(0, self.d_end))[part]
        ref = self.block(part, j, columns)
        return remote(
            self.source(ref, part, j),
            ref,
            self.send.at[5 * part + number],
            self.recv.at[3 * part + receiver_j - 1],
            self.place.along_z(z),
        )

    def z_own(self, part):
        place = self.place
        self.z_copy(part, 0, 0, place.main, 1 + place.middle).start()
        place.if_middle(lambda: self.z_copy(part, 0, 1, place.minor, 1).start())

    def z_pass(self, part, j):
        place = self.place
        first = 1 - (j + 2) // 4
        z = place.minor + first * (place.main - place.minor)
        return self.z_copy(part, j, 1 + j, z, j + 2 * first)

    def z_arrive(self, part, j):
        self.z_copy(part, j, 0, self.place.main, j).wait_recv()
        self.place.if_middle(lambda: self.z_pass(part, j).start())

    def begin(self):
        self.z_own(0)
        self.copy("x0", 0).start()
        self.copy("y0", 0).start()
        self.copy("core", 0, 0).start()

    def line(self, j):
        self.z_arrive(0, j)
        self.copy("x", j).start()
        self.copy("y", j).start()
        self.copy("core", j, 0).start()

    def side_x(self, j):
        self.copy("x" if j else "x0", j).wait_recv()
        self.copy("a", j).start()
        self.copy("core", j, 1).start()

    def side_y(self, j):
        self.copy("y" if j else "y0", j).wait_recv()
        self.copy("b", j).start()
        self.copy("core", j, 2).start()

    def own_c(self):
        self.z_own(1)

    def own_d(self):
        self.z_own(2)

    def pass_c(self, j):
        self.z_arrive(1, j)

    def pass_d(self, j):
        self.z_arrive(2, j)

    def corner(self, j):
        self.copy("a", j).wait_recv()
        self.copy("b", j).wait_recv()
        self.copy("core", j, 3).start()

    def whole(self, q, j):
        self.copy("core", j, q).wait_recv()

    def wait_all(self):
        def step(k, carry):
            self.whole(k // 4, k % 4)
            return carry

        lax.fori_loop(0, 16, step, 0)

    def finish(self):
        place = self.place
        for part in range(3):
            self.z_copy(part, 0, 0, place.main, 1).wait_send()

        def middle():
            for part in range(3):
                self.z_copy(part, 0, 1, place.minor, 1).wait_send()

                def passed(j, carry):
                    self.z_pass(part, j).wait_send()
                    return carry

                lax.fori_loop(1, 4, passed, 0)

        place.if_middle(middle)
        self.copy("x0", 0).wait_send()
        self.copy("y0", 0).wait_send()

        def line(j, carry):
            self.copy("x", j).wait_send()
            self.copy("y", j).wait_send()
            return carry

        lax.fori_loop(1, 4, line, 0)

        def step(j, carry):
            self.copy("a", j).wait_send()
            self.copy("b", j).wait_send()
            for q in range(4):
                self.copy("core", j, q).wait_send()
            return carry

        lax.fori_loop(0, 4, step, 0)


class Reduce:
    def __init__(self, name, place, own, other, boxes, sems, held=None):
        self.place, self.other = place, other
        self.other_in, self.a_in, self.b_in, self.x_in, self.y_in = boxes[:5]
        self.own = own or (lambda k: self.other_in.at[k])
        self.extra = held or (lambda k: self.other_in.at[k])
        self.z_in = boxes[5:]
        self.rows, self.width = self.other_in.shape[1:]
        self.d_end, self.split, self.c_start = cut_columns(name, self.width)
        self.send, self.recv = sems.at[0], sems.at[1]

    def copy(self, kind, k):
        place = self.place
        j = k % 4
        if kind == "core":
            src, dst, number, peer = self.other(k), self.other_in.at[k], k, place.core_peer
        elif kind == "a":
            src = self.own(k).at[:, self.split :]
            dst, number, peer = self.a_in.at[j], 16 + j, place.y_peer
        elif kind == "b":
            src = self.own(k).at[:, : self.split]
            dst, number, peer = self.b_in.at[j], 20 + j, place.x_peer
        elif kind == "x0":
            src, dst, number, peer = self.own(k), self.x_in.at[0], 24, place.x_peer
        elif kind == "y0":
            src, dst, number, peer = self.own(k), self.y_in.at[0], 28, place.y_peer
        elif kind == "x":
            src = self.own(k).at[:, : self.c_start]
            dst, number, peer = self.x_in.at[j, :, : self.c_start], 24 + j, place.x_peer
        else:
            src = self.own(k).at[:, self.d_end :]
            dst, number, peer = self.y_in.at[j, :, self.d_end :], 28 + j, place.y_peer
        return remote(src, dst, self.send.at[number], self.recv.at[number], peer)

    def z_columns(self, part):
        return (slice(None), slice(self.c_start, None), slice(0, self.d_end))[part]

    def z_copy(self, part, j):
        place = self.place
        first = 1 - (j + 2) // 4
        box = place.middle * (j // 3) + (1 - place.middle) * (j + 1)
        z = place.main + place.middle * first * (place.minor - place.main)
        return remote(
            self.own(4 * part + j).at[:, self.z_columns(part)],
            self.z_in[part].at[box],
            self.send.at[32 + 5 * part + j],
            self.recv.at[32 + 5 * part + box],
            place.along_z(z),
        )

    def z_wait(self, part, box):
        self.copy_box(part, box).wait_recv()

    def copy_box(self, part, box):
        ref = self.z_in[part].at[box]
        return remote(
            ref,
            ref,
            self.send.at[32 + 5 * part],
            self.recv.at[32 + 5 * part + box],
            self.place.along_z(self.place.main),
        )

    def z_give(self, part, j):
        def middle():
            box = j + (j + 2) // 4
            self.z_wait(part, box)
            self.add(4 * part + j, self.z_columns(part), [lambda at: self.z_in[part][box, at, :]])

        self.place.if_middle(middle)
        self.z_copy(part, j).start()

    def z_last(self, part):
        columns = self.z_columns(part)
        self.z_wait(part, 0)
        self.add(4 * part, columns, [lambda at: self.z_in[part][0, at, :]])

        def middle():
            self.z_wait(part, 2)
            self.add(4 * part, columns, [lambda at: self.z_in[part][2, at, :]])

        self.place.if_middle(middle)

    def add(self, k, columns, terms):
        own = self.own(k)

        def step(number, carry):
            at = pl.ds(pl.multiple_of(number * 16, 16), 16)
            total = own[at, columns].astype(jnp.float32)
            for term in terms:
                total = total + term(at).astype(jnp.float32)
            own[at, columns] = total.astype(own.dtype)
            return carry

        lax.fori_loop(0, self.rows // 16, step, 0)

    def corner(self, j):
        k = 12 + j
        self.copy("core", k).wait_recv()
        self.add(k, slice(None), [lambda at: self.extra(k)[at, :]])
        self.copy("a", k).start()
        self.copy("b", k).start()

    def side_x(self, j):
        k, split = 4 + j, self.split
        self.copy("core", k).wait_recv()
        self.add(k, slice(0, split), [lambda at: self.extra(k)[at, :split]])
        self.copy("a", k).wait_recv()
        self.add(
            k,
            slice(split, None),
            [lambda at: self.extra(k)[at, split:], lambda at: self.a_in[j, at, :]],
        )
        if j:
            self.copy("x", k).start()

    def side_y(self, j):
        k, split = 8 + j, self.split
        self.copy("core", k).wait_recv()
        self.add(k, slice(split, None), [lambda at: self.extra(k)[at, split:]])
        self.copy("b", k).wait_recv()
        self.add(
            k,
            slice(0, split),
            [lambda at: self.extra(k)[at, :split], lambda at: self.b_in[j, at, :]],
        )
        if j:
            self.copy("y", k).start()

    def give_c(self, j):
        if j:
            self.z_give(1, j)
        else:
            self.z_last(1)
            self.copy("x0", 4).start()

    def give_d(self, j):
        if j:
            self.z_give(2, j)
        else:
            self.z_last(2)
            self.copy("y0", 8).start()

    def hand_over(self):
        def step(number, carry):
            self.copy("core", 15 - number).start()
            return carry

        lax.fori_loop(0, 16, step, 0)

    def line(self, j):
        self.copy("core", j).wait_recv()
        self.copy("x", j).wait_recv()
        self.copy("y", j).wait_recv()
        d_end, c_start = self.d_end, self.c_start
        boxes = (self.extra(j), self.x_in.at[j], self.y_in.at[j])
        for columns, used in (
            (slice(0, d_end), boxes[:2]),
            (slice(d_end, c_start), boxes),
            (slice(c_start, None), (boxes[0], boxes[2])),
        ):
            self.add(j, columns, [lambda at, box=box: box[at, columns] for box in used])
        self.z_give(0, j)

    def last(self, put):
        self.copy("core", 0).wait_recv()
        self.copy("x0", 0).wait_recv()
        self.copy("y0", 0).wait_recv()
        self.z_wait(0, 0)
        own = self.own(0)

        def sum_up(middle):
            def step(number, carry):
                at = pl.ds(pl.multiple_of(number * 16, 16), 16)
                total = own[at, :].astype(jnp.float32)
                for box in (self.extra(0), self.x_in.at[0], self.y_in.at[0], self.z_in[0].at[0]):
                    total = total + box[at, :].astype(jnp.float32)
                if middle:
                    total = total + self.z_in[0][2, at, :].astype(jnp.float32)
                put(at, total)
                return carry

            lax.fori_loop(0, own.shape[0] // 16, step, 0)

        if self.place.middle:
            self.z_wait(0, 2)
        sum_up(self.place.middle == 1)

    def finish(self):
        def step(j, carry):
            self.copy("a", 12 + j).wait_send()
            self.copy("b", 12 + j).wait_send()
            for q in range(4):
                self.copy("core", 4 * q + j).wait_send()
            return carry

        lax.fori_loop(0, 4, step, 0)

        def outer(j, carry):
            self.copy("x", 4 + j).wait_send()
            self.copy("y", 8 + j).wait_send()
            for part in range(3):
                self.z_copy(part, j).wait_send()
            return carry

        lax.fori_loop(1, 4, outer, 0)
        self.copy("x0", 4).wait_send()
        self.copy("y0", 8).wait_send()


def reduce_scratch(name, rows, width):
    low = jnp.bfloat16
    d_end, split, c_start = cut_columns(name, width)
    return [
        pltpu.VMEM((16, rows, width), low),
        pltpu.VMEM((4, rows, width - split), low),
        pltpu.VMEM((4, rows, split), low),
        pltpu.VMEM((4, rows, width), low),
        pltpu.VMEM((4, rows, width), low),
        pltpu.VMEM((5, rows, width), low),
        pltpu.VMEM((5, rows, width - c_start), low),
        pltpu.VMEM((5, rows, d_end), low),
    ]


GELU_C = math.sqrt(2.0 / math.pi)
GELU_K = 0.044715


def mm(left, right):
    return jnp.dot(left, right, preferred_element_type=jnp.float32)


def mm_tn(left, right):
    return lax.dot_general(left, right, (((0,), (0,)), ((), ())), preferred_element_type=jnp.float32)


def norm_parts(stream):
    average = jnp.mean(stream, axis=-1, keepdims=True)
    centred = stream - average
    variance = jnp.mean(centred * centred, axis=-1, keepdims=True)
    scale = lax.rsqrt(variance + 1e-05)
    return centred * scale, scale


def norm_pull(normed_grad, unit, scale, gain):
    inner = normed_grad * gain
    mean = jnp.mean(inner, axis=-1, keepdims=True)
    along = jnp.mean(inner * unit, axis=-1, keepdims=True)
    gain_grad = jnp.sum(normed_grad * unit, axis=0, keepdims=True)
    return scale * (inner - mean - unit * along), gain_grad


def mm_nt(left, right):
    return lax.dot_general(left, right, (((1,), (1,)), ((), ())), preferred_element_type=jnp.float32)


OUTPUT_LANE = 32


def join_routers(joined, value_router_ref, output_router_ref):
    count = value_router_ref.shape[0]
    joined[...] = jnp.zeros_like(joined)
    joined[:count, :] = value_router_ref[...]
    joined[OUTPUT_LANE : OUTPUT_LANE + count, :] = output_router_ref[...]


HELD = 6
GAIN_LANE = 64


FETCHED = (
    ("rows", "after", "normed_ffn", "expert_slope", "cotangent"),
    ("gated",),
    (
        "tokens",
        "normed",
        "queries",
        "keys",
        "projected",
        "values",
        "probability",
        "mixed",
        "gates",
        "slopes",
    ),
)
FETCHED_NAMES = tuple(name for group in FETCHED for name in group)


def backward_kernel(
    gain_attention_ref,
    gain_feedforward_ref,
    value_router_ref,
    output_router_ref,
    expert_router_ref,
    query_in,
    key_in,
    value_in,
    output_in,
    result_in,
    block_out,
    stream_out,
    low_out,
    output_low_out,
    query_ref,
    key_ref,
    value_ref,
    output_ref,
    routers,
    expert_router,
    after_grad,
    after_low,
    gated_grad,
    projected_grad,
    both_grad,
    held,
    low_part,
    output_part,
    low_own,
    output_own,
    weight_sems,
    held_sems,
    own_sems,
    fetch_sems,
    *refs,
):
    place = Place()
    count = len(FETCHED_NAMES)
    fetched_in, fetched_refs, refs = refs[:count], refs[count : 2 * count], refs[2 * count :]
    fetched_ref = dict(zip(FETCHED_NAMES, fetched_refs))
    fetches = {
        name: pltpu.make_async_copy(src, dst, fetch_sems.at[number])
        for number, (name, src, dst) in enumerate(zip(FETCHED_NAMES, fetched_in, fetched_refs))
    }

    def fetched_now(group):
        for name in FETCHED[group]:
            fetches[name].wait()

    rows_ref = fetched_ref["rows"]
    after_ref = fetched_ref["after"]
    normed_ffn_ref = fetched_ref["normed_ffn"]
    expert_slope_ref = fetched_ref["expert_slope"]
    cotangent_ref = fetched_ref["cotangent"]
    gated_ref = fetched_ref["gated"]
    tokens_ref = fetched_ref["tokens"]
    normed_ref = fetched_ref["normed"]
    queries_ref = fetched_ref["queries"]
    keys_ref = fetched_ref["keys"]
    projected_ref = fetched_ref["projected"]
    values_ref = fetched_ref["values"]
    probability_ref = fetched_ref["probability"]
    mixed_ref = fetched_ref["mixed"]
    gates_ref = fetched_ref["gates"]
    slopes_ref = fetched_ref["slopes"]
    length, model_width = tokens_ref.shape
    wide = value_ref.shape[1]
    narrow = query_ref.shape[1]
    expert_count = expert_router_ref.shape[0]
    low_rows, output_rows = low_own.shape[0], output_own.shape[0]
    low_type = jnp.bfloat16

    def other_rows(ref, rows, place):
        def get(k):
            start = (2 * place.chip(k // 4, k % 4) + 1 - place.core) * rows
            return ref.at[pl.ds(pl.multiple_of(start, rows), rows)]

        return get

    def own_rows(ref, rows, place):
        def get(k):
            start = (2 * place.chip(k // 4, k % 4) + place.core) * rows
            return ref.at[pl.ds(pl.multiple_of(start, rows), rows)]

        return get

    weights = ((output_in, output_ref), (query_in, query_ref), (key_in, key_ref), (value_in, value_ref))
    loads = [
        pltpu.make_async_copy(src, dst, weight_sems.at[number])
        for number, (src, dst) in enumerate(weights)
    ]
    tile = 256
    small_column = wide + 2 * narrow
    expert_column = small_column + 128
    first_base = {"corner": 12, "side_x": 4, "side_y": 8, "line": 0, "last": 0}
    values = {}

    def c1():
        fetched_now(0)
        join_routers(routers, value_router_ref, output_router_ref)
        expert_router[...] = jnp.zeros_like(expert_router)
        expert_router[:expert_count, :] = expert_router_ref[...]
        logit_grad = (rows_ref[:, model_width:] * expert_slope_ref[...]).astype(low_type)
        unit, scale = norm_parts(after_ref[...])
        through, values["gain_feedforward"] = norm_pull(
            mm(logit_grad, expert_router[...]), unit, scale, gain_feedforward_ref[...]
        )
        after_grad[...] = cotangent_ref[...].astype(jnp.float32) + rows_ref[:, :model_width] + through
        after_low[...] = after_grad[...].astype(low_type)
        low_part[:, expert_column:] = mm_tn(normed_ffn_ref[...], logit_grad).astype(low_type)

    def c2():
        fetched_now(1)
        def output_tile(number, carry):
            at = pl.ds(pl.multiple_of(number * tile, tile), tile)
            output_part[at, :] = mm_tn(gated_ref[:, at], after_low[...]).astype(low_type)
            return carry

        lax.fori_loop(0, wide // tile, output_tile, 0)

    def c3():
        loads[0].wait()

        def gated_tile(number, carry):
            at = pl.ds(pl.multiple_of(number * tile, tile), tile)
            gated_grad[:, at] = mm_nt(after_low[...], output_ref[at, :]).astype(low_type)
            return carry

        lax.fori_loop(0, wide // tile, gated_tile, 0)

    def c4():
        fetched_now(2)
        lane = lax.broadcasted_iota(jnp.int32, (length, 128), 1)
        gate_grads = jnp.zeros((length, 128), jnp.float32)
        inverse = 1.0 / math.sqrt(HEAD)
        for head in range(HEADS):
            columns = slice(head * HEAD, (head + 1) * HEAD)
            mixed = mixed_ref[:, columns]
            mixed_grad = jnp.zeros((length, HEAD), jnp.float32)
            for e in range(ATT_EXP):
                at = head * ATT_EXP + e
                part = gated_grad[:, at * HEAD : (at + 1) * HEAD].astype(jnp.float32)
                lane_at = OUTPUT_LANE + at
                mixed_grad = mixed_grad + gates_ref[:, lane_at : lane_at + 1] * part
                gate_grads = jnp.where(
                    lane == lane_at, jnp.sum(part * mixed, axis=1, keepdims=True), gate_grads
                )
            mixed_grad = mixed_grad.astype(low_type)
            probability = probability_ref[head]
            prob_grad = mm_nt(mixed_grad, values_ref[:, columns])
            inner = jnp.sum(probability * prob_grad, axis=-1, keepdims=True)
            score_grad = (probability * (prob_grad - inner)).astype(low_type)
            both_grad[:, columns] = (mm(score_grad, keys_ref[:, columns]) * inverse).astype(low_type)
            both_grad[:, narrow + head * HEAD : narrow + (head + 1) * HEAD] = (
                mm_tn(score_grad, queries_ref[:, columns]) * inverse
            ).astype(low_type)
            values_grad = mm_tn(probability.astype(low_type), mixed_grad)
            values_grad = values_grad.astype(low_type).astype(jnp.float32)
            for e in range(ATT_EXP):
                at = head * ATT_EXP + e
                wide_at = slice(at * HEAD, (at + 1) * HEAD)
                projected_grad[:, wide_at] = (gates_ref[:, at : at + 1] * values_grad).astype(low_type)
                gate_grad = jnp.sum(values_grad * projected_ref[:, wide_at], axis=1, keepdims=True)
                gate_grads = jnp.where(lane == at, gate_grad, gate_grads)
        values["router"] = (gate_grads * slopes_ref[...]).astype(low_type)

    def c5a():
        def value_tile(number, carry):
            at = pl.ds(pl.multiple_of(number * tile, tile), tile)
            to = pl.ds(pl.multiple_of(2 * narrow + number * tile, tile), tile)
            low_part[:, to] = mm_tn(tokens_ref[...], projected_grad[:, at]).astype(low_type)
            return carry

        lax.fori_loop(0, wide // tile, value_tile, 0)

    def c5b():
        def both_tile(number, carry):
            at = pl.ds(pl.multiple_of(number * tile, tile), tile)
            low_part[:, at] = mm_tn(normed_ref[...], both_grad[:, at]).astype(low_type)
            return carry

        lax.fori_loop(0, 2 * narrow // tile, both_tile, 0)

    def c6():
        loads[1].wait()
        loads[2].wait()
        normed_grad = mm_nt(both_grad[:, :narrow], query_ref[...])
        normed_grad = normed_grad + mm_nt(both_grad[:, narrow:], key_ref[...])
        normed_grad = normed_grad + mm(values["router"], routers[...])
        unit, scale = norm_parts(tokens_ref[...].astype(jnp.float32))
        through, gain_attention_grad = norm_pull(normed_grad, unit, scale, gain_attention_ref[...])
        after_grad[...] += through
        gain_columns = [
            jnp.broadcast_to(grad, (128, model_width)).T
            for grad in (gain_attention_grad, values["gain_feedforward"])
        ]
        small = mm_tn(normed_ref[...], values["router"])
        small_lane = lax.broadcasted_iota(jnp.int32, (model_width, 128), 1)
        small = jnp.where(small_lane == GAIN_LANE, gain_columns[0], small)
        small = jnp.where(small_lane == GAIN_LANE + 1, gain_columns[1], small)
        low_part[:, small_column:expert_column] = small.astype(low_type)

    def c7():
        loads[3].wait()
        through_values = mm_nt(projected_grad[...], value_ref[...])
        stream_out[...] = through_values

    computes = {"c1": c1, "c2": c2, "c3": c3, "c4": c4, "c5a": c5a, "c5b": c5b, "c6": c6, "c7": c7}

    def run(middle):
        known = place.fixed(middle)
        order = BACKWARD_ORDER[middle]
        held_order = [
            first_base[event[1]] + (event[2] if len(event) > 2 else 0)
            for event in order
            if event[0] == "Y" and event[1] in first_base
        ]
        slots = {k: number % HELD for number, k in enumerate(held_order)}

        def held_copy(number):
            k = held_order[number]
            start = (2 * known.chip(k // 4, k % 4) + known.core) * length
            return pltpu.make_async_copy(
                result_in.at[pl.ds(pl.multiple_of(start, length), length)],
                held.at[number % HELD],
                held_sems.at[number % HELD],
            )

        reduces = {
            "Y": Reduce(
                "Y",
                known,
                None,
                other_rows(result_in, length, known),
                refs[0:8],
                refs[8],
                lambda k: held.at[slots[k]],
            ),
            "O": Reduce(
                "O",
                known,
                own_rows(output_part, output_rows, known),
                other_rows(output_part, output_rows, known),
                refs[9:17],
                refs[17],
            ),
            "L": Reduce(
                "L",
                known,
                own_rows(low_part, low_rows, known),
                other_rows(low_part, low_rows, known),
                refs[18:26],
                refs[26],
            ),
        }
        gathers = {
            "GO": Gather("GO", known, output_low_out, output_rows, refs[27], output_own),
            "GL": Gather("GL", known, low_out, low_rows, refs[28], low_own),
        }
        owns = {"O": ("GO", output_own, own_sems.at[0]), "L": ("GL", low_own, own_sems.at[1])}
        own_copies = {
            target: pltpu.make_async_copy(own, gathers[target].block(0, 0), sem)
            for target, own, sem in owns.values()
        }

        def last(name):
            if name == "Y":

                def put(at, total):
                    block_out[at, :] = (after_ref[at, :] + total).astype(low_type)

            else:
                target, own, _ = owns[name]

                def put(at, total):
                    own[at, :] = total.astype(low_type)

            reduces[name].last(put)
            if name != "Y":
                own_copies[target].start()

        for number in range(HELD):
            held_copy(number).start()
        fetched = 0
        for number, (name, method, *arguments) in enumerate(order):
            if number == len(order) - 6:
                for reduce in reduces.values():
                    reduce.finish()
            if name == "C":
                computes[method]()
                continue
            uses_held = name == "Y" and method in first_base
            if uses_held:
                held_copy(fetched).wait()
            if method == "last":
                last(name)
            else:
                getattr({**reduces, **gathers}[name], method)(*arguments)
            if uses_held:
                if fetched + HELD < len(held_order):
                    held_copy(fetched + HELD).start()
                fetched += 1
        for copy in own_copies.values():
            copy.wait()
        for item in gathers.values():
            item.finish()

    for copy in (*fetches.values(), *loads):
        copy.start()
    enter(place)
    pl.when(place.middle == 0)(lambda: run(0))
    pl.when(place.middle == 1)(lambda: run(1))
    stream_out[...] += after_grad[...]


def call_backward(rows, tokens, cotangent, gains, routers, saved, weights, result):
    length, model_width = tokens.shape
    total = GRID[0] * GRID[1]
    wide, narrow = weights[2].shape[1], weights[0].shape[1]
    low_width = wide + 2 * narrow + 256
    low_rows, output_rows = model_width // total, wide // total
    low, full = jnp.bfloat16, jnp.float32
    vmem = pl.BlockSpec(memory_space=pltpu.VMEM)
    hbm = pl.BlockSpec(memory_space=pl.ANY)
    sems = pltpu.SemaphoreType.DMA((2, N_SEM))
    names = (
        "after",
        "normed",
        "normed_ffn",
        "queries",
        "keys",
        "projected",
        "values",
        "probability",
        "mixed",
        "gated",
        "gates",
        "slopes",
        "expert_slope",
    )
    sources = dict(zip(names, saved), rows=rows, tokens=tokens, cotangent=cotangent)
    fetched = [sources[name] for name in FETCHED_NAMES]
    inputs, outputs, scratch = 10, 4, 20

    def kernel(*refs):
        fetched_in, refs = refs[inputs : inputs + len(fetched)], refs[:inputs] + refs[inputs + len(fetched) :]
        head = inputs + outputs + scratch
        backward_kernel(*refs[:head], *fetched_in, *refs[head:])

    return pl.pallas_call(
        kernel,
        out_shape=(
            jax.ShapeDtypeStruct((length, model_width), low),
            jax.ShapeDtypeStruct((length, model_width), full),
            jax.ShapeDtypeStruct((model_width, low_width), low),
            jax.ShapeDtypeStruct((wide, model_width), low),
        ),
        in_specs=[vmem] * 5 + [hbm] * (5 + len(fetched)),
        out_specs=(vmem, vmem, hbm, hbm),
        scratch_shapes=[
            *(pltpu.VMEM(weight.shape, low) for weight in weights),
            pltpu.VMEM((128, model_width), low),
            pltpu.VMEM((128, model_width), low),
            pltpu.VMEM((length, model_width), full),
            pltpu.VMEM((length, model_width), low),
            pltpu.VMEM((length, wide), low),
            pltpu.VMEM((length, wide), low),
            pltpu.VMEM((length, 2 * narrow), low),
            pltpu.VMEM((HELD, length, model_width), low),
            pltpu.VMEM((model_width, low_width), low),
            pltpu.VMEM((wide, model_width), low),
            pltpu.VMEM((low_rows, low_width), low),
            pltpu.VMEM((output_rows, model_width), low),
            pltpu.SemaphoreType.DMA((4,)),
            pltpu.SemaphoreType.DMA((HELD,)),
            pltpu.SemaphoreType.DMA((2,)),
            pltpu.SemaphoreType.DMA((len(fetched),)),
            *(pltpu.VMEM(array.shape, array.dtype) for array in fetched),
            *reduce_scratch("Y", length, model_width),
            sems,
            *reduce_scratch("O", output_rows, model_width),
            sems,
            *reduce_scratch("L", low_rows, low_width),
            sems,
            sems,
            sems,
        ],
        compiler_params=pltpu.CompilerParams(
            collective_id=1, has_side_effects=True, vmem_limit_bytes=VMEM_LIMIT
        ),
        name="backward",
    )(*gains, *routers, *weights, result, *fetched)


def widen_kernel(
    low_ref,
    output_low_ref,
    first_ref,
    second_ref,
    block_ref,
    stream_ref,
    query,
    key,
    value,
    output,
    value_router,
    output_router,
    expert_router,
    gain_attention,
    gain_feedforward,
    first,
    second,
    block,
    stream,
):
    full = jnp.float32
    narrow, wide = query.shape[1], value.shape[1]
    query[...] = low_ref[:, :narrow].astype(full)
    key[...] = low_ref[:, narrow : 2 * narrow].astype(full)
    value[...] = low_ref[:, 2 * narrow : 2 * narrow + wide].astype(full)
    output[...] = output_low_ref[...].astype(full)
    start = 2 * narrow + wide
    small = low_ref[:, start : start + 128].astype(full).T
    count = value_router.shape[0]
    value_router[...] = small[:count]
    output_router[...] = small[OUTPUT_LANE : OUTPUT_LANE + count]
    gain_attention[...] = small[GAIN_LANE : GAIN_LANE + 1]
    gain_feedforward[...] = small[GAIN_LANE + 1 : GAIN_LANE + 2]
    expert_router[...] = low_ref[:, start + 128 :].astype(full).T[: expert_router.shape[0]]
    hidden_width = second.shape[1]
    for e in range(first.shape[0]):
        rows = slice(e * hidden_width, (e + 1) * hidden_width)
        first[e] = first_ref[rows, :].T
        second[e] = second_ref[rows, :]
    block[...] = block_ref[...]
    stream[...] = stream_ref[...]


def call_widen(low, output_low, first_sum, second_sum, block_output, stream_grad, narrow, expert_count, local_count):
    model_width, low_width = low.shape
    wide = output_low.shape[0]
    hidden = first_sum.shape[0]
    hidden_width = hidden // local_count
    length = block_output.shape[0]
    steps = 2
    height = model_width // steps
    full = jnp.float32
    router_width = HEADS * ATT_EXP
    rows = lambda count, width: pl.BlockSpec((count, width), lambda i: (i, 0))
    columns = lambda count: pl.BlockSpec((count, height), lambda i: (0, i))
    first_spec = pl.BlockSpec((local_count, height, hidden_width), lambda i: (0, i, 0))
    second_spec = pl.BlockSpec((local_count, hidden_width, height), lambda i: (0, 0, i))
    shape = lambda *dims, kind=full: jax.ShapeDtypeStruct(dims, kind)
    return pl.pallas_call(
        widen_kernel,
        grid=(steps,),
        out_shape=(
            shape(model_width, narrow),
            shape(model_width, narrow),
            shape(model_width, wide),
            shape(wide, model_width),
            shape(router_width, model_width),
            shape(router_width, model_width),
            shape(expert_count, model_width),
            shape(1, model_width),
            shape(1, model_width),
            shape(local_count, model_width, hidden_width),
            shape(local_count, hidden_width, model_width),
            shape(length, model_width, kind=block_output.dtype),
            shape(length, model_width),
        ),
        in_specs=[
            rows(height, low_width),
            rows(wide // steps, model_width),
            columns(hidden),
            columns(hidden),
            rows(length // steps, model_width),
            rows(length // steps, model_width),
        ],
        out_specs=(
            rows(height, narrow),
            rows(height, narrow),
            rows(height, wide),
            rows(wide // steps, model_width),
            columns(router_width),
            columns(router_width),
            columns(expert_count),
            columns(1),
            columns(1),
            first_spec,
            second_spec,
            rows(length // steps, model_width),
            rows(length // steps, model_width),
        ),
        compiler_params=pltpu.CompilerParams(vmem_limit_bytes=VMEM_LIMIT),
        name="widen",
    )(low, output_low, first_sum, second_sum, block_output, stream_grad)


BACKWARD_ORDER = (
    (
        ("Y", "hand_over"), ("Y", "corner", 3), ("C", "c1"), ("Y", "corner", 2), ("Y", "corner",
        0), ("C", "c2"), ("Y", "side_x", 3), ("O", "hand_over"), ("Y", "side_y", 3), ("C",
        "c3"), ("O", "corner", 3), ("O", "corner", 2), ("O", "corner", 1), ("Y", "give_d", 3),
        ("Y", "give_c", 3), ("C", "c4"), ("O", "side_y", 3), ("O", "side_y", 2), ("O", "side_x",
        2), ("C", "c5b"), ("O", "side_x", 1), ("O", "give_d", 2), ("Y", "corner", 1), ("O",
        "side_y", 1), ("Y", "line", 3), ("O", "corner", 0), ("O", "give_d", 3), ("O", "side_x",
        3), ("C", "c5a"), ("O", "line", 2), ("C", "c6"), ("L", "hand_over"), ("L", "corner", 3),
        ("O", "give_c", 3), ("O", "line", 3), ("O", "give_c", 2), ("O", "side_y", 0), ("L",
        "corner", 1), ("Y", "side_y", 0), ("L", "side_x", 3), ("L", "side_y", 3), ("L",
        "give_c", 3), ("L", "corner", 0), ("L", "corner", 2), ("L", "side_y", 1), ("O",
        "give_c", 1), ("O", "give_d", 0), ("O", "give_d", 1), ("O", "side_x", 0), ("L",
        "side_x", 1), ("L", "line", 3), ("O", "line", 1), ("L", "give_d", 1), ("Y", "side_y",
        2), ("L", "give_d", 3), ("L", "side_x", 2), ("L", "give_c", 2), ("L", "side_y", 2),
        ("C", "c7"), ("L", "give_c", 1), ("L", "side_y", 0), ("Y", "side_x", 0), ("O", "give_c",
        0), ("Y", "side_x", 2), ("O", "last"), ("GO", "begin"), ("L", "give_d", 2), ("Y",
        "side_y", 1), ("GO", "line", 1), ("L", "line", 2), ("GO", "side_y", 0), ("GO", "own_d"),
        ("L", "side_x", 0), ("GO", "side_x", 0), ("L", "give_c", 0), ("GO", "own_c"), ("L",
        "give_d", 0), ("GO", "pass_d", 1), ("L", "line", 1), ("GO", "line", 2), ("Y", "give_d",
        2), ("Y", "give_c", 0), ("L", "last"), ("GL", "begin"), ("GO", "line", 3), ("Y", "line",
        2), ("Y", "give_d", 0), ("GL", "side_x", 0), ("Y", "give_c", 2), ("GL", "side_y", 0),
        ("GO", "pass_d", 2), ("GL", "line", 1), ("GO", "pass_c", 1), ("GO", "pass_d", 3), ("Y",
        "side_x", 1), ("GL", "own_d"), ("GL", "own_c"), ("GL", "line", 2), ("GO", "side_x", 1),
        ("GO", "side_y", 3), ("GO", "pass_c", 3), ("Y", "give_c", 1), ("GO", "side_x", 3),
        ("GO", "side_y", 1), ("GL", "pass_c", 1), ("GL", "pass_d", 1), ("GO", "pass_c", 2),
        ("Y", "give_d", 1), ("GL", "line", 3), ("GO", "side_y", 2), ("GO", "corner", 1), ("GL",
        "pass_d", 2), ("GO", "side_x", 2), ("GL", "side_x", 1), ("GL", "side_y", 2), ("Y",
        "line", 1), ("GL", "pass_d", 3), ("GO", "corner", 0), ("GO", "corner", 2), ("GL",
        "side_y", 1), ("GL", "pass_c", 3), ("GL", "side_y", 3), ("GL", "pass_c", 2), ("GL",
        "side_x", 2), ("GO", "corner", 3), ("GL", "side_x", 3), ("GL", "corner", 2), ("GL",
        "corner", 1), ("GL", "corner", 0), ("GL", "corner", 3), ("Y", "last"), ("GO",
        "wait_all"), ("GL", "wait_all"),
    ),
    (
        ("Y", "hand_over"), ("Y", "corner", 3), ("C", "c1"), ("Y", "corner", 2), ("C", "c2"),
        ("Y", "corner", 1), ("O", "hand_over"), ("O", "corner", 3), ("O", "corner", 1), ("Y",
        "side_x", 3), ("O", "corner", 2), ("Y", "side_y", 2), ("Y", "side_y", 3), ("C", "c3"),
        ("O", "corner", 0), ("C", "c4"), ("O", "side_x", 1), ("C", "c5b"), ("Y", "give_c", 3),
        ("C", "c5a"), ("O", "side_y", 2), ("Y", "side_x", 1), ("O", "side_y", 3), ("O",
        "give_d", 2), ("O", "side_x", 2), ("O", "side_y", 1), ("O", "side_x", 0), ("C", "c6"),
        ("Y", "give_d", 3), ("O", "side_y", 0), ("L", "hand_over"), ("O", "side_x", 3), ("L",
        "corner", 3), ("L", "corner", 0), ("L", "corner", 1), ("O", "give_c", 3), ("O",
        "give_d", 3), ("L", "side_x", 3), ("O", "line", 2), ("L", "side_y", 3), ("O", "give_d",
        1), ("O", "give_c", 2), ("O", "line", 3), ("L", "side_x", 0), ("L", "corner", 2), ("Y",
        "line", 3), ("L", "side_y", 0), ("O", "give_d", 0), ("O", "give_c", 0), ("L", "give_c",
        3), ("Y", "give_c", 1), ("O", "give_c", 1), ("Y", "side_y", 1), ("L", "side_y", 2),
        ("L", "side_x", 1), ("L", "line", 3), ("O", "line", 1), ("O", "last"), ("GO", "begin"),
        ("Y", "side_x", 2), ("Y", "give_d", 1), ("L", "give_c", 1), ("L", "side_x", 2), ("L",
        "side_y", 1), ("GO", "side_x", 0), ("L", "give_d", 3), ("GO", "own_c"), ("C", "c7"),
        ("L", "give_d", 1), ("L", "give_c", 2), ("GO", "side_y", 0), ("GO", "line", 2), ("L",
        "give_d", 2), ("GO", "own_d"), ("GO", "line", 1), ("L", "line", 1), ("GO", "pass_c", 2),
        ("L", "give_d", 0), ("L", "line", 2), ("GO", "pass_d", 2), ("GO", "pass_c", 1), ("L",
        "give_c", 0), ("GO", "line", 3), ("L", "last"), ("GL", "begin"), ("Y", "corner", 0),
        ("GO", "pass_d", 1), ("GL", "line", 1), ("GO", "pass_c", 3), ("GL", "side_y", 0), ("GO",
        "corner", 0), ("GL", "side_x", 0), ("GO", "pass_d", 3), ("GL", "line", 2), ("GL",
        "own_d"), ("GL", "own_c"), ("GL", "line", 3), ("GL", "pass_d", 1), ("GO", "side_y", 1),
        ("Y", "give_c", 2), ("GL", "pass_d", 3), ("Y", "side_x", 0), ("GO", "side_x", 3), ("GL",
        "pass_d", 2), ("GL", "side_y", 1), ("GL", "pass_c", 2), ("GO", "side_x", 2), ("Y",
        "give_d", 2), ("GL", "pass_c", 1), ("GO", "side_y", 3), ("Y", "line", 2), ("GO",
        "side_y", 2), ("GL", "side_x", 1), ("GL", "side_y", 3), ("GL", "side_y", 2), ("Y",
        "side_y", 0), ("Y", "give_c", 0), ("GL", "side_x", 2), ("GL", "pass_c", 3), ("Y",
        "line", 1), ("GO", "side_x", 1), ("GO", "corner", 3), ("GL", "side_x", 3), ("GO",
        "corner", 1), ("Y", "give_d", 0), ("GL", "corner", 0), ("GO", "corner", 2), ("GL",
        "corner", 1), ("GL", "corner", 2), ("GL", "corner", 3), ("Y", "last"), ("GO",
        "wait_all"), ("GL", "wait_all"),
    ),
)
LAYER_ORDER = (
    (
        ("U", "begin"), ("C", "a1"), ("U", "side_x", 0), ("U", "side_y", 0), ("U", "line", 1),
        ("U", "own_d"), ("C", "prep"), ("U", "own_c"), ("C", "a2"), ("X", "begin"), ("X",
        "line", 1), ("X", "side_y", 0), ("X", "side_x", 0), ("X", "own_d"), ("S", "go", 0, 1),
        ("U", "corner", 0), ("X", "own_c"), ("U", "line", 3), ("U", "line", 2), ("S", "go", 0,
        0), ("X", "corner", 0), ("U", "pass_c", 3), ("U", "pass_d", 3), ("S", "go", 3, 0), ("U",
        "side_x", 3), ("S", "go", 2, 0), ("S", "go", 1, 0), ("X", "line", 3), ("X", "pass_c",
        1), ("U", "side_y", 3), ("X", "pass_c", 3), ("X", "side_x", 3), ("X", "side_x", 1),
        ("X", "pass_d", 3), ("X", "side_y", 3), ("S", "go", 1, 3), ("U", "corner", 3), ("X",
        "corner", 3), ("X", "line", 2), ("S", "go", 3, 3), ("X", "pass_d", 1), ("X", "pass_c",
        2), ("X", "side_y", 1), ("R", "corner", 3), ("S", "go", 2, 3), ("X", "pass_d", 2), ("U",
        "pass_c", 1), ("X", "side_y", 2), ("X", "side_x", 2), ("U", "pass_c", 2), ("S", "go", 0,
        2), ("U", "side_x", 2), ("U", "pass_d", 1), ("S", "go", 0, 3), ("U", "pass_d", 2), ("U",
        "side_y", 2), ("R", "side_x", 3), ("R", "give_c", 3), ("U", "side_y", 1), ("R",
        "side_y", 3), ("R", "give_d", 3), ("X", "corner", 2), ("S", "go", 1, 2), ("U", "corner",
        2), ("U", "side_x", 1), ("S", "go", 3, 2), ("R", "line", 3), ("R", "corner", 2), ("X",
        "corner", 1), ("S", "go", 2, 2), ("U", "corner", 1), ("R", "side_y", 2), ("R", "side_x",
        2), ("R", "give_d", 2), ("S", "go", 3, 1), ("R", "give_c", 2), ("S", "go", 1, 1), ("R",
        "corner", 1), ("R", "corner", 0), ("R", "line", 2), ("S", "go", 2, 1), ("S", "dw", 0),
        ("R", "side_y", 1), ("R", "give_d", 1), ("S", "dw", 1), ("R", "side_x", 1), ("S", "dw",
        2), ("R", "side_y", 0), ("R", "give_c", 1), ("S", "dw", 3), ("R", "side_x", 0), ("S",
        "dw", 4), ("R", "give_d", 0), ("R", "give_c", 0), ("R", "line", 1), ("S", "dw", 5),
        ("S", "dw", 6), ("S", "dw", 7), ("R", "last"),
    ),
    (
        ("U", "begin"), ("C", "a1"), ("U", "line", 2), ("U", "line", 1), ("C", "a2"), ("U",
        "side_y", 0), ("X", "begin"), ("U", "line", 3), ("C", "prep"), ("U", "pass_d", 1), ("U",
        "pass_c", 1), ("X", "line", 1), ("U", "pass_d", 3), ("U", "side_y", 1), ("X", "side_x",
        0), ("U", "side_x", 1), ("X", "pass_d", 1), ("U", "side_x", 0), ("X", "own_c"), ("X",
        "pass_c", 1), ("U", "pass_c", 3), ("X", "line", 3), ("X", "side_x", 1), ("X", "pass_c",
        3), ("U", "side_x", 3), ("X", "side_y", 0), ("X", "pass_d", 3), ("X", "line", 2), ("S",
        "go", 1, 0), ("X", "own_d"), ("S", "go", 2, 0), ("U", "side_y", 3), ("S", "go", 0, 1),
        ("X", "pass_c", 2), ("U", "corner", 0), ("U", "own_c"), ("X", "pass_d", 2), ("X",
        "side_y", 1), ("X", "corner", 0), ("S", "go", 0, 0), ("X", "side_y", 3), ("X", "side_x",
        3), ("S", "go", 1, 1), ("U", "corner", 1), ("S", "go", 0, 2), ("S", "go", 2, 3), ("X",
        "corner", 1), ("U", "pass_c", 2), ("U", "own_d"), ("X", "side_x", 2), ("S", "go", 3, 0),
        ("U", "pass_d", 2), ("U", "side_y", 2), ("U", "corner", 3), ("U", "side_x", 2), ("R",
        "corner", 0), ("X", "corner", 3), ("S", "go", 2, 1), ("X", "side_y", 2), ("S", "go", 3,
        3), ("S", "go", 1, 3), ("U", "corner", 2), ("R", "corner", 3), ("S", "go", 3, 1), ("R",
        "side_y", 0), ("S", "go", 1, 2), ("R", "side_x", 3), ("R", "corner", 1), ("R", "side_y",
        3), ("X", "corner", 2), ("S", "go", 2, 2), ("R", "give_c", 3), ("R", "side_x", 0), ("S",
        "go", 3, 2), ("R", "give_d", 3), ("S", "go", 0, 3), ("R", "corner", 2), ("S", "dw", 0),
        ("R", "side_y", 1), ("R", "side_x", 1), ("R", "line", 3), ("S", "dw", 1), ("R",
        "give_d", 1), ("R", "side_y", 2), ("S", "dw", 2), ("R", "give_d", 2), ("R", "side_x",
        2), ("S", "dw", 3), ("S", "dw", 4), ("R", "give_c", 2), ("R", "give_c", 1), ("S", "dw",
        5), ("S", "dw", 6), ("S", "dw", 7), ("R", "line", 1), ("R", "line", 2), ("R", "give_d",
        0), ("R", "give_c", 0), ("R", "last"),
    ),
)


def choose(step, values):
    total = 0
    for number, value in enumerate(values):
        total = total + value * jnp.where(step == number, 1, 0)
    return total


SAVED = 15


def layer_kernel(
    local_count,
    tokens_ref,
    cotangent_ref,
    gain_attention_ref,
    gain_feedforward_ref,
    value_router_ref,
    output_router_ref,
    expert_router_ref,
    segments_ref,
    value_ids_ref,
    output_ids_ref,
    ffn_ids_ref,
    query_in,
    key_in,
    value_in,
    output_in,
    first_in,
    second_in,
    rows_out,
    result_out,
    routers,
    all_ids,
    gathered,
    upstream,
    first_ref,
    first_t_ref,
    second_t_ref,
    hidden_parts,
    partial,
    result_stage,
    weight_sems,
    upstream_sems,
    gather_sems,
    reduce_sems,
    result_sems,
    early_sems,
    saved_sems,
    *refs,
):
    place = Place()
    saved_outs, refs = refs[:SAVED], refs[SAVED:]
    saved_refs, refs = refs[:SAVED], refs[SAVED:]
    (
        first_out,
        second_out,
        after_out,
        normed_out,
        normed_ffn_out,
        queries_out,
        keys_out,
        projected_out,
        values_out,
        probability_out,
        mixed_out,
        gated_out,
        gates_out,
        slopes_out,
        expert_slope_out,
    ) = saved_refs
    first_part, second_ref, boxes = refs[0], refs[1], refs[2:]
    saves = [
        pltpu.make_async_copy(src, dst, saved_sems.at[number])
        for number, (src, dst) in enumerate(zip(saved_refs, saved_outs))
    ]
    length, model_width = tokens_ref.shape
    pair = 2 * length
    expert_count = expert_router_ref.shape[0]
    width = gathered.shape[1]
    gate_width = width - model_width
    hidden_width = first_ref.shape[1] // local_count
    narrow, wide = query_in.shape[1], value_in.shape[1]
    mine = pl.ds(pl.multiple_of(place.me * length, length), length)

    pieces = [
        (start, min(wide, start + width), number)
        for number, start in enumerate(range(0, wide, width), 1)
    ]
    value_refs = [
        partial.at[number * model_width : (number + 1) * model_width, : end - start]
        for start, end, number in pieces
    ]
    query_ref = partial.at[:model_width, :narrow]
    key_ref = partial.at[:model_width, narrow : 2 * narrow]
    hidden = first_ref.shape[1]
    gated_hidden = hidden_parts.at[:, :hidden]
    pre_grads = hidden_parts.at[:, hidden:]
    main_columns, side_columns = 2 * hidden, model_width - 2 * hidden
    last_rows = len(pieces) * model_width
    output_parts = [
        (0, wide, slice(0, main_columns), hidden_parts.at[:wide, :])
    ]
    for number, start in enumerate(range(0, wide, model_width), 1):
        end = min(wide, start + model_width)
        place_at = slice(number * side_columns, (number + 1) * side_columns)
        ref = partial.at[last_rows : last_rows + end - start, place_at]
        output_parts.append((start, end, slice(main_columns, None), ref))
    loads = [
        pltpu.make_async_copy(src, dst, weight_sems.at[number])
        for number, (src, dst) in enumerate(
            [
                (query_in, query_ref),
                (key_in, key_ref),
                *(
                    (value_in.at[:, start:end], ref)
                    for (start, end, _), ref in zip(pieces, value_refs)
                ),
                *(
                    (output_in.at[start:end, columns], ref)
                    for start, end, columns, ref in output_parts
                ),
            ]
        )
    ]
    values = {}
    lane = lax.broadcasted_iota(jnp.int32, (length, gates_out.shape[1]), 1).astype(jnp.float32)

    def named(columns):
        ids = values["ids"]
        mask = jnp.zeros(lane.shape, jnp.float32)
        for at in columns:
            mask = jnp.where(lane == ids[:, at : at + 1], 1.0, mask)
        return mask

    ffn_top = ffn_ids_ref.shape[0]

    def a1():
        join_routers(routers, value_router_ref, output_router_ref)
        top = value_ids_ref.shape[1]
        all_ids[...] = jnp.zeros_like(all_ids)
        for head in range(HEADS):
            at = head * top
            all_ids[at : at + top, :] = value_ids_ref[head].astype(jnp.float32) + float(head * ATT_EXP)
            all_ids[16 + at : 16 + at + top, :] = output_ids_ref[head].astype(jnp.float32) + float(
                OUTPUT_LANE + head * ATT_EXP
            )
        all_ids[32 : 32 + ffn_top, :] = ffn_ids_ref[...].astype(jnp.float32)
        values["ids"] = all_ids[...].T
        stream_low = tokens_ref[...]
        stream = stream_low.astype(jnp.float32)
        unit, _ = norm_parts(stream)
        normed = (unit * gain_attention_ref[...]).astype(jnp.bfloat16)
        normed_out[...] = normed
        sig = jax.nn.sigmoid(mm_nt(normed, routers[...]))
        gates = named([*range(HEADS * top), *range(16, 16 + HEADS * top)]) * sig
        gates_out[...] = gates
        slopes_out[...] = gates * (1.0 - sig)
        loads[0].wait()
        queries_out[...] = mm(normed, query_ref[...]).astype(jnp.bfloat16)
        loads[1].wait()
        keys_out[...] = mm(normed, key_ref[...]).astype(jnp.bfloat16)
        for (start, end, _), ref, load in zip(pieces, value_refs, loads[2:]):
            load.wait()
            projected_out[:, start:end] = mm(stream_low, ref[...])
        for head in range(HEADS):
            total = jnp.zeros((length, HEAD), jnp.float32)
            for e in range(ATT_EXP):
                at = head * ATT_EXP + e
                total = total + gates[:, at : at + 1] * projected_out[:, at * HEAD : (at + 1) * HEAD]
            values_out[:, head * HEAD : (head + 1) * HEAD] = total.astype(jnp.bfloat16)
        documents = jnp.broadcast_to(segments_ref[...].astype(jnp.float32), (length, length))
        row = lax.broadcasted_iota(jnp.int32, (length, length), 0)
        column = lax.broadcasted_iota(jnp.int32, (length, length), 1)
        allowed = (documents == documents.T) & (row >= column)
        for head in range(HEADS):
            columns = slice(head * HEAD, (head + 1) * HEAD)
            scores = mm_nt(queries_out[:, columns], keys_out[:, columns]) * (1.0 / math.sqrt(HEAD))
            scores = jnp.where(allowed, scores, NEG_FILL)
            exponent = jnp.exp(scores - jnp.max(scores, axis=-1, keepdims=True))
            probability = exponent / jnp.sum(exponent, axis=-1, keepdims=True)
            probability_out[head] = probability
            mixed = mm(probability.astype(jnp.bfloat16), values_out[:, columns])
            mixed_out[:, columns] = mixed
            for e in range(ATT_EXP):
                at = head * ATT_EXP + e
                gate = gates[:, OUTPUT_LANE + at : OUTPUT_LANE + at + 1]
                gated_out[:, at * HEAD : (at + 1) * HEAD] = (gate * mixed).astype(jnp.bfloat16)
    def a2():
        stream = tokens_ref[...].astype(jnp.float32)
        side = stream[:, main_columns:]
        for (start, end, columns, ref), load in zip(output_parts, loads[2 + len(pieces) :]):
            load.wait()
            if start == 0 and end == wide:
                after_out[:, columns] = stream[:, columns] + mm(gated_out[...], ref[...])
            else:
                side = side + mm(gated_out[:, start:end], ref[...])
        after_out[:, main_columns:] = side
        after = after_out[...]
        gathered[mine, :model_width] = after.astype(jnp.bfloat16)
        unit, _ = norm_parts(after)
        normed_ffn = (unit * gain_feedforward_ref[...]).astype(jnp.bfloat16)
        normed_ffn_out[...] = normed_ffn
        expert_sig = jax.nn.sigmoid(mm_nt(normed_ffn, expert_router_ref[...]))
        expert_gates = named(range(32, 32 + ffn_top))[:, :expert_count] * expert_sig
        gathered[mine, model_width:] = jnp.zeros((length, gate_width), jnp.bfloat16)
        gathered[mine, model_width : model_width + expert_count] = expert_gates.astype(jnp.bfloat16)
        expert_slope_out[...] = jnp.zeros((length, gate_width), jnp.float32)
        expert_slope_out[:, :expert_count] = expert_gates * (1.0 - expert_sig)
        for save in saves[2:]:
            save.start()

    def prep():
        early[1].wait()
        early[2].wait()
        for e in range(local_count):
            columns = slice(e * hidden_width, (e + 1) * hidden_width)
            first_ref[:, columns] = first_part[e]
            first_t_ref[columns, :] = first_part[e].astype(jnp.float32).T.astype(jnp.bfloat16)
            second_t_ref[:, columns] = second_ref[columns, :].astype(jnp.float32).T.astype(jnp.bfloat16)
    computes = {"a1": a1, "a2": a2, "prep": prep}
    pick_row = lax.broadcasted_iota(jnp.int32, (gate_width, first_ref.shape[1]), 0)
    pick_column = lax.broadcasted_iota(jnp.int32, (gate_width, first_ref.shape[1]), 1)
    pick_gates = jnp.where(
        pick_row == place.me * local_count + pick_column // hidden_width, 1.0, 0.0
    ).astype(jnp.bfloat16)
    def result_copy(slot, chip):
        return pltpu.make_async_copy(
            result_stage.at[slot],
            result_out.at[pl.ds(pl.multiple_of(chip * pair, pair), pair)],
            result_sems.at[slot],
        )

    def compute(step, place, reduce, q, j):
        chip = place.chip(q, j)
        rows = pl.ds(pl.multiple_of(chip * pair, pair), pair)
        hidden_pre = mm(gathered[rows, :model_width], first_ref[...])
        back = mm(upstream[rows, :], second_t_ref[...])
        gates = mm(gathered[rows, model_width:], pick_gates)
        square = hidden_pre * hidden_pre
        bent = jnp.tanh(GELU_C * hidden_pre * (1.0 + GELU_K * square))
        grow = 0.5 * (1.0 + bent)
        slope = grow + 0.5 * hidden_pre * (1.0 - bent * bent) * (
            GELU_C * (1.0 + 3.0 * GELU_K * square)
        )
        hidden = (hidden_pre * grow).astype(jnp.bfloat16).astype(jnp.float32)
        gated = (gates * hidden).astype(jnp.bfloat16)
        pre_grad = (gates * back * slope).astype(jnp.bfloat16)
        gated_hidden[rows, :] = gated
        pre_grads[rows, :] = pre_grad
        k = 4 * q + j
        to = pl.ds(pl.multiple_of(k * pair, pair), pair)
        partial[to, :model_width] = mm(pre_grad, first_t_ref[...]).astype(jnp.bfloat16)
        product = hidden * back
        column = lax.broadcasted_iota(jnp.int32, (pair, gate_width), 1) - place.me * local_count
        gate_grad = jnp.zeros((pair, gate_width), jnp.float32)
        for e in range(local_count):
            own_sum = jnp.sum(
                product[:, e * hidden_width : (e + 1) * hidden_width], axis=1, keepdims=True
            )
            gate_grad = jnp.where(column == e, own_sum, gate_grad)
        partial[to, model_width:] = gate_grad.astype(jnp.bfloat16)
        reduce.copy("core", k).start()
        slot = step % 2

        @pl.when(step >= 2)
        def _():
            result_copy(slot, chip).wait()

        result_stage[slot] = mm(gated, second_ref[...]).astype(jnp.bfloat16)
        result_copy(slot, chip).start()

    piece = gathered.shape[0] // 8

    def weight_piece(number):
        rows = pl.ds(pl.multiple_of(number * piece, piece), piece)
        second = mm_tn(gated_hidden[rows, :], upstream[rows, :])
        first = mm_tn(pre_grads[rows, :], gathered[rows, :model_width])

        @pl.when(number == 0)
        def _():
            second_out[...] = second
            first_out[...] = first

        @pl.when(number > 0)
        def _():
            second_out[...] += second
            first_out[...] += first

    def run(middle):
        known = place.fixed(middle)

        def share(k, core):
            return partial.at[pl.ds(pl.multiple_of(k * pair + core * length, length), length)]

        items = {
            "U": Gather("U", known, upstream, length, upstream_sems),
            "X": Gather("X", known, gathered, length, gather_sems),
            "R": Reduce(
                "R",
                known,
                lambda k: share(k, known.core),
                lambda k: share(k, 1 - known.core),
                boxes,
                reduce_sems,
            ),
        }

        def put(at, total):
            rows_out[at, :] = total

        def act(events):
            for name, method, *arguments in events:
                if name == "C":
                    computes[method]()
                elif method == "last":
                    items[name].last(put)
                else:
                    getattr(items[name], method)(*arguments)

        stops, pieces_at, waiting = [], [], []
        for event in LAYER_ORDER[middle]:
            if event[0] != "S":
                waiting.append(event)
                continue
            (stops if event[1] == "go" else pieces_at).append((event[2:], waiting))
            waiting = []
        act(stops[0][1])

        def walk(step, carry):
            for number, (_, events) in enumerate(stops):
                if number and events:
                    pl.when(step == number)(functools.partial(act, events))
            q = choose(step, [stop[0] for stop, _ in stops])
            j = choose(step, [stop[1] for stop, _ in stops])
            items["X"].whole(q, j)
            items["U"].whole(q, j)
            compute(step, known, items["R"], q, j)
            return carry

        lax.fori_loop(0, len(stops), walk, 0)
        items["U"].finish()

        def give(step, carry):
            for number, (_, events) in enumerate(pieces_at):
                if events:
                    pl.when(step == number)(functools.partial(act, events))
            weight_piece(step)
            return carry

        lax.fori_loop(0, len(pieces_at), give, 0)
        for save in saves[:2]:
            save.start()
        items["X"].finish()
        act(waiting)
        items["R"].finish()

    early = [
        pltpu.make_async_copy(src, dst, early_sems.at[number])
        for number, (src, dst) in enumerate(
            ((cotangent_ref, upstream.at[mine]), (first_in, first_part), (second_in, second_ref))
        )
    ]
    for copy in (*early, *loads):
        copy.start()
    enter(place)
    early[0].wait()
    pl.when(place.middle == 0)(lambda: run(0))
    pl.when(place.middle == 1)(lambda: run(1))
    for slot in range(2):
        result_copy(slot, 0).wait()
    for save in saves:
        save.wait()


def call_layer(
    tokens,
    cotangent,
    gains,
    weights,
    routers,
    segments,
    value_ids,
    output_ids,
    ffn_ids,
    expert_first,
    expert_second,
):
    length, model_width = tokens.shape
    local_count, _, hidden_width = expert_first.shape
    hidden = local_count * hidden_width
    expert_count = routers[2].shape[0]
    gate_width = -(-expert_count // 128) * 128
    width = model_width + gate_width
    total = GRID[0] * GRID[1] * length
    wide = weights[3].shape[0]
    narrow = HEADS * HEAD
    low, full = jnp.bfloat16, jnp.float32
    shapes = (
        ((length, width), full),
        ((hidden, model_width), full),
        ((hidden, model_width), full),
        ((length, model_width), full),
        ((length, model_width), low),
        ((length, model_width), low),
        ((length, narrow), low),
        ((length, narrow), low),
        ((length, wide), full),
        ((length, narrow), low),
        ((HEADS, length, length), full),
        ((length, narrow), full),
        ((length, wide), low),
        ((length, 128), full),
        ((length, 128), full),
        ((length, gate_width), full),
        ((total, model_width), low),
    )
    vmem = pl.BlockSpec(memory_space=pltpu.VMEM)
    hbm = pl.BlockSpec(memory_space=pl.ANY)
    sems = pltpu.SemaphoreType.DMA((2, N_SEM))
    inputs, scratch = 17, 17

    def kernel(*refs):
        rows_out, *saved_outs, result_out = refs[inputs : inputs + SAVED + 2]
        rest = refs[inputs + SAVED + 2 :]
        layer_kernel(
            local_count,
            *refs[:inputs],
            rows_out,
            result_out,
            *rest[:scratch],
            *saved_outs,
            *rest[scratch:],
        )

    return pl.pallas_call(
        kernel,
        out_shape=tuple(jax.ShapeDtypeStruct(*shape) for shape in shapes),
        in_specs=[vmem, hbm] + [vmem] * 9 + [hbm] * 6,
        out_specs=(vmem, *([hbm] * (len(shapes) - 1))),
        scratch_shapes=[
            pltpu.VMEM((128, model_width), low),
            pltpu.VMEM((128, length), full),
            pltpu.VMEM((total, width), low),
            pltpu.VMEM((total, model_width), low),
            pltpu.VMEM((model_width, hidden), low),
            pltpu.VMEM((hidden, model_width), low),
            pltpu.VMEM((model_width, hidden), low),
            pltpu.VMEM((total, 2 * hidden), low),
            pltpu.VMEM((total, width), low),
            pltpu.VMEM((2, 2 * length, model_width), low),
            pltpu.SemaphoreType.DMA((3 + -(-wide // width) + -(-wide // model_width),)),
            sems,
            sems,
            sems,
            pltpu.SemaphoreType.DMA((2,)),
            pltpu.SemaphoreType.DMA((3,)),
            pltpu.SemaphoreType.DMA((SAVED,)),
            *(pltpu.VMEM(*shape) for shape in shapes[1:-1]),
            pltpu.VMEM(expert_first.shape, low),
            pltpu.VMEM((hidden, model_width), low),
            *reduce_scratch("R", length, width),
        ],
        compiler_params=pltpu.CompilerParams(
            collective_id=0, has_side_effects=True, vmem_limit_bytes=VMEM_LIMIT
        ),
        name="layer",
    )(
        tokens,
        cotangent,
        *gains,
        *routers,
        segments,
        value_ids.transpose(1, 2, 0),
        output_ids.transpose(1, 2, 0),
        ffn_ids.T,
        *weights,
        expert_first,
        expert_second.reshape(hidden, model_width),
    )


def general_body(
    tokens,
    cotangent,
    gain_attention,
    gain_feedforward,
    query_weight,
    key_weight,
    value_weight,
    output_weight,
    value_router,
    output_router,
    expert_router,
    expert_first,
    expert_second,
    segments,
    value_ids,
    output_ids,
    ffn_ids,
):
    owner_total = lax.axis_size("dp") * lax.axis_size("expert")
    local_count = expert_first.shape[0]
    expert_count = local_count * owner_total
    shared = (
        gain_attention,
        query_weight,
        key_weight,
        value_weight,
        output_weight,
        value_router,
        output_router,
    )
    stream = tokens.astype(jnp.float32)
    upstream = cotangent.astype(jnp.float32)
    after_attention, saved_parts = attention_forward(
        stream, segments[0], value_ids[0], output_ids[0], shared
    )
    normed_low = layer_norm(after_attention, gain_feedforward).astype(jnp.bfloat16)
    logits = jnp.dot(normed_low, expert_router, preferred_element_type=jnp.float32)
    sigmoid_out = jax.nn.sigmoid(logits)
    dense_gates = sigmoid_out * expert_mask(ffn_ids[0], expert_count)
    expert_slope = dense_gates * (1.0 - sigmoid_out)
    result, token_grad, gate_back, first_sum, second_sum = expert_exchange(
        after_attention.astype(jnp.bfloat16),
        cotangent,
        dense_gates.astype(jnp.bfloat16),
        expert_first,
        expert_second,
        max(1, owner_total // 32),
    )
    logit_grad = (gate_back.astype(jnp.float32) * expert_slope).astype(jnp.bfloat16)
    router_sum = jnp.einsum("sa,sb->ab", normed_low, logit_grad, preferred_element_type=jnp.float32)
    normed_grad = jnp.einsum(
        "sb,ab->sa", logit_grad, expert_router, preferred_element_type=jnp.float32
    )
    norm_value, norm_pull = jax.vjp(layer_norm, after_attention, gain_feedforward)
    after_extra, feed_gain_part = norm_pull(normed_grad)
    after_grad = upstream + token_grad.astype(jnp.float32) + after_extra
    stream_grad, attention_parts = attention_backward(after_grad, saved_parts, stream, shared)
    gain_part, query_part, key_part, value_part, output_part, value_router_part, output_router_part = attention_parts
    parts = (
        query_part,
        key_part,
        value_part,
        value_router_part,
        output_router_part,
        router_sum,
        gain_part[:, None],
        feed_gain_part[:, None],
    )
    low = jnp.concatenate([part.astype(jnp.bfloat16) for part in parts], axis=1)
    low = jnp.pad(low, ((0, 0), (0, -low.shape[1] % 256)))
    output_low = output_part.astype(jnp.bfloat16)
    low, output_low = lax.psum((low, output_low), BOTH)
    block_output = (after_attention + result.astype(jnp.float32)).astype(jnp.bfloat16)
    summed, start = [], 0
    for part in parts:
        summed.append(low[:, start : start + part.shape[1]].astype(jnp.float32))
        start += part.shape[1]
    query_sum, key_sum, value_sum, value_router_sum, output_router_sum, router_sum, *gains = summed
    summed = (
        gains[0][:, 0],
        gains[1][:, 0],
        query_sum,
        key_sum,
        value_sum,
        output_low.astype(jnp.float32),
        value_router_sum,
        output_router_sum,
        router_sum,
    )
    return (
        block_output,
        stream_grad,
        *summed,
        first_sum,
        second_sum,
    )


def kernel_body(
    tokens,
    cotangent,
    gain_attention,
    gain_feedforward,
    query_weight,
    key_weight,
    value_weight,
    output_weight,
    value_router,
    output_router,
    expert_router,
    expert_first,
    expert_second,
    segments,
    value_ids,
    output_ids,
    ffn_ids,
):
    gains = (gain_attention[None], gain_feedforward[None])
    weights = (query_weight, key_weight, value_weight, output_weight)
    routers = (value_router.T, output_router.T, expert_router.T)
    rows_sum, first_sum, second_sum, *saved, result = call_layer(
        tokens,
        cotangent,
        gains,
        weights,
        routers,
        segments,
        value_ids[0],
        output_ids[0],
        ffn_ids[0],
        expert_first,
        expert_second,
    )
    block_output, stream_grad, low, output_low = call_backward(
        rows_sum, tokens, cotangent, gains, routers, saved, weights, result
    )
    (
        query_sum,
        key_sum,
        value_sum,
        output_sum,
        value_router_sum,
        output_router_sum,
        expert_router_sum,
        gain_attention_sum,
        gain_feedforward_sum,
        first_sum,
        second_sum,
        block_output,
        stream_grad,
    ) = call_widen(
        low,
        output_low,
        first_sum,
        second_sum,
        block_output,
        stream_grad,
        query_weight.shape[1],
        expert_router.shape[1],
        expert_first.shape[0],
    )
    return (
        block_output,
        stream_grad,
        gain_attention_sum[0],
        gain_feedforward_sum[0],
        query_sum,
        key_sum,
        value_sum,
        output_sum,
        value_router_sum.T,
        output_router_sum.T,
        expert_router_sum.T,
        first_sum,
        second_sum,
    )


def body(*args):
    if (lax.axis_size("dp"), lax.axis_size("expert")) == GRID:
        return kernel_body(*args)
    return general_body(*args)


def solution(mesh):
    placed = (
        P(("dp", "expert"), None),
        P(("dp", "expert"), None),
        P(),
        P(),
        P(),
        P(),
        P(),
        P(),
        P(),
        P(),
        P(),
        P(("dp", "expert"), None, None),
        P(("dp", "expert"), None, None),
        P(("dp", "expert"), None),
        P(None, ("dp", "expert"), None, None),
        P(None, ("dp", "expert"), None, None),
        P(None, ("dp", "expert"), None),
    )
    return jax.shard_map(
        body,
        mesh=mesh,
        in_specs=placed,
        out_specs=(
            P(("dp", "expert"), None),
            P(("dp", "expert"), None),
            P(),
            P(),
            P(),
            P(),
            P(),
            P(),
            P(),
            P(),
            P(),
            P(("dp", "expert"), None, None),
            P(("dp", "expert"), None, None),
        ),
        check_vma=False,
    )
```

```python
import functools
import math

import jax
import jax.numpy as jnp
from jax import lax
from jax.experimental import pallas as pl
from jax.experimental.pallas import tpu as pltpu
from jax.sharding import PartitionSpec as P

HEADS = 4
HEAD = 128
ATT_EXP = 5


NEG_FILL = -1000000000.0


def layer_norm(stream, norm_gain):
    average = jnp.mean(stream, axis=-1, keepdims=True)
    centred = stream - average
    variance = jnp.mean(centred * centred, axis=-1, keepdims=True)
    return centred * lax.rsqrt(variance + 1e-05) * norm_gain


def expert_mask(picked_ids, expert_count):
    matches = picked_ids[..., None] == jnp.arange(expert_count, dtype=jnp.int32)
    return jnp.sum(matches.astype(jnp.float32), axis=-2)


def attention_forward(stream, document_ids, value_picks, output_picks, shared):
    (
        gain_attention,
        query_weight,
        key_weight,
        value_weight,
        output_weight,
        value_router,
        output_router,
    ) = shared
    length = stream.shape[0]
    normed_low = layer_norm(stream, gain_attention).astype(jnp.bfloat16)
    queries = (
        jnp.dot(normed_low, query_weight, preferred_element_type=jnp.float32)
        .astype(jnp.bfloat16)
        .reshape(length, HEADS, HEAD)
    )
    key_rows = (
        jnp.dot(normed_low, key_weight, preferred_element_type=jnp.float32)
        .astype(jnp.bfloat16)
        .reshape(length, HEADS, HEAD)
    )
    value_sig = jax.nn.sigmoid(
        jnp.dot(normed_low, value_router, preferred_element_type=jnp.float32)
    ).reshape(length, HEADS, ATT_EXP)
    output_sig = jax.nn.sigmoid(
        jnp.dot(normed_low, output_router, preferred_element_type=jnp.float32)
    ).reshape(length, HEADS, ATT_EXP)
    value_mask = expert_mask(value_picks, ATT_EXP)
    output_mask = expert_mask(output_picks, ATT_EXP)
    value_gates = value_mask * value_sig
    output_gates = output_mask * output_sig
    stream_low = stream.astype(jnp.bfloat16)
    projected = jnp.dot(stream_low, value_weight, preferred_element_type=jnp.float32).reshape(
        length, HEADS, ATT_EXP, HEAD
    )
    values = jnp.sum(value_gates[..., None] * projected, axis=2).astype(jnp.bfloat16)
    scores = jnp.einsum("qhd,khd->hqk", queries, key_rows, preferred_element_type=jnp.float32) * (
        1.0 / math.sqrt(HEAD)
    )
    positions = jnp.arange(length, dtype=jnp.int32)
    allowed = (document_ids[:, None] == document_ids[None, :]) & (
        positions[:, None] >= positions[None, :]
    )
    scores = jnp.where(allowed[None], scores, NEG_FILL)
    row_max = jnp.max(scores, axis=-1, keepdims=True)
    exponent = jnp.exp(scores - row_max)
    row_total = jnp.sum(exponent, axis=-1, keepdims=True)
    probability = exponent / row_total
    weights_low = probability.astype(jnp.bfloat16)
    mixed = jnp.einsum("hqk,khd->qhd", weights_low, values, preferred_element_type=jnp.float32)
    gated_rows = (
        (output_gates[..., None] * mixed[:, :, None, :])
        .reshape(length, HEADS * ATT_EXP * HEAD)
        .astype(jnp.bfloat16)
    )
    after_attention = stream + jnp.dot(
        gated_rows, output_weight, preferred_element_type=jnp.float32
    )
    saved_parts = (
        normed_low,
        queries,
        key_rows,
        value_gates * (1.0 - value_sig),
        output_gates * (1.0 - output_sig),
        value_gates,
        output_gates,
        stream_low,
        projected,
        values,
        probability,
        weights_low,
        mixed,
        gated_rows,
    )
    return (after_attention, saved_parts)


def attention_backward(after_grad, saved_parts, stream, shared):
    (
        gain_attention,
        query_weight,
        key_weight,
        value_weight,
        output_weight,
        value_router,
        output_router,
    ) = shared
    (
        normed_low,
        queries,
        key_rows,
        value_slope,
        output_slope,
        value_gates,
        output_gates,
        stream_low,
        projected,
        values,
        probability,
        weights_low,
        mixed,
        gated_rows,
    ) = saved_parts
    length = after_grad.shape[0]
    scale = 1.0 / math.sqrt(HEAD)
    after_low = after_grad.astype(jnp.bfloat16)
    output_part = jnp.einsum("sa,sb->ab", gated_rows, after_low, preferred_element_type=jnp.float32)
    gated_grad = jnp.einsum(
        "sb,ab->sa", after_low, output_weight, preferred_element_type=jnp.float32
    ).astype(jnp.bfloat16)
    gated_grad = gated_grad.reshape(length, HEADS, ATT_EXP, HEAD).astype(jnp.float32)
    mixed_grad = jnp.sum(output_gates[..., None] * gated_grad, axis=2).astype(jnp.bfloat16)
    output_gate_grad = jnp.sum(gated_grad * mixed[:, :, None, :], axis=3)
    prob_grad = jnp.einsum("qhd,khd->hqk", mixed_grad, values, preferred_element_type=jnp.float32)
    values_grad = jnp.einsum(
        "hqk,qhd->khd", weights_low, mixed_grad, preferred_element_type=jnp.float32
    ).astype(jnp.bfloat16)
    values_grad = values_grad.astype(jnp.float32)
    score_grad = (
        probability * (prob_grad - jnp.sum(probability * prob_grad, axis=-1, keepdims=True))
    ).astype(jnp.bfloat16)
    query_grad = (
        (
            jnp.einsum("hqk,khd->qhd", score_grad, key_rows, preferred_element_type=jnp.float32)
            * scale
        )
        .astype(jnp.bfloat16)
        .reshape(length, HEADS * HEAD)
    )
    key_grad = (
        (
            jnp.einsum("hqk,qhd->khd", score_grad, queries, preferred_element_type=jnp.float32)
            * scale
        )
        .astype(jnp.bfloat16)
        .reshape(length, HEADS * HEAD)
    )
    projected_grad = (
        (value_gates[..., None] * values_grad[:, :, None, :])
        .astype(jnp.bfloat16)
        .reshape(length, HEADS * ATT_EXP * HEAD)
    )
    value_gate_grad = jnp.sum(values_grad[:, :, None, :] * projected, axis=3)
    value_logit_grad = (
        (value_gate_grad * value_slope)
        .astype(jnp.bfloat16)
        .reshape(length, HEADS * ATT_EXP)
    )
    output_logit_grad = (
        (output_gate_grad * output_slope)
        .astype(jnp.bfloat16)
        .reshape(length, HEADS * ATT_EXP)
    )
    value_part = jnp.einsum(
        "sa,sb->ab", stream_low, projected_grad, preferred_element_type=jnp.float32
    )
    query_part = jnp.einsum("sa,sb->ab", normed_low, query_grad, preferred_element_type=jnp.float32)
    key_part = jnp.einsum("sa,sb->ab", normed_low, key_grad, preferred_element_type=jnp.float32)
    value_router_part = jnp.einsum(
        "sa,sb->ab", normed_low, value_logit_grad, preferred_element_type=jnp.float32
    )
    output_router_part = jnp.einsum(
        "sa,sb->ab", normed_low, output_logit_grad, preferred_element_type=jnp.float32
    )
    normed_grad = jnp.einsum(
        "sb,ab->sa", query_grad, query_weight, preferred_element_type=jnp.float32
    )
    normed_grad = normed_grad + jnp.einsum(
        "sb,ab->sa", key_grad, key_weight, preferred_element_type=jnp.float32
    )
    normed_grad = normed_grad + jnp.einsum(
        "sb,ab->sa", value_logit_grad, value_router, preferred_element_type=jnp.float32
    )
    normed_grad = normed_grad + jnp.einsum(
        "sb,ab->sa", output_logit_grad, output_router, preferred_element_type=jnp.float32
    )
    norm_value, norm_pull = jax.vjp(layer_norm, stream, gain_attention)
    stream_extra, gain_part = norm_pull(normed_grad)
    value_input = jnp.einsum(
        "sb,ab->sa", projected_grad, value_weight, preferred_element_type=jnp.float32
    )
    stream_grad = after_grad + stream_extra + value_input
    return (
        stream_grad,
        (
            gain_part,
            query_part,
            key_part,
            value_part,
            output_part,
            value_router_part,
            output_router_part,
        ),
    )


def expert_pass(rows, upstream_rows, gates, expert_first, expert_second):
    local_count, model_width, hidden_width = expert_first.shape
    wide = local_count * hidden_width
    first = expert_first.transpose(1, 0, 2).reshape(model_width, wide)
    second = expert_second.reshape(wide, model_width)
    gates_wide = jnp.repeat(gates.astype(jnp.float32), hidden_width, axis=1)
    hidden_pre = jnp.dot(rows, first, preferred_element_type=jnp.float32)
    hidden, gelu_pull = jax.vjp(jax.nn.gelu, hidden_pre)
    hidden = hidden.astype(jnp.bfloat16).astype(jnp.float32)
    gated_hidden = (gates_wide * hidden).astype(jnp.bfloat16)
    back = jnp.einsum("sd,fd->sf", upstream_rows, second, preferred_element_type=jnp.float32)
    gate_grad = jnp.sum((back * hidden).reshape(-1, local_count, hidden_width), axis=2)
    pre_grad = gelu_pull(gates_wide * back)[0].astype(jnp.bfloat16)
    result = jnp.dot(gated_hidden, second, preferred_element_type=jnp.float32)
    row_grad = jnp.einsum("sf,df->sd", pre_grad, first, preferred_element_type=jnp.float32)
    second_sum = jnp.einsum(
        "sf,sd->fd", gated_hidden, upstream_rows, preferred_element_type=jnp.float32
    )
    first_sum = jnp.einsum("sd,sf->df", rows, pre_grad, preferred_element_type=jnp.float32)
    first_sum = first_sum.reshape(model_width, local_count, hidden_width).transpose(1, 0, 2)
    return (
        result.astype(jnp.bfloat16),
        row_grad.astype(jnp.bfloat16),
        gate_grad.astype(jnp.bfloat16),
        first_sum,
        second_sum.reshape(expert_second.shape),
    )


BOTH = ("dp", "expert")


def expert_piece(after_low, upstream_low, dense_gates, expert_first, expert_second):
    local_count = expert_first.shape[0]
    me = lax.axis_index("dp") * lax.axis_size("expert") + lax.axis_index("expert")
    upstream_rows = lax.all_gather(upstream_low, BOTH, axis=0, tiled=True)
    rows = lax.all_gather(after_low, BOTH, axis=0, tiled=True)
    gates = lax.all_gather(dense_gates, BOTH, axis=0, tiled=True)
    gates = lax.dynamic_slice_in_dim(gates, me * local_count, local_count, axis=1)
    result, row_grad, gate_grad, first_sum, second_sum = expert_pass(
        rows, upstream_rows, gates, expert_first, expert_second
    )
    gate_back = lax.all_to_all(gate_grad, BOTH, split_axis=0, concat_axis=1, tiled=True)
    token_grad = lax.psum_scatter(row_grad, BOTH, scatter_dimension=0, tiled=True)
    result = lax.psum_scatter(result, BOTH, scatter_dimension=0, tiled=True)
    return (result, token_grad, gate_back), (first_sum, second_sum)


def expert_exchange(after_low, upstream_low, dense_gates, expert_first, expert_second, pieces):
    if pieces == 1:
        back, sums = expert_piece(
            after_low, upstream_low, dense_gates, expert_first, expert_second
        )
        return (*back, *sums)

    def step(totals, piece):
        back, sums = expert_piece(*piece, expert_first, expert_second)
        return (totals[0] + sums[0], totals[1] + sums[1]), back

    cut = lambda array: array.reshape(pieces, -1, array.shape[1])
    start = (
        jnp.zeros(expert_first.shape, jnp.float32),
        jnp.zeros(expert_second.shape, jnp.float32),
    )
    sums, back = lax.scan(step, start, (cut(after_low), cut(upstream_low), cut(dense_gates)))
    return (*(part.reshape(-1, part.shape[2]) for part in back), *sums)


MESH = pl.DeviceIdType.MESH
GRID = (4, 8)
N_SEM = 47
VMEM_LIMIT = 63 * 2**20


class Place:
    def __init__(self):
        dp, expert = lax.axis_index("dp"), lax.axis_index("expert")
        self.y, self.x = dp // 2, dp % 2
        self.z, self.core = expert // 2, expert % 2
        self.dp = dp
        self.me = dp * GRID[1] + expert
        self.x_peer = (2 * self.y + 1 - self.x, expert)
        self.y_peer = (2 * (1 - self.y) + self.x, expert)
        self.core_peer = (dp, 2 * self.z + 1 - self.core)
        self.middle = (self.z + self.z // 2) % 2
        self.main = 1 + self.z % 2
        self.minor = 3 * (self.z // 2)

    def along_z(self, z):
        return (self.dp, 2 * z + self.core)

    def z_at(self, j):
        near = j + self.middle * (1 - 2 * j) * (1 - j // 2)
        return near + self.z // 2 * (3 - 2 * near)

    def chip(self, q, j):
        return ((self.y + q // 2) % 2 * 2 + (self.x + q % 2) % 2) * 4 + self.z_at(j)

    def fixed(self, middle):
        known = Place.__new__(Place)
        known.__dict__.update(self.__dict__)
        known.middle = middle
        return known

    def if_middle(self, action):
        if not isinstance(self.middle, int):
            pl.when(self.middle == 1)(action)
        elif self.middle:
            action()


def enter(place):
    barrier = pltpu.get_barrier_semaphore()

    def signal(peer):
        pl.semaphore_signal(barrier, inc=1, device_id=peer, device_id_type=MESH)

    for peer in (place.x_peer, place.y_peer, place.core_peer, place.along_z(place.main)):
        signal(peer)
    place.if_middle(lambda: signal(place.along_z(place.minor)))
    pl.when(place.middle == 0)(lambda: pl.semaphore_wait(barrier, 4))
    place.if_middle(lambda: pl.semaphore_wait(barrier, 5))


def remote(src, dst, send, recv, peer):
    return pltpu.make_async_remote_copy(
        src_ref=src,
        dst_ref=dst,
        send_sem=send,
        recv_sem=recv,
        device_id=peer,
        device_id_type=MESH,
    )


CUTS = {
    "U": (2, 3),
    "X": (3, 3),
    "R": (3, 3),
    "Y": (2, 3),
    "O": (3, 2),
    "L": (10, 10),
    "GO": (3, 2),
    "GL": (10, 10),
}


def cut_columns(name, width):
    c_tiles, d_tiles = CUTS[name]
    return d_tiles * 128, width // 256 * 128, width - c_tiles * 128


class Gather:
    def __init__(self, name, place, buf, rows, sems, own=None):
        self.place, self.buf, self.rows, self.own = place, buf, rows, own
        self.width = buf.shape[1]
        self.d_end, self.split, self.c_start = cut_columns(name, self.width)
        self.send, self.recv = sems.at[0], sems.at[1]

    def block(self, q, j, columns=slice(None)):
        chip, core = self.place.chip(q, j), self.place.core
        start = (2 * chip + core if self.own is None else 16 * core + chip) * self.rows
        return self.buf.at[pl.ds(pl.multiple_of(start, self.rows), self.rows), columns]

    def copy(self, kind, j, q=0):
        place = self.place
        if kind == "x0":
            ref, number, peer = self.block(0, 0), 15, place.x_peer
        elif kind == "y0":
            ref, number, peer = self.block(0, 0), 19, place.y_peer
        elif kind == "x":
            ref, number, peer = self.block(0, j, slice(0, self.c_start)), 15 + j, place.x_peer
        elif kind == "y":
            ref, number, peer = self.block(0, j, slice(self.d_end, None)), 19 + j, place.y_peer
        elif kind == "a":
            ref, number, peer = self.block(1, j, slice(self.split, None)), 23 + j, place.y_peer
        elif kind == "b":
            ref, number, peer = self.block(2, j, slice(0, self.split)), 27 + j, place.x_peer
        else:
            ref, number, peer = self.block(q, j), 31 + 4 * q + j, place.core_peer
        if kind in ("a", "b"):
            return remote(ref, ref, self.send.at[number], self.recv.at[number], peer)
        return remote(self.source(ref, q, j), ref, self.send.at[number], self.recv.at[number], peer)

    def source(self, ref, q, j):
        mine = self.own is not None and isinstance(j, int) and q == 0 and j == 0
        return self.own if mine else ref

    def z_copy(self, part, j, number, z, receiver_j):
        columns = (slice(None), slice(self.c_start, None), slice(0, self.d_end))[part]
        ref = self.block(part, j, columns)
        return remote(
            self.source(ref, part, j),
            ref,
            self.send.at[5 * part + number],
            self.recv.at[3 * part + receiver_j - 1],
            self.place.along_z(z),
        )

    def z_own(self, part):
        place = self.place
        self.z_copy(part, 0, 0, place.main, 1 + place.middle).start()
        place.if_middle(lambda: self.z_copy(part, 0, 1, place.minor, 1).start())

    def z_pass(self, part, j):
        place = self.place
        first = 1 - (j + 2) // 4
        z = place.minor + first * (place.main - place.minor)
        return self.z_copy(part, j, 1 + j, z, j + 2 * first)

    def z_arrive(self, part, j):
        self.z_copy(part, j, 0, self.place.main, j).wait_recv()
        self.place.if_middle(lambda: self.z_pass(part, j).start())

    def begin(self):
        self.z_own(0)
        self.copy("x0", 0).start()
        self.copy("y0", 0).start()
        self.copy("core", 0, 0).start()

    def line(self, j):
        self.z_arrive(0, j)
        self.copy("x", j).start()
        self.copy("y", j).start()
        self.copy("core", j, 0).start()

    def side_x(self, j):
        self.copy("x" if j else "x0", j).wait_recv()
        self.copy("a", j).start()
        self.copy("core", j, 1).start()

    def side_y(self, j):
        self.copy("y" if j else "y0", j).wait_recv()
        self.copy("b", j).start()
        self.copy("core", j, 2).start()

    def own_c(self):
        self.z_own(1)

    def own_d(self):
        self.z_own(2)

    def pass_c(self, j):
        self.z_arrive(1, j)

    def pass_d(self, j):
        self.z_arrive(2, j)

    def corner(self, j):
        self.copy("a", j).wait_recv()
        self.copy("b", j).wait_recv()
        self.copy("core", j, 3).start()

    def whole(self, q, j):
        self.copy("core", j, q).wait_recv()

    def wait_all(self):
        def step(k, carry):
            self.whole(k // 4, k % 4)
            return carry

        lax.fori_loop(0, 16, step, 0)

    def finish(self):
        place = self.place
        for part in range(3):
            self.z_copy(part, 0, 0, place.main, 1).wait_send()

        def middle():
            for part in range(3):
                self.z_copy(part, 0, 1, place.minor, 1).wait_send()

                def passed(j, carry):
                    self.z_pass(part, j).wait_send()
                    return carry

                lax.fori_loop(1, 4, passed, 0)

        place.if_middle(middle)
        self.copy("x0", 0).wait_send()
        self.copy("y0", 0).wait_send()

        def line(j, carry):
            self.copy("x", j).wait_send()
            self.copy("y", j).wait_send()
            return carry

        lax.fori_loop(1, 4, line, 0)

        def step(j, carry):
            self.copy("a", j).wait_send()
            self.copy("b", j).wait_send()
            for q in range(4):
                self.copy("core", j, q).wait_send()
            return carry

        lax.fori_loop(0, 4, step, 0)


class Reduce:
    def __init__(self, name, place, own, other, boxes, sems, held=None):
        self.place, self.other = place, other
        if other is not None:
            self.other_in, boxes = boxes[0], boxes[1:]
        self.a_in, self.b_in, self.x_in, self.y_in = boxes[:4]
        self.own = own or (lambda k: self.other_in.at[k])
        self.extra = held or (lambda k: self.other_in.at[k])
        self.z_in = boxes[4:]
        self.rows, self.width = self.x_in.shape[1:]
        self.d_end, self.split, self.c_start = cut_columns(name, self.width)
        self.send, self.recv = sems.at[0], sems.at[1]

    def copy(self, kind, k):
        place = self.place
        j = k % 4
        if kind == "core":
            src, dst, number, peer = self.other(k), self.other_in.at[k], k, place.core_peer
        elif kind == "a":
            src = self.own(k).at[:, self.split :]
            dst, number, peer = self.a_in.at[j], 16 + j, place.y_peer
        elif kind == "b":
            src = self.own(k).at[:, : self.split]
            dst, number, peer = self.b_in.at[j], 20 + j, place.x_peer
        elif kind == "x0":
            src, dst, number, peer = self.own(k), self.x_in.at[0], 24, place.x_peer
        elif kind == "y0":
            src, dst, number, peer = self.own(k), self.y_in.at[0], 28, place.y_peer
        elif kind == "x":
            src = self.own(k).at[:, : self.c_start]
            dst, number, peer = self.x_in.at[j, :, : self.c_start], 24 + j, place.x_peer
        else:
            src = self.own(k).at[:, self.d_end :]
            dst, number, peer = self.y_in.at[j, :, self.d_end :], 28 + j, place.y_peer
        return remote(src, dst, self.send.at[number], self.recv.at[number], peer)

    def z_columns(self, part):
        return (slice(None), slice(self.c_start, None), slice(0, self.d_end))[part]

    def z_copy(self, part, j):
        place = self.place
        first = 1 - (j + 2) // 4
        box = place.middle * (j // 3) + (1 - place.middle) * (j + 1)
        z = place.main + place.middle * first * (place.minor - place.main)
        return remote(
            self.own(4 * part + j).at[:, self.z_columns(part)],
            self.z_in[part].at[box],
            self.send.at[32 + 5 * part + j],
            self.recv.at[32 + 5 * part + box],
            place.along_z(z),
        )

    def z_wait(self, part, box):
        self.copy_box(part, box).wait_recv()

    def copy_box(self, part, box):
        ref = self.z_in[part].at[box]
        return remote(
            ref,
            ref,
            self.send.at[32 + 5 * part],
            self.recv.at[32 + 5 * part + box],
            self.place.along_z(self.place.main),
        )

    def z_give(self, part, j):
        def middle():
            box = j + (j + 2) // 4
            self.z_wait(part, box)
            self.add(4 * part + j, self.z_columns(part), [lambda at: self.z_in[part][box, at, :]])

        self.place.if_middle(middle)
        self.z_copy(part, j).start()

    def z_last(self, part):
        columns = self.z_columns(part)
        self.z_wait(part, 0)
        self.add(4 * part, columns, [lambda at: self.z_in[part][0, at, :]])

        def middle():
            self.z_wait(part, 2)
            self.add(4 * part, columns, [lambda at: self.z_in[part][2, at, :]])

        self.place.if_middle(middle)

    def add(self, k, columns, terms):
        own = self.own(k)

        def step(number, carry):
            at = pl.ds(pl.multiple_of(number * 16, 16), 16)
            total = own[at, columns].astype(jnp.float32)
            for term in terms:
                total = total + term(at).astype(jnp.float32)
            own[at, columns] = total.astype(own.dtype)
            return carry

        lax.fori_loop(0, self.rows // 16, step, 0)

    def meet(self, k):
        if self.other is None:
            return []
        self.copy("core", k).wait_recv()
        return [self.extra(k)]

    def add_columns(self, k, columns, boxes):
        if boxes:
            self.add(k, columns, [lambda at, box=box: box[at, :] for box in boxes])

    def corner(self, j):
        k = 12 + j
        self.add_columns(k, slice(None), self.meet(k))
        self.copy("a", k).start()
        self.copy("b", k).start()

    def side_x(self, j):
        k, split = 4 + j, self.split
        shares = self.meet(k)
        self.add_columns(k, slice(0, split), [share.at[:, :split] for share in shares])
        self.copy("a", k).wait_recv()
        shares = [share.at[:, split:] for share in shares]
        self.add_columns(k, slice(split, None), [*shares, self.a_in.at[j]])
        if j:
            self.copy("x", k).start()

    def side_y(self, j):
        k, split = 8 + j, self.split
        shares = self.meet(k)
        self.add_columns(k, slice(split, None), [share.at[:, split:] for share in shares])
        self.copy("b", k).wait_recv()
        shares = [share.at[:, :split] for share in shares]
        self.add_columns(k, slice(0, split), [*shares, self.b_in.at[j]])
        if j:
            self.copy("y", k).start()

    def give_c(self, j):
        if j:
            self.z_give(1, j)
        else:
            self.z_last(1)
            self.copy("x0", 4).start()

    def give_d(self, j):
        if j:
            self.z_give(2, j)
        else:
            self.z_last(2)
            self.copy("y0", 8).start()

    def hand_over(self):
        def step(number, carry):
            self.copy("core", 15 - number).start()
            return carry

        lax.fori_loop(0, 16, step, 0)

    def line(self, j):
        shares = self.meet(j)
        self.copy("x", j).wait_recv()
        self.copy("y", j).wait_recv()
        d_end, c_start = self.d_end, self.c_start
        x_box, y_box = self.x_in.at[j], self.y_in.at[j]
        for columns, used in (
            (slice(0, d_end), [*shares, x_box]),
            (slice(d_end, c_start), [*shares, x_box, y_box]),
            (slice(c_start, None), [*shares, y_box]),
        ):
            self.add_columns(j, columns, [box.at[:, columns] for box in used])
        self.z_give(0, j)

    def last(self, put):
        shares = self.meet(0)
        self.copy("x0", 0).wait_recv()
        self.copy("y0", 0).wait_recv()
        self.z_wait(0, 0)
        own = self.own(0)

        def sum_up(middle):
            def step(number, carry):
                at = pl.ds(pl.multiple_of(number * 16, 16), 16)
                total = own[at, :].astype(jnp.float32)
                for box in (*shares, self.x_in.at[0], self.y_in.at[0], self.z_in[0].at[0]):
                    total = total + box[at, :].astype(jnp.float32)
                if middle:
                    total = total + self.z_in[0][2, at, :].astype(jnp.float32)
                put(at, total)
                return carry

            lax.fori_loop(0, own.shape[0] // 16, step, 0)

        if self.place.middle:
            self.z_wait(0, 2)
        sum_up(self.place.middle == 1)

    def finish(self):
        def step(j, carry):
            self.copy("a", 12 + j).wait_send()
            self.copy("b", 12 + j).wait_send()
            for q in range(4 if self.other else 0):
                self.copy("core", 4 * q + j).wait_send()
            return carry

        lax.fori_loop(0, 4, step, 0)

        def outer(j, carry):
            self.copy("x", 4 + j).wait_send()
            self.copy("y", 8 + j).wait_send()
            for part in range(3):
                self.z_copy(part, j).wait_send()
            return carry

        lax.fori_loop(1, 4, outer, 0)
        self.copy("x0", 4).wait_send()
        self.copy("y0", 8).wait_send()


def reduce_scratch(name, rows, width, paired=False):
    low = jnp.bfloat16
    d_end, split, c_start = cut_columns(name, width)
    return [
        *([] if paired else [pltpu.VMEM((16, rows, width), low)]),
        pltpu.VMEM((4, rows, width - split), low),
        pltpu.VMEM((4, rows, split), low),
        pltpu.VMEM((4, rows, width), low),
        pltpu.VMEM((4, rows, width), low),
        pltpu.VMEM((5, rows, width), low),
        pltpu.VMEM((5, rows, width - c_start), low),
        pltpu.VMEM((5, rows, d_end), low),
    ]


GELU_C = math.sqrt(2.0 / math.pi)
GELU_K = 0.044715


def mm(left, right):
    return jnp.dot(left, right, preferred_element_type=jnp.float32)


def mm_tn(left, right):
    return lax.dot_general(left, right, (((0,), (0,)), ((), ())), preferred_element_type=jnp.float32)


def norm_parts(stream):
    average = jnp.mean(stream, axis=-1, keepdims=True)
    centred = stream - average
    variance = jnp.mean(centred * centred, axis=-1, keepdims=True)
    scale = lax.rsqrt(variance + 1e-05)
    return centred * scale, scale


def norm_pull(normed_grad, unit, scale, gain):
    inner = normed_grad * gain
    mean = jnp.mean(inner, axis=-1, keepdims=True)
    along = jnp.mean(inner * unit, axis=-1, keepdims=True)
    gain_grad = jnp.sum(normed_grad * unit, axis=0, keepdims=True)
    return scale * (inner - mean - unit * along), gain_grad


def mm_nt(left, right):
    return lax.dot_general(left, right, (((1,), (1,)), ((), ())), preferred_element_type=jnp.float32)


OUTPUT_LANE = 32


def join_routers(joined, value_router_ref, output_router_ref):
    count = value_router_ref.shape[0]
    joined[...] = jnp.zeros_like(joined)
    joined[:count, :] = value_router_ref[...]
    joined[OUTPUT_LANE : OUTPUT_LANE + count, :] = output_router_ref[...]


HELD = 6
GAIN_LANE = 64


FETCHED = (
    ("rows", "after", "expert_slope", "cotangent"),
    (
        "tokens",
        "queries",
        "keys",
        "projected",
        "values",
        "probability",
        "mixed",
        "gates",
        "slopes",
    ),
)
PAIRED = ("gated", "tokens", "normed", "normed_ffn")
FETCHED_NAMES = tuple(name for group in FETCHED for name in group)


def backward_kernel(
    gain_attention_ref,
    gain_feedforward_ref,
    value_router_ref,
    output_router_ref,
    expert_router_ref,
    query_in,
    key_in,
    value_in,
    output_in,
    result_in,
    block_out,
    stream_out,
    low_out,
    output_low_out,
    query_ref,
    key_ref,
    value_ref,
    output_ref,
    routers,
    expert_router,
    after_grad,
    gated_grad,
    held,
    low_part,
    output_part,
    low_own,
    output_own,
    gated_pair,
    tokens_pair,
    normed_pair,
    normed_ffn_pair,
    after_pair,
    projected_pair,
    both_pair,
    small_pair,
    gain_pair,
    gain_rows,
    weight_sems,
    held_sems,
    own_sems,
    fetch_sems,
    pair_sems,
    *refs,
):
    place = Place()
    count = len(FETCHED_NAMES)
    fetched_in, refs = refs[:count], refs[count:]
    paired_in, refs = refs[: len(PAIRED)], refs[len(PAIRED) :]
    fetched_refs, refs = refs[:count], refs[count:]
    fetched_ref = dict(zip(FETCHED_NAMES, fetched_refs))
    fetches = {
        name: pltpu.make_async_copy(src, dst, fetch_sems.at[number])
        for number, (name, src, dst) in enumerate(zip(FETCHED_NAMES, fetched_in, fetched_refs))
    }

    def fetched_now(group):
        for name in FETCHED[group]:
            fetches[name].wait()

    rows_ref = fetched_ref["rows"]
    after_ref = fetched_ref["after"]
    expert_slope_ref = fetched_ref["expert_slope"]
    cotangent_ref = fetched_ref["cotangent"]
    tokens_ref = fetched_ref["tokens"]
    queries_ref = fetched_ref["queries"]
    keys_ref = fetched_ref["keys"]
    projected_ref = fetched_ref["projected"]
    values_ref = fetched_ref["values"]
    probability_ref = fetched_ref["probability"]
    mixed_ref = fetched_ref["mixed"]
    gates_ref = fetched_ref["gates"]
    slopes_ref = fetched_ref["slopes"]
    length, model_width = tokens_ref.shape
    wide = value_ref.shape[1]
    narrow = query_ref.shape[1]
    expert_count = expert_router_ref.shape[0]
    low_rows, output_rows = low_own.shape[0], output_own.shape[0]
    low_type = jnp.bfloat16

    def other_rows(ref, rows, place):
        def get(k):
            start = (2 * place.chip(k // 4, k % 4) + 1 - place.core) * rows
            return ref.at[pl.ds(pl.multiple_of(start, rows), rows)]

        return get

    def chip_rows(ref, rows, place):
        def get(k):
            start = place.chip(k // 4, k % 4) * rows
            return ref.at[pl.ds(pl.multiple_of(start, rows), rows)]

        return get

    mine = pl.ds(pl.multiple_of(place.core * length, length), length)
    after_low, projected_grad = after_pair.at[mine], projected_pair.at[mine]
    both_grad, small_grad = both_pair.at[mine], small_pair.at[mine]
    paired = {}
    pair_locals = []
    for number, (src, dst) in enumerate(
        zip(paired_in, (gated_pair, tokens_pair, normed_pair, normed_ffn_pair))
    ):
        width = dst.shape[1]
        kept = pl.ds(pl.multiple_of(place.core * width, width), width)
        given = pl.ds(pl.multiple_of((1 - place.core) * width, width), width)
        pair_locals.append(
            pltpu.make_async_copy(src.at[:, kept], dst.at[mine], pair_sems.at[2, number])
        )
        paired[PAIRED[number]] = (src.at[:, given], dst.at[mine], number)
    paired["after"] = (after_low, after_low, 4)
    paired["projected"] = (projected_grad, projected_grad, 5)
    paired["both"] = (both_grad, both_grad, 6)
    paired["small"] = (small_grad, small_grad, 7)
    paired["gain"] = (gain_pair.at[place.core], gain_pair.at[place.core], 8)

    def pair_copy(name):
        src, dst, number = paired[name]
        return remote(src, dst, pair_sems.at[0, number], pair_sems.at[1, number], place.core_peer)

    def half(ref):
        width = ref.shape[1] // 2
        return ref[:, pl.ds(pl.multiple_of(place.core * width, width), width)]

    weights = ((output_in, output_ref), (query_in, query_ref), (key_in, key_ref), (value_in, value_ref))
    loads = [
        pltpu.make_async_copy(src, dst, weight_sems.at[number])
        for number, (src, dst) in enumerate(weights)
    ]
    tile = 256
    small_column = wide + 2 * narrow
    expert_column = small_column + 128
    first_base = {"corner": 12, "side_x": 4, "side_y": 8, "line": 0, "last": 0}
    values = {}

    def c1():
        fetched_now(0)
        join_routers(routers, value_router_ref, output_router_ref)
        expert_router[...] = jnp.zeros_like(expert_router)
        expert_router[:expert_count, :] = expert_router_ref[...]
        logit_grad = (rows_ref[:, model_width:] * expert_slope_ref[...]).astype(low_type)
        small_grad[:, 128:] = logit_grad
        unit, scale = norm_parts(after_ref[...])
        through, values["gain_feedforward"] = norm_pull(
            mm(logit_grad, expert_router[...]), unit, scale, gain_feedforward_ref[...]
        )
        after_grad[...] = cotangent_ref[...].astype(jnp.float32) + rows_ref[:, :model_width] + through
        after_low[...] = after_grad[...].astype(low_type)
        pair_copy("after").start()

    def c2():
        pair_copy("after").wait_recv()
        pair_copy("gated").wait_recv()
        pair_locals[0].wait()

        def output_tile(number, carry):
            at = pl.ds(pl.multiple_of(number * tile, tile), tile)
            output_part[at, :] = mm_tn(gated_pair[:, at], after_pair[...]).astype(low_type)
            return carry

        lax.fori_loop(0, output_part.shape[0] // tile, output_tile, 0)

    def c3():
        loads[0].wait()

        def gated_tile(number, carry):
            at = pl.ds(pl.multiple_of(number * tile, tile), tile)
            gated_grad[:, at] = mm_nt(after_low[...], output_ref[at, :]).astype(low_type)
            return carry

        lax.fori_loop(0, wide // tile, gated_tile, 0)

    def c4():
        fetched_now(1)
        lane = lax.broadcasted_iota(jnp.int32, (length, 128), 1)
        gate_grads = jnp.zeros((length, 128), jnp.float32)
        inverse = 1.0 / math.sqrt(HEAD)
        for head in range(HEADS):
            columns = slice(head * HEAD, (head + 1) * HEAD)
            mixed = mixed_ref[:, columns]
            mixed_grad = jnp.zeros((length, HEAD), jnp.float32)
            for e in range(ATT_EXP):
                at = head * ATT_EXP + e
                part = gated_grad[:, at * HEAD : (at + 1) * HEAD].astype(jnp.float32)
                lane_at = OUTPUT_LANE + at
                mixed_grad = mixed_grad + gates_ref[:, lane_at : lane_at + 1] * part
                gate_grads = jnp.where(
                    lane == lane_at, jnp.sum(part * mixed, axis=1, keepdims=True), gate_grads
                )
            mixed_grad = mixed_grad.astype(low_type)
            probability = probability_ref[head]
            prob_grad = mm_nt(mixed_grad, values_ref[:, columns])
            inner = jnp.sum(probability * prob_grad, axis=-1, keepdims=True)
            score_grad = (probability * (prob_grad - inner)).astype(low_type)
            both_grad[:, columns] = (mm(score_grad, keys_ref[:, columns]) * inverse).astype(low_type)
            both_grad[:, narrow + head * HEAD : narrow + (head + 1) * HEAD] = (
                mm_tn(score_grad, queries_ref[:, columns]) * inverse
            ).astype(low_type)
            values_grad = mm_tn(probability.astype(low_type), mixed_grad)
            values_grad = values_grad.astype(low_type).astype(jnp.float32)
            for e in range(ATT_EXP):
                at = head * ATT_EXP + e
                wide_at = slice(at * HEAD, (at + 1) * HEAD)
                projected_grad[:, wide_at] = (gates_ref[:, at : at + 1] * values_grad).astype(low_type)
                gate_grad = jnp.sum(values_grad * projected_ref[:, wide_at], axis=1, keepdims=True)
                gate_grads = jnp.where(lane == at, gate_grad, gate_grads)
        small_grad[:, :128] = (gate_grads * slopes_ref[...]).astype(low_type)
        for name in ("both", "projected", "small"):
            pair_copy(name).start()

    def c5a():
        pair_copy("projected").wait_recv()
        pair_copy("tokens").wait_recv()
        pair_locals[1].wait()

        def value_tile(number, carry):
            at = pl.ds(pl.multiple_of(number * tile, tile), tile)
            to = pl.ds(pl.multiple_of(2 * narrow + number * tile, tile), tile)
            low_part[:, to] = mm_tn(tokens_pair[...], projected_pair[:, at]).astype(low_type)
            return carry

        lax.fori_loop(0, wide // tile, value_tile, 0)

    def c5b():
        pair_copy("both").wait_recv()
        pair_copy("normed").wait_recv()
        pair_locals[2].wait()

        def both_tile(number, carry):
            at = pl.ds(pl.multiple_of(number * tile, tile), tile)
            low_part[:, at] = mm_tn(normed_pair[...], both_pair[:, at]).astype(low_type)
            return carry

        lax.fori_loop(0, 2 * narrow // tile, both_tile, 0)

    def c6():
        loads[1].wait()
        loads[2].wait()
        normed_grad = mm_nt(both_grad[:, :narrow], query_ref[...])
        normed_grad = normed_grad + mm_nt(both_grad[:, narrow:], key_ref[...])
        normed_grad = normed_grad + mm(small_grad[:, :128], routers[...])
        unit, scale = norm_parts(tokens_ref[...].astype(jnp.float32))
        through, gain_attention_grad = norm_pull(normed_grad, unit, scale, gain_attention_ref[...])
        after_grad[...] += through
        row = lax.broadcasted_iota(jnp.int32, gain_pair.shape[1:], 0)
        gain_pair[place.core] = jnp.where(
            row == 0, gain_attention_grad, jnp.where(row == 1, values["gain_feedforward"], 0.0)
        )
        pair_copy("gain").start()

    def c8():
        pair_copy("small").wait_recv()
        pair_copy("gain").wait_recv()
        pair_copy("normed_ffn").wait_recv()
        pair_locals[3].wait()
        gain_rows[...] = jnp.zeros_like(gain_rows)
        gain_rows[GAIN_LANE : GAIN_LANE + 8, :] = gain_pair[0] + gain_pair[1]
        small = mm_tn(normed_pair[...], small_pair[:, :128]) + half(gain_rows).T
        low_part[:, small_column:expert_column] = small.astype(low_type)
        low_part[:, expert_column:] = mm_tn(normed_ffn_pair[...], small_pair[:, 128:]).astype(low_type)

    def c7():
        loads[3].wait()
        through_values = mm_nt(projected_grad[...], value_ref[...])
        stream_out[...] = through_values

    computes = {"c1": c1, "c2": c2, "c3": c3, "c4": c4, "c5a": c5a, "c5b": c5b, "c6": c6, "c7": c7, "c8": c8}

    def run(middle):
        known = place.fixed(middle)
        order = BACKWARD_ORDER[middle]
        held_order = [
            first_base[event[1]] + (event[2] if len(event) > 2 else 0)
            for event in order
            if event[0] == "Y" and event[1] in first_base
        ]
        slots = {k: number % HELD for number, k in enumerate(held_order)}

        def held_copy(number):
            k = held_order[number]
            start = (2 * known.chip(k // 4, k % 4) + known.core) * length
            return pltpu.make_async_copy(
                result_in.at[pl.ds(pl.multiple_of(start, length), length)],
                held.at[number % HELD],
                held_sems.at[number % HELD],
            )

        reduces = {
            "Y": Reduce(
                "Y",
                known,
                None,
                other_rows(result_in, length, known),
                refs[0:8],
                refs[8],
                lambda k: held.at[slots[k]],
            ),
            "O": Reduce(
                "O",
                known,
                chip_rows(output_part, output_rows, known),
                None,
                refs[9:16],
                refs[16],
            ),
            "L": Reduce(
                "L",
                known,
                chip_rows(low_part, low_rows, known),
                None,
                refs[17:24],
                refs[24],
            ),
        }
        gathers = {
            "GO": Gather("GO", known, output_low_out, output_rows, refs[25], output_own),
            "GL": Gather("GL", known, low_out, low_rows, refs[26], low_own),
        }
        owns = {"O": ("GO", output_own, own_sems.at[0]), "L": ("GL", low_own, own_sems.at[1])}
        own_copies = {
            target: pltpu.make_async_copy(own, gathers[target].block(0, 0), sem)
            for target, own, sem in owns.values()
        }

        def last(name):
            if name == "Y":

                def put(at, total):
                    block_out[at, :] = (after_ref[at, :] + total).astype(low_type)

            else:
                target, own, _ = owns[name]

                def put(at, total):
                    own[at, :] = total.astype(low_type)

            reduces[name].last(put)
            if name != "Y":
                own_copies[target].start()

        for number in range(HELD):
            held_copy(number).start()
        fetched = 0
        last_sum = max(number for number, event in enumerate(order) if event[0] in reduces)
        for number, (name, method, *arguments) in enumerate(order):
            if number == last_sum + 8:
                for reduce in reduces.values():
                    reduce.finish()
            if name == "C":
                computes[method]()
                continue
            uses_held = name == "Y" and method in first_base
            if uses_held:
                held_copy(fetched).wait()
            if method == "last":
                last(name)
            else:
                getattr({**reduces, **gathers}[name], method)(*arguments)
            if uses_held:
                if fetched + HELD < len(held_order):
                    held_copy(fetched + HELD).start()
                fetched += 1
        for copy in own_copies.values():
            copy.wait()
        for item in gathers.values():
            item.finish()

    for copy in (*fetches.values(), *pair_locals, *loads):
        copy.start()
    enter(place)
    for name in PAIRED:
        pair_copy(name).start()
    pl.when(place.middle == 0)(lambda: run(0))
    pl.when(place.middle == 1)(lambda: run(1))
    for name in paired:
        pair_copy(name).wait_send()
    stream_out[...] += after_grad[...]


def call_backward(rows, tokens, cotangent, gains, routers, saved, weights, result):
    length, model_width = tokens.shape
    total = GRID[0] * GRID[1]
    wide, narrow = weights[2].shape[1], weights[0].shape[1]
    low_width = wide + 2 * narrow + 256
    low_rows, output_rows = model_width // total, wide // total
    low, full = jnp.bfloat16, jnp.float32
    vmem = pl.BlockSpec(memory_space=pltpu.VMEM)
    hbm = pl.BlockSpec(memory_space=pl.ANY)
    sems = pltpu.SemaphoreType.DMA((2, N_SEM))
    names = (
        "after",
        "normed",
        "normed_ffn",
        "queries",
        "keys",
        "projected",
        "values",
        "probability",
        "mixed",
        "gated",
        "gates",
        "slopes",
        "expert_slope",
    )
    sources = dict(zip(names, saved), rows=rows, tokens=tokens, cotangent=cotangent)
    fetched = [sources[name] for name in FETCHED_NAMES]
    paired = [sources[name] for name in PAIRED]
    inputs, outputs, scratch = 10, 4, 28
    copied = inputs + len(fetched) + len(paired)

    def kernel(*refs):
        copied_in, refs = refs[inputs:copied], refs[:inputs] + refs[copied:]
        head = inputs + outputs + scratch
        backward_kernel(*refs[:head], *copied_in, *refs[head:])

    return pl.pallas_call(
        kernel,
        out_shape=(
            jax.ShapeDtypeStruct((length, model_width), low),
            jax.ShapeDtypeStruct((length, model_width), full),
            jax.ShapeDtypeStruct((model_width, low_width), low),
            jax.ShapeDtypeStruct((wide, model_width), low),
        ),
        in_specs=[vmem] * 5 + [hbm] * (5 + len(fetched) + len(paired)),
        out_specs=(vmem, vmem, hbm, hbm),
        scratch_shapes=[
            *(pltpu.VMEM(weight.shape, low) for weight in weights),
            pltpu.VMEM((128, model_width), low),
            pltpu.VMEM((128, model_width), low),
            pltpu.VMEM((length, model_width), full),
            pltpu.VMEM((length, wide), low),
            pltpu.VMEM((HELD, length, model_width), low),
            pltpu.VMEM((model_width // 2, low_width), low),
            pltpu.VMEM((wide // 2, model_width), low),
            pltpu.VMEM((low_rows, low_width), low),
            pltpu.VMEM((output_rows, model_width), low),
            *(pltpu.VMEM((2 * length, array.shape[1] // 2), low) for array in paired),
            pltpu.VMEM((2 * length, model_width), low),
            pltpu.VMEM((2 * length, wide), low),
            pltpu.VMEM((2 * length, 2 * narrow), low),
            pltpu.VMEM((2 * length, 256), low),
            pltpu.VMEM((2, 8, model_width), full),
            pltpu.VMEM((128, model_width), full),
            pltpu.SemaphoreType.DMA((4,)),
            pltpu.SemaphoreType.DMA((HELD,)),
            pltpu.SemaphoreType.DMA((2,)),
            pltpu.SemaphoreType.DMA((len(fetched),)),
            pltpu.SemaphoreType.DMA((3, 9)),
            *(pltpu.VMEM(array.shape, array.dtype) for array in fetched),
            *reduce_scratch("Y", length, model_width),
            sems,
            *reduce_scratch("O", output_rows, model_width, True),
            sems,
            *reduce_scratch("L", low_rows, low_width, True),
            sems,
            sems,
            sems,
        ],
        compiler_params=pltpu.CompilerParams(
            collective_id=1, has_side_effects=True, vmem_limit_bytes=VMEM_LIMIT
        ),
        name="backward",
    )(*gains, *routers, *weights, result, *fetched, *paired)


def widen_kernel(
    low_ref,
    output_low_ref,
    first_ref,
    second_ref,
    block_ref,
    stream_ref,
    query,
    key,
    value,
    output,
    value_router,
    output_router,
    expert_router,
    gain_attention,
    gain_feedforward,
    first,
    second,
    block,
    stream,
):
    full = jnp.float32
    narrow, wide = query.shape[1], value.shape[1]
    query[...] = low_ref[:, :narrow].astype(full)
    key[...] = low_ref[:, narrow : 2 * narrow].astype(full)
    value[...] = low_ref[:, 2 * narrow : 2 * narrow + wide].astype(full)
    output[...] = output_low_ref[...].astype(full)
    start = 2 * narrow + wide
    small = low_ref[:, start : start + 128].astype(full).T
    count = value_router.shape[0]
    value_router[...] = small[:count]
    output_router[...] = small[OUTPUT_LANE : OUTPUT_LANE + count]
    gain_attention[...] = small[GAIN_LANE : GAIN_LANE + 1]
    gain_feedforward[...] = small[GAIN_LANE + 1 : GAIN_LANE + 2]
    expert_router[...] = low_ref[:, start + 128 :].astype(full).T[: expert_router.shape[0]]
    hidden_width = second.shape[1]
    for e in range(first.shape[0]):
        rows = slice(e * hidden_width, (e + 1) * hidden_width)
        first[e] = first_ref[rows, :].T
        second[e] = second_ref[rows, :]
    block[...] = block_ref[...]
    stream[...] = stream_ref[...]


def call_widen(low, output_low, first_sum, second_sum, block_output, stream_grad, narrow, expert_count, local_count):
    model_width, low_width = low.shape
    wide = output_low.shape[0]
    hidden = first_sum.shape[0]
    hidden_width = hidden // local_count
    length = block_output.shape[0]
    steps = 2
    height = model_width // steps
    full = jnp.float32
    router_width = HEADS * ATT_EXP
    rows = lambda count, width: pl.BlockSpec((count, width), lambda i: (i, 0))
    columns = lambda count: pl.BlockSpec((count, height), lambda i: (0, i))
    first_spec = pl.BlockSpec((local_count, height, hidden_width), lambda i: (0, i, 0))
    second_spec = pl.BlockSpec((local_count, hidden_width, height), lambda i: (0, 0, i))
    shape = lambda *dims, kind=full: jax.ShapeDtypeStruct(dims, kind)
    return pl.pallas_call(
        widen_kernel,
        grid=(steps,),
        out_shape=(
            shape(model_width, narrow),
            shape(model_width, narrow),
            shape(model_width, wide),
            shape(wide, model_width),
            shape(router_width, model_width),
            shape(router_width, model_width),
            shape(expert_count, model_width),
            shape(1, model_width),
            shape(1, model_width),
            shape(local_count, model_width, hidden_width),
            shape(local_count, hidden_width, model_width),
            shape(length, model_width, kind=block_output.dtype),
            shape(length, model_width),
        ),
        in_specs=[
            rows(height, low_width),
            rows(wide // steps, model_width),
            columns(hidden),
            columns(hidden),
            rows(length // steps, model_width),
            rows(length // steps, model_width),
        ],
        out_specs=(
            rows(height, narrow),
            rows(height, narrow),
            rows(height, wide),
            rows(wide // steps, model_width),
            columns(router_width),
            columns(router_width),
            columns(expert_count),
            columns(1),
            columns(1),
            first_spec,
            second_spec,
            rows(length // steps, model_width),
            rows(length // steps, model_width),
        ),
        compiler_params=pltpu.CompilerParams(vmem_limit_bytes=VMEM_LIMIT),
        name="widen",
    )(low, output_low, first_sum, second_sum, block_output, stream_grad)


BACKWARD_ORDER = (
    (
        ("Y", "hand_over"), ("Y", "corner", 3), ("Y", "corner", 2), ("C", "c1"), ("Y", "side_x",
        3), ("Y", "give_c", 3), ("Y", "side_y", 3), ("C", "c3"), ("Y", "side_y", 2), ("Y",
        "give_d", 3), ("C", "c2"), ("O", "corner", 2), ("O", "corner", 3), ("Y", "give_d", 2),
        ("Y", "side_x", 2), ("Y", "line", 3), ("O", "corner", 1), ("C", "c4"), ("O", "side_x",
        3), ("O", "corner", 0), ("O", "give_c", 3), ("O", "side_y", 3), ("O", "give_d", 3),
        ("Y", "line", 2), ("O", "side_x", 2), ("O", "side_y", 2), ("Y", "corner", 0), ("Y",
        "give_c", 2), ("O", "side_x", 1), ("O", "give_c", 2), ("O", "side_y", 1), ("C", "c5a"),
        ("C", "c6"), ("Y", "corner", 1), ("O", "give_d", 2), ("O", "line", 3), ("C", "c5b"),
        ("C", "c8"), ("L", "corner", 3), ("Y", "side_y", 0), ("L", "corner", 2), ("O", "line",
        1), ("O", "give_c", 1), ("O", "line", 2), ("L", "side_x", 3), ("O", "side_y", 0), ("L",
        "side_y", 3), ("L", "side_y", 2), ("L", "give_c", 3), ("L", "side_x", 2), ("L",
        "corner", 1), ("L", "give_d", 3), ("O", "side_x", 0), ("O", "give_d", 1), ("O",
        "give_d", 0), ("O", "give_c", 0), ("L", "give_c", 2), ("Y", "side_x", 1), ("L", "line",
        3), ("L", "corner", 0), ("Y", "give_c", 1), ("O", "last"), ("GO", "begin"), ("L",
        "side_x", 1), ("Y", "side_x", 0), ("Y", "side_y", 1), ("L", "give_d", 2), ("Y",
        "give_d", 0), ("L", "side_x", 0), ("Y", "give_d", 1), ("GO", "side_y", 0), ("L", "line",
        2), ("Y", "give_c", 0), ("GO", "own_d"), ("L", "side_y", 0), ("L", "give_c", 1), ("L",
        "side_y", 1), ("L", "give_c", 0), ("L", "give_d", 1), ("C", "c7"), ("Y", "line", 1),
        ("L", "give_d", 0), ("GO", "pass_d", 1), ("L", "line", 1), ("GO", "line", 1), ("GO",
        "pass_c", 1), ("GO", "line", 2), ("L", "last"), ("Y", "last"), ("GL", "begin"), ("GO",
        "side_x", 1), ("GO", "pass_d", 2), ("GL", "side_y", 0), ("GO", "side_x", 0), ("GO",
        "side_y", 1), ("GO", "pass_c", 2), ("GL", "side_x", 0), ("GO", "side_x", 2), ("GO",
        "own_c"), ("GO", "pass_d", 3), ("GL", "own_d"), ("GO", "side_y", 2), ("GO", "line", 3),
        ("GL", "line", 1), ("GO", "side_y", 3), ("GL", "own_c"), ("GL", "line", 2), ("GO",
        "corner", 0), ("GL", "line", 3), ("GO", "corner", 2), ("GO", "pass_c", 3), ("GL",
        "pass_c", 1), ("GL", "pass_d", 1), ("GL", "side_x", 1), ("GO", "side_x", 3), ("GL",
        "side_y", 1), ("GL", "corner", 0), ("GL", "pass_c", 2), ("GL", "side_x", 2), ("GL",
        "pass_d", 2), ("GL", "side_y", 2), ("GL", "pass_d", 3), ("GO", "corner", 1), ("GL",
        "corner", 1), ("GO", "corner", 3), ("GL", "side_y", 3), ("GL", "pass_c", 3), ("GL",
        "side_x", 3), ("GL", "corner", 2), ("GL", "corner", 3), ("GL", "wait_all"), ("GO",
        "wait_all"),
    ),
    (
        ("Y", "hand_over"), ("Y", "corner", 3), ("Y", "corner", 2), ("C", "c1"), ("Y", "corner",
        0), ("C", "c3"), ("Y", "corner", 1), ("Y", "side_y", 3), ("C", "c2"), ("O", "corner",
        3), ("Y", "side_x", 3), ("Y", "side_y", 2), ("C", "c4"), ("Y", "side_x", 2), ("O",
        "corner", 0), ("O", "corner", 2), ("C", "c5a"), ("Y", "line", 3), ("O", "side_y", 3),
        ("Y", "give_d", 2), ("O", "give_d", 3), ("Y", "side_y", 1), ("O", "side_x", 2), ("O",
        "side_x", 3), ("O", "corner", 1), ("C", "c6"), ("Y", "side_x", 1), ("O", "side_y", 2),
        ("O", "give_c", 2), ("Y", "give_c", 3), ("C", "c5b"), ("C", "c8"), ("O", "side_x", 0),
        ("L", "corner", 0), ("O", "side_y", 1), ("L", "corner", 3), ("O", "give_d", 1), ("O",
        "give_c", 3), ("O", "side_x", 1), ("O", "line", 3), ("O", "give_d", 2), ("L", "corner",
        1), ("L", "corner", 2), ("Y", "give_d", 3), ("O", "give_c", 1), ("O", "give_c", 0),
        ("Y", "give_c", 1), ("O", "line", 2), ("O", "side_y", 0), ("Y", "give_c", 2), ("O",
        "line", 1), ("O", "give_d", 0), ("Y", "give_d", 1), ("L", "side_y", 3), ("L", "side_x",
        3), ("L", "give_d", 3), ("L", "give_c", 3), ("L", "side_y", 2), ("L", "side_x", 2),
        ("L", "side_x", 0), ("L", "give_c", 2), ("L", "side_y", 1), ("L", "side_x", 1), ("Y",
        "side_y", 0), ("O", "last"), ("GO", "begin"), ("L", "give_c", 1), ("Y", "line", 1),
        ("L", "line", 3), ("Y", "side_x", 0), ("GO", "line", 2), ("GO", "line", 1), ("L",
        "give_d", 1), ("Y", "give_d", 0), ("Y", "give_c", 0), ("GO", "side_y", 0), ("GO",
        "own_d"), ("L", "line", 1), ("L", "give_d", 2), ("L", "line", 2), ("L", "side_y", 0),
        ("L", "give_c", 0), ("GO", "side_x", 0), ("L", "give_d", 0), ("GO", "own_c"), ("Y",
        "line", 2), ("GO", "pass_d", 1), ("GO", "pass_c", 2), ("GO", "line", 3), ("C", "c7"),
        ("GO", "pass_d", 2), ("Y", "last"), ("GO", "pass_d", 3), ("L", "last"), ("GL", "begin"),
        ("GO", "side_y", 2), ("GL", "line", 1), ("GL", "line", 2), ("GL", "side_y", 0), ("GO",
        "side_y", 1), ("GL", "line", 3), ("GO", "pass_c", 1), ("GL", "side_x", 0), ("GL",
        "own_d"), ("GL", "own_c"), ("GO", "side_x", 1), ("GO", "pass_c", 3), ("GO", "side_x",
        3), ("GL", "pass_d", 1), ("GL", "pass_d", 2), ("GL", "pass_c", 2), ("GL", "pass_c", 1),
        ("GO", "side_x", 2), ("GL", "side_y", 2), ("GL", "pass_d", 3), ("GL", "pass_c", 3),
        ("GL", "side_x", 2), ("GO", "side_y", 3), ("GL", "side_y", 3), ("GL", "side_y", 1),
        ("GL", "side_x", 3), ("GL", "corner", 2), ("GO", "corner", 0), ("GL", "side_x", 1),
        ("GL", "corner", 0), ("GO", "corner", 3), ("GL", "corner", 3), ("GO", "corner", 1),
        ("GO", "corner", 2), ("GO", "wait_all"), ("GL", "corner", 1), ("GL", "wait_all"),
    ),
)
LAYER_ORDER = (
    (
        ("U", "begin"), ("C", "a1"), ("U", "side_x", 0), ("U", "side_y", 0), ("U", "line", 1),
        ("U", "own_d"), ("C", "prep"), ("U", "own_c"), ("C", "a2"), ("X", "begin"), ("X",
        "line", 1), ("X", "side_y", 0), ("X", "side_x", 0), ("X", "own_d"), ("S", "go", 0, 1),
        ("U", "corner", 0), ("X", "own_c"), ("U", "line", 3), ("U", "line", 2), ("S", "go", 0,
        0), ("X", "corner", 0), ("U", "pass_c", 3), ("U", "pass_d", 3), ("S", "go", 3, 0), ("U",
        "side_x", 3), ("S", "go", 2, 0), ("S", "go", 1, 0), ("X", "line", 3), ("X", "pass_c",
        1), ("U", "side_y", 3), ("X", "pass_c", 3), ("X", "side_x", 3), ("X", "side_x", 1),
        ("X", "pass_d", 3), ("X", "side_y", 3), ("S", "go", 1, 3), ("U", "corner", 3), ("X",
        "corner", 3), ("X", "line", 2), ("S", "go", 3, 3), ("X", "pass_d", 1), ("X", "pass_c",
        2), ("X", "side_y", 1), ("R", "corner", 3), ("S", "go", 2, 3), ("X", "pass_d", 2), ("U",
        "pass_c", 1), ("X", "side_y", 2), ("X", "side_x", 2), ("U", "pass_c", 2), ("S", "go", 0,
        2), ("U", "side_x", 2), ("U", "pass_d", 1), ("S", "go", 0, 3), ("U", "pass_d", 2), ("U",
        "side_y", 2), ("R", "side_x", 3), ("R", "give_c", 3), ("U", "side_y", 1), ("R",
        "side_y", 3), ("R", "give_d", 3), ("X", "corner", 2), ("S", "go", 1, 2), ("U", "corner",
        2), ("U", "side_x", 1), ("S", "go", 3, 2), ("R", "line", 3), ("R", "corner", 2), ("X",
        "corner", 1), ("S", "go", 2, 2), ("U", "corner", 1), ("R", "side_y", 2), ("R", "side_x",
        2), ("R", "give_d", 2), ("S", "go", 3, 1), ("R", "give_c", 2), ("S", "go", 1, 1), ("R",
        "corner", 1), ("R", "corner", 0), ("R", "line", 2), ("S", "go", 2, 1), ("S", "dw", 0),
        ("R", "side_y", 1), ("R", "give_d", 1), ("S", "dw", 1), ("R", "side_x", 1), ("S", "dw",
        2), ("R", "side_y", 0), ("R", "give_c", 1), ("S", "dw", 3), ("R", "side_x", 0), ("S",
        "dw", 4), ("R", "give_d", 0), ("R", "give_c", 0), ("R", "line", 1), ("S", "dw", 5),
        ("S", "dw", 6), ("S", "dw", 7), ("R", "last"),
    ),
    (
        ("U", "begin"), ("C", "a1"), ("U", "line", 2), ("U", "line", 1), ("C", "a2"), ("U",
        "side_y", 0), ("X", "begin"), ("U", "line", 3), ("C", "prep"), ("U", "pass_d", 1), ("U",
        "pass_c", 1), ("X", "line", 1), ("U", "pass_d", 3), ("U", "side_y", 1), ("X", "side_x",
        0), ("U", "side_x", 1), ("X", "pass_d", 1), ("U", "side_x", 0), ("X", "own_c"), ("X",
        "pass_c", 1), ("U", "pass_c", 3), ("X", "line", 3), ("X", "side_x", 1), ("X", "pass_c",
        3), ("U", "side_x", 3), ("X", "side_y", 0), ("X", "pass_d", 3), ("X", "line", 2), ("S",
        "go", 1, 0), ("X", "own_d"), ("S", "go", 2, 0), ("U", "side_y", 3), ("S", "go", 0, 1),
        ("X", "pass_c", 2), ("U", "corner", 0), ("U", "own_c"), ("X", "pass_d", 2), ("X",
        "side_y", 1), ("X", "corner", 0), ("S", "go", 0, 0), ("X", "side_y", 3), ("X", "side_x",
        3), ("S", "go", 1, 1), ("U", "corner", 1), ("S", "go", 0, 2), ("S", "go", 2, 3), ("X",
        "corner", 1), ("U", "pass_c", 2), ("U", "own_d"), ("X", "side_x", 2), ("S", "go", 3, 0),
        ("U", "pass_d", 2), ("U", "side_y", 2), ("U", "corner", 3), ("U", "side_x", 2), ("R",
        "corner", 0), ("X", "corner", 3), ("S", "go", 2, 1), ("X", "side_y", 2), ("S", "go", 3,
        3), ("S", "go", 1, 3), ("U", "corner", 2), ("R", "corner", 3), ("S", "go", 3, 1), ("R",
        "side_y", 0), ("S", "go", 1, 2), ("R", "side_x", 3), ("R", "corner", 1), ("R", "side_y",
        3), ("X", "corner", 2), ("S", "go", 2, 2), ("R", "give_c", 3), ("R", "side_x", 0), ("S",
        "go", 3, 2), ("R", "give_d", 3), ("S", "go", 0, 3), ("R", "corner", 2), ("S", "dw", 0),
        ("R", "side_y", 1), ("R", "side_x", 1), ("R", "line", 3), ("S", "dw", 1), ("R",
        "give_d", 1), ("R", "side_y", 2), ("S", "dw", 2), ("R", "give_d", 2), ("R", "side_x",
        2), ("S", "dw", 3), ("S", "dw", 4), ("R", "give_c", 2), ("R", "give_c", 1), ("S", "dw",
        5), ("S", "dw", 6), ("S", "dw", 7), ("R", "line", 1), ("R", "line", 2), ("R", "give_d",
        0), ("R", "give_c", 0), ("R", "last"),
    ),
)


def choose(step, values):
    total = 0
    for number, value in enumerate(values):
        total = total + value * jnp.where(step == number, 1, 0)
    return total


SAVED = 15


def layer_kernel(
    local_count,
    tokens_ref,
    cotangent_ref,
    gain_attention_ref,
    gain_feedforward_ref,
    value_router_ref,
    output_router_ref,
    expert_router_ref,
    segments_ref,
    value_ids_ref,
    output_ids_ref,
    ffn_ids_ref,
    query_in,
    key_in,
    value_in,
    output_in,
    first_in,
    second_in,
    rows_out,
    result_out,
    routers,
    all_ids,
    gathered,
    upstream,
    first_ref,
    first_t_ref,
    second_t_ref,
    hidden_parts,
    partial,
    result_stage,
    weight_sems,
    upstream_sems,
    gather_sems,
    reduce_sems,
    result_sems,
    early_sems,
    saved_sems,
    *refs,
):
    place = Place()
    saved_outs, refs = refs[:SAVED], refs[SAVED:]
    saved_refs, refs = refs[:SAVED], refs[SAVED:]
    (
        first_out,
        second_out,
        after_out,
        normed_out,
        normed_ffn_out,
        queries_out,
        keys_out,
        projected_out,
        values_out,
        probability_out,
        mixed_out,
        gated_out,
        gates_out,
        slopes_out,
        expert_slope_out,
    ) = saved_refs
    first_part, second_ref, boxes = refs[0], refs[1], refs[2:]
    saves = [
        pltpu.make_async_copy(src, dst, saved_sems.at[number])
        for number, (src, dst) in enumerate(zip(saved_refs, saved_outs))
    ]
    length, model_width = tokens_ref.shape
    pair = 2 * length
    expert_count = expert_router_ref.shape[0]
    width = gathered.shape[1]
    gate_width = width - model_width
    hidden_width = first_ref.shape[1] // local_count
    narrow, wide = query_in.shape[1], value_in.shape[1]
    mine = pl.ds(pl.multiple_of(place.me * length, length), length)

    pieces = [
        (start, min(wide, start + width), number)
        for number, start in enumerate(range(0, wide, width), 1)
    ]
    value_refs = [
        partial.at[number * model_width : (number + 1) * model_width, : end - start]
        for start, end, number in pieces
    ]
    query_ref = partial.at[:model_width, :narrow]
    key_ref = partial.at[:model_width, narrow : 2 * narrow]
    hidden = first_ref.shape[1]
    gated_hidden = hidden_parts.at[:, :hidden]
    pre_grads = hidden_parts.at[:, hidden:]
    main_columns, side_columns = 2 * hidden, model_width - 2 * hidden
    last_rows = len(pieces) * model_width
    output_parts = [
        (0, wide, slice(0, main_columns), hidden_parts.at[:wide, :])
    ]
    for number, start in enumerate(range(0, wide, model_width), 1):
        end = min(wide, start + model_width)
        place_at = slice(number * side_columns, (number + 1) * side_columns)
        ref = partial.at[last_rows : last_rows + end - start, place_at]
        output_parts.append((start, end, slice(main_columns, None), ref))
    loads = [
        pltpu.make_async_copy(src, dst, weight_sems.at[number])
        for number, (src, dst) in enumerate(
            [
                (query_in, query_ref),
                (key_in, key_ref),
                *(
                    (value_in.at[:, start:end], ref)
                    for (start, end, _), ref in zip(pieces, value_refs)
                ),
                *(
                    (output_in.at[start:end, columns], ref)
                    for start, end, columns, ref in output_parts
                ),
            ]
        )
    ]
    values = {}
    lane = lax.broadcasted_iota(jnp.int32, (length, gates_out.shape[1]), 1).astype(jnp.float32)

    def named(columns):
        ids = values["ids"]
        mask = jnp.zeros(lane.shape, jnp.float32)
        for at in columns:
            mask = jnp.where(lane == ids[:, at : at + 1], 1.0, mask)
        return mask

    ffn_top = ffn_ids_ref.shape[0]

    def a1():
        join_routers(routers, value_router_ref, output_router_ref)
        top = value_ids_ref.shape[1]
        all_ids[...] = jnp.zeros_like(all_ids)
        for head in range(HEADS):
            at = head * top
            all_ids[at : at + top, :] = value_ids_ref[head].astype(jnp.float32) + float(head * ATT_EXP)
            all_ids[16 + at : 16 + at + top, :] = output_ids_ref[head].astype(jnp.float32) + float(
                OUTPUT_LANE + head * ATT_EXP
            )
        all_ids[32 : 32 + ffn_top, :] = ffn_ids_ref[...].astype(jnp.float32)
        values["ids"] = all_ids[...].T
        stream_low = tokens_ref[...]
        stream = stream_low.astype(jnp.float32)
        unit, _ = norm_parts(stream)
        normed = (unit * gain_attention_ref[...]).astype(jnp.bfloat16)
        normed_out[...] = normed
        sig = jax.nn.sigmoid(mm_nt(normed, routers[...]))
        gates = named([*range(HEADS * top), *range(16, 16 + HEADS * top)]) * sig
        gates_out[...] = gates
        slopes_out[...] = gates * (1.0 - sig)
        loads[0].wait()
        queries_out[...] = mm(normed, query_ref[...]).astype(jnp.bfloat16)
        loads[1].wait()
        keys_out[...] = mm(normed, key_ref[...]).astype(jnp.bfloat16)
        for (start, end, _), ref, load in zip(pieces, value_refs, loads[2:]):
            load.wait()
            projected_out[:, start:end] = mm(stream_low, ref[...])
        for head in range(HEADS):
            total = jnp.zeros((length, HEAD), jnp.float32)
            for e in range(ATT_EXP):
                at = head * ATT_EXP + e
                total = total + gates[:, at : at + 1] * projected_out[:, at * HEAD : (at + 1) * HEAD]
            values_out[:, head * HEAD : (head + 1) * HEAD] = total.astype(jnp.bfloat16)
        documents = jnp.broadcast_to(segments_ref[...].astype(jnp.float32), (length, length))
        row = lax.broadcasted_iota(jnp.int32, (length, length), 0)
        column = lax.broadcasted_iota(jnp.int32, (length, length), 1)
        allowed = (documents == documents.T) & (row >= column)
        for head in range(HEADS):
            columns = slice(head * HEAD, (head + 1) * HEAD)
            scores = mm_nt(queries_out[:, columns], keys_out[:, columns]) * (1.0 / math.sqrt(HEAD))
            scores = jnp.where(allowed, scores, NEG_FILL)
            exponent = jnp.exp(scores - jnp.max(scores, axis=-1, keepdims=True))
            probability = exponent / jnp.sum(exponent, axis=-1, keepdims=True)
            probability_out[head] = probability
            mixed = mm(probability.astype(jnp.bfloat16), values_out[:, columns])
            mixed_out[:, columns] = mixed
            for e in range(ATT_EXP):
                at = head * ATT_EXP + e
                gate = gates[:, OUTPUT_LANE + at : OUTPUT_LANE + at + 1]
                gated_out[:, at * HEAD : (at + 1) * HEAD] = (gate * mixed).astype(jnp.bfloat16)
    def a2():
        stream = tokens_ref[...].astype(jnp.float32)
        side = stream[:, main_columns:]
        for (start, end, columns, ref), load in zip(output_parts, loads[2 + len(pieces) :]):
            load.wait()
            if start == 0 and end == wide:
                after_out[:, columns] = stream[:, columns] + mm(gated_out[...], ref[...])
            else:
                side = side + mm(gated_out[:, start:end], ref[...])
        after_out[:, main_columns:] = side
        after = after_out[...]
        gathered[mine, :model_width] = after.astype(jnp.bfloat16)
        unit, _ = norm_parts(after)
        normed_ffn = (unit * gain_feedforward_ref[...]).astype(jnp.bfloat16)
        normed_ffn_out[...] = normed_ffn
        expert_sig = jax.nn.sigmoid(mm_nt(normed_ffn, expert_router_ref[...]))
        expert_gates = named(range(32, 32 + ffn_top))[:, :expert_count] * expert_sig
        gathered[mine, model_width:] = jnp.zeros((length, gate_width), jnp.bfloat16)
        gathered[mine, model_width : model_width + expert_count] = expert_gates.astype(jnp.bfloat16)
        expert_slope_out[...] = jnp.zeros((length, gate_width), jnp.float32)
        expert_slope_out[:, :expert_count] = expert_gates * (1.0 - expert_sig)
        for save in saves[2:]:
            save.start()

    def prep():
        early[1].wait()
        early[2].wait()
        for e in range(local_count):
            columns = slice(e * hidden_width, (e + 1) * hidden_width)
            first_ref[:, columns] = first_part[e]
            first_t_ref[columns, :] = first_part[e].astype(jnp.float32).T.astype(jnp.bfloat16)
            second_t_ref[:, columns] = second_ref[columns, :].astype(jnp.float32).T.astype(jnp.bfloat16)
    computes = {"a1": a1, "a2": a2, "prep": prep}
    pick_row = lax.broadcasted_iota(jnp.int32, (gate_width, first_ref.shape[1]), 0)
    pick_column = lax.broadcasted_iota(jnp.int32, (gate_width, first_ref.shape[1]), 1)
    pick_gates = jnp.where(
        pick_row == place.me * local_count + pick_column // hidden_width, 1.0, 0.0
    ).astype(jnp.bfloat16)
    def result_copy(slot, chip):
        return pltpu.make_async_copy(
            result_stage.at[slot],
            result_out.at[pl.ds(pl.multiple_of(chip * pair, pair), pair)],
            result_sems.at[slot],
        )

    def compute(step, place, reduce, q, j):
        chip = place.chip(q, j)
        rows = pl.ds(pl.multiple_of(chip * pair, pair), pair)
        hidden_pre = mm(gathered[rows, :model_width], first_ref[...])
        back = mm(upstream[rows, :], second_t_ref[...])
        gates = mm(gathered[rows, model_width:], pick_gates)
        square = hidden_pre * hidden_pre
        bent = jnp.tanh(GELU_C * hidden_pre * (1.0 + GELU_K * square))
        grow = 0.5 * (1.0 + bent)
        slope = grow + 0.5 * hidden_pre * (1.0 - bent * bent) * (
            GELU_C * (1.0 + 3.0 * GELU_K * square)
        )
        hidden = (hidden_pre * grow).astype(jnp.bfloat16).astype(jnp.float32)
        gated = (gates * hidden).astype(jnp.bfloat16)
        pre_grad = (gates * back * slope).astype(jnp.bfloat16)
        gated_hidden[rows, :] = gated
        pre_grads[rows, :] = pre_grad
        k = 4 * q + j
        to = pl.ds(pl.multiple_of(k * pair, pair), pair)
        partial[to, :model_width] = mm(pre_grad, first_t_ref[...]).astype(jnp.bfloat16)
        product = hidden * back
        column = lax.broadcasted_iota(jnp.int32, (pair, gate_width), 1) - place.me * local_count
        gate_grad = jnp.zeros((pair, gate_width), jnp.float32)
        for e in range(local_count):
            own_sum = jnp.sum(
                product[:, e * hidden_width : (e + 1) * hidden_width], axis=1, keepdims=True
            )
            gate_grad = jnp.where(column == e, own_sum, gate_grad)
        partial[to, model_width:] = gate_grad.astype(jnp.bfloat16)
        reduce.copy("core", k).start()
        slot = step % 2

        @pl.when(step >= 2)
        def _():
            result_copy(slot, chip).wait()

        result_stage[slot] = mm(gated, second_ref[...]).astype(jnp.bfloat16)
        result_copy(slot, chip).start()

    piece = gathered.shape[0] // 8

    def weight_piece(number):
        rows = pl.ds(pl.multiple_of(number * piece, piece), piece)
        second = mm_tn(gated_hidden[rows, :], upstream[rows, :])
        first = mm_tn(pre_grads[rows, :], gathered[rows, :model_width])

        @pl.when(number == 0)
        def _():
            second_out[...] = second
            first_out[...] = first

        @pl.when(number > 0)
        def _():
            second_out[...] += second
            first_out[...] += first

    def run(middle):
        known = place.fixed(middle)

        def share(k, core):
            return partial.at[pl.ds(pl.multiple_of(k * pair + core * length, length), length)]

        items = {
            "U": Gather("U", known, upstream, length, upstream_sems),
            "X": Gather("X", known, gathered, length, gather_sems),
            "R": Reduce(
                "R",
                known,
                lambda k: share(k, known.core),
                lambda k: share(k, 1 - known.core),
                boxes,
                reduce_sems,
            ),
        }

        def put(at, total):
            rows_out[at, :] = total

        def act(events):
            for name, method, *arguments in events:
                if name == "C":
                    computes[method]()
                elif method == "last":
                    items[name].last(put)
                else:
                    getattr(items[name], method)(*arguments)

        stops, pieces_at, waiting = [], [], []
        for event in LAYER_ORDER[middle]:
            if event[0] != "S":
                waiting.append(event)
                continue
            (stops if event[1] == "go" else pieces_at).append((event[2:], waiting))
            waiting = []
        act(stops[0][1])

        def walk(step, carry):
            for number, (_, events) in enumerate(stops):
                if number and events:
                    pl.when(step == number)(functools.partial(act, events))
            q = choose(step, [stop[0] for stop, _ in stops])
            j = choose(step, [stop[1] for stop, _ in stops])
            items["X"].whole(q, j)
            items["U"].whole(q, j)
            compute(step, known, items["R"], q, j)
            return carry

        lax.fori_loop(0, len(stops), walk, 0)
        items["U"].finish()

        def give(step, carry):
            for number, (_, events) in enumerate(pieces_at):
                if events:
                    pl.when(step == number)(functools.partial(act, events))
            weight_piece(step)
            return carry

        lax.fori_loop(0, len(pieces_at), give, 0)
        for save in saves[:2]:
            save.start()
        items["X"].finish()
        act(waiting)
        items["R"].finish()

    early = [
        pltpu.make_async_copy(src, dst, early_sems.at[number])
        for number, (src, dst) in enumerate(
            ((cotangent_ref, upstream.at[mine]), (first_in, first_part), (second_in, second_ref))
        )
    ]
    for copy in (*early, *loads):
        copy.start()
    enter(place)
    early[0].wait()
    pl.when(place.middle == 0)(lambda: run(0))
    pl.when(place.middle == 1)(lambda: run(1))
    for slot in range(2):
        result_copy(slot, 0).wait()
    for save in saves:
        save.wait()


def call_layer(
    tokens,
    cotangent,
    gains,
    weights,
    routers,
    segments,
    value_ids,
    output_ids,
    ffn_ids,
    expert_first,
    expert_second,
):
    length, model_width = tokens.shape
    local_count, _, hidden_width = expert_first.shape
    hidden = local_count * hidden_width
    expert_count = routers[2].shape[0]
    gate_width = -(-expert_count // 128) * 128
    width = model_width + gate_width
    total = GRID[0] * GRID[1] * length
    wide = weights[3].shape[0]
    narrow = HEADS * HEAD
    low, full = jnp.bfloat16, jnp.float32
    shapes = (
        ((length, width), full),
        ((hidden, model_width), full),
        ((hidden, model_width), full),
        ((length, model_width), full),
        ((length, model_width), low),
        ((length, model_width), low),
        ((length, narrow), low),
        ((length, narrow), low),
        ((length, wide), full),
        ((length, narrow), low),
        ((HEADS, length, length), full),
        ((length, narrow), full),
        ((length, wide), low),
        ((length, 128), full),
        ((length, 128), full),
        ((length, gate_width), full),
        ((total, model_width), low),
    )
    vmem = pl.BlockSpec(memory_space=pltpu.VMEM)
    hbm = pl.BlockSpec(memory_space=pl.ANY)
    sems = pltpu.SemaphoreType.DMA((2, N_SEM))
    inputs, scratch = 17, 17

    def kernel(*refs):
        rows_out, *saved_outs, result_out = refs[inputs : inputs + SAVED + 2]
        rest = refs[inputs + SAVED + 2 :]
        layer_kernel(
            local_count,
            *refs[:inputs],
            rows_out,
            result_out,
            *rest[:scratch],
            *saved_outs,
            *rest[scratch:],
        )

    return pl.pallas_call(
        kernel,
        out_shape=tuple(jax.ShapeDtypeStruct(*shape) for shape in shapes),
        in_specs=[vmem, hbm] + [vmem] * 9 + [hbm] * 6,
        out_specs=(vmem, *([hbm] * (len(shapes) - 1))),
        scratch_shapes=[
            pltpu.VMEM((128, model_width), low),
            pltpu.VMEM((128, length), full),
            pltpu.VMEM((total, width), low),
            pltpu.VMEM((total, model_width), low),
            pltpu.VMEM((model_width, hidden), low),
            pltpu.VMEM((hidden, model_width), low),
            pltpu.VMEM((model_width, hidden), low),
            pltpu.VMEM((total, 2 * hidden), low),
            pltpu.VMEM((total, width), low),
            pltpu.VMEM((2, 2 * length, model_width), low),
            pltpu.SemaphoreType.DMA((3 + -(-wide // width) + -(-wide // model_width),)),
            sems,
            sems,
            sems,
            pltpu.SemaphoreType.DMA((2,)),
            pltpu.SemaphoreType.DMA((3,)),
            pltpu.SemaphoreType.DMA((SAVED,)),
            *(pltpu.VMEM(*shape) for shape in shapes[1:-1]),
            pltpu.VMEM(expert_first.shape, low),
            pltpu.VMEM((hidden, model_width), low),
            *reduce_scratch("R", length, width),
        ],
        compiler_params=pltpu.CompilerParams(
            collective_id=0, has_side_effects=True, vmem_limit_bytes=VMEM_LIMIT
        ),
        name="layer",
    )(
        tokens,
        cotangent,
        *gains,
        *routers,
        segments,
        value_ids.transpose(1, 2, 0),
        output_ids.transpose(1, 2, 0),
        ffn_ids.T,
        *weights,
        expert_first,
        expert_second.reshape(hidden, model_width),
    )


def general_body(
    tokens,
    cotangent,
    gain_attention,
    gain_feedforward,
    query_weight,
    key_weight,
    value_weight,
    output_weight,
    value_router,
    output_router,
    expert_router,
    expert_first,
    expert_second,
    segments,
    value_ids,
    output_ids,
    ffn_ids,
):
    owner_total = lax.axis_size("dp") * lax.axis_size("expert")
    local_count = expert_first.shape[0]
    expert_count = local_count * owner_total
    shared = (
        gain_attention,
        query_weight,
        key_weight,
        value_weight,
        output_weight,
        value_router,
        output_router,
    )
    stream = tokens.astype(jnp.float32)
    upstream = cotangent.astype(jnp.float32)
    after_attention, saved_parts = attention_forward(
        stream, segments[0], value_ids[0], output_ids[0], shared
    )
    normed_low = layer_norm(after_attention, gain_feedforward).astype(jnp.bfloat16)
    logits = jnp.dot(normed_low, expert_router, preferred_element_type=jnp.float32)
    sigmoid_out = jax.nn.sigmoid(logits)
    dense_gates = sigmoid_out * expert_mask(ffn_ids[0], expert_count)
    expert_slope = dense_gates * (1.0 - sigmoid_out)
    result, token_grad, gate_back, first_sum, second_sum = expert_exchange(
        after_attention.astype(jnp.bfloat16),
        cotangent,
        dense_gates.astype(jnp.bfloat16),
        expert_first,
        expert_second,
        max(1, owner_total // 32),
    )
    logit_grad = (gate_back.astype(jnp.float32) * expert_slope).astype(jnp.bfloat16)
    router_sum = jnp.einsum("sa,sb->ab", normed_low, logit_grad, preferred_element_type=jnp.float32)
    normed_grad = jnp.einsum(
        "sb,ab->sa", logit_grad, expert_router, preferred_element_type=jnp.float32
    )
    norm_value, norm_pull = jax.vjp(layer_norm, after_attention, gain_feedforward)
    after_extra, feed_gain_part = norm_pull(normed_grad)
    after_grad = upstream + token_grad.astype(jnp.float32) + after_extra
    stream_grad, attention_parts = attention_backward(after_grad, saved_parts, stream, shared)
    gain_part, query_part, key_part, value_part, output_part, value_router_part, output_router_part = attention_parts
    parts = (
        query_part,
        key_part,
        value_part,
        value_router_part,
        output_router_part,
        router_sum,
        gain_part[:, None],
        feed_gain_part[:, None],
    )
    low = jnp.concatenate([part.astype(jnp.bfloat16) for part in parts], axis=1)
    low = jnp.pad(low, ((0, 0), (0, -low.shape[1] % 256)))
    output_low = output_part.astype(jnp.bfloat16)
    low, output_low = lax.psum((low, output_low), BOTH)
    block_output = (after_attention + result.astype(jnp.float32)).astype(jnp.bfloat16)
    summed, start = [], 0
    for part in parts:
        summed.append(low[:, start : start + part.shape[1]].astype(jnp.float32))
        start += part.shape[1]
    query_sum, key_sum, value_sum, value_router_sum, output_router_sum, router_sum, *gains = summed
    summed = (
        gains[0][:, 0],
        gains[1][:, 0],
        query_sum,
        key_sum,
        value_sum,
        output_low.astype(jnp.float32),
        value_router_sum,
        output_router_sum,
        router_sum,
    )
    return (
        block_output,
        stream_grad,
        *summed,
        first_sum,
        second_sum,
    )


def kernel_body(
    tokens,
    cotangent,
    gain_attention,
    gain_feedforward,
    query_weight,
    key_weight,
    value_weight,
    output_weight,
    value_router,
    output_router,
    expert_router,
    expert_first,
    expert_second,
    segments,
    value_ids,
    output_ids,
    ffn_ids,
):
    gains = (gain_attention[None], gain_feedforward[None])
    weights = (query_weight, key_weight, value_weight, output_weight)
    routers = (value_router.T, output_router.T, expert_router.T)
    rows_sum, first_sum, second_sum, *saved, result = call_layer(
        tokens,
        cotangent,
        gains,
        weights,
        routers,
        segments,
        value_ids[0],
        output_ids[0],
        ffn_ids[0],
        expert_first,
        expert_second,
    )
    block_output, stream_grad, low, output_low = call_backward(
        rows_sum, tokens, cotangent, gains, routers, saved, weights, result
    )
    (
        query_sum,
        key_sum,
        value_sum,
        output_sum,
        value_router_sum,
        output_router_sum,
        expert_router_sum,
        gain_attention_sum,
        gain_feedforward_sum,
        first_sum,
        second_sum,
        block_output,
        stream_grad,
    ) = call_widen(
        low,
        output_low,
        first_sum,
        second_sum,
        block_output,
        stream_grad,
        query_weight.shape[1],
        expert_router.shape[1],
        expert_first.shape[0],
    )
    return (
        block_output,
        stream_grad,
        gain_attention_sum[0],
        gain_feedforward_sum[0],
        query_sum,
        key_sum,
        value_sum,
        output_sum,
        value_router_sum.T,
        output_router_sum.T,
        expert_router_sum.T,
        first_sum,
        second_sum,
    )


def body(*args):
    if (lax.axis_size("dp"), lax.axis_size("expert")) == GRID:
        return kernel_body(*args)
    return general_body(*args)


def solution(mesh):
    placed = (
        P(("dp", "expert"), None),
        P(("dp", "expert"), None),
        P(),
        P(),
        P(),
        P(),
        P(),
        P(),
        P(),
        P(),
        P(),
        P(("dp", "expert"), None, None),
        P(("dp", "expert"), None, None),
        P(("dp", "expert"), None),
        P(None, ("dp", "expert"), None, None),
        P(None, ("dp", "expert"), None, None),
        P(None, ("dp", "expert"), None),
    )
    return jax.shard_map(
        body,
        mesh=mesh,
        in_specs=placed,
        out_specs=(
            P(("dp", "expert"), None),
            P(("dp", "expert"), None),
            P(),
            P(),
            P(),
            P(),
            P(),
            P(),
            P(),
            P(),
            P(),
            P(("dp", "expert"), None, None),
            P(("dp", "expert"), None, None),
        ),
        check_vma=False,
    )
```
